32 devices in a mesh: seq: 8 (over z, x), head: 4 (over y, core).
Axes of the slice: x: 2, y: 2, z: 4, core: 2. Of those that a mesh axis runs over, the one named last changes fastest.
Arguments:
- stream_one: bfloat16 [4096, 1024], P('seq', 'head'), may hold values from -6 to 6
- stream_two: bfloat16 [4096, 1024], P('seq', 'head'), may hold values from -6 to 6
- grad_one: bfloat16 [4096, 1024], P('seq', 'head'), may hold values from -6 to 6
- grad_two: bfloat16 [4096, 1024], P('seq', 'head'), may hold values from -6 to 6
- query_weight: bfloat16 [1024, 1024], P('seq', 'head'), may hold values from -3 to 3
- value_weight: bfloat16 [1024, 1024], P('seq', 'head'), may hold values from -0.1875 to 0.1875
- merge_weight: bfloat16 [1024, 1024], P('head', 'seq'), may hold values from -1.5 to 1.5
- expand_weight: bfloat16 [1024, 4096], P('seq', 'head'), may hold values from -0.1875 to 0.1875
- shrink_weight: bfloat16 [4096, 1024], P('head', 'seq'), may hold values from -0.09375 to 0.09375
- first_gain: float32 [1024], P('head'), may hold values from 0.1 to 1.9
- first_bias: float32 [1024], P('head'), may hold values from -2.5 to 2.5
- second_gain: float32 [1024], P('head'), may hold values from 0.1 to 1.9
- second_bias: float32 [1024], P('head'), may hold values from -2.5 to 2.5
- bucket_ids: int32 [4, 4096], replicated, may hold values from 0 to 72, as said below
- sort_order: int32 [4, 4096], replicated, may hold values from 0 to 4095, as said below
Outputs:
- result_one: bfloat16 [4096, 1024], P('seq', 'head')
- result_two: bfloat16 [4096, 1024], P('seq', 'head')
- input_grad_one: bfloat16 [4096, 1024], P('seq', 'head')
- input_grad_two: bfloat16 [4096, 1024], P('seq', 'head')
- grad_query_weight: float32 [1024, 1024], P('seq', 'head')
- grad_value_weight: float32 [1024, 1024], P('seq', 'head')
- grad_merge_weight: float32 [1024, 1024], P('head', 'seq')
- grad_expand_weight: float32 [1024, 4096], P('seq', 'head')
- grad_shrink_weight: float32 [4096, 1024], P('head', 'seq')
- grad_first_gain: float32 [1024], P('head')
- grad_first_bias: float32 [1024], P('head')
- grad_second_gain: float32 [1024], P('head')
- grad_second_bias: float32 [1024], P('head')
The draws below stay inside these ranges and needn't reach their ends.
Inputs may be any that keep to these rules, and one draw needn't show every extreme that they name: Tokens whose sorted positions of round r fall in the d-th block of 512 positions have bucket_ids from d * (9) to (d + 1) * 9. Of the 512 tokens of one device, 0, 64 or 128 fall into one such block in a round, and 128 occurs in every round. sort_order[r] lists every token once, ordered by bucket_ids[r]; tokens of one bucket stand in an order drawn from the seed.
All inputs are finite; a program needn't handle non-finite values.
Results may differ from the reference program's by a relative error of at most 0.015.
Values may be sent and summed in bfloat16 or wider, within the bound.
A program may use at most 128 MiB of HBM per device.

```python
import jax
import jax.numpy as jnp
from jax import lax

D = 1024
HEADS = 8
HEAD_DIM = 128
FF = 4096
GROUP = 64
ROUNDS = 4
TOK_DEV = 512
TOKENS = 4096
N_SEQ = 8


def lsh_layout(key):
    share = TOK_DEV // N_SEQ
    inner_count = TOK_DEV // GROUP
    edge_rows = GROUP // 2
    streams = jax.random.split(key, 4)
    offset = jax.random.randint(streams[0], (ROUNDS, 1, 1), 0, N_SEQ)
    source = jnp.arange(N_SEQ, dtype=jnp.int32)[None, :, None]
    target = jnp.arange(N_SEQ, dtype=jnp.int32)[None, None, :]
    relative = (target - source - offset) % N_SEQ
    counts = share + share * (relative == 0).astype(jnp.int32) - share * (relative == 1).astype(jnp.int32)
    bounds = jnp.cumsum(counts, axis=2)
    scores = jax.random.randint(streams[1], (ROUNDS, N_SEQ, TOK_DEV), 0, 1 << 16) * TOK_DEV + jnp.arange(TOK_DEV, dtype=jnp.int32)[None, None, :]
    ranks = jnp.argsort(jnp.argsort(scores, axis=-1), axis=-1)
    target_block = jnp.sum((bounds[:, :, None, :] <= ranks[..., None]).astype(jnp.int32), axis=-1).reshape(ROUNDS, TOKENS)
    shuffle = jax.random.randint(streams[2], (ROUNDS, TOKENS), 0, 1 << 12) * TOKENS + jnp.arange(TOKENS, dtype=jnp.int32)[None, :]
    first_order = jnp.argsort(shuffle, axis=-1)
    blocks_then = jnp.take_along_axis(target_block, first_order, 1)
    layout = jnp.take_along_axis(first_order, jnp.argsort(blocks_then, axis=-1, stable=True), 1)
    places = jax.vmap(lambda line: jnp.zeros_like(line).at[line].set(jnp.arange(TOKENS, dtype=jnp.int32)))(layout)
    rank_in = places - target_block * TOK_DEV
    base = target_block * (inner_count + 1)
    inner = jax.random.randint(streams[3], (ROUNDS, TOKENS), 1, inner_count + 1)
    bucket = jnp.where(rank_in < edge_rows, base, jnp.where(rank_in >= TOK_DEV - edge_rows, base + inner_count + 1, base + inner)).astype(jnp.int32)
    order = jnp.argsort(bucket * TOKENS + places, axis=-1)
    return (bucket, order.astype(jnp.int32))


def draw_bucket_ids(key, part):
    return lsh_layout(key)[0]


def draw_sort_order(key, part):
    return lsh_layout(key)[1]


def raised(result, rng, source, target, blocks, factor):
    owner, partner = [(jnp.arange(result.shape[position]) // (result.shape[position] // blocks)).reshape([-1 if axis == position else 1 for axis in range(result.ndim)]) for position in (source, target)]
    chosen = jax.random.permutation(rng, blocks)[partner]
    strong = (owner == chosen) | (owner == (partner + blocks // 2) % blocks)
    return jnp.where(strong, factor * result, result)


def shard_levels(stream_key, shape, cuts, least, high):
    def one(position, blocks):
        steps = jax.random.uniform(jax.random.fold_in(jax.random.fold_in(stream_key, 6), position), (blocks,), jnp.float32, least / len(cuts), high / len(cuts))
        return jnp.repeat(jnp.exp(steps), shape[position] // blocks).reshape((-1,) + (1,) * (len(shape) - position - 1))

    level = one(*cuts[0])
    for cut in cuts[1:]:
        level = level * one(*cut)
    return level


def scatter_about(key, shape, width, most, cuts=(), held_as=jnp.bfloat16):
    drawn = width * jax.random.normal(key, shape, jnp.float32)
    if cuts:
        drawn = drawn * shard_levels(key, shape, cuts, -0.22, 0.18)
    return jnp.clip(drawn, -most, most).astype(held_as)


def noise_with(key, dims, scale, most, cuts, heavy, held_as=jnp.bfloat16):
    array = scale * jax.random.normal(key, dims, jnp.float32)
    if cuts:
        array = array * shard_levels(key, dims, cuts, -0.22, 0.18)
    return jnp.clip(raised(array, jax.random.fold_in(key, 3), *heavy), -most, most).astype(held_as)


def setup_inputs(seed: int = 0) -> dict:
    arg_keys = jax.random.split(jax.random.key(seed), 16)
    stream_one = scatter_about(arg_keys[0], (TOKENS, D), 1.0, 6.0, ((0, 8), (1, 4)))
    stream_two = noise_with(arg_keys[1], (TOKENS, D), 1.0, 6.0, ((0, 8), (1, 4)), (0, 1, 8, 2.0))
    grad_one = noise_with(arg_keys[2], (TOKENS, D), 1.0, 6.0, ((0, 8), (1, 4)), (0, 1, 8, 2.0))
    grad_two = noise_with(arg_keys[3], (TOKENS, D), 1.0, 6.0, ((0, 8), (1, 4)), (0, 1, 8, 2.0))
    query_weight = scatter_about(arg_keys[4], (D, D), (max(D // (2 * HEAD_DIM), 1)) ** -0.5, 3.0, ((0, 8), (1, 4)))
    value_weight = scatter_about(arg_keys[5], (D, D), D ** -0.5, 0.1875, ((0, 8), (1, 4)))
    merge_weight = scatter_about(arg_keys[6], (D, D), (max(D // 64, 1)) ** -0.5, 1.5, ((0, 4), (1, 8)))
    expand_weight = scatter_about(arg_keys[7], (D, FF), D ** -0.5, 0.1875, ((0, 8), (1, 4)))
    shrink_weight = scatter_about(arg_keys[8], (FF, D), FF ** -0.5, 0.09375, ((0, 4), (1, 8)))
    first_gain = jnp.clip(1.0 + 0.18 * jax.random.normal(arg_keys[9], (D,), jnp.float32), 0.1, 1.9)
    first_bias = scatter_about(arg_keys[10], (D,), 0.5, 2.5, ((0, 4),), jnp.float32)
    second_gain = jnp.clip(1.0 + 0.18 * jax.random.normal(arg_keys[11], (D,), jnp.float32), 0.1, 1.9)
    second_bias = scatter_about(arg_keys[12], (D,), 0.5, 2.5, ((0, 4),), jnp.float32)
    bucket_ids = draw_bucket_ids(jax.random.fold_in(arg_keys[15], 71), 0)
    sort_order = draw_sort_order(jax.random.fold_in(arg_keys[15], 71), 0)
    return {"stream_one": stream_one, "stream_two": stream_two, "grad_one": grad_one, "grad_two": grad_two, "query_weight": query_weight, "value_weight": value_weight, "merge_weight": merge_weight, "expand_weight": expand_weight, "shrink_weight": shrink_weight, "first_gain": first_gain, "first_bias": first_bias, "second_gain": second_gain, "second_bias": second_bias, "bucket_ids": bucket_ids, "sort_order": sort_order}


@jax.custom_vjp
def low(v):
    return lax.optimization_barrier(v.astype(jnp.bfloat16)).astype(jnp.float32)

@jax.custom_vjp
def low_back(v):
    return v

def low_keep(v):
    return (low(v), None)

def low_pass(kept, grad):
    return (grad,)

def back_keep(v):
    return (v, None)

def back_low(kept, grad):
    return (low(grad),)
low.defvjp(low_keep, low_pass)
low_back.defvjp(back_keep, back_low)
masked_score = -1000000000.0
own_score = -100000.0

def matmul(left, right):
    return jnp.dot(left, right, precision=lax.Precision.HIGHEST, preferred_element_type=jnp.float32)

def layer_norm(value, gain, shift):
    center = lax.optimization_barrier(jnp.mean(value, -1, keepdims=True))
    offset = value - center
    spread = lax.optimization_barrier(jnp.mean(offset * offset, -1, keepdims=True))
    return offset * lax.rsqrt(spread + 1e-05) * gain + shift

def attend_block(parts):
    query, key_unit, key_value, query_place, key_place, query_bucket, key_bucket = parts
    raw = jnp.einsum('ncha,nkha->nhck', query, key_unit, precision=lax.Precision.HIGHEST) * HEAD_DIM ** (-0.5)
    raw = low_back(raw)
    allowed = (key_place[:, None, :] <= query_place[:, :, None]) & (key_bucket[:, None, :] == query_bucket[:, :, None])
    itself = key_place[:, None, :] == query_place[:, :, None]
    masked = jnp.where(allowed[:, None], raw, masked_score)
    masked = jnp.where(itself[:, None], own_score, masked)
    totals = jax.nn.logsumexp(masked, axis=-1)
    probs = low(jnp.exp(masked - totals[..., None]))
    output = jnp.einsum('nhck,nkha->ncha', probs, key_value, precision=lax.Precision.HIGHEST)
    return (low(low_back(output)), jnp.transpose(totals, (0, 2, 1)))

def round_attend(query_all, value_all, order_round, bucket_round):
    count = query_all.shape[0]
    sorted_query = query_all[order_round]
    sorted_value = value_all[order_round]
    unit = low(sorted_query * lax.rsqrt(lax.optimization_barrier(jnp.sum(sorted_query * sorted_query, -1, keepdims=True)) + 1e-06))
    sorted_bucket = bucket_round[order_round]
    groups = count // GROUP

    def grouped(value):
        return value.reshape((groups, GROUP) + value.shape[1:])

    def with_prior(value):
        pieces = grouped(value)
        return jnp.concatenate([pieces, jnp.roll(pieces, 1, axis=0)], axis=1)
    blocks = count // TOK_DEV

    def blocked(value):
        return value.reshape((blocks, TOK_DEV // GROUP) + value.shape[1:])
    inputs = (grouped(sorted_query), with_prior(unit), with_prior(sorted_value), grouped(order_round), with_prior(order_round), grouped(sorted_bucket), with_prior(sorted_bucket))
    output, totals = lax.map(jax.checkpoint(attend_block), tuple((blocked(item) for item in inputs)))
    output = output.reshape(count, HEADS, HEAD_DIM)
    totals = totals.reshape(count, HEADS)
    inverse = jnp.zeros((count,), jnp.int32).at[order_round].set(jnp.arange(count, dtype=jnp.int32))
    return (output[inverse], totals[inverse])

def layer(stream_one, stream_two, query_weight, value_weight, merge_weight, expand_weight, shrink_weight, first_gain, first_bias, second_gain, second_bias, bucket_ids, sort_order):
    normed_one = low(layer_norm(stream_two, first_gain, first_bias))
    queries = low(low_back(matmul(normed_one, query_weight))).reshape(TOKENS, HEADS, HEAD_DIM)
    values = low(low_back(matmul(normed_one, value_weight))).reshape(TOKENS, HEADS, HEAD_DIM)
    outputs = []
    totals = []
    for turn in range(ROUNDS):
        output, total = jax.checkpoint(round_attend)(queries, values, sort_order[turn], bucket_ids[turn])
        outputs.append(output)
        totals.append(total)
    outputs = jnp.stack(outputs, 0)
    mix = jax.nn.softmax(jnp.stack(totals, 0), axis=0)
    attended = low(low_back(lax.optimization_barrier(jnp.sum(mix[..., None] * outputs, 0)))).reshape(TOKENS, D)
    sum_one = stream_one + low_back(matmul(attended, merge_weight))

    def feed_block(rows):
        normed_two = low(layer_norm(rows, second_gain, second_bias))
        hidden = low_back(matmul(normed_two, expand_weight))
        active = low(jax.nn.gelu(hidden, approximate=False))
        return matmul(active, shrink_weight)
    feed = lax.map(jax.checkpoint(feed_block), sum_one.reshape(TOKENS // TOK_DEV, TOK_DEV, D)).reshape(TOKENS, D)
    sum_two = stream_two + feed
    return (sum_one, sum_two)

def reference(stream_one, stream_two, grad_one, grad_two, query_weight, value_weight, merge_weight, expand_weight, shrink_weight, first_gain, first_bias, second_gain, second_bias, bucket_ids, sort_order):
    floats = tuple((item.astype(jnp.float32) for item in (stream_one, stream_two, query_weight, value_weight, merge_weight, expand_weight, shrink_weight, first_gain, first_bias, second_gain, second_bias)))

    def forward(*items):
        return layer(*items, bucket_ids, sort_order)
    results, pullback = jax.vjp(forward, *floats)
    grads = pullback((grad_one.astype(jnp.float32), grad_two.astype(jnp.float32)))
    return (results[0].astype(jnp.bfloat16), results[1].astype(jnp.bfloat16), grads[0].astype(jnp.bfloat16), grads[1].astype(jnp.bfloat16), grads[2], grads[3], grads[4], grads[5], grads[6], grads[7], grads[8], grads[9], grads[10])
```

```python
from functools import partial

import jax
import jax.numpy as jnp
from jax import lax
from jax.sharding import PartitionSpec as P

HEADS = 8
HEAD_DIM = 128
GROUP = 64


masked_score = -1000000000.0
own_score = -100000.0


def as_sent(shard):

    def short(part):
        return part.astype(jnp.bfloat16) if part.dtype == jnp.float32 else part

    return jax.tree.map(short, shard)


def from_behind(block, axis, distance):
    devices = range(lax.axis_size(axis))
    route = [(i - distance, i) for i in devices if i - distance in devices]
    return lax.ppermute(block, axis, route)


def row_sums(first, second):
    return lax.psum((first, second), "head")


def full_rows(part):
    return lax.all_gather(part, "head", axis=1, tiled=True)


def branch_sum(part):
    return lax.psum_scatter(part, "head", scatter_dimension=1, tiled=True)


def norm_forward(value, gain, shift):
    width = value.shape[1] * lax.axis_size("head")
    total, square = row_sums(
        jnp.sum(value, 1, keepdims=True), jnp.sum(value * value, 1, keepdims=True)
    )
    center = total / width
    spread = square / width - center * center
    factor = lax.rsqrt(spread + 1e-05)
    normal = (value - center) * factor
    return (normal, factor, normal * gain + shift)


def norm_backward(grad, normal, factor, gain):
    width = grad.shape[1] * lax.axis_size("head")
    scaled = grad * gain
    first, second = row_sums(
        jnp.sum(scaled, 1, keepdims=True), jnp.sum(scaled * normal, 1, keepdims=True)
    )
    result = factor * (scaled - first / width - normal * (second / width))
    return (result, jnp.sum(grad * normal, 0), jnp.sum(grad, 0))


def regroup_rows(buffer):
    turns = []
    for turn in range(buffer.shape[1]):
        turns.append(
            lax.all_to_all(buffer[:, turn], "seq", split_axis=0, concat_axis=0, tiled=True)
        )
    result = jnp.stack(turns, 1)
    return result


def regroup_totals(buffer):
    moved = lax.all_to_all(
        buffer.reshape(buffer.shape[0], -1, buffer.shape[3]),
        "seq",
        split_axis=0,
        concat_axis=0,
        tiled=True,
    )
    return moved.reshape(buffer.shape)


def regroup_pair(first, second):
    firsts = []
    seconds = []
    for turn in range(first.shape[1]):
        moved_first, moved_second = (
            lax.all_to_all(as_sent(first[:, turn]), "seq", split_axis=0, concat_axis=0, tiled=True),
            lax.all_to_all(
                as_sent(second[:, turn]), "seq", split_axis=0, concat_axis=0, tiled=True
            ),
        )
        firsts.append(moved_first)
        seconds.append(moved_second)
    result = (jnp.stack(firsts, 1), jnp.stack(seconds, 1))
    return result


def by_blocks(
    stream_one,
    stream_two,
    grad_one,
    grad_two,
    query_weight,
    value_weight,
    merge_weight,
    expand_weight,
    shrink_weight,
    first_gain,
    first_bias,
    second_gain,
    second_bias,
    bucket_ids,
    sort_order,
):
    devices = lax.axis_size("seq")
    place = lax.axis_index("seq")
    rows = stream_one.shape[0]
    rounds = sort_order.shape[0]
    capacity = 2 * rows // devices
    blocks = rows // GROUP
    heads_here = HEADS // lax.axis_size("head")
    local_width = heads_here * HEAD_DIM
    scale = HEAD_DIM ** (-0.5)
    round_index = jnp.arange(rounds, dtype=jnp.int32)[:, None]
    counter = jnp.arange(rows, dtype=jnp.int32)

    def invert(line):
        return jnp.zeros_like(line).at[line].set(jnp.arange(line.shape[0], dtype=jnp.int32))

    inverse = jax.vmap(invert)(sort_order)
    my_sorted = lax.dynamic_slice_in_dim(inverse, place * rows, rows, 1)
    send_block = my_sorted // rows
    same_block = send_block[:, :, None] == send_block[:, None, :]
    send_slot = jnp.sum(
        (same_block & (my_sorted[:, None, :] < my_sorted[:, :, None])).astype(jnp.int32), -1
    )
    block_tokens = lax.dynamic_slice_in_dim(sort_order, place * rows, rows, 1)
    source_block = block_tokens // rows
    earlier = counter[None, :] < counter[:, None]
    recv_slot = jnp.sum(
        ((source_block[:, :, None] == source_block[:, None, :]) & earlier[None]).astype(jnp.int32),
        -1,
    )
    query_bucket = jnp.take_along_axis(bucket_ids, block_tokens, 1)
    prior_start = (place - 1) % devices * rows + rows - GROUP
    prior_tokens = lax.dynamic_slice_in_dim(sort_order, prior_start, GROUP, 1)
    prior_bucket = jnp.take_along_axis(bucket_ids, prior_tokens, 1)

    def with_prior(own, prior):
        pieces = own.reshape((rounds, blocks, GROUP) + own.shape[2:])
        before = jnp.concatenate([prior[:, None], pieces[:, :-1]], 1)
        return jnp.concatenate([pieces, before], 2)

    query_place = block_tokens.reshape(rounds, blocks, GROUP)
    key_place = with_prior(block_tokens, prior_tokens)
    key_bucket = with_prior(query_bucket, prior_bucket)
    allowed = (key_place[:, :, None, :] <= query_place[:, :, :, None]) & (
        key_bucket[:, :, None, :] == query_bucket.reshape(rounds, blocks, GROUP)[:, :, :, None]
    )
    itself = key_place[:, :, None, :] == query_place[:, :, :, None]
    live = allowed & jnp.logical_not(itself)

    def fill(values, block, slot):
        empty = jnp.zeros((devices, rounds, capacity, values.shape[-1]), values.dtype)
        return empty.at[block, round_index, slot].set(values)

    normal_one, factor_one, normed_one = norm_forward(
        stream_two.astype(jnp.float32), first_gain, first_bias
    )
    rows_one = full_rows(normed_one.astype(jnp.bfloat16))
    query_full, value_full, merge_full = (
        lax.all_gather(query_weight, "seq", axis=0, tiled=True),
        lax.all_gather(value_weight, "seq", axis=0, tiled=True),
        lax.all_gather(merge_weight, "seq", axis=1, tiled=True),
    )
    queries = jnp.dot(rows_one, query_full, preferred_element_type=jnp.float32).astype(jnp.bfloat16)
    values = jnp.dot(rows_one, value_full, preferred_element_type=jnp.float32).astype(jnp.bfloat16)
    packed = jnp.concatenate([queries, values], 1)
    outgoing = fill(jnp.broadcast_to(packed[None], (rounds,) + packed.shape), send_block, send_slot)
    incoming = regroup_rows(outgoing)
    sorted_rows = incoming[source_block, round_index, recv_slot]
    sorted_query = sorted_rows[:, :, :local_width].reshape(rounds, rows, heads_here, HEAD_DIM)
    sorted_value = sorted_rows[:, :, local_width:].reshape(rounds, rows, heads_here, HEAD_DIM)
    query_float = sorted_query.astype(jnp.float32)
    inverse_norm = lax.rsqrt(jnp.sum(query_float * query_float, -1, keepdims=True) + 1e-06)
    unit_float = query_float * inverse_norm
    unit_low = unit_float.astype(jnp.bfloat16)
    edge = from_behind(
        jnp.concatenate([unit_low[:, -GROUP:], sorted_value[:, -GROUP:]], -1), "seq", 1
    )
    key_unit = with_prior(unit_low, edge[..., :HEAD_DIM])
    key_value = with_prior(sorted_value, edge[..., HEAD_DIM:])
    query_groups = sorted_query.reshape(rounds, blocks, GROUP, heads_here, HEAD_DIM)

    def masked_scores():
        raw = (
            jnp.einsum(
                "rncha,rnkha->rnhck", query_groups, key_unit, preferred_element_type=jnp.float32
            )
            * scale
        )
        return jnp.where(
            itself[:, :, None], own_score, jnp.where(allowed[:, :, None], raw, masked_score)
        )

    scores = masked_scores()
    peak = jnp.max(scores, -1, keepdims=True)
    totals = peak + jnp.log(jnp.sum(jnp.exp(scores - peak), -1, keepdims=True))
    probs_low = jnp.exp(scores - totals).astype(jnp.bfloat16)
    round_out = jnp.einsum(
        "rnhck,rnkha->rncha", probs_low, key_value, preferred_element_type=jnp.float32
    ).astype(jnp.bfloat16)
    out_flat = round_out.reshape(rounds, rows, local_width)
    total_flat = jnp.transpose(totals[..., 0], (0, 1, 3, 2)).reshape(rounds, rows, heads_here)
    token_out = regroup_rows(fill(out_flat, source_block, recv_slot))[
        send_block, round_index, send_slot
    ].astype(jnp.float32)
    token_total = regroup_totals(fill(total_flat, source_block, recv_slot))[
        send_block, round_index, send_slot
    ]
    mix = jax.nn.softmax(token_total, axis=0)
    token_out4 = token_out.reshape(rounds, rows, heads_here, HEAD_DIM)
    attended_low = (
        jnp.sum(mix[..., None] * token_out4, 0).reshape(rows, local_width).astype(jnp.bfloat16)
    )
    sum_one = stream_one.astype(jnp.float32) + branch_sum(
        jnp.dot(attended_low, merge_full, preferred_element_type=jnp.float32)
    )
    normal_two, factor_two, normed_two = norm_forward(sum_one, second_gain, second_bias)
    rows_two = full_rows(normed_two.astype(jnp.bfloat16))
    expand_full, shrink_full = (
        lax.all_gather(expand_weight, "seq", axis=0, tiled=True),
        lax.all_gather(shrink_weight, "seq", axis=1, tiled=True),
    )
    hidden = jnp.dot(rows_two, expand_full, preferred_element_type=jnp.float32)
    active, gelu_pull = jax.vjp(partial(jax.nn.gelu, approximate=False), hidden)
    active_low = active.astype(jnp.bfloat16)
    sum_two = stream_two.astype(jnp.float32) + branch_sum(
        jnp.dot(active_low, shrink_full, preferred_element_type=jnp.float32)
    )
    grad_rows_two = full_rows(grad_two)
    grad_active = jnp.dot(grad_rows_two, shrink_full.T, preferred_element_type=jnp.float32)
    grad_hidden = gelu_pull(grad_active)[0].astype(jnp.bfloat16)
    grad_shrink = jnp.dot(active_low.T, grad_rows_two, preferred_element_type=jnp.float32)
    grad_expand = jnp.dot(rows_two.T, grad_hidden, preferred_element_type=jnp.float32)
    grad_normed_two = branch_sum(
        jnp.dot(grad_hidden, expand_full.T, preferred_element_type=jnp.float32)
    )
    extra_one, grad_second_gain, grad_second_bias = norm_backward(
        grad_normed_two, normal_two, factor_two, second_gain
    )
    total_one = grad_one.astype(jnp.float32) + extra_one
    total_low = total_one.astype(jnp.bfloat16)
    grad_rows_one = full_rows(total_low)
    grad_attended = jnp.dot(grad_rows_one, merge_full.T, preferred_element_type=jnp.float32).astype(
        jnp.bfloat16
    )
    grad_merge = jnp.dot(attended_low.T, grad_rows_one, preferred_element_type=jnp.float32)
    grad_float = grad_attended.astype(jnp.float32).reshape(rows, heads_here, HEAD_DIM)
    dots = jnp.sum(token_out4 * grad_float[None], -1)
    grad_total = mix * (dots - jnp.sum(mix * dots, 0, keepdims=True))
    grad_out_low = (
        (mix[..., None] * grad_float[None]).astype(jnp.bfloat16).reshape(rounds, rows, local_width)
    )
    sorted_grad_out = regroup_rows(fill(grad_out_low, send_block, send_slot))[
        source_block, round_index, recv_slot
    ]
    sorted_grad_total = regroup_totals(fill(grad_total, send_block, send_slot))[
        source_block, round_index, recv_slot
    ]
    grad_groups = sorted_grad_out.reshape(rounds, blocks, GROUP, heads_here, HEAD_DIM)
    total_grad_groups = jnp.transpose(
        sorted_grad_total.reshape(rounds, blocks, GROUP, heads_here), (0, 1, 3, 2)
    )[..., None]
    probs = jnp.exp(masked_scores() - totals)
    probs_again = probs.astype(jnp.bfloat16)
    grad_probs = jnp.einsum(
        "rncha,rnkha->rnhck", grad_groups, key_value, preferred_element_type=jnp.float32
    )
    grad_key_value = jnp.einsum(
        "rnhck,rncha->rnkha", probs_again, grad_groups, preferred_element_type=jnp.float32
    )
    inner = jnp.sum(probs * grad_probs, -1, keepdims=True)
    grad_scores = jnp.where(
        live[:, :, None], probs * (grad_probs - inner + total_grad_groups), 0.0
    ).astype(jnp.bfloat16)
    grad_query_groups = (
        jnp.einsum("rnhck,rnkha->rncha", grad_scores, key_unit, preferred_element_type=jnp.float32)
        * scale
    )
    grad_key_unit = (
        jnp.einsum(
            "rnhck,rncha->rnkha", grad_scores, query_groups, preferred_element_type=jnp.float32
        )
        * scale
    )
    edge_grad = from_behind(
        jnp.concatenate([grad_key_unit[:, 0, GROUP:], grad_key_value[:, 0, GROUP:]], -1).astype(
            jnp.bfloat16
        ),
        "seq",
        -1,
    ).astype(jnp.float32)

    def fold_keys(grad_keys, arriving):
        own = grad_keys[:, :, :GROUP]
        later = jnp.concatenate([grad_keys[:, 1:, GROUP:], arriving[:, None]], 1)
        return (own + later).reshape(rounds, rows, heads_here, HEAD_DIM)

    grad_unit = fold_keys(grad_key_unit, edge_grad[..., :HEAD_DIM])
    grad_sorted_value = fold_keys(grad_key_value, edge_grad[..., HEAD_DIM:])
    grad_sorted_query = grad_query_groups.reshape(
        rounds, rows, heads_here, HEAD_DIM
    ) + inverse_norm * (grad_unit - unit_float * jnp.sum(unit_float * grad_unit, -1, keepdims=True))
    moved_first, moved_second = regroup_pair(
        fill(grad_sorted_query.reshape(rounds, rows, local_width), source_block, recv_slot),
        fill(grad_sorted_value.reshape(rounds, rows, local_width), source_block, recv_slot),
    )
    token_grad_query = moved_first[send_block, round_index, send_slot]
    token_grad_value = moved_second[send_block, round_index, send_slot]
    grad_query_low = jnp.sum(token_grad_query, 0).astype(jnp.bfloat16)
    grad_value_low = jnp.sum(token_grad_value, 0).astype(jnp.bfloat16)
    grad_query_full = jnp.dot(rows_one.T, grad_query_low, preferred_element_type=jnp.float32)
    grad_value_full = jnp.dot(rows_one.T, grad_value_low, preferred_element_type=jnp.float32)
    grad_normed_one = branch_sum(
        jnp.dot(grad_query_low, query_full.T, preferred_element_type=jnp.float32)
        + jnp.dot(grad_value_low, value_full.T, preferred_element_type=jnp.float32)
    )
    extra_two, grad_first_gain, grad_first_bias = norm_backward(
        grad_normed_one, normal_one, factor_one, first_gain
    )
    input_grad_two = (grad_two.astype(jnp.float32) + extra_two).astype(jnp.bfloat16)
    query_part, value_part, merge_part, expand_part, shrink_part = (
        lax.psum_scatter(grad_query_full, "seq", scatter_dimension=0, tiled=True),
        lax.psum_scatter(grad_value_full, "seq", scatter_dimension=0, tiled=True),
        lax.psum_scatter(grad_merge, "seq", scatter_dimension=1, tiled=True),
        lax.psum_scatter(grad_expand, "seq", scatter_dimension=0, tiled=True),
        lax.psum_scatter(grad_shrink, "seq", scatter_dimension=1, tiled=True),
    )
    first_gain_sum, first_bias_sum, second_gain_sum, second_bias_sum = lax.psum(
        (grad_first_gain, grad_first_bias, grad_second_gain, grad_second_bias), "seq"
    )
    return (
        sum_one.astype(jnp.bfloat16),
        sum_two.astype(jnp.bfloat16),
        total_low,
        input_grad_two,
        query_part,
        value_part,
        merge_part,
        expand_part,
        shrink_part,
        first_gain_sum,
        first_bias_sum,
        second_gain_sum,
        second_bias_sum,
    )


def seq_groups():
    heads_here = HEADS // lax.axis_size("head")
    devices = lax.axis_size("seq")
    across = [[i * heads_here + j for j in range(heads_here)] for i in range(devices // heads_here)]
    along = [[i * heads_here + j for i in range(devices // heads_here)] for j in range(heads_here)]
    return across, along


def split_columns(value, parts):
    return value.reshape(value.shape[0], parts, value.shape[1] // parts)


def one_hot(order, count):
    return (order[:, None] == jnp.arange(count, dtype=order.dtype)[None]).astype(jnp.bfloat16)


def three_parts(value):
    parts = []
    for _ in range(3):
        part = value.astype(jnp.bfloat16)
        parts.append(part)
        value = value - part.astype(jnp.float32)
    return jnp.stack(parts, -1)


def plain_norm(value, gain, shift):
    center = jnp.mean(value, 1, keepdims=True)
    offset = value - center
    factor = lax.rsqrt(jnp.mean(offset * offset, 1, keepdims=True) + 1e-05)
    normal = offset * factor
    return normal, factor, normal * gain + shift


def by_rounds(
    stream_one,
    stream_two,
    grad_one,
    grad_two,
    query_weight,
    value_weight,
    merge_weight,
    expand_weight,
    shrink_weight,
    first_gain,
    first_bias,
    second_gain,
    second_bias,
    bucket_ids,
    sort_order,
):
    bf16, f32 = jnp.bfloat16, jnp.float32
    devices = lax.axis_size("seq")
    place = lax.axis_index("seq")
    rows = stream_one.shape[0]
    rounds, tokens = sort_order.shape
    heads_here = HEADS // lax.axis_size("head")
    turn, which = place // heads_here, place % heads_here
    blocks = tokens // GROUP
    scale = HEAD_DIM ** (-0.5)
    across, along = seq_groups()
    pair_rows = rows * heads_here

    def to_heads(value):
        moved = lax.all_to_all(
            split_columns(value, heads_here), "seq", split_axis=1, concat_axis=0,
            axis_index_groups=across, tiled=True,
        )
        return moved.reshape(pair_rows, value.shape[1] // heads_here)

    def to_tokens(value):
        moved = lax.all_to_all(
            value.reshape(heads_here, rows, value.shape[1]), "seq", split_axis=0, concat_axis=0,
            axis_index_groups=across, tiled=True,
        )
        return jnp.swapaxes(moved, 0, 1).reshape(rows, heads_here * value.shape[1])

    def to_rounds(value):
        return lax.all_gather(value, "seq", axis=0, axis_index_groups=along, tiled=True)

    def swap_rounds(value):
        return lax.all_to_all(
            value, "seq", split_axis=0, concat_axis=0, axis_index_groups=along, tiled=True
        )

    my_order = lax.dynamic_slice_in_dim(sort_order, turn, 1, 0)[0]
    my_bucket = lax.dynamic_slice_in_dim(bucket_ids, turn, 1, 0)[0]
    my_bucket = jnp.sort(my_bucket)
    sorter = one_hot(my_order, tokens)

    def sort_rows(value):
        return jnp.dot(sorter, value, preferred_element_type=f32)

    def unsort_rows(value):
        return lax.dot_general(
            sorter, value, (((0,), (0,)), ((), ())), preferred_element_type=f32
        )

    def with_prior(own):
        pieces = own.reshape((blocks, GROUP) + own.shape[1:])
        return jnp.concatenate([pieces, jnp.roll(pieces, 1, 0)], 1)

    query_place = my_order.reshape(blocks, GROUP)
    query_bucket = my_bucket.reshape(blocks, GROUP)
    key_place, key_bucket = with_prior(my_order), with_prior(my_bucket)
    allowed = (key_place[:, None] <= query_place[:, :, None]) & (
        key_bucket[:, None] == query_bucket[:, :, None]
    )
    itself = key_place[:, None] == query_place[:, :, None]
    live = allowed & jnp.logical_not(itself)

    gain_one, bias_one, gain_two, bias_two = (
        lax.all_gather(item, "head", axis=0, tiled=True)
        for item in (first_gain, first_bias, second_gain, second_bias)
    )
    two_full = full_rows(stream_two).astype(f32)
    normal_one, factor_one, normed_one = plain_norm(two_full, gain_one, bias_one)
    rows_one = normed_one.astype(bf16)
    query_full = lax.all_gather(query_weight, "seq", axis=0, tiled=True)
    value_full = lax.all_gather(value_weight, "seq", axis=0, tiled=True)
    queries = jnp.dot(rows_one, query_full, preferred_element_type=f32).astype(bf16)
    values = jnp.dot(rows_one, value_full, preferred_element_type=f32).astype(bf16)
    packed = jnp.concatenate(
        [split_columns(queries, heads_here), split_columns(values, heads_here)], -1
    ).reshape(rows, heads_here * 2 * HEAD_DIM)
    everyone = to_rounds(to_heads(packed))
    sorted_rows = sort_rows(everyone).astype(bf16)
    sorted_query, sorted_value = sorted_rows[:, :HEAD_DIM], sorted_rows[:, HEAD_DIM:]
    query_float = sorted_query.astype(f32)
    inverse_norm = lax.rsqrt(jnp.sum(query_float * query_float, -1, keepdims=True) + 1e-06)
    unit_float = query_float * inverse_norm
    key_unit = with_prior(unit_float.astype(bf16))
    key_value = with_prior(sorted_value)
    query_groups = sorted_query.reshape(blocks, GROUP, HEAD_DIM)
    raw = jnp.einsum("nca,nka->nck", query_groups, key_unit, preferred_element_type=f32) * scale
    scores = jnp.where(itself, own_score, jnp.where(allowed, raw, masked_score))
    peak = jnp.max(scores, -1, keepdims=True)
    totals = peak + jnp.log(jnp.sum(jnp.exp(scores - peak), -1, keepdims=True))
    probs = jnp.exp(scores - totals)
    probs_low = probs.astype(bf16)
    round_out = jnp.einsum(
        "nck,nka->nca", probs_low, key_value, preferred_element_type=f32
    ).astype(bf16)
    back = unsort_rows(
        jnp.concatenate(
            [round_out.reshape(tokens, HEAD_DIM), three_parts(totals.reshape(tokens))], 1
        )
    )
    outs = swap_rounds(back[:, :HEAD_DIM].astype(bf16).reshape(rounds, pair_rows, HEAD_DIM))
    sums = swap_rounds(jnp.sum(back[:, HEAD_DIM:], 1).reshape(rounds, pair_rows))
    mix = jax.nn.softmax(sums, axis=0)
    outs_float = outs.astype(f32)
    attended_pair = jnp.sum(mix[..., None] * outs_float, 0).astype(bf16)
    attended_low = to_tokens(attended_pair)
    merge_full = lax.all_gather(merge_weight, "seq", axis=1, tiled=True)
    sum_one = stream_one.astype(f32) + branch_sum(
        jnp.dot(attended_low, merge_full, preferred_element_type=f32)
    )
    normal_two, factor_two, normed_two = norm_forward(sum_one, second_gain, second_bias)
    rows_two = full_rows(normed_two.astype(bf16))
    expand_full = lax.all_gather(expand_weight, "seq", axis=0, tiled=True)
    shrink_full = lax.all_gather(shrink_weight, "seq", axis=1, tiled=True)
    hidden = jnp.dot(rows_two, expand_full, preferred_element_type=f32)
    active, gelu_pull = jax.vjp(partial(jax.nn.gelu, approximate=False), hidden)
    active_low = active.astype(bf16)
    sum_two = stream_two.astype(f32) + branch_sum(
        jnp.dot(active_low, shrink_full, preferred_element_type=f32)
    )
    grad_rows_two = full_rows(grad_two)
    grad_active = jnp.dot(grad_rows_two, shrink_full.T, preferred_element_type=f32)
    grad_hidden = gelu_pull(grad_active)[0].astype(bf16)
    grad_shrink = jnp.dot(active_low.T, grad_rows_two, preferred_element_type=f32).astype(bf16)
    grad_expand = jnp.dot(rows_two.T, grad_hidden, preferred_element_type=f32).astype(bf16)
    grad_normed_two = branch_sum(jnp.dot(grad_hidden, expand_full.T, preferred_element_type=f32))
    extra_one, grad_second_gain, grad_second_bias = norm_backward(
        grad_normed_two, normal_two, factor_two, second_gain
    )
    total_low = (grad_one.astype(f32) + extra_one).astype(bf16)
    grad_rows_one = full_rows(total_low)
    grad_attended = jnp.dot(grad_rows_one, merge_full.T, preferred_element_type=f32).astype(bf16)
    grad_merge = jnp.dot(attended_low.T, grad_rows_one, preferred_element_type=f32).astype(bf16)
    grad_float = to_heads(grad_attended).astype(f32)
    dots = jnp.sum(outs_float * grad_float[None], -1)
    grad_sums = mix * (dots - jnp.sum(mix * dots, 0, keepdims=True))
    grad_outs = swap_rounds((mix[..., None] * grad_float[None]).astype(bf16))
    grad_sums = swap_rounds(grad_sums)
    sorted_grads = sort_rows(
        jnp.concatenate(
            [grad_outs.reshape(tokens, HEAD_DIM), three_parts(grad_sums.reshape(tokens))], 1
        )
    )
    grad_groups = sorted_grads[:, :HEAD_DIM].astype(bf16).reshape(blocks, GROUP, HEAD_DIM)
    total_grads = jnp.sum(sorted_grads[:, HEAD_DIM:], 1).reshape(blocks, GROUP, 1)
    grad_probs = jnp.einsum("nca,nka->nck", grad_groups, key_value, preferred_element_type=f32)
    grad_key_value = jnp.einsum("nck,nca->nka", probs_low, grad_groups, preferred_element_type=f32)
    inner = jnp.sum(probs * grad_probs, -1, keepdims=True)
    grad_scores = jnp.where(live, probs * (grad_probs - inner + total_grads), 0.0).astype(bf16)
    grad_query_groups = (
        jnp.einsum("nck,nka->nca", grad_scores, key_unit, preferred_element_type=f32) * scale
    )
    grad_key_unit = (
        jnp.einsum("nck,nca->nka", grad_scores, query_groups, preferred_element_type=f32) * scale
    )

    def fold_keys(grad_keys):
        return (grad_keys[:, :GROUP] + jnp.roll(grad_keys[:, GROUP:], -1, 0)).reshape(
            tokens, HEAD_DIM
        )

    grad_unit = fold_keys(grad_key_unit)
    grad_sorted_query = grad_query_groups.reshape(tokens, HEAD_DIM) + inverse_norm * (
        grad_unit - unit_float * jnp.sum(unit_float * grad_unit, -1, keepdims=True)
    )
    grad_back = unsort_rows(
        jnp.concatenate([grad_sorted_query, fold_keys(grad_key_value)], 1).astype(bf16)
    )
    grad_parts = swap_rounds(grad_back.astype(bf16).reshape(rounds, pair_rows, 2 * HEAD_DIM))
    grad_pair = to_tokens(jnp.sum(grad_parts.astype(f32), 0).astype(bf16)).reshape(
        rows, heads_here, 2, HEAD_DIM
    )
    grad_query_low = grad_pair[:, :, 0].reshape(rows, heads_here * HEAD_DIM)
    grad_value_low = grad_pair[:, :, 1].reshape(rows, heads_here * HEAD_DIM)
    grad_query_full = jnp.dot(rows_one.T, grad_query_low, preferred_element_type=f32).astype(bf16)
    grad_value_full = jnp.dot(rows_one.T, grad_value_low, preferred_element_type=f32).astype(bf16)
    grad_normed_one = branch_sum(
        jnp.dot(grad_query_low, query_full.T, preferred_element_type=f32)
        + jnp.dot(grad_value_low, value_full.T, preferred_element_type=f32)
    )
    column = lax.axis_index("head") * stream_two.shape[1]
    my_normal = lax.dynamic_slice_in_dim(normal_one, column, stream_two.shape[1], 1)
    extra_two, grad_first_gain, grad_first_bias = norm_backward(
        grad_normed_one, my_normal, factor_one, first_gain
    )
    input_grad_two = (grad_two.astype(f32) + extra_two).astype(bf16)
    query_part, value_part, merge_part, expand_part, shrink_part = (
        lax.psum_scatter(grad_query_full, "seq", scatter_dimension=0, tiled=True).astype(f32),
        lax.psum_scatter(grad_value_full, "seq", scatter_dimension=0, tiled=True).astype(f32),
        lax.psum_scatter(grad_merge, "seq", scatter_dimension=1, tiled=True).astype(f32),
        lax.psum_scatter(grad_expand, "seq", scatter_dimension=0, tiled=True).astype(f32),
        lax.psum_scatter(grad_shrink, "seq", scatter_dimension=1, tiled=True).astype(f32),
    )
    first_gain_sum, first_bias_sum, second_gain_sum, second_bias_sum = lax.psum(
        (grad_first_gain, grad_first_bias, grad_second_gain, grad_second_bias), "seq"
    )
    return (
        sum_one.astype(bf16),
        sum_two.astype(bf16),
        total_low,
        input_grad_two,
        query_part,
        value_part,
        merge_part,
        expand_part,
        shrink_part,
        first_gain_sum,
        first_bias_sum,
        second_gain_sum,
        second_bias_sum,
    )


def solution(mesh):
    placed = (
        P("seq", "head"),
        P("seq", "head"),
        P("seq", "head"),
        P("seq", "head"),
        P("seq", "head"),
        P("seq", "head"),
        P("head", "seq"),
        P("seq", "head"),
        P("head", "seq"),
        P("head"),
        P("head"),
        P("head"),
        P("head"),
        P(),
        P(),
    )

    def local(*arguments):
        rounds = arguments[-1].shape[0]
        if mesh.shape["seq"] * mesh.shape["head"] == rounds * HEADS:
            return by_rounds(*arguments)
        return by_blocks(*arguments)

    return jax.shard_map(
        local,
        mesh=mesh,
        in_specs=placed,
        out_specs=(
            P("seq", "head"),
            P("seq", "head"),
            P("seq", "head"),
            P("seq", "head"),
            P("seq", "head"),
            P("seq", "head"),
            P("head", "seq"),
            P("seq", "head"),
            P("head", "seq"),
            P("head"),
            P("head"),
            P("head"),
            P("head"),
        ),
        check_vma=False,
    )
```

```python
from functools import partial

import jax
import jax.numpy as jnp
from jax import lax
from jax.experimental import pallas as pl
from jax.experimental.pallas import tpu as pltpu
from jax.sharding import PartitionSpec as P

HEADS = 8
HEAD_DIM = 128
GROUP = 64
MESH = pl.DeviceIdType.MESH


masked_score = -1000000000.0
own_score = -100000.0


def as_sent(shard):

    def short(part):
        return part.astype(jnp.bfloat16) if part.dtype == jnp.float32 else part

    return jax.tree.map(short, shard)


def from_behind(block, axis, distance):
    devices = range(lax.axis_size(axis))
    route = [(i - distance, i) for i in devices if i - distance in devices]
    return lax.ppermute(block, axis, route)


def row_sums(first, second):
    return lax.psum((first, second), "head")


def full_rows(part):
    return lax.all_gather(part, "head", axis=1, tiled=True)


def branch_sum(part):
    return lax.psum_scatter(part, "head", scatter_dimension=1, tiled=True)


def norm_forward(value, gain, shift):
    width = value.shape[1] * lax.axis_size("head")
    total, square = row_sums(
        jnp.sum(value, 1, keepdims=True), jnp.sum(value * value, 1, keepdims=True)
    )
    center = total / width
    spread = square / width - center * center
    factor = lax.rsqrt(spread + 1e-05)
    normal = (value - center) * factor
    return (normal, factor, normal * gain + shift)


def norm_backward(grad, normal, factor, gain):
    width = grad.shape[1] * lax.axis_size("head")
    scaled = grad * gain
    first, second = row_sums(
        jnp.sum(scaled, 1, keepdims=True), jnp.sum(scaled * normal, 1, keepdims=True)
    )
    result = factor * (scaled - first / width - normal * (second / width))
    return (result, jnp.sum(grad * normal, 0), jnp.sum(grad, 0))


def regroup_rows(buffer):
    turns = []
    for turn in range(buffer.shape[1]):
        turns.append(
            lax.all_to_all(buffer[:, turn], "seq", split_axis=0, concat_axis=0, tiled=True)
        )
    result = jnp.stack(turns, 1)
    return result


def regroup_totals(buffer):
    moved = lax.all_to_all(
        buffer.reshape(buffer.shape[0], -1, buffer.shape[3]),
        "seq",
        split_axis=0,
        concat_axis=0,
        tiled=True,
    )
    return moved.reshape(buffer.shape)


def regroup_pair(first, second):
    firsts = []
    seconds = []
    for turn in range(first.shape[1]):
        moved_first, moved_second = (
            lax.all_to_all(as_sent(first[:, turn]), "seq", split_axis=0, concat_axis=0, tiled=True),
            lax.all_to_all(
                as_sent(second[:, turn]), "seq", split_axis=0, concat_axis=0, tiled=True
            ),
        )
        firsts.append(moved_first)
        seconds.append(moved_second)
    result = (jnp.stack(firsts, 1), jnp.stack(seconds, 1))
    return result


def by_blocks(
    stream_one,
    stream_two,
    grad_one,
    grad_two,
    query_weight,
    value_weight,
    merge_weight,
    expand_weight,
    shrink_weight,
    first_gain,
    first_bias,
    second_gain,
    second_bias,
    bucket_ids,
    sort_order,
):
    devices = lax.axis_size("seq")
    place = lax.axis_index("seq")
    rows = stream_one.shape[0]
    rounds = sort_order.shape[0]
    capacity = 2 * rows // devices
    blocks = rows // GROUP
    heads_here = HEADS // lax.axis_size("head")
    local_width = heads_here * HEAD_DIM
    scale = HEAD_DIM ** (-0.5)
    round_index = jnp.arange(rounds, dtype=jnp.int32)[:, None]
    counter = jnp.arange(rows, dtype=jnp.int32)

    def invert(line):
        return jnp.zeros_like(line).at[line].set(jnp.arange(line.shape[0], dtype=jnp.int32))

    inverse = jax.vmap(invert)(sort_order)
    my_sorted = lax.dynamic_slice_in_dim(inverse, place * rows, rows, 1)
    send_block = my_sorted // rows
    same_block = send_block[:, :, None] == send_block[:, None, :]
    send_slot = jnp.sum(
        (same_block & (my_sorted[:, None, :] < my_sorted[:, :, None])).astype(jnp.int32), -1
    )
    block_tokens = lax.dynamic_slice_in_dim(sort_order, place * rows, rows, 1)
    source_block = block_tokens // rows
    earlier = counter[None, :] < counter[:, None]
    recv_slot = jnp.sum(
        ((source_block[:, :, None] == source_block[:, None, :]) & earlier[None]).astype(jnp.int32),
        -1,
    )
    query_bucket = jnp.take_along_axis(bucket_ids, block_tokens, 1)
    prior_start = (place - 1) % devices * rows + rows - GROUP
    prior_tokens = lax.dynamic_slice_in_dim(sort_order, prior_start, GROUP, 1)
    prior_bucket = jnp.take_along_axis(bucket_ids, prior_tokens, 1)

    def with_prior(own, prior):
        pieces = own.reshape((rounds, blocks, GROUP) + own.shape[2:])
        before = jnp.concatenate([prior[:, None], pieces[:, :-1]], 1)
        return jnp.concatenate([pieces, before], 2)

    query_place = block_tokens.reshape(rounds, blocks, GROUP)
    key_place = with_prior(block_tokens, prior_tokens)
    key_bucket = with_prior(query_bucket, prior_bucket)
    allowed = (key_place[:, :, None, :] <= query_place[:, :, :, None]) & (
        key_bucket[:, :, None, :] == query_bucket.reshape(rounds, blocks, GROUP)[:, :, :, None]
    )
    itself = key_place[:, :, None, :] == query_place[:, :, :, None]
    live = allowed & jnp.logical_not(itself)

    def fill(values, block, slot):
        empty = jnp.zeros((devices, rounds, capacity, values.shape[-1]), values.dtype)
        return empty.at[block, round_index, slot].set(values)

    normal_one, factor_one, normed_one = norm_forward(
        stream_two.astype(jnp.float32), first_gain, first_bias
    )
    rows_one = full_rows(normed_one.astype(jnp.bfloat16))
    query_full, value_full, merge_full = (
        lax.all_gather(query_weight, "seq", axis=0, tiled=True),
        lax.all_gather(value_weight, "seq", axis=0, tiled=True),
        lax.all_gather(merge_weight, "seq", axis=1, tiled=True),
    )
    queries = jnp.dot(rows_one, query_full, preferred_element_type=jnp.float32).astype(jnp.bfloat16)
    values = jnp.dot(rows_one, value_full, preferred_element_type=jnp.float32).astype(jnp.bfloat16)
    packed = jnp.concatenate([queries, values], 1)
    outgoing = fill(jnp.broadcast_to(packed[None], (rounds,) + packed.shape), send_block, send_slot)
    incoming = regroup_rows(outgoing)
    sorted_rows = incoming[source_block, round_index, recv_slot]
    sorted_query = sorted_rows[:, :, :local_width].reshape(rounds, rows, heads_here, HEAD_DIM)
    sorted_value = sorted_rows[:, :, local_width:].reshape(rounds, rows, heads_here, HEAD_DIM)
    query_float = sorted_query.astype(jnp.float32)
    inverse_norm = lax.rsqrt(jnp.sum(query_float * query_float, -1, keepdims=True) + 1e-06)
    unit_float = query_float * inverse_norm
    unit_low = unit_float.astype(jnp.bfloat16)
    edge = from_behind(
        jnp.concatenate([unit_low[:, -GROUP:], sorted_value[:, -GROUP:]], -1), "seq", 1
    )
    key_unit = with_prior(unit_low, edge[..., :HEAD_DIM])
    key_value = with_prior(sorted_value, edge[..., HEAD_DIM:])
    query_groups = sorted_query.reshape(rounds, blocks, GROUP, heads_here, HEAD_DIM)

    def masked_scores():
        raw = (
            jnp.einsum(
                "rncha,rnkha->rnhck", query_groups, key_unit, preferred_element_type=jnp.float32
            )
            * scale
        )
        return jnp.where(
            itself[:, :, None], own_score, jnp.where(allowed[:, :, None], raw, masked_score)
        )

    scores = masked_scores()
    peak = jnp.max(scores, -1, keepdims=True)
    totals = peak + jnp.log(jnp.sum(jnp.exp(scores - peak), -1, keepdims=True))
    probs_low = jnp.exp(scores - totals).astype(jnp.bfloat16)
    round_out = jnp.einsum(
        "rnhck,rnkha->rncha", probs_low, key_value, preferred_element_type=jnp.float32
    ).astype(jnp.bfloat16)
    out_flat = round_out.reshape(rounds, rows, local_width)
    total_flat = jnp.transpose(totals[..., 0], (0, 1, 3, 2)).reshape(rounds, rows, heads_here)
    token_out = regroup_rows(fill(out_flat, source_block, recv_slot))[
        send_block, round_index, send_slot
    ].astype(jnp.float32)
    token_total = regroup_totals(fill(total_flat, source_block, recv_slot))[
        send_block, round_index, send_slot
    ]
    mix = jax.nn.softmax(token_total, axis=0)
    token_out4 = token_out.reshape(rounds, rows, heads_here, HEAD_DIM)
    attended_low = (
        jnp.sum(mix[..., None] * token_out4, 0).reshape(rows, local_width).astype(jnp.bfloat16)
    )
    sum_one = stream_one.astype(jnp.float32) + branch_sum(
        jnp.dot(attended_low, merge_full, preferred_element_type=jnp.float32)
    )
    normal_two, factor_two, normed_two = norm_forward(sum_one, second_gain, second_bias)
    rows_two = full_rows(normed_two.astype(jnp.bfloat16))
    expand_full, shrink_full = (
        lax.all_gather(expand_weight, "seq", axis=0, tiled=True),
        lax.all_gather(shrink_weight, "seq", axis=1, tiled=True),
    )
    hidden = jnp.dot(rows_two, expand_full, preferred_element_type=jnp.float32)
    active, gelu_pull = jax.vjp(partial(jax.nn.gelu, approximate=False), hidden)
    active_low = active.astype(jnp.bfloat16)
    sum_two = stream_two.astype(jnp.float32) + branch_sum(
        jnp.dot(active_low, shrink_full, preferred_element_type=jnp.float32)
    )
    grad_rows_two = full_rows(grad_two)
    grad_active = jnp.dot(grad_rows_two, shrink_full.T, preferred_element_type=jnp.float32)
    grad_hidden = gelu_pull(grad_active)[0].astype(jnp.bfloat16)
    grad_shrink = jnp.dot(active_low.T, grad_rows_two, preferred_element_type=jnp.float32)
    grad_expand = jnp.dot(rows_two.T, grad_hidden, preferred_element_type=jnp.float32)
    grad_normed_two = branch_sum(
        jnp.dot(grad_hidden, expand_full.T, preferred_element_type=jnp.float32)
    )
    extra_one, grad_second_gain, grad_second_bias = norm_backward(
        grad_normed_two, normal_two, factor_two, second_gain
    )
    total_one = grad_one.astype(jnp.float32) + extra_one
    total_low = total_one.astype(jnp.bfloat16)
    grad_rows_one = full_rows(total_low)
    grad_attended = jnp.dot(grad_rows_one, merge_full.T, preferred_element_type=jnp.float32).astype(
        jnp.bfloat16
    )
    grad_merge = jnp.dot(attended_low.T, grad_rows_one, preferred_element_type=jnp.float32)
    grad_float = grad_attended.astype(jnp.float32).reshape(rows, heads_here, HEAD_DIM)
    dots = jnp.sum(token_out4 * grad_float[None], -1)
    grad_total = mix * (dots - jnp.sum(mix * dots, 0, keepdims=True))
    grad_out_low = (
        (mix[..., None] * grad_float[None]).astype(jnp.bfloat16).reshape(rounds, rows, local_width)
    )
    sorted_grad_out = regroup_rows(fill(grad_out_low, send_block, send_slot))[
        source_block, round_index, recv_slot
    ]
    sorted_grad_total = regroup_totals(fill(grad_total, send_block, send_slot))[
        source_block, round_index, recv_slot
    ]
    grad_groups = sorted_grad_out.reshape(rounds, blocks, GROUP, heads_here, HEAD_DIM)
    total_grad_groups = jnp.transpose(
        sorted_grad_total.reshape(rounds, blocks, GROUP, heads_here), (0, 1, 3, 2)
    )[..., None]
    probs = jnp.exp(masked_scores() - totals)
    probs_again = probs.astype(jnp.bfloat16)
    grad_probs = jnp.einsum(
        "rncha,rnkha->rnhck", grad_groups, key_value, preferred_element_type=jnp.float32
    )
    grad_key_value = jnp.einsum(
        "rnhck,rncha->rnkha", probs_again, grad_groups, preferred_element_type=jnp.float32
    )
    inner = jnp.sum(probs * grad_probs, -1, keepdims=True)
    grad_scores = jnp.where(
        live[:, :, None], probs * (grad_probs - inner + total_grad_groups), 0.0
    ).astype(jnp.bfloat16)
    grad_query_groups = (
        jnp.einsum("rnhck,rnkha->rncha", grad_scores, key_unit, preferred_element_type=jnp.float32)
        * scale
    )
    grad_key_unit = (
        jnp.einsum(
            "rnhck,rncha->rnkha", grad_scores, query_groups, preferred_element_type=jnp.float32
        )
        * scale
    )
    edge_grad = from_behind(
        jnp.concatenate([grad_key_unit[:, 0, GROUP:], grad_key_value[:, 0, GROUP:]], -1).astype(
            jnp.bfloat16
        ),
        "seq",
        -1,
    ).astype(jnp.float32)

    def fold_keys(grad_keys, arriving):
        own = grad_keys[:, :, :GROUP]
        later = jnp.concatenate([grad_keys[:, 1:, GROUP:], arriving[:, None]], 1)
        return (own + later).reshape(rounds, rows, heads_here, HEAD_DIM)

    grad_unit = fold_keys(grad_key_unit, edge_grad[..., :HEAD_DIM])
    grad_sorted_value = fold_keys(grad_key_value, edge_grad[..., HEAD_DIM:])
    grad_sorted_query = grad_query_groups.reshape(
        rounds, rows, heads_here, HEAD_DIM
    ) + inverse_norm * (grad_unit - unit_float * jnp.sum(unit_float * grad_unit, -1, keepdims=True))
    moved_first, moved_second = regroup_pair(
        fill(grad_sorted_query.reshape(rounds, rows, local_width), source_block, recv_slot),
        fill(grad_sorted_value.reshape(rounds, rows, local_width), source_block, recv_slot),
    )
    token_grad_query = moved_first[send_block, round_index, send_slot]
    token_grad_value = moved_second[send_block, round_index, send_slot]
    grad_query_low = jnp.sum(token_grad_query, 0).astype(jnp.bfloat16)
    grad_value_low = jnp.sum(token_grad_value, 0).astype(jnp.bfloat16)
    grad_query_full = jnp.dot(rows_one.T, grad_query_low, preferred_element_type=jnp.float32)
    grad_value_full = jnp.dot(rows_one.T, grad_value_low, preferred_element_type=jnp.float32)
    grad_normed_one = branch_sum(
        jnp.dot(grad_query_low, query_full.T, preferred_element_type=jnp.float32)
        + jnp.dot(grad_value_low, value_full.T, preferred_element_type=jnp.float32)
    )
    extra_two, grad_first_gain, grad_first_bias = norm_backward(
        grad_normed_one, normal_one, factor_one, first_gain
    )
    input_grad_two = (grad_two.astype(jnp.float32) + extra_two).astype(jnp.bfloat16)
    query_part, value_part, merge_part, expand_part, shrink_part = (
        lax.psum_scatter(grad_query_full, "seq", scatter_dimension=0, tiled=True),
        lax.psum_scatter(grad_value_full, "seq", scatter_dimension=0, tiled=True),
        lax.psum_scatter(grad_merge, "seq", scatter_dimension=1, tiled=True),
        lax.psum_scatter(grad_expand, "seq", scatter_dimension=0, tiled=True),
        lax.psum_scatter(grad_shrink, "seq", scatter_dimension=1, tiled=True),
    )
    first_gain_sum, first_bias_sum, second_gain_sum, second_bias_sum = lax.psum(
        (grad_first_gain, grad_first_bias, grad_second_gain, grad_second_bias), "seq"
    )
    return (
        sum_one.astype(jnp.bfloat16),
        sum_two.astype(jnp.bfloat16),
        total_low,
        input_grad_two,
        query_part,
        value_part,
        merge_part,
        expand_part,
        shrink_part,
        first_gain_sum,
        first_bias_sum,
        second_gain_sum,
        second_bias_sum,
    )


def seq_groups():
    heads_here = HEADS // lax.axis_size("head")
    devices = lax.axis_size("seq")
    across = [[i * heads_here + j for j in range(heads_here)] for i in range(devices // heads_here)]
    along = [[i * heads_here + j for i in range(devices // heads_here)] for j in range(heads_here)]
    return across, along


def split_columns(value, parts):
    return value.reshape(value.shape[0], parts, value.shape[1] // parts)


def one_hot(order, count):
    return (order[:, None] == jnp.arange(count, dtype=order.dtype)[None]).astype(jnp.bfloat16)


def three_parts(value):
    parts = []
    for _ in range(3):
        part = lax.reduce_precision(value, 8, 7)
        parts.append(part.astype(jnp.bfloat16))
        value = value - part
    return jnp.stack(parts, -1)


def plain_norm(value, gain, shift):
    center = jnp.mean(value, 1, keepdims=True)
    offset = value - center
    factor = lax.rsqrt(jnp.mean(offset * offset, 1, keepdims=True) + 1e-05)
    normal = offset * factor
    return normal, factor, normal * gain + shift


class Place:
    def __init__(self, turns, pair):
        self.turns, self.pair = turns, pair
        self.seq, self.head = lax.axis_index("seq"), lax.axis_index("head")
        self.turn, self.which = self.seq // pair, self.seq % pair
        self.ahead = (self.turn + 1) % turns
        self.behind = (self.turn + turns - 1) % turns
        self.across = (self.turn + 2) % turns
        self.other = 1 - self.which
        self.twin = self.head + 1 - 2 * (self.head % 2)
        self.far = (self.head + 2) % 4
        self.far_twin = self.twin + 2 - 4 * (self.twin // 2)

    def at(self, turn=None, which=None, head=None):
        turn = self.turn if turn is None else turn
        which = self.which if which is None else which
        return (turn * self.pair + which, self.head if head is None else head)

    def greet(self):
        peers = []
        for turn in (self.turn, self.ahead, self.behind, self.across):
            for which in (self.which, self.other):
                if turn is not self.turn or which is not self.which:
                    peers.append(self.at(turn, which))
        for head in (self.twin, self.far, self.far_twin):
            for which in (self.which, self.other):
                peers.append(self.at(which=which, head=head))
        barrier = pltpu.get_barrier_semaphore()
        for peer in peers:
            pl.semaphore_signal(barrier, inc=1, device_id=peer, device_id_type=MESH)
        pl.semaphore_wait(barrier, len(peers))


class Wires:
    def __init__(self, send, receive):
        self.send, self.receive, self.copies = send, receive, []

    def push(self, source, target, device):
        index = len(self.copies)
        copy = pltpu.make_async_remote_copy(
            src_ref=source,
            dst_ref=target,
            send_sem=self.send.at[index],
            recv_sem=self.receive.at[index],
            device_id=device,
            device_id_type=MESH,
        )
        copy.start()
        self.copies.append(copy)
        return copy

    def drain(self):
        for copy in self.copies:
            copy.wait_send()


class RingGather:
    def __init__(self, wires, place, half, whole):
        self.wires, self.place, self.half, self.whole = wires, place, half, whole

    def cross(self, source):
        p = self.place
        self.first = self.wires.push(source, self.half(p.turn, p.which), p.at(which=p.other))

    def along(self):
        p = self.place
        self.first.wait_recv()
        mine = self.whole(p.turn)
        self.right = self.wires.push(mine, mine, p.at(p.ahead))
        self.left = self.wires.push(mine, mine, p.at(p.behind))

    def relay(self):
        p = self.place
        self.right.wait_recv()
        one = self.half(p.behind, 0)
        self.right_on = self.wires.push(one, one, p.at(p.ahead))
        self.left.wait_recv()
        two = self.half(p.ahead, 1)
        self.left_on = self.wires.push(two, two, p.at(p.behind))

    def finish(self):
        self.right_on.wait_recv()
        self.left_on.wait_recv()


class HeadGather:
    def __init__(self, wires, place, slot):
        self.wires, self.place, self.slot = wires, place, slot

    def start(self, source):
        p = self.place
        mine = self.slot(p.head)
        self.long = self.wires.push(source, mine, p.at(head=p.far))
        self.short = self.wires.push(source, mine, p.at(head=p.twin))

    def relay(self):
        p = self.place
        self.long.wait_recv()
        moved = self.slot(p.far)
        self.last = self.wires.push(moved, moved, p.at(head=p.twin))

    def finish(self):
        self.short.wait_recv()
        self.last.wait_recv()


def columns_at(ref, index, width):
    return ref.at[:, pl.ds(pl.multiple_of(index * width, width), width)]


def rows_at(ref, index, width):
    return ref.at[pl.ds(pl.multiple_of(index * width, width), width)]


def front_kernel(
    turns,
    pair,
    one,
    two,
    grad_two,
    query,
    value,
    merge,
    expand,
    shrink,
    params,
    everyone,
    rows_one,
    normal_one,
    factor_one,
    query_full,
    value_full,
    merge_full,
    expand_full,
    shrink_full,
    grad_full,
    two_full,
    params_full,
    packed,
    send,
    receive,
):
    bf16, f32 = jnp.bfloat16, jnp.float32
    place = Place(turns, pair)
    wires = Wires(send, receive)
    rows, width = two.shape
    count = params_full.shape[0]
    whole_width = width * count
    weight_rows, merge_columns = query.shape[0], merge.shape[1]
    place.greet()

    def over_rows(ref, step):
        return RingGather(
            wires,
            place,
            lambda turn, which: rows_at(ref, turn * pair + which, step),
            lambda turn: rows_at(ref, turn, pair * step),
        )

    def over_columns(ref, step):
        return RingGather(
            wires,
            place,
            lambda turn, which: columns_at(ref, turn * pair + which, step),
            lambda turn: columns_at(ref, turn, pair * step),
        )

    def keep(gather, source):
        gather.half(place.turn, place.which)[...] = source[...]

    stream = HeadGather(wires, place, lambda head: two_full.at[head])
    stream.start(two)
    small = HeadGather(wires, place, lambda head: params_full.at[head])
    small.start(params)
    for_query = over_rows(query_full, weight_rows)
    for_value = over_rows(value_full, weight_rows)
    for gather, source in ((for_query, query), (for_value, value)):
        gather.cross(source)
        keep(gather, source)
    two_full[place.head] = two[...]
    params_full[place.head] = params[...]
    for_query.along()
    for_value.along()
    small.relay()
    stream.relay()
    for_query.relay()
    for_value.relay()
    small.finish()
    stream.finish()

    def normalise(tile, carry):
        here = pl.ds(pl.multiple_of(tile * 128, 128), 128)
        parts = [two_full[i, here, :].astype(f32) for i in range(count)]
        center = sum(jnp.sum(part, 1, keepdims=True) for part in parts) / whole_width
        offsets = [part - center for part in parts]
        spread = sum(jnp.sum(part * part, 1, keepdims=True) for part in offsets) / whole_width
        factor = lax.rsqrt(spread + 1e-05)
        factor_one[here, :] = jnp.broadcast_to(factor, (128, factor_one.shape[1]))
        for i, part in enumerate(offsets):
            normal = part * factor
            columns = pl.ds(i * width, width)
            normal_one[here, columns] = normal
            rows_one[here, columns] = (
                normal * params_full[i, 0:1, :] + params_full[i, 1:2, :]
            ).astype(bf16)
        return carry

    lax.fori_loop(0, rows // 128, normalise, 0)
    for_query.finish()
    for_value.finish()

    def project(tile, carry):
        here = pl.ds(pl.multiple_of(tile * 128, 128), 128)
        left = rows_one[here, :]
        for full, place_in in ((query_full, 0), (value_full, 1)):
            result = jnp.dot(left, full[...], preferred_element_type=f32).astype(bf16)
            for which in range(pair):
                packed[which, here, pl.ds(place_in * HEAD_DIM, HEAD_DIM)] = result[
                    :, which * HEAD_DIM : (which + 1) * HEAD_DIM
                ]
        return carry

    lax.fori_loop(0, rows // 128, project, 0)
    tokens = over_rows(everyone, rows)
    tokens.cross(packed.at[place.other])
    tokens.half(place.turn, place.which)[...] = packed[place.which]
    tokens.along()
    bulk = []
    for gather, source in (
        (over_columns(merge_full, merge_columns), merge),
        (over_rows(expand_full, weight_rows), expand),
        (over_columns(shrink_full, merge_columns), shrink),
    ):
        gather.cross(source)
        keep(gather, source)
        bulk.append(gather)
    grads = HeadGather(wires, place, lambda head: columns_at(grad_full, head, width))
    grads.start(grad_two)
    grads.slot(place.head)[...] = grad_two[...]
    tokens.relay()
    for gather in bulk:
        gather.along()
    grads.relay()
    for gather in bulk:
        gather.relay()
    tokens.finish()
    grads.finish()
    for gather in bulk:
        gather.finish()
    wires.drain()


def front(turns, pair, one, two, grad_two, query, value, merge, expand, shrink, params):
    bf16, f32 = jnp.bfloat16, jnp.float32
    rows, width = two.shape
    heads = lax.axis_size("head")
    devices = lax.axis_size("seq")
    shape = jax.ShapeDtypeStruct
    outs = (
        shape((devices * rows, 2 * HEAD_DIM), bf16),
        shape((rows, heads * width), bf16),
        shape((rows, heads * width), f32),
        shape((rows, 128), f32),
        shape((devices * query.shape[0], query.shape[1]), bf16),
        shape((devices * value.shape[0], value.shape[1]), bf16),
        shape((merge.shape[0], devices * merge.shape[1]), bf16),
        shape((devices * expand.shape[0], expand.shape[1]), bf16),
        shape((shrink.shape[0], devices * shrink.shape[1]), bf16),
        shape((rows, heads * width), bf16),
    )
    vmem = pl.BlockSpec(memory_space=pltpu.VMEM)
    return pl.pallas_call(
        partial(front_kernel, turns, pair),
        out_shape=outs,
        in_specs=[vmem] * 9,
        out_specs=[vmem] * len(outs),
        scratch_shapes=[
            pltpu.VMEM((heads, rows, width), bf16),
            pltpu.VMEM((heads,) + params.shape, f32),
            pltpu.VMEM((pair, rows, 2 * HEAD_DIM), bf16),
            pltpu.SemaphoreType.DMA((64,)),
            pltpu.SemaphoreType.DMA((64,)),
        ],
        compiler_params=pltpu.CompilerParams(
            collective_id=0, has_side_effects=True, vmem_limit_bytes=56 << 20
        ),
    )(one, two, grad_two, query, value, merge, expand, shrink, params)


def by_rounds(
    stream_one,
    stream_two,
    grad_one,
    grad_two,
    query_weight,
    value_weight,
    merge_weight,
    expand_weight,
    shrink_weight,
    first_gain,
    first_bias,
    second_gain,
    second_bias,
    bucket_ids,
    sort_order,
):
    bf16, f32 = jnp.bfloat16, jnp.float32
    devices = lax.axis_size("seq")
    place = lax.axis_index("seq")
    rows = stream_one.shape[0]
    rounds, tokens = sort_order.shape
    heads_here = HEADS // lax.axis_size("head")
    turn, which = place // heads_here, place % heads_here
    blocks = tokens // GROUP
    scale = HEAD_DIM ** (-0.5)
    across, along = seq_groups()
    pair_rows = rows * heads_here

    def to_heads(value):
        moved = lax.all_to_all(
            split_columns(value, heads_here), "seq", split_axis=1, concat_axis=0,
            axis_index_groups=across, tiled=True,
        )
        return moved.reshape(pair_rows, value.shape[1] // heads_here)

    def to_tokens(value):
        moved = lax.all_to_all(
            value.reshape(heads_here, rows, value.shape[1]), "seq", split_axis=0, concat_axis=0,
            axis_index_groups=across, tiled=True,
        )
        return jnp.swapaxes(moved, 0, 1).reshape(rows, heads_here * value.shape[1])

    def to_rounds(value):
        return lax.all_gather(value, "seq", axis=0, axis_index_groups=along, tiled=True)

    def swap_rounds(value):
        return lax.all_to_all(
            value, "seq", split_axis=0, concat_axis=0, axis_index_groups=along, tiled=True
        )

    my_order = lax.dynamic_slice_in_dim(sort_order, turn, 1, 0)[0]
    my_bucket = lax.dynamic_slice_in_dim(bucket_ids, turn, 1, 0)[0]
    my_bucket = jnp.sort(my_bucket)
    sorter = one_hot(my_order, tokens)

    def sort_rows(value):
        return jnp.dot(sorter, value, preferred_element_type=f32)

    def unsort_rows(value):
        return lax.dot_general(
            sorter, value, (((0,), (0,)), ((), ())), preferred_element_type=f32
        )

    def with_prior(own):
        pieces = own.reshape((blocks, GROUP) + own.shape[1:])
        return jnp.concatenate([pieces, jnp.roll(pieces, 1, 0)], 1)

    query_place = my_order.reshape(blocks, GROUP)
    query_bucket = my_bucket.reshape(blocks, GROUP)
    key_place, key_bucket = with_prior(my_order), with_prior(my_bucket)
    allowed = (key_place[:, None] <= query_place[:, :, None]) & (
        key_bucket[:, None] == query_bucket[:, :, None]
    )
    itself = key_place[:, None] == query_place[:, :, None]
    live = allowed & jnp.logical_not(itself)

    params = jnp.pad(
        jnp.stack([first_gain, first_bias, second_gain, second_bias]), ((0, 4), (0, 0))
    )
    (
        everyone,
        rows_one,
        normal_one,
        factor_one,
        query_full,
        value_full,
        merge_full,
        expand_full,
        shrink_full,
        grad_rows_two,
    ) = front(
        rounds,
        heads_here,
        stream_one,
        stream_two,
        grad_two,
        query_weight,
        value_weight,
        merge_weight,
        expand_weight,
        shrink_weight,
        params,
    )
    factor_one = factor_one[:, :1]
    sorted_rows = sort_rows(everyone).astype(bf16)
    sorted_query, sorted_value = sorted_rows[:, :HEAD_DIM], sorted_rows[:, HEAD_DIM:]
    query_float = sorted_query.astype(f32)
    inverse_norm = lax.rsqrt(jnp.sum(query_float * query_float, -1, keepdims=True) + 1e-06)
    unit_float = query_float * inverse_norm
    key_unit = with_prior(unit_float.astype(bf16))
    key_value = with_prior(sorted_value)
    query_groups = sorted_query.reshape(blocks, GROUP, HEAD_DIM)
    raw = jnp.einsum("nca,nka->nck", query_groups, key_unit, preferred_element_type=f32) * scale
    scores = jnp.where(itself, own_score, jnp.where(allowed, raw, masked_score))
    peak = jnp.max(scores, -1, keepdims=True)
    totals = peak + jnp.log(jnp.sum(jnp.exp(scores - peak), -1, keepdims=True))
    probs = jnp.exp(scores - totals)
    probs_low = probs.astype(bf16)
    round_out = jnp.einsum(
        "nck,nka->nca", probs_low, key_value, preferred_element_type=f32
    ).astype(bf16)
    back = unsort_rows(
        jnp.concatenate(
            [round_out.reshape(tokens, HEAD_DIM), three_parts(totals.reshape(tokens))], 1
        )
    )
    outs = swap_rounds(back[:, :HEAD_DIM].astype(bf16).reshape(rounds, pair_rows, HEAD_DIM))
    sums = swap_rounds(jnp.sum(back[:, HEAD_DIM:], 1).reshape(rounds, pair_rows))
    mix = jax.nn.softmax(sums, axis=0)
    outs_float = outs.astype(f32)
    attended_pair = jnp.sum(mix[..., None] * outs_float, 0).astype(bf16)
    attended_low = to_tokens(attended_pair)
    sum_one = stream_one.astype(f32) + branch_sum(
        jnp.dot(attended_low, merge_full, preferred_element_type=f32)
    )
    normal_two, factor_two, normed_two = norm_forward(sum_one, second_gain, second_bias)
    rows_two = full_rows(normed_two.astype(bf16))
    hidden = jnp.dot(rows_two, expand_full, preferred_element_type=f32)
    active, gelu_pull = jax.vjp(partial(jax.nn.gelu, approximate=False), hidden)
    active_low = active.astype(bf16)
    sum_two = stream_two.astype(f32) + branch_sum(
        jnp.dot(active_low, shrink_full, preferred_element_type=f32)
    )
    grad_active = jnp.dot(grad_rows_two, shrink_full.T, preferred_element_type=f32)
    grad_hidden = gelu_pull(grad_active)[0].astype(bf16)
    grad_shrink = jnp.dot(active_low.T, grad_rows_two, preferred_element_type=f32).astype(bf16)
    grad_expand = jnp.dot(rows_two.T, grad_hidden, preferred_element_type=f32).astype(bf16)
    grad_normed_two = branch_sum(jnp.dot(grad_hidden, expand_full.T, preferred_element_type=f32))
    extra_one, grad_second_gain, grad_second_bias = norm_backward(
        grad_normed_two, normal_two, factor_two, second_gain
    )
    total_low = (grad_one.astype(f32) + extra_one).astype(bf16)
    grad_rows_one = full_rows(total_low)
    grad_attended = jnp.dot(grad_rows_one, merge_full.T, preferred_element_type=f32).astype(bf16)
    grad_merge = jnp.dot(attended_low.T, grad_rows_one, preferred_element_type=f32).astype(bf16)
    grad_float = to_heads(grad_attended).astype(f32)
    dots = jnp.sum(outs_float * grad_float[None], -1)
    grad_sums = mix * (dots - jnp.sum(mix * dots, 0, keepdims=True))
    grad_outs = swap_rounds((mix[..., None] * grad_float[None]).astype(bf16))
    grad_sums = swap_rounds(grad_sums)
    sorted_grads = sort_rows(
        jnp.concatenate(
            [grad_outs.reshape(tokens, HEAD_DIM), three_parts(grad_sums.reshape(tokens))], 1
        )
    )
    grad_groups = sorted_grads[:, :HEAD_DIM].astype(bf16).reshape(blocks, GROUP, HEAD_DIM)
    total_grads = jnp.sum(sorted_grads[:, HEAD_DIM:], 1).reshape(blocks, GROUP, 1)
    grad_probs = jnp.einsum("nca,nka->nck", grad_groups, key_value, preferred_element_type=f32)
    grad_key_value = jnp.einsum("nck,nca->nka", probs_low, grad_groups, preferred_element_type=f32)
    inner = jnp.sum(probs * grad_probs, -1, keepdims=True)
    grad_scores = jnp.where(live, probs * (grad_probs - inner + total_grads), 0.0).astype(bf16)
    grad_query_groups = (
        jnp.einsum("nck,nka->nca", grad_scores, key_unit, preferred_element_type=f32) * scale
    )
    grad_key_unit = (
        jnp.einsum("nck,nca->nka", grad_scores, query_groups, preferred_element_type=f32) * scale
    )

    def fold_keys(grad_keys):
        return (grad_keys[:, :GROUP] + jnp.roll(grad_keys[:, GROUP:], -1, 0)).reshape(
            tokens, HEAD_DIM
        )

    grad_unit = fold_keys(grad_key_unit)
    grad_sorted_query = grad_query_groups.reshape(tokens, HEAD_DIM) + inverse_norm * (
        grad_unit - unit_float * jnp.sum(unit_float * grad_unit, -1, keepdims=True)
    )
    grad_back = unsort_rows(
        jnp.concatenate([grad_sorted_query, fold_keys(grad_key_value)], 1).astype(bf16)
    )
    grad_parts = swap_rounds(grad_back.astype(bf16).reshape(rounds, pair_rows, 2 * HEAD_DIM))
    grad_pair = to_tokens(jnp.sum(grad_parts.astype(f32), 0).astype(bf16)).reshape(
        rows, heads_here, 2, HEAD_DIM
    )
    grad_query_low = grad_pair[:, :, 0].reshape(rows, heads_here * HEAD_DIM)
    grad_value_low = grad_pair[:, :, 1].reshape(rows, heads_here * HEAD_DIM)
    grad_query_full = jnp.dot(rows_one.T, grad_query_low, preferred_element_type=f32).astype(bf16)
    grad_value_full = jnp.dot(rows_one.T, grad_value_low, preferred_element_type=f32).astype(bf16)
    grad_normed_one = branch_sum(
        jnp.dot(grad_query_low, query_full.T, preferred_element_type=f32)
        + jnp.dot(grad_value_low, value_full.T, preferred_element_type=f32)
    )
    column = lax.axis_index("head") * stream_two.shape[1]
    my_normal = lax.dynamic_slice_in_dim(normal_one, column, stream_two.shape[1], 1)
    extra_two, grad_first_gain, grad_first_bias = norm_backward(
        grad_normed_one, my_normal, factor_one, first_gain
    )
    input_grad_two = (grad_two.astype(f32) + extra_two).astype(bf16)
    query_part, value_part, merge_part, expand_part, shrink_part = (
        lax.psum_scatter(grad_query_full, "seq", scatter_dimension=0, tiled=True).astype(f32),
        lax.psum_scatter(grad_value_full, "seq", scatter_dimension=0, tiled=True).astype(f32),
        lax.psum_scatter(grad_merge, "seq", scatter_dimension=1, tiled=True).astype(f32),
        lax.psum_scatter(grad_expand, "seq", scatter_dimension=0, tiled=True).astype(f32),
        lax.psum_scatter(grad_shrink, "seq", scatter_dimension=1, tiled=True).astype(f32),
    )
    first_gain_sum, first_bias_sum, second_gain_sum, second_bias_sum = lax.psum(
        (grad_first_gain, grad_first_bias, grad_second_gain, grad_second_bias), "seq"
    )
    return (
        sum_one.astype(bf16),
        sum_two.astype(bf16),
        total_low,
        input_grad_two,
        query_part,
        value_part,
        merge_part,
        expand_part,
        shrink_part,
        first_gain_sum,
        first_bias_sum,
        second_gain_sum,
        second_bias_sum,
    )


def solution(mesh):
    placed = (
        P("seq", "head"),
        P("seq", "head"),
        P("seq", "head"),
        P("seq", "head"),
        P("seq", "head"),
        P("seq", "head"),
        P("head", "seq"),
        P("seq", "head"),
        P("head", "seq"),
        P("head"),
        P("head"),
        P("head"),
        P("head"),
        P(),
        P(),
    )

    def local(*arguments):
        rounds = arguments[-1].shape[0]
        if mesh.shape["seq"] * mesh.shape["head"] == rounds * HEADS:
            return by_rounds(*arguments)
        return by_blocks(*arguments)

    return jax.shard_map(
        local,
        mesh=mesh,
        in_specs=placed,
        out_specs=(
            P("seq", "head"),
            P("seq", "head"),
            P("seq", "head"),
            P("seq", "head"),
            P("seq", "head"),
            P("seq", "head"),
            P("head", "seq"),
            P("seq", "head"),
            P("head", "seq"),
            P("head"),
            P("head"),
            P("head"),
            P("head"),
        ),
        check_vma=False,
    )
```

```python
from functools import partial
from types import SimpleNamespace

import jax
import jax.numpy as jnp
from jax import lax
from jax.experimental import pallas as pl
from jax.experimental.pallas import tpu as pltpu
from jax.sharding import PartitionSpec as P

HEADS = 8
HEAD_DIM = 128
GROUP = 64
MESH = pl.DeviceIdType.MESH


masked_score = -1000000000.0
own_score = -100000.0


def as_sent(shard):

    def short(part):
        return part.astype(jnp.bfloat16) if part.dtype == jnp.float32 else part

    return jax.tree.map(short, shard)


def from_behind(block, axis, distance):
    devices = range(lax.axis_size(axis))
    route = [(i - distance, i) for i in devices if i - distance in devices]
    return lax.ppermute(block, axis, route)


def row_sums(first, second):
    return lax.psum((first, second), "head")


def full_rows(part):
    return lax.all_gather(part, "head", axis=1, tiled=True)


def branch_sum(part):
    return lax.psum_scatter(part, "head", scatter_dimension=1, tiled=True)


def norm_forward(value, gain, shift):
    width = value.shape[1] * lax.axis_size("head")
    total, square = row_sums(
        jnp.sum(value, 1, keepdims=True), jnp.sum(value * value, 1, keepdims=True)
    )
    center = total / width
    spread = square / width - center * center
    factor = lax.rsqrt(spread + 1e-05)
    normal = (value - center) * factor
    return (normal, factor, normal * gain + shift)


def norm_backward(grad, normal, factor, gain):
    width = grad.shape[1] * lax.axis_size("head")
    scaled = grad * gain
    first, second = row_sums(
        jnp.sum(scaled, 1, keepdims=True), jnp.sum(scaled * normal, 1, keepdims=True)
    )
    result = factor * (scaled - first / width - normal * (second / width))
    return (result, jnp.sum(grad * normal, 0), jnp.sum(grad, 0))


def regroup_rows(buffer):
    turns = []
    for turn in range(buffer.shape[1]):
        turns.append(
            lax.all_to_all(buffer[:, turn], "seq", split_axis=0, concat_axis=0, tiled=True)
        )
    result = jnp.stack(turns, 1)
    return result


def regroup_totals(buffer):
    moved = lax.all_to_all(
        buffer.reshape(buffer.shape[0], -1, buffer.shape[3]),
        "seq",
        split_axis=0,
        concat_axis=0,
        tiled=True,
    )
    return moved.reshape(buffer.shape)


def regroup_pair(first, second):
    firsts = []
    seconds = []
    for turn in range(first.shape[1]):
        moved_first, moved_second = (
            lax.all_to_all(as_sent(first[:, turn]), "seq", split_axis=0, concat_axis=0, tiled=True),
            lax.all_to_all(
                as_sent(second[:, turn]), "seq", split_axis=0, concat_axis=0, tiled=True
            ),
        )
        firsts.append(moved_first)
        seconds.append(moved_second)
    result = (jnp.stack(firsts, 1), jnp.stack(seconds, 1))
    return result


def by_blocks(
    stream_one,
    stream_two,
    grad_one,
    grad_two,
    query_weight,
    value_weight,
    merge_weight,
    expand_weight,
    shrink_weight,
    first_gain,
    first_bias,
    second_gain,
    second_bias,
    bucket_ids,
    sort_order,
):
    devices = lax.axis_size("seq")
    place = lax.axis_index("seq")
    rows = stream_one.shape[0]
    rounds = sort_order.shape[0]
    capacity = 2 * rows // devices
    blocks = rows // GROUP
    heads_here = HEADS // lax.axis_size("head")
    local_width = heads_here * HEAD_DIM
    scale = HEAD_DIM ** (-0.5)
    round_index = jnp.arange(rounds, dtype=jnp.int32)[:, None]
    counter = jnp.arange(rows, dtype=jnp.int32)

    def invert(line):
        return jnp.zeros_like(line).at[line].set(jnp.arange(line.shape[0], dtype=jnp.int32))

    inverse = jax.vmap(invert)(sort_order)
    my_sorted = lax.dynamic_slice_in_dim(inverse, place * rows, rows, 1)
    send_block = my_sorted // rows
    same_block = send_block[:, :, None] == send_block[:, None, :]
    send_slot = jnp.sum(
        (same_block & (my_sorted[:, None, :] < my_sorted[:, :, None])).astype(jnp.int32), -1
    )
    block_tokens = lax.dynamic_slice_in_dim(sort_order, place * rows, rows, 1)
    source_block = block_tokens // rows
    earlier = counter[None, :] < counter[:, None]
    recv_slot = jnp.sum(
        ((source_block[:, :, None] == source_block[:, None, :]) & earlier[None]).astype(jnp.int32),
        -1,
    )
    query_bucket = jnp.take_along_axis(bucket_ids, block_tokens, 1)
    prior_start = (place - 1) % devices * rows + rows - GROUP
    prior_tokens = lax.dynamic_slice_in_dim(sort_order, prior_start, GROUP, 1)
    prior_bucket = jnp.take_along_axis(bucket_ids, prior_tokens, 1)

    def with_prior(own, prior):
        pieces = own.reshape((rounds, blocks, GROUP) + own.shape[2:])
        before = jnp.concatenate([prior[:, None], pieces[:, :-1]], 1)
        return jnp.concatenate([pieces, before], 2)

    query_place = block_tokens.reshape(rounds, blocks, GROUP)
    key_place = with_prior(block_tokens, prior_tokens)
    key_bucket = with_prior(query_bucket, prior_bucket)
    allowed = (key_place[:, :, None, :] <= query_place[:, :, :, None]) & (
        key_bucket[:, :, None, :] == query_bucket.reshape(rounds, blocks, GROUP)[:, :, :, None]
    )
    itself = key_place[:, :, None, :] == query_place[:, :, :, None]
    live = allowed & jnp.logical_not(itself)

    def fill(values, block, slot):
        empty = jnp.zeros((devices, rounds, capacity, values.shape[-1]), values.dtype)
        return empty.at[block, round_index, slot].set(values)

    normal_one, factor_one, normed_one = norm_forward(
        stream_two.astype(jnp.float32), first_gain, first_bias
    )
    rows_one = full_rows(normed_one.astype(jnp.bfloat16))
    query_full, value_full, merge_full = (
        lax.all_gather(query_weight, "seq", axis=0, tiled=True),
        lax.all_gather(value_weight, "seq", axis=0, tiled=True),
        lax.all_gather(merge_weight, "seq", axis=1, tiled=True),
    )
    queries = jnp.dot(rows_one, query_full, preferred_element_type=jnp.float32).astype(jnp.bfloat16)
    values = jnp.dot(rows_one, value_full, preferred_element_type=jnp.float32).astype(jnp.bfloat16)
    packed = jnp.concatenate([queries, values], 1)
    outgoing = fill(jnp.broadcast_to(packed[None], (rounds,) + packed.shape), send_block, send_slot)
    incoming = regroup_rows(outgoing)
    sorted_rows = incoming[source_block, round_index, recv_slot]
    sorted_query = sorted_rows[:, :, :local_width].reshape(rounds, rows, heads_here, HEAD_DIM)
    sorted_value = sorted_rows[:, :, local_width:].reshape(rounds, rows, heads_here, HEAD_DIM)
    query_float = sorted_query.astype(jnp.float32)
    inverse_norm = lax.rsqrt(jnp.sum(query_float * query_float, -1, keepdims=True) + 1e-06)
    unit_float = query_float * inverse_norm
    unit_low = unit_float.astype(jnp.bfloat16)
    edge = from_behind(
        jnp.concatenate([unit_low[:, -GROUP:], sorted_value[:, -GROUP:]], -1), "seq", 1
    )
    key_unit = with_prior(unit_low, edge[..., :HEAD_DIM])
    key_value = with_prior(sorted_value, edge[..., HEAD_DIM:])
    query_groups = sorted_query.reshape(rounds, blocks, GROUP, heads_here, HEAD_DIM)

    def masked_scores():
        raw = (
            jnp.einsum(
                "rncha,rnkha->rnhck", query_groups, key_unit, preferred_element_type=jnp.float32
            )
            * scale
        )
        return jnp.where(
            itself[:, :, None], own_score, jnp.where(allowed[:, :, None], raw, masked_score)
        )

    scores = masked_scores()
    peak = jnp.max(scores, -1, keepdims=True)
    totals = peak + jnp.log(jnp.sum(jnp.exp(scores - peak), -1, keepdims=True))
    probs_low = jnp.exp(scores - totals).astype(jnp.bfloat16)
    round_out = jnp.einsum(
        "rnhck,rnkha->rncha", probs_low, key_value, preferred_element_type=jnp.float32
    ).astype(jnp.bfloat16)
    out_flat = round_out.reshape(rounds, rows, local_width)
    total_flat = jnp.transpose(totals[..., 0], (0, 1, 3, 2)).reshape(rounds, rows, heads_here)
    token_out = regroup_rows(fill(out_flat, source_block, recv_slot))[
        send_block, round_index, send_slot
    ].astype(jnp.float32)
    token_total = regroup_totals(fill(total_flat, source_block, recv_slot))[
        send_block, round_index, send_slot
    ]
    mix = jax.nn.softmax(token_total, axis=0)
    token_out4 = token_out.reshape(rounds, rows, heads_here, HEAD_DIM)
    attended_low = (
        jnp.sum(mix[..., None] * token_out4, 0).reshape(rows, local_width).astype(jnp.bfloat16)
    )
    sum_one = stream_one.astype(jnp.float32) + branch_sum(
        jnp.dot(attended_low, merge_full, preferred_element_type=jnp.float32)
    )
    normal_two, factor_two, normed_two = norm_forward(sum_one, second_gain, second_bias)
    rows_two = full_rows(normed_two.astype(jnp.bfloat16))
    expand_full, shrink_full = (
        lax.all_gather(expand_weight, "seq", axis=0, tiled=True),
        lax.all_gather(shrink_weight, "seq", axis=1, tiled=True),
    )
    hidden = jnp.dot(rows_two, expand_full, preferred_element_type=jnp.float32)
    active, gelu_pull = jax.vjp(partial(jax.nn.gelu, approximate=False), hidden)
    active_low = active.astype(jnp.bfloat16)
    sum_two = stream_two.astype(jnp.float32) + branch_sum(
        jnp.dot(active_low, shrink_full, preferred_element_type=jnp.float32)
    )
    grad_rows_two = full_rows(grad_two)
    grad_active = jnp.dot(grad_rows_two, shrink_full.T, preferred_element_type=jnp.float32)
    grad_hidden = gelu_pull(grad_active)[0].astype(jnp.bfloat16)
    grad_shrink = jnp.dot(active_low.T, grad_rows_two, preferred_element_type=jnp.float32)
    grad_expand = jnp.dot(rows_two.T, grad_hidden, preferred_element_type=jnp.float32)
    grad_normed_two = branch_sum(
        jnp.dot(grad_hidden, expand_full.T, preferred_element_type=jnp.float32)
    )
    extra_one, grad_second_gain, grad_second_bias = norm_backward(
        grad_normed_two, normal_two, factor_two, second_gain
    )
    total_one = grad_one.astype(jnp.float32) + extra_one
    total_low = total_one.astype(jnp.bfloat16)
    grad_rows_one = full_rows(total_low)
    grad_attended = jnp.dot(grad_rows_one, merge_full.T, preferred_element_type=jnp.float32).astype(
        jnp.bfloat16
    )
    grad_merge = jnp.dot(attended_low.T, grad_rows_one, preferred_element_type=jnp.float32)
    grad_float = grad_attended.astype(jnp.float32).reshape(rows, heads_here, HEAD_DIM)
    dots = jnp.sum(token_out4 * grad_float[None], -1)
    grad_total = mix * (dots - jnp.sum(mix * dots, 0, keepdims=True))
    grad_out_low = (
        (mix[..., None] * grad_float[None]).astype(jnp.bfloat16).reshape(rounds, rows, local_width)
    )
    sorted_grad_out = regroup_rows(fill(grad_out_low, send_block, send_slot))[
        source_block, round_index, recv_slot
    ]
    sorted_grad_total = regroup_totals(fill(grad_total, send_block, send_slot))[
        source_block, round_index, recv_slot
    ]
    grad_groups = sorted_grad_out.reshape(rounds, blocks, GROUP, heads_here, HEAD_DIM)
    total_grad_groups = jnp.transpose(
        sorted_grad_total.reshape(rounds, blocks, GROUP, heads_here), (0, 1, 3, 2)
    )[..., None]
    probs = jnp.exp(masked_scores() - totals)
    probs_again = probs.astype(jnp.bfloat16)
    grad_probs = jnp.einsum(
        "rncha,rnkha->rnhck", grad_groups, key_value, preferred_element_type=jnp.float32
    )
    grad_key_value = jnp.einsum(
        "rnhck,rncha->rnkha", probs_again, grad_groups, preferred_element_type=jnp.float32
    )
    inner = jnp.sum(probs * grad_probs, -1, keepdims=True)
    grad_scores = jnp.where(
        live[:, :, None], probs * (grad_probs - inner + total_grad_groups), 0.0
    ).astype(jnp.bfloat16)
    grad_query_groups = (
        jnp.einsum("rnhck,rnkha->rncha", grad_scores, key_unit, preferred_element_type=jnp.float32)
        * scale
    )
    grad_key_unit = (
        jnp.einsum(
            "rnhck,rncha->rnkha", grad_scores, query_groups, preferred_element_type=jnp.float32
        )
        * scale
    )
    edge_grad = from_behind(
        jnp.concatenate([grad_key_unit[:, 0, GROUP:], grad_key_value[:, 0, GROUP:]], -1).astype(
            jnp.bfloat16
        ),
        "seq",
        -1,
    ).astype(jnp.float32)

    def fold_keys(grad_keys, arriving):
        own = grad_keys[:, :, :GROUP]
        later = jnp.concatenate([grad_keys[:, 1:, GROUP:], arriving[:, None]], 1)
        return (own + later).reshape(rounds, rows, heads_here, HEAD_DIM)

    grad_unit = fold_keys(grad_key_unit, edge_grad[..., :HEAD_DIM])
    grad_sorted_value = fold_keys(grad_key_value, edge_grad[..., HEAD_DIM:])
    grad_sorted_query = grad_query_groups.reshape(
        rounds, rows, heads_here, HEAD_DIM
    ) + inverse_norm * (grad_unit - unit_float * jnp.sum(unit_float * grad_unit, -1, keepdims=True))
    moved_first, moved_second = regroup_pair(
        fill(grad_sorted_query.reshape(rounds, rows, local_width), source_block, recv_slot),
        fill(grad_sorted_value.reshape(rounds, rows, local_width), source_block, recv_slot),
    )
    token_grad_query = moved_first[send_block, round_index, send_slot]
    token_grad_value = moved_second[send_block, round_index, send_slot]
    grad_query_low = jnp.sum(token_grad_query, 0).astype(jnp.bfloat16)
    grad_value_low = jnp.sum(token_grad_value, 0).astype(jnp.bfloat16)
    grad_query_full = jnp.dot(rows_one.T, grad_query_low, preferred_element_type=jnp.float32)
    grad_value_full = jnp.dot(rows_one.T, grad_value_low, preferred_element_type=jnp.float32)
    grad_normed_one = branch_sum(
        jnp.dot(grad_query_low, query_full.T, preferred_element_type=jnp.float32)
        + jnp.dot(grad_value_low, value_full.T, preferred_element_type=jnp.float32)
    )
    extra_two, grad_first_gain, grad_first_bias = norm_backward(
        grad_normed_one, normal_one, factor_one, first_gain
    )
    input_grad_two = (grad_two.astype(jnp.float32) + extra_two).astype(jnp.bfloat16)
    query_part, value_part, merge_part, expand_part, shrink_part = (
        lax.psum_scatter(grad_query_full, "seq", scatter_dimension=0, tiled=True),
        lax.psum_scatter(grad_value_full, "seq", scatter_dimension=0, tiled=True),
        lax.psum_scatter(grad_merge, "seq", scatter_dimension=1, tiled=True),
        lax.psum_scatter(grad_expand, "seq", scatter_dimension=0, tiled=True),
        lax.psum_scatter(grad_shrink, "seq", scatter_dimension=1, tiled=True),
    )
    first_gain_sum, first_bias_sum, second_gain_sum, second_bias_sum = lax.psum(
        (grad_first_gain, grad_first_bias, grad_second_gain, grad_second_bias), "seq"
    )
    return (
        sum_one.astype(jnp.bfloat16),
        sum_two.astype(jnp.bfloat16),
        total_low,
        input_grad_two,
        query_part,
        value_part,
        merge_part,
        expand_part,
        shrink_part,
        first_gain_sum,
        first_bias_sum,
        second_gain_sum,
        second_bias_sum,
    )


def seq_groups():
    pair = HEADS // lax.axis_size("head")
    turns = lax.axis_size("seq") // pair
    across = [[j * turns + i for j in range(pair)] for i in range(turns)]
    along = [[j * turns + i for i in range(turns)] for j in range(pair)]
    return across, along


def split_columns(value, parts):
    return value.reshape(value.shape[0], parts, value.shape[1] // parts)


def one_hot(order, count):
    return (order[:, None] == jnp.arange(count, dtype=order.dtype)[None]).astype(jnp.bfloat16)


def three_parts(value):
    parts = []
    for _ in range(3):
        part = lax.reduce_precision(value, 8, 7)
        parts.append(part.astype(jnp.bfloat16))
        value = value - part
    return jnp.stack(parts, -1)


def plain_norm(value, gain, shift):
    center = jnp.mean(value, 1, keepdims=True)
    offset = value - center
    factor = lax.rsqrt(jnp.mean(offset * offset, 1, keepdims=True) + 1e-05)
    normal = offset * factor
    return normal, factor, normal * gain + shift


def flip(index, bit):
    return index + bit - 2 * bit * ((index // bit) % 2)


def flipped(index, bits):
    for bit in (1, 2, 4):
        if bits & bit:
            index = flip(index, bit)
    return index


class Place:
    def __init__(self, turns):
        self.turns = turns
        self.seq, self.head = lax.axis_index("seq"), lax.axis_index("head")
        self.which, self.turn = self.seq // turns, self.seq % turns

    def peer(self, seq_bits, head_bits=0):
        return (flipped(self.seq, seq_bits), flipped(self.head, head_bits))

    def greet(self):
        peers = [self.peer(bits) for bits in range(1, 8)]
        peers += [self.peer(0, bits) for bits in range(1, 4)]
        barrier = pltpu.get_barrier_semaphore()
        for peer in peers:
            pl.semaphore_signal(barrier, inc=1, device_id=peer, device_id_type=MESH)
        pl.semaphore_wait(barrier, len(peers))


class Wires:
    def __init__(self, send, receive):
        self.send, self.receive, self.copies = send, receive, []

    def push(self, source, target, device):
        index = len(self.copies)
        copy = pltpu.make_async_remote_copy(
            src_ref=source,
            dst_ref=target,
            send_sem=self.send.at[index],
            recv_sem=self.receive.at[index],
            device_id=device,
            device_id_type=MESH,
        )
        copy.start()
        self.copies.append(copy)
        return copy

    def drain(self):
        for copy in self.copies:
            if copy is not None:
                copy.wait_send()


class SeqGather:
    lines = (6, 4, 2)

    def __init__(self, wires, place, slot):
        self.wires, self.place, self.slot = wires, place, slot

    def start(self, source, source_for=None):
        p, mine = self.place, self.slot(self.place.seq)
        self.arriving = {}
        for bits in self.lines:
            block = source if source_for is None else source_for(bits)
            self.arriving[bits] = self.wires.push(block, mine, p.peer(bits))
        self.beside = {0: self.wires.push(source, mine, p.peer(1))}

    def forward(self, bits):
        p = self.place
        self.arriving[bits].wait_recv()
        block = self.slot(flipped(p.seq, bits))
        self.beside[bits] = self.wires.push(block, block, p.peer(1))

    def land(self, bits):
        self.beside[bits].wait_recv()

    def finish(self):
        for bits in self.beside:
            self.land(bits)


class HeadGather:
    def __init__(self, wires, place, slot):
        self.wires, self.place, self.slot = wires, place, slot

    def start(self, source):
        p = self.place
        mine = self.slot(p.head)
        self.long = self.wires.push(source, mine, p.peer(0, 2))
        self.short = self.wires.push(source, mine, p.peer(0, 1))

    def relay(self):
        p = self.place
        self.long.wait_recv()
        moved = self.slot(flip(p.head, 2))
        self.last = self.wires.push(moved, moved, p.peer(0, 1))

    def finish(self):
        self.short.wait_recv()
        self.last.wait_recv()


def columns_at(ref, index, width):
    return ref.at[:, pl.ds(pl.multiple_of(index * width, width), width)]


def rows_at(ref, index, width):
    return ref.at[pl.ds(pl.multiple_of(index * width, width), width)]


def span(index, width):
    return pl.ds(pl.multiple_of(index * width, width), width)


def dot(left, right, contract=((1,), (0,))):
    return lax.dot_general(
        left, right, (contract, ((), ())), preferred_element_type=jnp.float32
    )


def diagonal(size):
    return lax.broadcasted_iota(jnp.int32, (size, size), 0) == lax.broadcasted_iota(
        jnp.int32, (size, size), 1
    )


def to_row(column):
    return jnp.sum(jnp.where(diagonal(column.shape[0]), column, 0.0), 0, keepdims=True)


def to_column(row):
    return jnp.sum(jnp.where(diagonal(row.shape[1]), row, 0.0), 1, keepdims=True)


def in_lanes(total):
    bf16, f32 = jnp.bfloat16, jnp.float32
    high = total.astype(bf16).astype(f32)
    middle = (total - high).astype(bf16).astype(f32)
    low = total - high - middle
    lane = lax.broadcasted_iota(jnp.int32, (total.shape[0], 128), 1)
    parts = jnp.where(lane == 0, high, jnp.where(lane == 1, middle, low))
    return jnp.where(lane < 3, parts, 0.0).astype(bf16)


class Phases:
    def __init__(self, r, turns):
        self.r, self.turns = r, turns
        self.place = Place(turns)
        self.wires = Wires(r.send, r.receive)
        self.rows, self.width = r.two.shape
        self.wide = r.rows_one.shape[1]
        self.count = self.wide // self.width
        self.devices = r.everyone.shape[0] // self.rows
        self.pair = self.devices // turns
        self.units = self.devices


    def spread_columns(self, ref, index):
        column = ref[span(index, self.rows), :].astype(jnp.int32)
        lane = lax.broadcasted_iota(jnp.int32, column.shape, 1)
        parts = [
            jnp.where(column == lane + 128 * i, 1.0, 0.0).astype(jnp.bfloat16)
            for i in range(self.rows // 128)
        ]
        return jnp.concatenate(parts, 1)

    def spread_rows(self, ref, index):
        row = ref[index]
        place = lax.broadcasted_iota(jnp.int32, (self.rows, self.rows), 0)
        return jnp.where(row == place, 1.0, 0.0).astype(jnp.bfloat16)

    def from_units(self, ref, table, index):
        first = index * self.units
        return jnp.concatenate([ref[table[first + unit]] for unit in range(self.units)], 0)

    def to_units(self, index, rows):
        first, step = index * self.units, self.rows // self.units
        for unit in range(self.units):
            self.r.mid[first + unit] = rows[unit * step : (unit + 1) * step].astype(jnp.bfloat16)

    def sort_chunk(self, source, index):
        r = self.r
        here = span(index, self.rows)
        self.to_units(index, dot(self.spread_columns(r.chunk_column, index), source[here, :]))

    def sorted_block(self, index):
        r = self.r
        return dot(
            self.spread_columns(r.block_column, index), self.from_units(r.mid, r.units, index)
        )

    def unsort_block(self, source, index):
        r = self.r
        here = span(index, self.rows)
        self.to_units(index, dot(self.spread_rows(r.block_row, index), source[here, :]))

    def unsorted_chunk(self, index):
        r = self.r
        return dot(
            self.spread_rows(r.chunk_row, index), self.from_units(r.mid, r.units_back, index)
        )

    def over_rows(self, ref):
        step = ref.shape[0] // self.devices
        return SeqGather(self.wires, self.place, lambda seq: rows_at(ref, seq, step))

    def over_columns(self, ref):
        step = ref.shape[1] // self.devices
        return SeqGather(self.wires, self.place, lambda seq: columns_at(ref, seq, step))

    def start_seq(self, gather, source):
        gather.start(source)
        gather.slot(self.place.seq)[...] = source[...]

    def start_head(self, gather, source):
        gather.start(source)
        gather.slot(self.place.head)[...] = source[...]

    def over_head(self, ref):
        return HeadGather(self.wires, self.place, lambda head: columns_at(ref, head, self.width))

    def project(self):
        r, place, wires = self.r, self.place, self.wires
        bf16, f32 = jnp.bfloat16, jnp.float32
        stream = self.over_head(r.two_full)
        small = self.over_head(r.params_full)
        self.start_head(stream, r.two)
        self.start_head(small, r.params)
        query, value = self.over_rows(r.query_full), self.over_rows(r.value_full)
        self.start_seq(query, r.query)
        self.start_seq(value, r.value)
        small.relay()
        stream.relay()
        for bits in SeqGather.lines:
            query.forward(bits)
            value.forward(bits)
        small.finish()
        stream.finish()

        def normalise(tile, carry):
            here = span(tile, 128)
            rows = r.two_full[here, :].astype(f32)
            center = jnp.mean(rows, 1, keepdims=True)
            offset = rows - center
            factor = lax.rsqrt(jnp.mean(offset * offset, 1, keepdims=True) + 1e-05)
            r.center_one[here, :] = jnp.broadcast_to(center, (128, 128))
            r.factor_one[here, :] = jnp.broadcast_to(factor, (128, 128))
            r.rows_one[here, :] = (
                offset * factor * r.params_full[0:1, :] + r.params_full[1:2, :]
            ).astype(bf16)
            return carry

        lax.fori_loop(0, self.rows // 128, normalise, 0)
        query.finish()
        value.finish()

        def multiply(tile, carry):
            here = span(tile, 128)
            left = r.rows_one[here, :]
            for full, column in ((r.query_full, 0), (r.value_full, HEAD_DIM)):
                result = dot(left, full[...]).astype(bf16)
                for which in range(self.pair):
                    r.packed[which, here, column : column + HEAD_DIM] = result[
                        :, which * HEAD_DIM : (which + 1) * HEAD_DIM
                    ]
            return carry

        lax.fori_loop(0, self.rows // 128, multiply, 0)
        self.tokens = self.over_rows(r.everyone)
        mine = r.packed.at[place.which]
        self.tokens.start(
            mine, lambda bits: mine if bits < self.turns else r.packed.at[1 - place.which]
        )
        self.tokens.slot(place.seq)[...] = mine[...]

    def start_bulk(self):
        r, place = self.r, self.place
        my_rows = rows_at(r.merge_full, place.head, r.merge.shape[0])
        self.merge = SeqGather(
            self.wires, place, lambda seq: columns_at(my_rows, seq, r.merge.shape[1])
        )
        self.expand, self.shrink = self.over_rows(r.expand_full), self.over_columns(r.shrink_full)
        self.start_seq(self.merge, r.merge)
        self.start_seq(self.expand, r.expand)
        self.start_seq(self.shrink, r.shrink)
        self.one, self.grads = self.over_head(r.one_full), self.over_head(r.grad_full)
        self.start_head(self.one, r.one)
        self.start_head(self.grads, r.grad_two)

    def forward_bulk(self):
        for bits in (2, 4, 6):
            for gather in (self.merge, self.expand, self.shrink):
                gather.forward(bits)

    def finish_bulk(self):
        r, place = self.r, self.place
        self.merge.finish()
        self.heads = HeadGather(
            self.wires, place, lambda head: rows_at(r.merge_full, head, r.merge.shape[0])
        )
        self.heads.start(self.heads.slot(place.head))

    def sort_tokens(self):
        r, place, tokens = self.r, self.place, self.tokens
        bf16, f32 = jnp.bfloat16, jnp.float32
        self.sort_chunk(r.everyone, place.seq)
        for bits in (2, 6, 4):
            tokens.forward(bits)
        self.start_bulk()
        for bits in (2, 6, 4):
            self.sort_chunk(r.everyone, flipped(place.seq, bits))
        for bits in (0, 2, 6, 4):
            tokens.land(bits)
            self.sort_chunk(r.everyone, flipped(place.seq, bits + 1))

        def second(block, carry):
            rows = self.sorted_block(block)
            here = span(block, self.rows)
            later = pl.ds(pl.multiple_of(block * self.rows + GROUP, GROUP), self.rows)
            query = rows[:, :HEAD_DIM]
            r.sorted_query[here, :] = query.astype(bf16)
            factor = lax.rsqrt(jnp.sum(query * query, 1, keepdims=True) + 1e-06)
            r.unit[later, :] = (query * factor).astype(bf16)
            r.key_value[later, :] = rows[:, HEAD_DIM:].astype(bf16)
            return carry

        lax.fori_loop(0, self.devices, second, 0)
        last = pl.ds(self.devices * self.rows, GROUP)
        r.unit[0:GROUP, :] = r.unit[last, :]
        r.key_value[0:GROUP, :] = r.key_value[last, :]

    def attend(self):
        r = self.r
        bf16, f32 = jnp.bfloat16, jnp.float32
        scale = HEAD_DIM ** (-0.5)
        some = 4 * GROUP

        def window(rows, block):
            return rows[block * GROUP : (block + 2) * GROUP]

        def group(index, carry):
            here = span(index, some)
            longer = pl.ds(pl.multiple_of(index * some, some), some + GROUP)
            query, unit, value = r.sorted_query[here, :], r.unit[longer, :], r.key_value[longer, :]
            raw = [
                dot(query[i * GROUP : (i + 1) * GROUP], window(unit, i), ((1,), (1,)))
                for i in range(4)
            ]
            code = r.code[here, :].astype(f32)
            scores = jnp.where(
                code == 0.0,
                jnp.concatenate(raw, 0) * scale,
                jnp.where(code == 1.0, own_score, masked_score),
            )
            peak = jnp.max(scores, 1, keepdims=True)
            power = jnp.exp(scores - peak)
            total = jnp.sum(power, 1, keepdims=True)
            probs = power * (1.0 / total)
            r.probs[here, :] = probs
            probs = probs.astype(bf16)
            result = [
                dot(probs[i * GROUP : (i + 1) * GROUP], window(value, i)) for i in range(4)
            ]
            r.round_rows[here, :HEAD_DIM] = jnp.concatenate(result, 0).astype(bf16)
            r.round_rows[here, HEAD_DIM:] = in_lanes(peak + jnp.log(total))
            return carry

        lax.fori_loop(0, self.devices * self.rows // some, group, 0)

    def return_rows(self):
        r, place, wires = self.r, self.place, self.wires
        bf16, f32 = jnp.bfloat16, jnp.float32

        def first(block, carry):
            self.unsort_block(r.round_rows, block)
            return carry

        lax.fori_loop(0, self.devices, first, 0)
        coming = []
        for bits in (3, 1, 2, 0):
            turn = flipped(place.turn, bits)

            def second(half, carry, turn=turn, bits=bits):
                rows = self.unsorted_chunk(half * self.turns + turn)
                total = jnp.sum(rows[:, HEAD_DIM:], 1, keepdims=True)
                lines = [to_row(total[i : i + 128]) for i in range(0, self.rows, 128)]
                total = jnp.concatenate(lines, 0)
                if bits:
                    r.out_send[bits - 1, half] = rows[:, :HEAD_DIM].astype(bf16)
                    r.total_send[bits - 1, half] = total
                else:
                    r.outs[place.turn, half] = rows[:, :HEAD_DIM].astype(bf16)
                    r.totals[place.turn, half] = total
                return carry

            lax.fori_loop(0, self.pair, second, 0)
            if bits:
                device = place.peer(bits)
                coming.append(
                    wires.push(r.total_send.at[bits - 1], r.totals.at[place.turn], device)
                )
                coming.append(wires.push(r.out_send.at[bits - 1], r.outs.at[place.turn], device))
        for copy in coming:
            copy.wait_recv()

    def mix_rounds(self):
        r, place = self.r, self.place
        bf16, f32 = jnp.bfloat16, jnp.float32
        totals = [r.totals[turn] for turn in range(self.turns)]
        peak = totals[0]
        for total in totals[1:]:
            peak = jnp.maximum(peak, total)
        power = [jnp.exp(total - peak) for total in totals]
        whole = sum(power[1:], power[0])
        for turn in range(self.turns):
            r.mix_rows[turn] = power[turn] / whole
        pieces = self.rows // 128

        def combine(piece, carry):
            half, part = piece // pieces, piece % pieces
            here = span(part, 128)
            attended = jnp.zeros((128, HEAD_DIM), f32)
            for turn in range(self.turns):
                mix = to_column(r.mix_rows[turn, half, pl.ds(part, 1), :])
                mix = jnp.broadcast_to(mix, (128, HEAD_DIM))
                r.mix[turn, half, here, :] = mix
                attended += mix * r.outs[turn, half, here, :].astype(f32)
            r.attended[half, here, :] = attended.astype(bf16)
            return carry

        lax.fori_loop(0, self.pair * pieces, combine, 0)
        head = place.head * self.pair + place.which
        mine = columns_at(r.attended_full, head, HEAD_DIM)
        swap = self.wires.push(r.attended.at[1 - place.which], mine, place.peer(4))
        mine[...] = r.attended[place.which]
        swap.wait_recv()
        gather = self.over_head(r.attended_full)
        gather.start(gather.slot(place.head))
        gather.relay()
        gather.finish()


def on_device(names, turns, *refs):
    r = SimpleNamespace(**dict(zip(names, refs)))
    steps = Phases(r, turns)
    steps.place.greet()
    steps.project()
    steps.sort_tokens()
    steps.attend()
    steps.forward_bulk()
    steps.return_rows()
    steps.finish_bulk()
    steps.mix_rounds()
    steps.one.relay()
    steps.grads.relay()
    steps.heads.relay()
    steps.one.finish()
    steps.grads.finish()
    steps.heads.finish()
    steps.expand.finish()
    steps.shrink.finish()
    steps.wires.drain()


def whole(turns, arguments, tables):
    bf16, f32, i32 = jnp.bfloat16, jnp.float32, jnp.int32
    heads, devices = lax.axis_size("head"), lax.axis_size("seq")
    pair = devices // turns
    rows, width = arguments["two"].shape
    tokens, wide = devices * rows, heads * width
    hidden = arguments["expand"].shape[1]
    lines = rows // 128
    results = dict(
        sorted_query=((tokens, HEAD_DIM), bf16),
        unit=((tokens + GROUP, HEAD_DIM), bf16),
        key_value=((tokens + GROUP, HEAD_DIM), bf16),
        probs=((tokens, 2 * GROUP), f32),
        outs=((turns, pair, rows, HEAD_DIM), bf16),
        mix=((turns, pair, rows, HEAD_DIM), f32),
        rows_one=((rows, wide), bf16),
        center_one=((rows, 128), f32),
        factor_one=((rows, 128), f32),
        query_full=((wide, width), bf16),
        value_full=((wide, width), bf16),
        merge_full=((wide, wide), bf16),
        expand_full=((wide, hidden), bf16),
        shrink_full=((hidden, wide), bf16),
        one_full=((rows, wide), bf16),
        two_full=((rows, wide), bf16),
        grad_full=((rows, wide), bf16),
        attended_full=((rows, wide), bf16),
    )
    scratch = dict(
        everyone=((tokens, 2 * HEAD_DIM), bf16),
        mid=((devices * devices, rows // devices, 2 * HEAD_DIM), bf16),
        params_full=((8, wide), f32),
        packed=((pair, rows, 2 * HEAD_DIM), bf16),
        round_rows=((tokens, 2 * HEAD_DIM), bf16),
        out_send=((turns - 1, pair, rows, HEAD_DIM), bf16),
        total_send=((turns - 1, pair, lines, 128), f32),
        totals=((turns, pair, lines, 128), f32),
        mix_rows=((turns, pair, lines, 128), f32),
        attended=((pair, rows, HEAD_DIM), bf16),
    )
    wires = dict(send=96, receive=96)
    vmem = pl.BlockSpec(memory_space=pltpu.VMEM)
    smem = pl.BlockSpec(memory_space=pltpu.SMEM)
    names = [*arguments, *tables, *results, *scratch, *wires]
    out = pl.pallas_call(
        partial(on_device, names, turns),
        out_shape=[jax.ShapeDtypeStruct(*item) for item in results.values()],
        in_specs=[vmem] * len(arguments)
        + [smem if name.startswith("units") else vmem for name in tables],
        out_specs=[vmem] * len(results),
        scratch_shapes=[pltpu.VMEM(*item) for item in scratch.values()]
        + [pltpu.SemaphoreType.DMA((number,)) for number in wires.values()],
        compiler_params=pltpu.CompilerParams(
            collective_id=0, has_side_effects=True, vmem_limit_bytes=62 << 20
        ),
    )(*arguments.values(), *tables.values())
    return SimpleNamespace(**dict(zip(results, out)))


def round_tables(order, bucket, devices, rows):
    i32 = jnp.int32
    tokens = order.shape[0]
    unit = rows // devices
    blocks = tokens // GROUP
    place = jnp.arange(tokens, dtype=i32)
    chunk, local = order // rows, order % rows
    by_block = (chunk * rows + place % rows).reshape(devices, rows)
    slot = jnp.sum((by_block[:, None, :] < by_block[:, :, None]).astype(i32), -1)
    token = jnp.sort((chunk * tokens + place) * rows + local) % rows
    token = token.reshape(devices, rows)
    each = jnp.arange(devices, dtype=i32)
    share = jnp.sum((chunk.reshape(devices, rows)[:, None] == each[None, :, None]).astype(i32), -1)
    before = (each[:, None] < each[None, :]).astype(i32)
    in_block = share @ before
    in_chunk = before.T @ share
    start = each * unit

    def find(offset, share, other):
        ends = offset + share
        segment = jnp.sum((ends[:, None, :] <= start[None, :, None]).astype(i32), -1)
        chosen = (segment[:, :, None] == each).astype(i32)
        move = jnp.sum(chosen * (other - offset)[:, None, :], -1)
        return ((segment * rows + start[None] + move) // unit).reshape(-1)

    units = find(in_block, share, in_chunk)
    units_back = find(in_chunk.T, share.T, in_block.T)
    most = devices * (rows // GROUP + 1)
    values = jnp.arange(most + 1, dtype=i32)
    until = jnp.sum((bucket[None] <= values[:, None]).astype(i32), 1)
    sorted_bucket = jnp.sum((until[:, None] <= place[None]).astype(i32), 0)

    def keys(line):
        pieces = line.reshape(blocks, GROUP)
        return jnp.concatenate([jnp.roll(pieces, 1, 0), pieces], 1)[:, None, :]

    def queries(line):
        return line.reshape(blocks, GROUP, 1)

    allowed = (keys(order) <= queries(order)) & (keys(sorted_bucket) == queries(sorted_bucket))
    itself = keys(order) == queries(order)
    code = jnp.where(itself, 1.0, jnp.where(allowed, 0.0, 2.0)).astype(jnp.bfloat16)

    def in_columns(item):
        return jnp.broadcast_to(item.reshape(tokens, 1), (tokens, 128)).astype(jnp.int16)

    return dict(
        block_row=slot.reshape(devices, 1, rows),
        block_column=in_columns(slot),
        chunk_row=token.reshape(devices, 1, rows),
        chunk_column=in_columns(token),
        code=code.reshape(tokens, 2 * GROUP),
        units=units,
        units_back=units_back,
    )


def by_rounds(
    stream_one,
    stream_two,
    grad_one,
    grad_two,
    query_weight,
    value_weight,
    merge_weight,
    expand_weight,
    shrink_weight,
    first_gain,
    first_bias,
    second_gain,
    second_bias,
    bucket_ids,
    sort_order,
):
    bf16, f32 = jnp.bfloat16, jnp.float32
    devices = lax.axis_size("seq")
    place = lax.axis_index("seq")
    rows = stream_one.shape[0]
    rounds, tokens = sort_order.shape
    heads_here = HEADS // lax.axis_size("head")
    turn, which = place % rounds, place // rounds
    blocks = tokens // GROUP
    scale = HEAD_DIM ** (-0.5)
    across, along = seq_groups()
    pair_rows = rows * heads_here

    def to_heads(value):
        moved = lax.all_to_all(
            split_columns(value, heads_here), "seq", split_axis=1, concat_axis=0,
            axis_index_groups=across, tiled=True,
        )
        return moved.reshape(pair_rows, value.shape[1] // heads_here)

    def to_tokens(value):
        moved = lax.all_to_all(
            value.reshape(heads_here, rows, value.shape[1]), "seq", split_axis=0, concat_axis=0,
            axis_index_groups=across, tiled=True,
        )
        return jnp.swapaxes(moved, 0, 1).reshape(rows, heads_here * value.shape[1])

    def to_rounds(value):
        return lax.all_gather(value, "seq", axis=0, axis_index_groups=along, tiled=True)

    def swap_rounds(value):
        return lax.all_to_all(
            value, "seq", split_axis=0, concat_axis=0, axis_index_groups=along, tiled=True
        )

    my_order = lax.dynamic_slice_in_dim(sort_order, turn, 1, 0)[0]
    my_bucket = lax.dynamic_slice_in_dim(bucket_ids, turn, 1, 0)[0]
    sorter = one_hot(my_order, tokens)

    def sort_rows(value):
        return jnp.dot(sorter, value, preferred_element_type=f32)

    def unsort_rows(value):
        return lax.dot_general(
            sorter, value, (((0,), (0,)), ((), ())), preferred_element_type=f32
        )

    def with_prior(longer):
        pieces = longer.reshape((blocks + 1, GROUP, longer.shape[1]))
        return jnp.concatenate([pieces[:-1], pieces[1:]], 1)

    def natural(value):
        pieces = value.reshape((rounds, heads_here, rows) + value.shape[2:])
        return jnp.swapaxes(pieces, 0, 1).reshape((tokens,) + value.shape[2:])

    params = jnp.pad(
        jnp.stack([first_gain, first_bias, second_gain, second_bias]), ((0, 4), (0, 0))
    )
    tables = round_tables(my_order, my_bucket, devices, rows)
    arguments = dict(
        one=stream_one,
        two=stream_two,
        grad_two=grad_two,
        query=query_weight,
        value=value_weight,
        merge=merge_weight,
        expand=expand_weight,
        shrink=shrink_weight,
        params=params,
    )
    k = whole(rounds, arguments, tables)
    mine_heads = lax.axis_index("head") * stream_one.shape[1]
    column = mine_heads

    def mine(value):
        return lax.dynamic_slice_in_dim(value, column, stream_one.shape[1], 1)

    attended_low = mine(k.attended_full)
    merge_full = lax.dynamic_slice_in_dim(k.merge_full, column, stream_one.shape[1], 0)
    rows_one, query_full, value_full = k.rows_one, k.query_full, k.value_full
    expand_full, shrink_full, grad_rows_two = k.expand_full, k.shrink_full, k.grad_full
    factor_one = k.factor_one[:, :1]
    normal_one = (k.two_full.astype(f32) - k.center_one[:, :1]) * factor_one
    outs_float = k.outs.reshape(rounds, pair_rows, HEAD_DIM).astype(f32)
    mix = k.mix.reshape(rounds, pair_rows, HEAD_DIM)[..., 0]
    key_unit, key_value = with_prior(k.unit), with_prior(k.key_value)
    query_groups = k.sorted_query.reshape(blocks, GROUP, HEAD_DIM)
    probs = k.probs.reshape(blocks, GROUP, 2 * GROUP)
    probs_low = probs.astype(bf16)
    live = (tables["code"] == 0).reshape(blocks, GROUP, 2 * GROUP)
    query_float = k.sorted_query.astype(f32)
    inverse_norm = lax.rsqrt(jnp.sum(query_float * query_float, -1, keepdims=True) + 1e-06)
    unit_float = query_float * inverse_norm
    sum_one = stream_one.astype(f32) + branch_sum(
        jnp.dot(attended_low, merge_full, preferred_element_type=f32)
    )
    normal_two, factor_two, normed_two = norm_forward(sum_one, second_gain, second_bias)
    rows_two = full_rows(normed_two.astype(bf16))
    hidden = jnp.dot(rows_two, expand_full, preferred_element_type=f32)
    active, gelu_pull = jax.vjp(partial(jax.nn.gelu, approximate=False), hidden)
    active_low = active.astype(bf16)
    sum_two = stream_two.astype(f32) + branch_sum(
        jnp.dot(active_low, shrink_full, preferred_element_type=f32)
    )
    grad_active = jnp.dot(grad_rows_two, shrink_full.T, preferred_element_type=f32)
    grad_hidden = gelu_pull(grad_active)[0].astype(bf16)
    grad_shrink = jnp.dot(active_low.T, grad_rows_two, preferred_element_type=f32).astype(bf16)
    grad_expand = jnp.dot(rows_two.T, grad_hidden, preferred_element_type=f32).astype(bf16)
    grad_normed_two = branch_sum(jnp.dot(grad_hidden, expand_full.T, preferred_element_type=f32))
    extra_one, grad_second_gain, grad_second_bias = norm_backward(
        grad_normed_two, normal_two, factor_two, second_gain
    )
    total_low = (grad_one.astype(f32) + extra_one).astype(bf16)
    grad_rows_one = full_rows(total_low)
    grad_attended = jnp.dot(grad_rows_one, merge_full.T, preferred_element_type=f32).astype(bf16)
    grad_merge = jnp.dot(attended_low.T, grad_rows_one, preferred_element_type=f32).astype(bf16)
    grad_float = to_heads(grad_attended).astype(f32)
    dots = jnp.sum(outs_float * grad_float[None], -1)
    grad_sums = mix * (dots - jnp.sum(mix * dots, 0, keepdims=True))
    grad_outs = swap_rounds((mix[..., None] * grad_float[None]).astype(bf16))
    grad_sums = swap_rounds(grad_sums)
    sorted_grads = sort_rows(
        jnp.concatenate(
            [natural(grad_outs), three_parts(natural(grad_sums))], 1
        )
    )
    grad_groups = sorted_grads[:, :HEAD_DIM].astype(bf16).reshape(blocks, GROUP, HEAD_DIM)
    total_grads = jnp.sum(sorted_grads[:, HEAD_DIM:], 1).reshape(blocks, GROUP, 1)
    grad_probs = jnp.einsum("nca,nka->nck", grad_groups, key_value, preferred_element_type=f32)
    grad_key_value = jnp.einsum("nck,nca->nka", probs_low, grad_groups, preferred_element_type=f32)
    inner = jnp.sum(probs * grad_probs, -1, keepdims=True)
    grad_scores = jnp.where(live, probs * (grad_probs - inner + total_grads), 0.0).astype(bf16)
    grad_query_groups = (
        jnp.einsum("nck,nka->nca", grad_scores, key_unit, preferred_element_type=f32) * scale
    )
    grad_key_unit = (
        jnp.einsum("nck,nca->nka", grad_scores, query_groups, preferred_element_type=f32) * scale
    )

    def fold_keys(grad_keys):
        return (grad_keys[:, GROUP:] + jnp.roll(grad_keys[:, :GROUP], -1, 0)).reshape(
            tokens, HEAD_DIM
        )

    grad_unit = fold_keys(grad_key_unit)
    grad_sorted_query = grad_query_groups.reshape(tokens, HEAD_DIM) + inverse_norm * (
        grad_unit - unit_float * jnp.sum(unit_float * grad_unit, -1, keepdims=True)
    )
    grad_back = unsort_rows(
        jnp.concatenate([grad_sorted_query, fold_keys(grad_key_value)], 1).astype(bf16)
    )
    grad_back = grad_back.astype(bf16).reshape(heads_here, rounds, rows, 2 * HEAD_DIM)
    grad_parts = swap_rounds(
        jnp.swapaxes(grad_back, 0, 1).reshape(rounds, pair_rows, 2 * HEAD_DIM)
    )
    grad_pair = to_tokens(jnp.sum(grad_parts.astype(f32), 0).astype(bf16)).reshape(
        rows, heads_here, 2, HEAD_DIM
    )
    grad_query_low = grad_pair[:, :, 0].reshape(rows, heads_here * HEAD_DIM)
    grad_value_low = grad_pair[:, :, 1].reshape(rows, heads_here * HEAD_DIM)
    grad_query_full = jnp.dot(rows_one.T, grad_query_low, preferred_element_type=f32).astype(bf16)
    grad_value_full = jnp.dot(rows_one.T, grad_value_low, preferred_element_type=f32).astype(bf16)
    grad_normed_one = branch_sum(
        jnp.dot(grad_query_low, query_full.T, preferred_element_type=f32)
        + jnp.dot(grad_value_low, value_full.T, preferred_element_type=f32)
    )
    my_normal = mine(normal_one)
    extra_two, grad_first_gain, grad_first_bias = norm_backward(
        grad_normed_one, my_normal, factor_one, first_gain
    )
    input_grad_two = (grad_two.astype(f32) + extra_two).astype(bf16)
    query_part, value_part, merge_part, expand_part, shrink_part = (
        lax.psum_scatter(grad_query_full, "seq", scatter_dimension=0, tiled=True).astype(f32),
        lax.psum_scatter(grad_value_full, "seq", scatter_dimension=0, tiled=True).astype(f32),
        lax.psum_scatter(grad_merge, "seq", scatter_dimension=1, tiled=True).astype(f32),
        lax.psum_scatter(grad_expand, "seq", scatter_dimension=0, tiled=True).astype(f32),
        lax.psum_scatter(grad_shrink, "seq", scatter_dimension=1, tiled=True).astype(f32),
    )
    first_gain_sum, first_bias_sum, second_gain_sum, second_bias_sum = lax.psum(
        (grad_first_gain, grad_first_bias, grad_second_gain, grad_second_bias), "seq"
    )
    return (
        sum_one.astype(bf16),
        sum_two.astype(bf16),
        total_low,
        input_grad_two,
        query_part,
        value_part,
        merge_part,
        expand_part,
        shrink_part,
        first_gain_sum,
        first_bias_sum,
        second_gain_sum,
        second_bias_sum,
    )


def solution(mesh):
    placed = (
        P("seq", "head"),
        P("seq", "head"),
        P("seq", "head"),
        P("seq", "head"),
        P("seq", "head"),
        P("seq", "head"),
        P("head", "seq"),
        P("seq", "head"),
        P("head", "seq"),
        P("head"),
        P("head"),
        P("head"),
        P("head"),
        P(),
        P(),
    )

    def local(*arguments):
        rounds = arguments[-1].shape[0]
        if mesh.shape["seq"] * mesh.shape["head"] == rounds * HEADS:
            return by_rounds(*arguments)
        return by_blocks(*arguments)

    return jax.shard_map(
        local,
        mesh=mesh,
        in_specs=placed,
        out_specs=(
            P("seq", "head"),
            P("seq", "head"),
            P("seq", "head"),
            P("seq", "head"),
            P("seq", "head"),
            P("seq", "head"),
            P("head", "seq"),
            P("seq", "head"),
            P("head", "seq"),
            P("head"),
            P("head"),
            P("head"),
            P("head"),
        ),
        check_vma=False,
    )
```

```python
from functools import partial
from types import SimpleNamespace

import jax
import jax.numpy as jnp
from jax import lax
from jax.experimental import pallas as pl
from jax.experimental.pallas import tpu as pltpu
from jax.sharding import PartitionSpec as P

HEADS = 8
HEAD_DIM = 128
GROUP = 64
MESH = pl.DeviceIdType.MESH


masked_score = -1000000000.0
own_score = -100000.0


def as_sent(shard):

    def short(part):
        return part.astype(jnp.bfloat16) if part.dtype == jnp.float32 else part

    return jax.tree.map(short, shard)


def from_behind(block, axis, distance):
    devices = range(lax.axis_size(axis))
    route = [(i - distance, i) for i in devices if i - distance in devices]
    return lax.ppermute(block, axis, route)


def row_sums(first, second):
    return lax.psum((first, second), "head")


def full_rows(part):
    return lax.all_gather(part, "head", axis=1, tiled=True)


def branch_sum(part):
    return lax.psum_scatter(part, "head", scatter_dimension=1, tiled=True)


def norm_forward(value, gain, shift):
    width = value.shape[1] * lax.axis_size("head")
    total, square = row_sums(
        jnp.sum(value, 1, keepdims=True), jnp.sum(value * value, 1, keepdims=True)
    )
    center = total / width
    spread = square / width - center * center
    factor = lax.rsqrt(spread + 1e-05)
    normal = (value - center) * factor
    return (normal, factor, normal * gain + shift)


def norm_backward(grad, normal, factor, gain):
    width = grad.shape[1] * lax.axis_size("head")
    scaled = grad * gain
    first, second = row_sums(
        jnp.sum(scaled, 1, keepdims=True), jnp.sum(scaled * normal, 1, keepdims=True)
    )
    result = factor * (scaled - first / width - normal * (second / width))
    return (result, jnp.sum(grad * normal, 0), jnp.sum(grad, 0))


def regroup_rows(buffer):
    turns = []
    for turn in range(buffer.shape[1]):
        turns.append(
            lax.all_to_all(buffer[:, turn], "seq", split_axis=0, concat_axis=0, tiled=True)
        )
    result = jnp.stack(turns, 1)
    return result


def regroup_totals(buffer):
    moved = lax.all_to_all(
        buffer.reshape(buffer.shape[0], -1, buffer.shape[3]),
        "seq",
        split_axis=0,
        concat_axis=0,
        tiled=True,
    )
    return moved.reshape(buffer.shape)


def regroup_pair(first, second):
    firsts = []
    seconds = []
    for turn in range(first.shape[1]):
        moved_first, moved_second = (
            lax.all_to_all(as_sent(first[:, turn]), "seq", split_axis=0, concat_axis=0, tiled=True),
            lax.all_to_all(
                as_sent(second[:, turn]), "seq", split_axis=0, concat_axis=0, tiled=True
            ),
        )
        firsts.append(moved_first)
        seconds.append(moved_second)
    result = (jnp.stack(firsts, 1), jnp.stack(seconds, 1))
    return result


def by_blocks(
    stream_one,
    stream_two,
    grad_one,
    grad_two,
    query_weight,
    value_weight,
    merge_weight,
    expand_weight,
    shrink_weight,
    first_gain,
    first_bias,
    second_gain,
    second_bias,
    bucket_ids,
    sort_order,
):
    devices = lax.axis_size("seq")
    place = lax.axis_index("seq")
    rows = stream_one.shape[0]
    rounds = sort_order.shape[0]
    capacity = 2 * rows // devices
    blocks = rows // GROUP
    heads_here = HEADS // lax.axis_size("head")
    local_width = heads_here * HEAD_DIM
    scale = HEAD_DIM ** (-0.5)
    round_index = jnp.arange(rounds, dtype=jnp.int32)[:, None]
    counter = jnp.arange(rows, dtype=jnp.int32)

    def invert(line):
        return jnp.zeros_like(line).at[line].set(jnp.arange(line.shape[0], dtype=jnp.int32))

    inverse = jax.vmap(invert)(sort_order)
    my_sorted = lax.dynamic_slice_in_dim(inverse, place * rows, rows, 1)
    send_block = my_sorted // rows
    same_block = send_block[:, :, None] == send_block[:, None, :]
    send_slot = jnp.sum(
        (same_block & (my_sorted[:, None, :] < my_sorted[:, :, None])).astype(jnp.int32), -1
    )
    block_tokens = lax.dynamic_slice_in_dim(sort_order, place * rows, rows, 1)
    source_block = block_tokens // rows
    earlier = counter[None, :] < counter[:, None]
    recv_slot = jnp.sum(
        ((source_block[:, :, None] == source_block[:, None, :]) & earlier[None]).astype(jnp.int32),
        -1,
    )
    query_bucket = jnp.take_along_axis(bucket_ids, block_tokens, 1)
    prior_start = (place - 1) % devices * rows + rows - GROUP
    prior_tokens = lax.dynamic_slice_in_dim(sort_order, prior_start, GROUP, 1)
    prior_bucket = jnp.take_along_axis(bucket_ids, prior_tokens, 1)

    def with_prior(own, prior):
        pieces = own.reshape((rounds, blocks, GROUP) + own.shape[2:])
        before = jnp.concatenate([prior[:, None], pieces[:, :-1]], 1)
        return jnp.concatenate([pieces, before], 2)

    query_place = block_tokens.reshape(rounds, blocks, GROUP)
    key_place = with_prior(block_tokens, prior_tokens)
    key_bucket = with_prior(query_bucket, prior_bucket)
    allowed = (key_place[:, :, None, :] <= query_place[:, :, :, None]) & (
        key_bucket[:, :, None, :] == query_bucket.reshape(rounds, blocks, GROUP)[:, :, :, None]
    )
    itself = key_place[:, :, None, :] == query_place[:, :, :, None]
    live = allowed & jnp.logical_not(itself)

    def fill(values, block, slot):
        empty = jnp.zeros((devices, rounds, capacity, values.shape[-1]), values.dtype)
        return empty.at[block, round_index, slot].set(values)

    normal_one, factor_one, normed_one = norm_forward(
        stream_two.astype(jnp.float32), first_gain, first_bias
    )
    rows_one = full_rows(normed_one.astype(jnp.bfloat16))
    query_full, value_full, merge_full = (
        lax.all_gather(query_weight, "seq", axis=0, tiled=True),
        lax.all_gather(value_weight, "seq", axis=0, tiled=True),
        lax.all_gather(merge_weight, "seq", axis=1, tiled=True),
    )
    queries = jnp.dot(rows_one, query_full, preferred_element_type=jnp.float32).astype(jnp.bfloat16)
    values = jnp.dot(rows_one, value_full, preferred_element_type=jnp.float32).astype(jnp.bfloat16)
    packed = jnp.concatenate([queries, values], 1)
    outgoing = fill(jnp.broadcast_to(packed[None], (rounds,) + packed.shape), send_block, send_slot)
    incoming = regroup_rows(outgoing)
    sorted_rows = incoming[source_block, round_index, recv_slot]
    sorted_query = sorted_rows[:, :, :local_width].reshape(rounds, rows, heads_here, HEAD_DIM)
    sorted_value = sorted_rows[:, :, local_width:].reshape(rounds, rows, heads_here, HEAD_DIM)
    query_float = sorted_query.astype(jnp.float32)
    inverse_norm = lax.rsqrt(jnp.sum(query_float * query_float, -1, keepdims=True) + 1e-06)
    unit_float = query_float * inverse_norm
    unit_low = unit_float.astype(jnp.bfloat16)
    edge = from_behind(
        jnp.concatenate([unit_low[:, -GROUP:], sorted_value[:, -GROUP:]], -1), "seq", 1
    )
    key_unit = with_prior(unit_low, edge[..., :HEAD_DIM])
    key_value = with_prior(sorted_value, edge[..., HEAD_DIM:])
    query_groups = sorted_query.reshape(rounds, blocks, GROUP, heads_here, HEAD_DIM)

    def masked_scores():
        raw = (
            jnp.einsum(
                "rncha,rnkha->rnhck", query_groups, key_unit, preferred_element_type=jnp.float32
            )
            * scale
        )
        return jnp.where(
            itself[:, :, None], own_score, jnp.where(allowed[:, :, None], raw, masked_score)
        )

    scores = masked_scores()
    peak = jnp.max(scores, -1, keepdims=True)
    totals = peak + jnp.log(jnp.sum(jnp.exp(scores - peak), -1, keepdims=True))
    probs_low = jnp.exp(scores - totals).astype(jnp.bfloat16)
    round_out = jnp.einsum(
        "rnhck,rnkha->rncha", probs_low, key_value, preferred_element_type=jnp.float32
    ).astype(jnp.bfloat16)
    out_flat = round_out.reshape(rounds, rows, local_width)
    total_flat = jnp.transpose(totals[..., 0], (0, 1, 3, 2)).reshape(rounds, rows, heads_here)
    token_out = regroup_rows(fill(out_flat, source_block, recv_slot))[
        send_block, round_index, send_slot
    ].astype(jnp.float32)
    token_total = regroup_totals(fill(total_flat, source_block, recv_slot))[
        send_block, round_index, send_slot
    ]
    mix = jax.nn.softmax(token_total, axis=0)
    token_out4 = token_out.reshape(rounds, rows, heads_here, HEAD_DIM)
    attended_low = (
        jnp.sum(mix[..., None] * token_out4, 0).reshape(rows, local_width).astype(jnp.bfloat16)
    )
    sum_one = stream_one.astype(jnp.float32) + branch_sum(
        jnp.dot(attended_low, merge_full, preferred_element_type=jnp.float32)
    )
    normal_two, factor_two, normed_two = norm_forward(sum_one, second_gain, second_bias)
    rows_two = full_rows(normed_two.astype(jnp.bfloat16))
    expand_full, shrink_full = (
        lax.all_gather(expand_weight, "seq", axis=0, tiled=True),
        lax.all_gather(shrink_weight, "seq", axis=1, tiled=True),
    )
    hidden = jnp.dot(rows_two, expand_full, preferred_element_type=jnp.float32)
    active, gelu_pull = jax.vjp(partial(jax.nn.gelu, approximate=False), hidden)
    active_low = active.astype(jnp.bfloat16)
    sum_two = stream_two.astype(jnp.float32) + branch_sum(
        jnp.dot(active_low, shrink_full, preferred_element_type=jnp.float32)
    )
    grad_rows_two = full_rows(grad_two)
    grad_active = jnp.dot(grad_rows_two, shrink_full.T, preferred_element_type=jnp.float32)
    grad_hidden = gelu_pull(grad_active)[0].astype(jnp.bfloat16)
    grad_shrink = jnp.dot(active_low.T, grad_rows_two, preferred_element_type=jnp.float32)
    grad_expand = jnp.dot(rows_two.T, grad_hidden, preferred_element_type=jnp.float32)
    grad_normed_two = branch_sum(
        jnp.dot(grad_hidden, expand_full.T, preferred_element_type=jnp.float32)
    )
    extra_one, grad_second_gain, grad_second_bias = norm_backward(
        grad_normed_two, normal_two, factor_two, second_gain
    )
    total_one = grad_one.astype(jnp.float32) + extra_one
    total_low = total_one.astype(jnp.bfloat16)
    grad_rows_one = full_rows(total_low)
    grad_attended = jnp.dot(grad_rows_one, merge_full.T, preferred_element_type=jnp.float32).astype(
        jnp.bfloat16
    )
    grad_merge = jnp.dot(attended_low.T, grad_rows_one, preferred_element_type=jnp.float32)
    grad_float = grad_attended.astype(jnp.float32).reshape(rows, heads_here, HEAD_DIM)
    dots = jnp.sum(token_out4 * grad_float[None], -1)
    grad_total = mix * (dots - jnp.sum(mix * dots, 0, keepdims=True))
    grad_out_low = (
        (mix[..., None] * grad_float[None]).astype(jnp.bfloat16).reshape(rounds, rows, local_width)
    )
    sorted_grad_out = regroup_rows(fill(grad_out_low, send_block, send_slot))[
        source_block, round_index, recv_slot
    ]
    sorted_grad_total = regroup_totals(fill(grad_total, send_block, send_slot))[
        source_block, round_index, recv_slot
    ]
    grad_groups = sorted_grad_out.reshape(rounds, blocks, GROUP, heads_here, HEAD_DIM)
    total_grad_groups = jnp.transpose(
        sorted_grad_total.reshape(rounds, blocks, GROUP, heads_here), (0, 1, 3, 2)
    )[..., None]
    probs = jnp.exp(masked_scores() - totals)
    probs_again = probs.astype(jnp.bfloat16)
    grad_probs = jnp.einsum(
        "rncha,rnkha->rnhck", grad_groups, key_value, preferred_element_type=jnp.float32
    )
    grad_key_value = jnp.einsum(
        "rnhck,rncha->rnkha", probs_again, grad_groups, preferred_element_type=jnp.float32
    )
    inner = jnp.sum(probs * grad_probs, -1, keepdims=True)
    grad_scores = jnp.where(
        live[:, :, None], probs * (grad_probs - inner + total_grad_groups), 0.0
    ).astype(jnp.bfloat16)
    grad_query_groups = (
        jnp.einsum("rnhck,rnkha->rncha", grad_scores, key_unit, preferred_element_type=jnp.float32)
        * scale
    )
    grad_key_unit = (
        jnp.einsum(
            "rnhck,rncha->rnkha", grad_scores, query_groups, preferred_element_type=jnp.float32
        )
        * scale
    )
    edge_grad = from_behind(
        jnp.concatenate([grad_key_unit[:, 0, GROUP:], grad_key_value[:, 0, GROUP:]], -1).astype(
            jnp.bfloat16
        ),
        "seq",
        -1,
    ).astype(jnp.float32)

    def fold_keys(grad_keys, arriving):
        own = grad_keys[:, :, :GROUP]
        later = jnp.concatenate([grad_keys[:, 1:, GROUP:], arriving[:, None]], 1)
        return (own + later).reshape(rounds, rows, heads_here, HEAD_DIM)

    grad_unit = fold_keys(grad_key_unit, edge_grad[..., :HEAD_DIM])
    grad_sorted_value = fold_keys(grad_key_value, edge_grad[..., HEAD_DIM:])
    grad_sorted_query = grad_query_groups.reshape(
        rounds, rows, heads_here, HEAD_DIM
    ) + inverse_norm * (grad_unit - unit_float * jnp.sum(unit_float * grad_unit, -1, keepdims=True))
    moved_first, moved_second = regroup_pair(
        fill(grad_sorted_query.reshape(rounds, rows, local_width), source_block, recv_slot),
        fill(grad_sorted_value.reshape(rounds, rows, local_width), source_block, recv_slot),
    )
    token_grad_query = moved_first[send_block, round_index, send_slot]
    token_grad_value = moved_second[send_block, round_index, send_slot]
    grad_query_low = jnp.sum(token_grad_query, 0).astype(jnp.bfloat16)
    grad_value_low = jnp.sum(token_grad_value, 0).astype(jnp.bfloat16)
    grad_query_full = jnp.dot(rows_one.T, grad_query_low, preferred_element_type=jnp.float32)
    grad_value_full = jnp.dot(rows_one.T, grad_value_low, preferred_element_type=jnp.float32)
    grad_normed_one = branch_sum(
        jnp.dot(grad_query_low, query_full.T, preferred_element_type=jnp.float32)
        + jnp.dot(grad_value_low, value_full.T, preferred_element_type=jnp.float32)
    )
    extra_two, grad_first_gain, grad_first_bias = norm_backward(
        grad_normed_one, normal_one, factor_one, first_gain
    )
    input_grad_two = (grad_two.astype(jnp.float32) + extra_two).astype(jnp.bfloat16)
    query_part, value_part, merge_part, expand_part, shrink_part = (
        lax.psum_scatter(grad_query_full, "seq", scatter_dimension=0, tiled=True),
        lax.psum_scatter(grad_value_full, "seq", scatter_dimension=0, tiled=True),
        lax.psum_scatter(grad_merge, "seq", scatter_dimension=1, tiled=True),
        lax.psum_scatter(grad_expand, "seq", scatter_dimension=0, tiled=True),
        lax.psum_scatter(grad_shrink, "seq", scatter_dimension=1, tiled=True),
    )
    first_gain_sum, first_bias_sum, second_gain_sum, second_bias_sum = lax.psum(
        (grad_first_gain, grad_first_bias, grad_second_gain, grad_second_bias), "seq"
    )
    return (
        sum_one.astype(jnp.bfloat16),
        sum_two.astype(jnp.bfloat16),
        total_low,
        input_grad_two,
        query_part,
        value_part,
        merge_part,
        expand_part,
        shrink_part,
        first_gain_sum,
        first_bias_sum,
        second_gain_sum,
        second_bias_sum,
    )


def flip(index, bit):
    return index + bit - 2 * bit * ((index // bit) % 2)


def flipped(index, bits):
    for bit in (1, 2, 4):
        if bits & bit:
            index = flip(index, bit)
    return index


class Place:
    def __init__(self, turns):
        self.turns = turns
        self.seq, self.head = lax.axis_index("seq"), lax.axis_index("head")
        self.which, self.turn = self.seq // turns, self.seq % turns

    def peer(self, seq_bits, head_bits=0):
        return (flipped(self.seq, seq_bits), flipped(self.head, head_bits))

    def greet(self):
        peers = [self.peer(bits) for bits in range(1, 8)]
        peers += [self.peer(0, bits) for bits in range(1, 4)]
        barrier = pltpu.get_barrier_semaphore()
        for peer in peers:
            pl.semaphore_signal(barrier, inc=1, device_id=peer, device_id_type=MESH)
        pl.semaphore_wait(barrier, len(peers))


class Wires:
    def __init__(self, send, receive):
        self.send, self.receive, self.copies = send, receive, []

    def push(self, source, target, device):
        index = len(self.copies)
        copy = pltpu.make_async_remote_copy(
            src_ref=source,
            dst_ref=target,
            send_sem=self.send.at[index],
            recv_sem=self.receive.at[index],
            device_id=device,
            device_id_type=MESH,
        )
        copy.start()
        self.copies.append(copy)
        return copy

    def settle(self, copies):
        for copy in copies:
            copy.wait_send()
        done = [id(copy) for copy in copies]
        self.copies = [None if id(copy) in done else copy for copy in self.copies]

    def drain(self):
        self.settle([copy for copy in self.copies if copy is not None])


class SeqGather:
    lines = (6, 4, 2)

    def __init__(self, wires, place, slot):
        self.wires, self.place, self.slot = wires, place, slot

    def start(self, source, source_for=None):
        p, mine = self.place, self.slot(self.place.seq)
        self.arriving = {}
        for bits in self.lines:
            block = source if source_for is None else source_for(bits)
            self.arriving[bits] = self.wires.push(block, mine, p.peer(bits))
        self.beside = {0: self.wires.push(source, mine, p.peer(1))}

    def forward(self, bits):
        p = self.place
        self.arriving[bits].wait_recv()
        block = self.slot(flipped(p.seq, bits))
        self.beside[bits] = self.wires.push(block, block, p.peer(1))

    def land(self, bits):
        self.beside[bits].wait_recv()

    def settle(self):
        self.wires.settle([*self.arriving.values(), *self.beside.values()])

    def finish(self):
        for bits in self.beside:
            self.land(bits)
        self.settle()


class HeadGather:
    def __init__(self, wires, place, slot):
        self.wires, self.place, self.slot = wires, place, slot

    def start(self, source):
        p = self.place
        mine = self.slot(p.head)
        self.long = self.wires.push(source, mine, p.peer(0, 2))
        self.short = self.wires.push(source, mine, p.peer(0, 1))

    def relay(self):
        p = self.place
        self.long.wait_recv()
        moved = self.slot(flip(p.head, 2))
        self.last = self.wires.push(moved, moved, p.peer(0, 1))

    def finish(self):
        self.short.wait_recv()
        self.last.wait_recv()
        self.wires.settle([self.long, self.short, self.last])


def columns_at(ref, index, width):
    return ref.at[:, pl.ds(pl.multiple_of(index * width, width), width)]


def rows_at(ref, index, width):
    return ref.at[pl.ds(pl.multiple_of(index * width, width), width)]


def span(index, width):
    return pl.ds(pl.multiple_of(index * width, width), width)


def dot(left, right, contract=((1,), (0,))):
    return lax.dot_general(
        left, right, (contract, ((), ())), preferred_element_type=jnp.float32
    )


def diagonal(size):
    return lax.broadcasted_iota(jnp.int32, (size, size), 0) == lax.broadcasted_iota(
        jnp.int32, (size, size), 1
    )


def to_row(column):
    return jnp.sum(jnp.where(diagonal(column.shape[0]), column, 0.0), 0, keepdims=True)


def to_column(row):
    return jnp.sum(jnp.where(diagonal(row.shape[1]), row, 0.0), 1, keepdims=True)


def in_lanes(total):
    bf16, f32 = jnp.bfloat16, jnp.float32
    high = total.astype(bf16).astype(f32)
    middle = (total - high).astype(bf16).astype(f32)
    low = total - high - middle
    lane = lax.broadcasted_iota(jnp.int32, (total.shape[0], 128), 1)
    parts = jnp.where(lane == 0, high, jnp.where(lane == 1, middle, low))
    return jnp.where(lane < 3, parts, 0.0).astype(bf16)


class SeqScatter:
    def __init__(self, wires, place, piece, pair, line):
        self.wires, self.place, self.piece = wires, place, piece
        self.pair, self.line = pair, line

    def start(self):
        p = self.place
        self.beside = {}
        for bits in (6, 4, 2, 0):
            source = self.piece(flipped(p.seq, bits + 1))
            self.beside[bits] = self.wires.push(source, self.pair.at[bits // 2], p.peer(1))

    def along(self):
        p, f32 = self.place, jnp.float32
        self.coming = []
        for bits in (6, 4, 2):
            self.beside[bits].wait_recv()
            at = self.pair.at[bits // 2]
            mine = self.piece(flipped(p.seq, bits))[...]
            at[...] = (at[...].astype(f32) + mine.astype(f32)).astype(jnp.bfloat16)
            self.coming.append(self.wires.push(at, self.line.at[bits // 2 - 1], p.peer(bits)))

    def finish(self, target):
        p, f32 = self.place, jnp.float32
        self.beside[0].wait_recv()
        total = self.piece(p.seq)[...].astype(f32) + self.pair[0].astype(f32)
        for copy in self.coming:
            copy.wait_recv()
        for other in range(3):
            total += self.line[other].astype(f32)
        target[...] = total


class Phases:
    def __init__(self, r, turns):
        self.r, self.turns = r, turns
        self.place = Place(turns)
        self.wires = Wires(r.send, r.receive)
        self.rows, self.width = r.two.shape
        self.wide = r.rows_one.shape[1]
        self.count = self.wide // self.width
        self.devices = r.everyone.shape[0] // self.rows
        self.pair = self.devices // turns
        self.units = self.devices


    def spread_columns(self, ref, index):
        column = ref[span(index, self.rows), :].astype(jnp.int32)
        lane = lax.broadcasted_iota(jnp.int32, column.shape, 1)
        parts = [
            jnp.where(column == lane + 128 * i, 1.0, 0.0).astype(jnp.bfloat16)
            for i in range(self.rows // 128)
        ]
        return jnp.concatenate(parts, 1)

    def spread_rows(self, ref, index):
        row = ref[index]
        place = lax.broadcasted_iota(jnp.int32, (self.rows, self.rows), 0)
        return jnp.where(row == place, 1.0, 0.0).astype(jnp.bfloat16)

    def from_units(self, ref, table, index):
        first = index * self.units
        return jnp.concatenate([ref[table[first + unit]] for unit in range(self.units)], 0)

    def to_units(self, index, rows):
        first, step = index * self.units, self.rows // self.units
        for unit in range(self.units):
            self.r.mid[first + unit] = rows[unit * step : (unit + 1) * step].astype(jnp.bfloat16)

    def sort_chunk(self, source, index):
        r = self.r
        here = span(index, self.rows)
        self.to_units(index, dot(self.spread_columns(r.chunk_column, index), source[here, :]))

    def sorted_block(self, index):
        r = self.r
        return dot(
            self.spread_columns(r.block_column, index), self.from_units(r.mid, r.units, index)
        )

    def unsort_block(self, source, index):
        r = self.r
        here = span(index, self.rows)
        self.to_units(index, dot(self.spread_rows(r.block_row, index), source[here, :]))

    def unsorted_chunk(self, index):
        r = self.r
        return dot(
            self.spread_rows(r.chunk_row, index), self.from_units(r.mid, r.units_back, index)
        )

    def over_rows(self, ref):
        step = ref.shape[0] // self.devices
        return SeqGather(self.wires, self.place, lambda seq: rows_at(ref, seq, step))

    def over_columns(self, ref):
        step = ref.shape[1] // self.devices
        return SeqGather(self.wires, self.place, lambda seq: columns_at(ref, seq, step))

    def start_seq(self, gather, source):
        gather.start(source)
        gather.slot(self.place.seq)[...] = source[...]

    def start_head(self, gather, source):
        gather.start(source)
        gather.slot(self.place.head)[...] = source[...]

    def over_head(self, ref):
        return HeadGather(self.wires, self.place, lambda head: columns_at(ref, head, self.width))

    def project(self):
        r, place, wires = self.r, self.place, self.wires
        bf16, f32 = jnp.bfloat16, jnp.float32
        stream = self.over_head(r.two_full)
        small = self.over_head(r.params_full)
        self.start_head(stream, r.two)
        self.start_head(small, r.params)
        query, value = self.over_rows(r.query_full), self.over_rows(r.value_full)
        self.start_seq(query, r.query)
        self.start_seq(value, r.value)
        small.relay()
        stream.relay()
        for bits in SeqGather.lines:
            query.forward(bits)
            value.forward(bits)
        small.finish()
        stream.finish()

        def normalise(tile, carry):
            here = span(tile, 128)
            rows = r.two_full[here, :].astype(f32)
            center = jnp.mean(rows, 1, keepdims=True)
            offset = rows - center
            factor = lax.rsqrt(jnp.mean(offset * offset, 1, keepdims=True) + 1e-05)
            r.center_one[here, :] = jnp.broadcast_to(center, (128, 128))
            r.factor_one[here, :] = jnp.broadcast_to(factor, (128, 128))
            r.rows_one[here, :] = (
                offset * factor * r.params_full[0:1, :] + r.params_full[1:2, :]
            ).astype(bf16)
            return carry

        lax.fori_loop(0, self.rows // 128, normalise, 0)
        query.finish()
        value.finish()

        def multiply(tile, carry):
            here = span(tile, 128)
            left = r.rows_one[here, :]
            for full, column in ((r.query_full, 0), (r.value_full, HEAD_DIM)):
                result = dot(left, full[...]).astype(bf16)
                for which in range(self.pair):
                    r.packed[which, here, column : column + HEAD_DIM] = result[
                        :, which * HEAD_DIM : (which + 1) * HEAD_DIM
                    ]
            return carry

        lax.fori_loop(0, self.rows // 128, multiply, 0)
        self.tokens = self.over_rows(r.everyone)
        mine = r.packed.at[place.which]
        self.tokens.start(
            mine, lambda bits: mine if bits < self.turns else r.packed.at[1 - place.which]
        )
        self.tokens.slot(place.seq)[...] = mine[...]

    def start_bulk(self):
        r, place = self.r, self.place
        my_rows = rows_at(r.merge_full, place.head, r.merge.shape[0])
        self.merge = SeqGather(
            self.wires, place, lambda seq: columns_at(my_rows, seq, r.merge.shape[1])
        )
        self.expand, self.shrink = self.over_rows(r.expand_full), self.over_columns(r.shrink_full)
        self.start_seq(self.merge, r.merge)
        self.start_seq(self.expand, r.expand)
        self.start_seq(self.shrink, r.shrink)
        self.one, self.grads = self.over_head(r.one_full), self.over_head(r.grad_full)
        self.start_head(self.one, r.one)
        self.start_head(self.grads, r.grad_two)

    def forward_bulk(self):
        for bits in (2, 4, 6):
            for gather in (self.merge, self.expand, self.shrink):
                gather.forward(bits)

    def finish_bulk(self):
        r, place = self.r, self.place
        self.merge.finish()
        self.heads = HeadGather(
            self.wires, place, lambda head: rows_at(r.merge_full, head, r.merge.shape[0])
        )
        self.heads.start(self.heads.slot(place.head))

    def sort_tokens(self):
        r, place, tokens = self.r, self.place, self.tokens
        bf16, f32 = jnp.bfloat16, jnp.float32
        self.sort_chunk(r.everyone, place.seq)
        for bits in (2, 6, 4):
            tokens.forward(bits)
        self.start_bulk()
        for bits in (2, 6, 4):
            self.sort_chunk(r.everyone, flipped(place.seq, bits))
        for bits in (0, 2, 6, 4):
            tokens.land(bits)
            self.sort_chunk(r.everyone, flipped(place.seq, bits + 1))
        tokens.settle()

        def second(block, carry):
            rows = self.sorted_block(block)
            here = span(block, self.rows)
            later = pl.ds(pl.multiple_of(block * self.rows + GROUP, GROUP), self.rows)
            query = rows[:, :HEAD_DIM]
            r.sorted_query[here, :] = query.astype(bf16)
            factor = lax.rsqrt(jnp.sum(query * query, 1, keepdims=True) + 1e-06)
            r.unit[later, :] = (query * factor).astype(bf16)
            r.key_value[later, :] = rows[:, HEAD_DIM:].astype(bf16)
            return carry

        lax.fori_loop(0, self.devices, second, 0)
        last = pl.ds(self.devices * self.rows, GROUP)
        r.unit[0:GROUP, :] = r.unit[last, :]
        r.key_value[0:GROUP, :] = r.key_value[last, :]

    def attend(self):
        r = self.r
        bf16, f32 = jnp.bfloat16, jnp.float32
        scale = HEAD_DIM ** (-0.5)
        some = 4 * GROUP

        def window(rows, block):
            return rows[block * GROUP : (block + 2) * GROUP]

        def group(index, carry):
            here = span(index, some)
            longer = pl.ds(pl.multiple_of(index * some, some), some + GROUP)
            query, unit, value = r.sorted_query[here, :], r.unit[longer, :], r.key_value[longer, :]
            raw = [
                dot(query[i * GROUP : (i + 1) * GROUP], window(unit, i), ((1,), (1,)))
                for i in range(4)
            ]
            code = r.code[here, :].astype(f32)
            scores = jnp.where(
                code == 0.0,
                jnp.concatenate(raw, 0) * scale,
                jnp.where(code == 1.0, own_score, masked_score),
            )
            peak = jnp.max(scores, 1, keepdims=True)
            power = jnp.exp(scores - peak)
            total = jnp.sum(power, 1, keepdims=True)
            probs = power * (1.0 / total)
            r.probs[here, :] = probs
            probs = probs.astype(bf16)
            result = [
                dot(probs[i * GROUP : (i + 1) * GROUP], window(value, i)) for i in range(4)
            ]
            r.round_rows[here, :HEAD_DIM] = jnp.concatenate(result, 0).astype(bf16)
            r.round_rows[here, HEAD_DIM:] = in_lanes(peak + jnp.log(total))
            return carry

        lax.fori_loop(0, self.devices * self.rows // some, group, 0)

    def return_rows(self):
        r, place, wires = self.r, self.place, self.wires
        bf16, f32 = jnp.bfloat16, jnp.float32

        def first(block, carry):
            self.unsort_block(r.round_rows, block)
            return carry

        lax.fori_loop(0, self.devices, first, 0)
        coming = []
        for bits in (3, 1, 2, 0):
            turn = flipped(place.turn, bits)

            def second(half, carry, turn=turn, bits=bits):
                rows = self.unsorted_chunk(half * self.turns + turn)
                total = jnp.sum(rows[:, HEAD_DIM:], 1, keepdims=True)
                lines = [to_row(total[i : i + 128]) for i in range(0, self.rows, 128)]
                total = jnp.concatenate(lines, 0)
                if bits:
                    r.out_send[bits - 1, half] = rows[:, :HEAD_DIM].astype(bf16)
                    r.total_send[bits - 1, half] = total
                else:
                    r.outs[place.turn, half] = rows[:, :HEAD_DIM].astype(bf16)
                    r.totals[place.turn, half] = total
                return carry

            lax.fori_loop(0, self.pair, second, 0)
            if bits:
                device = place.peer(bits)
                coming.append(
                    wires.push(r.total_send.at[bits - 1], r.totals.at[place.turn], device)
                )
                coming.append(wires.push(r.out_send.at[bits - 1], r.outs.at[place.turn], device))
        for copy in coming:
            copy.wait_recv()
        wires.settle(coming)

    def mix_rounds(self):
        r, place = self.r, self.place
        bf16, f32 = jnp.bfloat16, jnp.float32
        totals = [r.totals[turn] for turn in range(self.turns)]
        peak = totals[0]
        for total in totals[1:]:
            peak = jnp.maximum(peak, total)
        power = [jnp.exp(total - peak) for total in totals]
        whole = sum(power[1:], power[0])
        for turn in range(self.turns):
            r.mix_rows[turn] = power[turn] / whole
        pieces = self.rows // 128

        def combine(piece, carry):
            half, part = piece // pieces, piece % pieces
            here = span(part, 128)
            attended = jnp.zeros((128, HEAD_DIM), f32)
            for turn in range(self.turns):
                mix = to_column(r.mix_rows[turn, half, pl.ds(part, 1), :])
                mix = jnp.broadcast_to(mix, (128, HEAD_DIM))
                r.mix[turn, half, here, :] = mix
                attended += mix * r.outs[turn, half, here, :].astype(f32)
            r.attended[half, here, :] = attended.astype(bf16)
            return carry

        lax.fori_loop(0, self.pair * pieces, combine, 0)
        head = place.head * self.pair + place.which
        mine = columns_at(r.attended_full, head, HEAD_DIM)
        swap = self.wires.push(r.attended.at[1 - place.which], mine, place.peer(4))
        mine[...] = r.attended[place.which]
        swap.wait_recv()
        gather = self.over_head(r.attended_full)
        gather.start(gather.slot(place.head))
        gather.relay()
        gather.finish()


    def feed_forward(self):
        r, place, wires = self.r, self.place, self.wires
        bf16, f32 = jnp.bfloat16, jnp.float32
        tile_rows = self.rows // 2
        self.parts_two = []
        for tile in range(2):
            here = pl.ds(tile * tile_rows, tile_rows)
            total = r.one_full[here, :].astype(f32) + dot(r.attended_full[here, :], r.merge_full[...])
            center = jnp.mean(total, 1, keepdims=True)
            offset = total - center
            factor = lax.rsqrt(jnp.mean(offset * offset, 1, keepdims=True) + 1e-05)
            normal = offset * factor
            r.tall[...] = total
            r.result_one[here, :] = columns_at(r.tall, place.head, self.width)[...].astype(bf16)
            r.tall[...] = normal
            r.normal_two[here, :] = columns_at(r.tall, place.head, self.width)[...]
            r.factor_two[here, :] = jnp.broadcast_to(factor, (tile_rows, 128))
            rows = (normal * r.params_full[2:3, :] + r.params_full[3:4, :]).astype(bf16)
            r.rows_two[here, :] = rows
            hidden = dot(rows, r.expand_full[...])
            below = 0.5 * (1.0 + lax.erf(hidden * (0.5**0.5)))
            r.active[here, :] = (hidden * below).astype(bf16)
            slope = below + hidden * jnp.exp(-0.5 * hidden * hidden) * ((2.0 * jnp.pi) ** -0.5)
            grad = dot(r.grad_full[here, :], r.shrink_full[...], ((1,), (1,)))
            grad = (grad * slope).astype(bf16)
            r.grad_hidden[here, :] = grad
            part = dot(grad, r.expand_full[...], ((1,), (1,)))
            self.send_part(
                tile, part, r.tall[...], r.params_full[2:3, :], r.part_two, r.stat_two,
                r.parts_two, self.parts_two,
            )
        self.send_stats(r.stat_two, r.stats_two, self.parts_two)

    def send_part(self, tile, part, normal, gain, part_ref, stat_ref, target, copies):
        tile_rows = part.shape[0]
        here = pl.ds(tile * tile_rows, tile_rows)
        scaled = part * gain
        first = jnp.sum(scaled, 1, keepdims=True)
        second = jnp.sum(scaled * normal, 1, keepdims=True)
        lines = tile_rows // 128
        for line in range(lines):
            at = slice(line * 128, (line + 1) * 128)
            row = tile * lines + line
            stat_ref[row : row + 1, :] = to_row(first[at])
            row += self.rows // 128
            stat_ref[row : row + 1, :] = to_row(second[at])
        part_ref[here, :] = part.astype(jnp.bfloat16)
        for bits in (2, 3, 1):
            device = self.place.peer(0, bits)
            source = columns_at(part_ref.at[here], device[1], self.width)
            copies.append(self.wires.push(source, target.at[bits - 1, here], device))

    def send_stats(self, stat_ref, target, copies):
        for bits in (2, 3, 1):
            device = self.place.peer(0, bits)
            copies.append(self.wires.push(stat_ref, target.at[bits - 1], device))

    def norm_back(self, part_ref, parts, stat_ref, stats, normal_at, factor_ref, gain, finish):
        f32 = jnp.float32
        lines = self.rows // 128

        def piece(line, carry):
            here = span(line, 128)
            grad = columns_at(part_ref.at[here], self.place.head, self.width)[...].astype(f32)
            first, second = stat_ref[pl.ds(line, 1), :], stat_ref[pl.ds(line + lines, 1), :]
            for other in range(3):
                grad += parts[other, here, :].astype(f32)
                first += stats[other, pl.ds(line, 1), :]
                second += stats[other, pl.ds(line + lines, 1), :]
            normal = normal_at(here)
            first, second = to_column(first) / self.wide, to_column(second) / self.wide
            finish(here, factor_ref[here, 0:1] * (grad * gain - first - normal * second))
            gains, biases = carry
            return (
                gains + jnp.sum(grad * normal, 0, keepdims=True),
                biases + jnp.sum(grad, 0, keepdims=True),
            )

        zero = jnp.zeros((1, self.width), f32)
        return lax.fori_loop(0, lines, piece, (zero, zero))

    def my_params(self, row):
        return columns_at(self.r.params_full, self.place.head, self.width)[row : row + 1, :]

    def feed_back(self):
        r, place, wires = self.r, self.place, self.wires
        bf16, f32 = jnp.bfloat16, jnp.float32
        self.weights(r.rows_two, r.grad_hidden, r.grad_expand)
        self.expand_out = SeqScatter(
            wires, place, lambda seq: rows_at(r.grad_expand, seq, r.expand.shape[0]),
            r.expand_pair, r.expand_line,
        )
        for copy in self.parts_two:
            copy.wait_recv()
        wires.settle(self.parts_two)

        def finish(here, change):
            total = r.grad_one[here, :].astype(f32) + change
            r.input_grad_one[here, :] = total.astype(bf16)

        gains, biases = self.norm_back(
            r.part_two, r.parts_two, r.stat_two, r.stats_two,
            lambda here: r.normal_two[here, :], r.factor_two, self.my_params(2), finish,
        )
        r.norm_send[2:3, :], r.norm_send[3:4, :] = gains, biases
        gather = self.over_head(r.grad_rows_one)
        self.start_head(gather, r.input_grad_one)
        self.expand_out.start()

        def feed(tile, carry):
            here = span(tile, 256)
            r.feed[here, :] = dot(r.active[here, :], r.shrink_full[...]).astype(bf16)
            return carry

        lax.fori_loop(0, self.rows // 256, feed, 0)
        self.weights(r.active, r.grad_full, r.grad_shrink)
        self.shrink_out = SeqScatter(
            wires, place, lambda seq: columns_at(r.grad_shrink, seq, r.shrink.shape[1]),
            r.shrink_pair, r.shrink_line,
        )
        self.shrink_out.start()
        gather.relay()
        gather.finish()

    def weights(self, left, right, target):
        step = min(256, left.shape[1])

        def piece(index, carry):
            columns = span(index, step)
            result = dot(left[:, columns], right[...], ((0,), (0,)))
            target[columns, :] = result.astype(jnp.bfloat16)
            return carry

        lax.fori_loop(0, left.shape[1] // step, piece, 0)

    def send_feed(self):
        r = self.r
        self.feeds = []
        for bits in (2, 3, 1):
            device = self.place.peer(0, bits)
            source = columns_at(r.feed, device[1], self.width)
            self.feeds.append(self.wires.push(source, r.feeds.at[bits - 1], device))

    def finish_feed(self):
        r = self.r
        f32 = jnp.float32
        for copy in self.feeds:
            copy.wait_recv()
        total = r.two[...].astype(f32)
        total += columns_at(r.feed, self.place.head, self.width)[...].astype(f32)
        for other in range(3):
            total += r.feeds[other].astype(f32)
        r.result_two[...] = total.astype(jnp.bfloat16)


    def grad_rounds(self):
        r, place, wires = self.r, self.place, self.wires
        bf16, f32 = jnp.bfloat16, jnp.float32
        my_rows = rows_at(r.merge_full, place.head, r.merge.shape[0])

        def attended(tile, carry):
            here = span(tile, 256)
            grad = dot(r.grad_rows_one[here, :], my_rows[...], ((1,), (1,))).astype(bf16)
            for which in range(self.pair):
                r.grad_heads[which, here, :] = grad[:, which * HEAD_DIM : (which + 1) * HEAD_DIM]
            return carry

        lax.fori_loop(0, self.rows // 256, attended, 0)
        mine = r.grad_attended.at[place.which]
        swap = wires.push(r.grad_heads.at[1 - place.which], mine, place.peer(4))
        mine[...] = r.grad_heads[place.which]
        lines = self.rows // 128

        def spread(half, carry):
            def piece(part, carry):
                here = span(part, 128)
                grad = r.grad_attended[half, here, :].astype(f32)
                turns = [flipped(place.turn, bits) for bits in range(self.turns)]
                mixes = [r.mix[turn, half, here, :] for turn in turns]
                dots = [
                    jnp.sum(r.outs[turn, half, here, :].astype(f32) * grad, 1, keepdims=True)
                    for turn in turns
                ]
                mean = sum(mix[:, 0:1] * value for mix, value in zip(mixes, dots))
                for bits in range(self.turns):
                    change = to_row(mixes[bits][:, 0:1] * (dots[bits] - mean))
                    rows = (mixes[bits] * grad).astype(bf16)
                    if bits:
                        r.grad_send[bits - 1, half, here, :] = rows
                        r.grad_total_send[bits - 1, half, pl.ds(part, 1), :] = change
                    else:
                        r.grad_outs[place.turn, half, here, :] = rows
                        r.grad_totals[place.turn, half, pl.ds(part, 1), :] = change
                return carry

            return lax.fori_loop(0, lines, piece, carry)

        spread(place.which, 0)
        self.weights(columns_at(r.attended_full, place.head, self.width), r.grad_rows_one, r.grad_merge)
        swap.wait_recv()
        spread(1 - place.which, 0)
        self.grads_coming = {}
        for bits in (3, 1, 2):
            device = place.peer(bits)
            self.grads_coming[bits] = (
                wires.push(r.grad_total_send.at[bits - 1], r.grad_totals.at[place.turn], device),
                wires.push(r.grad_send.at[bits - 1], r.grad_outs.at[place.turn], device),
            )
        self.merge_out = SeqScatter(
            wires, place, lambda seq: columns_at(r.grad_merge, seq, r.merge.shape[1]),
            r.merge_pair, r.merge_line,
        )
        self.merge_out.start()

    def sort_grads(self):
        r, place = self.r, self.place
        bf16 = jnp.bfloat16
        lines = self.rows // 128
        for bits in (0, 1, 2, 3):
            turn = flipped(place.turn, bits)
            if bits:
                for copy in self.grads_coming[bits]:
                    copy.wait_recv()

            def stage(half, carry, turn=turn):
                chunk = half * self.turns + turn
                r.everyone[span(chunk, self.rows), :HEAD_DIM] = r.grad_outs[turn, half]

                def piece(part, carry):
                    total = to_column(r.grad_totals[turn, half, pl.ds(part, 1), :])
                    r.everyone[span(chunk * lines + part, 128), HEAD_DIM:] = in_lanes(total)
                    return carry

                lax.fori_loop(0, lines, piece, 0)
                self.sort_chunk(r.everyone, chunk)
                return carry

            lax.fori_loop(0, self.pair, stage, 0)

        def second(block, carry):
            r.round_rows[span(block, self.rows), :] = self.sorted_block(block).astype(bf16)
            return carry

        lax.fori_loop(0, self.devices, second, 0)

    def attend_back(self):
        r = self.r
        bf16, f32 = jnp.bfloat16, jnp.float32
        scale = HEAD_DIM ** (-0.5)
        some = 4 * GROUP
        r.grad_unit[0:GROUP, :] = jnp.zeros((GROUP, HEAD_DIM), f32)
        r.grad_value[0:GROUP, :] = jnp.zeros((GROUP, HEAD_DIM), f32)

        def window(rows, block):
            return rows[block * GROUP : (block + 2) * GROUP]

        def one(rows, block):
            return rows[block * GROUP : (block + 1) * GROUP]

        def fold(pieces):
            middle = [pieces[i][GROUP:] + pieces[i + 1][:GROUP] for i in range(3)]
            return pieces[0][:GROUP], jnp.concatenate(middle + [pieces[3][GROUP:]], 0)

        def group(index, carry):
            here = span(index, some)
            longer = pl.ds(pl.multiple_of(index * some, some), some + GROUP)
            before = pl.ds(pl.multiple_of(index * some, some), GROUP)
            after = pl.ds(pl.multiple_of(index * some + GROUP, GROUP), some)
            query, unit, value = r.sorted_query[here, :], r.unit[longer, :], r.key_value[longer, :]
            grad = r.round_rows[here, :HEAD_DIM]
            total = jnp.sum(r.round_rows[here, HEAD_DIM:].astype(f32), 1, keepdims=True)
            probs = r.probs[here, :]
            low = probs.astype(bf16)
            live = jnp.where(r.code[here, :].astype(f32) == 0.0, probs, 0.0)
            grad_probs = jnp.concatenate(
                [dot(one(grad, i), window(value, i), ((1,), (1,))) for i in range(4)], 0
            )
            inner = jnp.sum(live * grad_probs, 1, keepdims=True)
            scores = (live * (grad_probs - inner + total)).astype(bf16)
            r.probs[here, :] = (
                jnp.concatenate([dot(one(scores, i), window(unit, i)) for i in range(4)], 0) * scale
            )
            for target, left, right, factor in (
                (r.grad_unit, scores, query, scale),
                (r.grad_value, low, grad, 1.0),
            ):
                first, rest = fold(
                    [dot(one(left, i), one(right, i), ((0,), (0,))) * factor for i in range(4)]
                )
                target[before, :] += first
                target[after, :] = rest
            return carry

        lax.fori_loop(0, self.devices * self.rows // some, group, 0)
        last = pl.ds(self.devices * self.rows, GROUP)
        r.grad_unit[last, :] += r.grad_unit[0:GROUP, :]
        r.grad_value[last, :] += r.grad_value[0:GROUP, :]

        def whole(index, carry):
            here = span(index, some)
            after = pl.ds(pl.multiple_of(index * some + GROUP, GROUP), some)
            query = r.sorted_query[here, :].astype(f32)
            factor = lax.rsqrt(jnp.sum(query * query, 1, keepdims=True) + 1e-06)
            unit = query * factor
            grad = r.grad_unit[after, :]
            along = jnp.sum(unit * grad, 1, keepdims=True)
            grad = r.probs[here, :] + factor * (grad - unit * along)
            r.round_rows[here, :HEAD_DIM] = grad.astype(bf16)
            r.round_rows[here, HEAD_DIM:] = r.grad_value[after, :].astype(bf16)
            return carry

        lax.fori_loop(0, self.devices * self.rows // some, whole, 0)

    def return_grads(self):
        r, place, wires = self.r, self.place, self.wires
        bf16, f32 = jnp.bfloat16, jnp.float32

        def first(block, carry):
            self.unsort_block(r.round_rows, block)
            return carry

        lax.fori_loop(0, self.devices, first, 0)
        coming = []
        both = self.pair * self.rows
        for bits in (3, 1, 2, 0):
            turn = flipped(place.turn, bits)

            def second(half, carry, turn=turn, bits=bits):
                rows = self.unsorted_chunk(half * self.turns + turn).astype(bf16)
                if bits:
                    r.everyone[span((bits - 1) * self.pair + half, self.rows), :] = rows
                else:
                    r.grad_pairs[place.turn, span(half, self.rows), :] = rows
                return carry

            lax.fori_loop(0, self.pair, second, 0)
            if bits:
                source = r.everyone.at[pl.ds((bits - 1) * both, both)]
                coming.append(wires.push(source, r.grad_pairs.at[place.turn], place.peer(bits)))
        for copy in coming:
            copy.wait_recv()

        def add(piece, carry):
            here = span(piece, 128)
            total = r.grad_pairs[0, here, :].astype(f32)
            for turn in range(1, self.turns):
                total += r.grad_pairs[turn, here, :].astype(f32)
            r.grad_pair[here, :] = total.astype(bf16)
            return carry

        lax.fori_loop(0, both // 128, add, 0)
        mine = r.grad_heads_two.at[place.which]
        swap = wires.push(rows_at(r.grad_pair, 1 - place.which, self.rows), mine, place.peer(4))
        mine[...] = rows_at(r.grad_pair, place.which, self.rows)[...]
        swap.wait_recv()
        for which in range(self.pair):
            columns = slice(which * HEAD_DIM, (which + 1) * HEAD_DIM)
            r.grad_query[:, columns] = r.grad_heads_two[which, :, :HEAD_DIM]
            r.grad_key[:, columns] = r.grad_heads_two[which, :, HEAD_DIM:]

    def project_back(self):
        r, place, wires = self.r, self.place, self.wires
        bf16, f32 = jnp.bfloat16, jnp.float32
        copies = []
        tile_rows = self.rows // 2
        for tile in range(2):
            here = pl.ds(tile * tile_rows, tile_rows)
            part = dot(r.grad_query[here, :], r.query_full[...], ((1,), (1,)))
            part += dot(r.grad_key[here, :], r.value_full[...], ((1,), (1,)))
            normal = (r.two_full[here, :].astype(f32) - r.center_one[here, 0:1]) * r.factor_one[
                here, 0:1
            ]
            self.send_part(
                tile, part, normal, r.params_full[0:1, :], r.part_one, r.stat_one,
                r.parts_one, copies,
            )
        self.send_stats(r.stat_one, r.stats_one, copies)
        self.weights(r.rows_one, r.grad_query, r.grad_query_full)
        self.query_out = SeqScatter(
            wires, place, lambda seq: rows_at(r.grad_query_full, seq, r.query.shape[0]),
            r.query_pair, r.query_line,
        )
        self.query_out.start()
        self.weights(r.rows_one, r.grad_key, r.grad_value_full)
        self.value_out = SeqScatter(
            wires, place, lambda seq: rows_at(r.grad_value_full, seq, r.value.shape[0]),
            r.value_pair, r.value_line,
        )
        self.value_out.start()
        for copy in copies:
            copy.wait_recv()

        def normal_at(here):
            rows = columns_at(r.two_full.at[here], place.head, self.width)[...].astype(f32)
            return (rows - r.center_one[here, 0:1]) * r.factor_one[here, 0:1]

        def finish(here, change):
            total = r.grad_two[here, :].astype(f32) + change
            r.input_grad_two[here, :] = total.astype(bf16)

        gains, biases = self.norm_back(
            r.part_one, r.parts_one, r.stat_one, r.stats_one, normal_at, r.factor_one,
            self.my_params(0), finish,
        )
        r.norm_send[0:1, :], r.norm_send[1:2, :] = gains, biases
        norms = [
            wires.push(r.norm_send, r.norms.at[bits - 1], place.peer(bits)) for bits in range(1, 8)
        ]
        self.query_out.along()
        self.value_out.along()
        self.expand_out.finish(r.expand_part)
        self.shrink_out.finish(r.shrink_part)
        self.merge_out.finish(r.merge_part)
        self.finish_feed()
        total = r.norm_send[...]
        for bits, copy in enumerate(norms):
            copy.wait_recv()
            total += r.norms[bits]
        r.norm_grads[...] = total
        self.query_out.finish(r.query_part)
        self.value_out.finish(r.value_part)


def on_device(names, turns, *refs):
    r = SimpleNamespace(**dict(zip(names, refs)))
    r.feed, r.grad_expand, r.grad_shrink = r.one_full, r.expand_full, r.shrink_full
    r.grad_heads_two, r.part_one, r.grad_send = r.packed, r.part_two, r.out_send
    steps = Phases(r, turns)
    steps.place.greet()
    steps.project()
    steps.sort_tokens()
    steps.attend()
    steps.forward_bulk()
    steps.return_rows()
    steps.finish_bulk()
    steps.mix_rounds()
    steps.one.relay()
    steps.grads.relay()
    steps.heads.relay()
    steps.one.finish()
    steps.grads.finish()
    steps.heads.finish()
    steps.expand.finish()
    steps.shrink.finish()
    steps.feed_forward()
    steps.feed_back()
    steps.grad_rounds()
    steps.send_feed()
    steps.expand_out.along()
    steps.sort_grads()
    steps.shrink_out.along()
    steps.attend_back()
    steps.merge_out.along()
    steps.return_grads()
    steps.project_back()
    steps.wires.drain()


def whole(turns, arguments, tables):
    bf16, f32 = jnp.bfloat16, jnp.float32
    heads, devices = lax.axis_size("head"), lax.axis_size("seq")
    pair = devices // turns
    rows, width = arguments["two"].shape
    tokens, wide = devices * rows, heads * width
    hidden = arguments["expand"].shape[1]
    lines = rows // 128
    shape = {name: value.shape for name, value in arguments.items()}
    results = dict(
        result_one=((rows, width), bf16),
        result_two=((rows, width), bf16),
        input_grad_one=((rows, width), bf16),
        input_grad_two=((rows, width), bf16),
        query_part=(shape["query"], f32),
        value_part=(shape["value"], f32),
        merge_part=(shape["merge"], f32),
        expand_part=(shape["expand"], f32),
        shrink_part=(shape["shrink"], f32),
        norm_grads=((8, width), f32),
    )
    scratch = dict(
        sorted_query=((tokens, HEAD_DIM), bf16),
        unit=((tokens + GROUP, HEAD_DIM), bf16),
        key_value=((tokens + GROUP, HEAD_DIM), bf16),
        probs=((tokens, 2 * GROUP), f32),
        outs=((turns, pair, rows, HEAD_DIM), bf16),
        mix=((turns, pair, rows, HEAD_DIM), f32),
        rows_one=((rows, wide), bf16),
        center_one=((rows, 128), f32),
        factor_one=((rows, 128), f32),
        query_full=((wide, width), bf16),
        value_full=((wide, width), bf16),
        merge_full=((wide, wide), bf16),
        expand_full=((wide, hidden), bf16),
        shrink_full=((hidden, wide), bf16),
        one_full=((rows, wide), bf16),
        two_full=((rows, wide), bf16),
        grad_full=((rows, wide), bf16),
        attended_full=((rows, wide), bf16),
        everyone=((tokens, 2 * HEAD_DIM), bf16),
        mid=((devices * devices, rows // devices, 2 * HEAD_DIM), bf16),
        params_full=((8, wide), f32),
        packed=((pair, rows, 2 * HEAD_DIM), bf16),
        round_rows=((tokens, 2 * HEAD_DIM), bf16),
        out_send=((turns - 1, pair, rows, HEAD_DIM), bf16),
        total_send=((turns - 1, pair, lines, 128), f32),
        totals=((turns, pair, lines, 128), f32),
        mix_rows=((turns, pair, lines, 128), f32),
        attended=((pair, rows, HEAD_DIM), bf16),
        tall=((rows // 2, wide), f32),
        normal_two=((rows, width), f32),
        factor_two=((rows, 128), f32),
        rows_two=((rows, wide), bf16),
        active=((rows, hidden), bf16),
        grad_hidden=((rows, hidden), bf16),
        part_two=((rows, wide), bf16),
        stat_two=((2 * lines, 128), f32),
        parts_two=((heads - 1, rows, width), bf16),
        stats_two=((heads - 1, 2 * lines, 128), f32),
        stat_one=((2 * lines, 128), f32),
        parts_one=((heads - 1, rows, width), bf16),
        stats_one=((heads - 1, 2 * lines, 128), f32),
        feeds=((heads - 1, rows, width), bf16),
        grad_rows_one=((rows, wide), bf16),
        grad_heads=((pair, rows, HEAD_DIM), bf16),
        grad_attended=((pair, rows, HEAD_DIM), bf16),
        grad_total_send=((turns - 1, pair, lines, 128), f32),
        grad_outs=((turns, pair, rows, HEAD_DIM), bf16),
        grad_totals=((turns, pair, lines, 128), f32),
        grad_unit=((tokens + GROUP, HEAD_DIM), f32),
        grad_value=((tokens + GROUP, HEAD_DIM), f32),
        grad_pairs=((turns, pair * rows, 2 * HEAD_DIM), bf16),
        grad_pair=((pair * rows, 2 * HEAD_DIM), bf16),
        grad_query=((rows, width), bf16),
        grad_key=((rows, width), bf16),
        norm_send=((8, width), f32),
        norms=((devices - 1, 8, width), f32),
    )
    for name, full in (
        ("query", (wide, width)),
        ("value", (wide, width)),
        ("merge", (width, wide)),
        ("expand", (wide, hidden)),
        ("shrink", (hidden, wide)),
    ):
        own = "grad_" + name + ("_full" if name in ("query", "value") else "")
        if name not in ("expand", "shrink"):
            scratch[own] = (full, bf16)
        scratch[name + "_pair"] = ((devices // 2,) + shape[name], bf16)
        scratch[name + "_line"] = ((devices // 2 - 1,) + shape[name], bf16)
    wires = dict(send=160, receive=160)
    vmem = pl.BlockSpec(memory_space=pltpu.VMEM)
    smem = pl.BlockSpec(memory_space=pltpu.SMEM)
    names = [*arguments, *tables, *results, *scratch, *wires]
    out = pl.pallas_call(
        partial(on_device, names, turns),
        out_shape=[jax.ShapeDtypeStruct(*item) for item in results.values()],
        in_specs=[vmem] * len(arguments)
        + [smem if name.startswith("units") else vmem for name in tables],
        out_specs=[vmem] * len(results),
        scratch_shapes=[pltpu.VMEM(*item) for item in scratch.values()]
        + [pltpu.SemaphoreType.DMA((number,)) for number in wires.values()],
        compiler_params=pltpu.CompilerParams(
            collective_id=0, has_side_effects=True, vmem_limit_bytes=63 << 20
        ),
    )(*arguments.values(), *tables.values())
    return SimpleNamespace(**dict(zip(results, out)))


def round_tables(order, bucket, devices, rows):
    i32 = jnp.int32
    tokens = order.shape[0]
    unit = rows // devices
    blocks = tokens // GROUP
    place = jnp.arange(tokens, dtype=i32)
    chunk, local = order // rows, order % rows
    by_block = (chunk * rows + place % rows).reshape(devices, rows)
    slot = jnp.sum((by_block[:, None, :] < by_block[:, :, None]).astype(i32), -1)
    token = jnp.sort((chunk * tokens + place) * rows + local) % rows
    token = token.reshape(devices, rows)
    each = jnp.arange(devices, dtype=i32)
    share = jnp.sum((chunk.reshape(devices, rows)[:, None] == each[None, :, None]).astype(i32), -1)
    before = (each[:, None] < each[None, :]).astype(i32)
    in_block = share @ before
    in_chunk = before.T @ share
    start = each * unit

    def find(offset, share, other):
        ends = offset + share
        segment = jnp.sum((ends[:, None, :] <= start[None, :, None]).astype(i32), -1)
        chosen = (segment[:, :, None] == each).astype(i32)
        move = jnp.sum(chosen * (other - offset)[:, None, :], -1)
        return ((segment * rows + start[None] + move) // unit).reshape(-1)

    units = find(in_block, share, in_chunk)
    units_back = find(in_chunk.T, share.T, in_block.T)
    most = devices * (rows // GROUP + 1)
    values = jnp.arange(most + 1, dtype=i32)
    until = jnp.sum((bucket[None] <= values[:, None]).astype(i32), 1)
    sorted_bucket = jnp.sum((until[:, None] <= place[None]).astype(i32), 0)

    def keys(line):
        pieces = line.reshape(blocks, GROUP)
        return jnp.concatenate([jnp.roll(pieces, 1, 0), pieces], 1)[:, None, :]

    def queries(line):
        return line.reshape(blocks, GROUP, 1)

    allowed = (keys(order) <= queries(order)) & (keys(sorted_bucket) == queries(sorted_bucket))
    itself = keys(order) == queries(order)
    code = jnp.where(itself, 1.0, jnp.where(allowed, 0.0, 2.0)).astype(jnp.bfloat16)

    def in_columns(item):
        return jnp.broadcast_to(item.reshape(tokens, 1), (tokens, 128)).astype(jnp.int16)

    return dict(
        block_row=slot.reshape(devices, 1, rows),
        block_column=in_columns(slot),
        chunk_row=token.reshape(devices, 1, rows),
        chunk_column=in_columns(token),
        code=code.reshape(tokens, 2 * GROUP),
        units=units,
        units_back=units_back,
    )


def by_rounds(
    stream_one,
    stream_two,
    grad_one,
    grad_two,
    query_weight,
    value_weight,
    merge_weight,
    expand_weight,
    shrink_weight,
    first_gain,
    first_bias,
    second_gain,
    second_bias,
    bucket_ids,
    sort_order,
):
    devices, place = lax.axis_size("seq"), lax.axis_index("seq")
    rounds = sort_order.shape[0]
    turn = place % rounds
    order = lax.dynamic_slice_in_dim(sort_order, turn, 1, 0)[0]
    bucket = lax.dynamic_slice_in_dim(bucket_ids, turn, 1, 0)[0]
    params = jnp.stack([first_gain, first_bias, second_gain, second_bias])
    arguments = dict(
        one=stream_one,
        two=stream_two,
        grad_one=grad_one,
        grad_two=grad_two,
        query=query_weight,
        value=value_weight,
        merge=merge_weight,
        expand=expand_weight,
        shrink=shrink_weight,
        params=jnp.pad(params, ((0, 4), (0, 0))),
    )
    k = whole(rounds, arguments, round_tables(order, bucket, devices, stream_one.shape[0]))
    return (
        k.result_one,
        k.result_two,
        k.input_grad_one,
        k.input_grad_two,
        k.query_part,
        k.value_part,
        k.merge_part,
        k.expand_part,
        k.shrink_part,
        k.norm_grads[0],
        k.norm_grads[1],
        k.norm_grads[2],
        k.norm_grads[3],
    )


def solution(mesh):
    placed = (
        P("seq", "head"),
        P("seq", "head"),
        P("seq", "head"),
        P("seq", "head"),
        P("seq", "head"),
        P("seq", "head"),
        P("head", "seq"),
        P("seq", "head"),
        P("head", "seq"),
        P("head"),
        P("head"),
        P("head"),
        P("head"),
        P(),
        P(),
    )

    def local(*arguments):
        rounds = arguments[-1].shape[0]
        if mesh.shape["seq"] * mesh.shape["head"] == rounds * HEADS:
            return by_rounds(*arguments)
        return by_blocks(*arguments)

    return jax.shard_map(
        local,
        mesh=mesh,
        in_specs=placed,
        out_specs=(
            P("seq", "head"),
            P("seq", "head"),
            P("seq", "head"),
            P("seq", "head"),
            P("seq", "head"),
            P("seq", "head"),
            P("head", "seq"),
            P("seq", "head"),
            P("head", "seq"),
            P("head"),
            P("head"),
            P("head"),
            P("head"),
        ),
        check_vma=False,
    )
```

```python
from functools import partial
from types import SimpleNamespace

import jax
import jax.numpy as jnp
from jax import lax
from jax.experimental import pallas as pl
from jax.experimental.pallas import tpu as pltpu
from jax.sharding import PartitionSpec as P

HEADS = 8
HEAD_DIM = 128
GROUP = 64
MESH = pl.DeviceIdType.MESH


masked_score = -1000000000.0
own_score = -100000.0


def as_sent(shard):

    def short(part):
        return part.astype(jnp.bfloat16) if part.dtype == jnp.float32 else part

    return jax.tree.map(short, shard)


def from_behind(block, axis, distance):
    devices = range(lax.axis_size(axis))
    route = [(i - distance, i) for i in devices if i - distance in devices]
    return lax.ppermute(block, axis, route)


def row_sums(first, second):
    return lax.psum((first, second), "head")


def full_rows(part):
    return lax.all_gather(part, "head", axis=1, tiled=True)


def branch_sum(part):
    return lax.psum_scatter(part, "head", scatter_dimension=1, tiled=True)


def norm_forward(value, gain, shift):
    width = value.shape[1] * lax.axis_size("head")
    total, square = row_sums(
        jnp.sum(value, 1, keepdims=True), jnp.sum(value * value, 1, keepdims=True)
    )
    center = total / width
    spread = square / width - center * center
    factor = lax.rsqrt(spread + 1e-05)
    normal = (value - center) * factor
    return (normal, factor, normal * gain + shift)


def norm_backward(grad, normal, factor, gain):
    width = grad.shape[1] * lax.axis_size("head")
    scaled = grad * gain
    first, second = row_sums(
        jnp.sum(scaled, 1, keepdims=True), jnp.sum(scaled * normal, 1, keepdims=True)
    )
    result = factor * (scaled - first / width - normal * (second / width))
    return (result, jnp.sum(grad * normal, 0), jnp.sum(grad, 0))


def regroup_rows(buffer):
    turns = []
    for turn in range(buffer.shape[1]):
        turns.append(
            lax.all_to_all(buffer[:, turn], "seq", split_axis=0, concat_axis=0, tiled=True)
        )
    result = jnp.stack(turns, 1)
    return result


def regroup_totals(buffer):
    moved = lax.all_to_all(
        buffer.reshape(buffer.shape[0], -1, buffer.shape[3]),
        "seq",
        split_axis=0,
        concat_axis=0,
        tiled=True,
    )
    return moved.reshape(buffer.shape)


def regroup_pair(first, second):
    firsts = []
    seconds = []
    for turn in range(first.shape[1]):
        moved_first, moved_second = (
            lax.all_to_all(as_sent(first[:, turn]), "seq", split_axis=0, concat_axis=0, tiled=True),
            lax.all_to_all(
                as_sent(second[:, turn]), "seq", split_axis=0, concat_axis=0, tiled=True
            ),
        )
        firsts.append(moved_first)
        seconds.append(moved_second)
    result = (jnp.stack(firsts, 1), jnp.stack(seconds, 1))
    return result


def by_blocks(
    stream_one,
    stream_two,
    grad_one,
    grad_two,
    query_weight,
    value_weight,
    merge_weight,
    expand_weight,
    shrink_weight,
    first_gain,
    first_bias,
    second_gain,
    second_bias,
    bucket_ids,
    sort_order,
):
    devices = lax.axis_size("seq")
    place = lax.axis_index("seq")
    rows = stream_one.shape[0]
    rounds = sort_order.shape[0]
    capacity = 2 * rows // devices
    blocks = rows // GROUP
    heads_here = HEADS // lax.axis_size("head")
    local_width = heads_here * HEAD_DIM
    scale = HEAD_DIM ** (-0.5)
    round_index = jnp.arange(rounds, dtype=jnp.int32)[:, None]
    counter = jnp.arange(rows, dtype=jnp.int32)

    def invert(line):
        return jnp.zeros_like(line).at[line].set(jnp.arange(line.shape[0], dtype=jnp.int32))

    inverse = jax.vmap(invert)(sort_order)
    my_sorted = lax.dynamic_slice_in_dim(inverse, place * rows, rows, 1)
    send_block = my_sorted // rows
    same_block = send_block[:, :, None] == send_block[:, None, :]
    send_slot = jnp.sum(
        (same_block & (my_sorted[:, None, :] < my_sorted[:, :, None])).astype(jnp.int32), -1
    )
    block_tokens = lax.dynamic_slice_in_dim(sort_order, place * rows, rows, 1)
    source_block = block_tokens // rows
    earlier = counter[None, :] < counter[:, None]
    recv_slot = jnp.sum(
        ((source_block[:, :, None] == source_block[:, None, :]) & earlier[None]).astype(jnp.int32),
        -1,
    )
    query_bucket = jnp.take_along_axis(bucket_ids, block_tokens, 1)
    prior_start = (place - 1) % devices * rows + rows - GROUP
    prior_tokens = lax.dynamic_slice_in_dim(sort_order, prior_start, GROUP, 1)
    prior_bucket = jnp.take_along_axis(bucket_ids, prior_tokens, 1)

    def with_prior(own, prior):
        pieces = own.reshape((rounds, blocks, GROUP) + own.shape[2:])
        before = jnp.concatenate([prior[:, None], pieces[:, :-1]], 1)
        return jnp.concatenate([pieces, before], 2)

    query_place = block_tokens.reshape(rounds, blocks, GROUP)
    key_place = with_prior(block_tokens, prior_tokens)
    key_bucket = with_prior(query_bucket, prior_bucket)
    allowed = (key_place[:, :, None, :] <= query_place[:, :, :, None]) & (
        key_bucket[:, :, None, :] == query_bucket.reshape(rounds, blocks, GROUP)[:, :, :, None]
    )
    itself = key_place[:, :, None, :] == query_place[:, :, :, None]
    live = allowed & jnp.logical_not(itself)

    def fill(values, block, slot):
        empty = jnp.zeros((devices, rounds, capacity, values.shape[-1]), values.dtype)
        return empty.at[block, round_index, slot].set(values)

    normal_one, factor_one, normed_one = norm_forward(
        stream_two.astype(jnp.float32), first_gain, first_bias
    )
    rows_one = full_rows(normed_one.astype(jnp.bfloat16))
    query_full, value_full, merge_full = (
        lax.all_gather(query_weight, "seq", axis=0, tiled=True),
        lax.all_gather(value_weight, "seq", axis=0, tiled=True),
        lax.all_gather(merge_weight, "seq", axis=1, tiled=True),
    )
    queries = jnp.dot(rows_one, query_full, preferred_element_type=jnp.float32).astype(jnp.bfloat16)
    values = jnp.dot(rows_one, value_full, preferred_element_type=jnp.float32).astype(jnp.bfloat16)
    packed = jnp.concatenate([queries, values], 1)
    outgoing = fill(jnp.broadcast_to(packed[None], (rounds,) + packed.shape), send_block, send_slot)
    incoming = regroup_rows(outgoing)
    sorted_rows = incoming[source_block, round_index, recv_slot]
    sorted_query = sorted_rows[:, :, :local_width].reshape(rounds, rows, heads_here, HEAD_DIM)
    sorted_value = sorted_rows[:, :, local_width:].reshape(rounds, rows, heads_here, HEAD_DIM)
    query_float = sorted_query.astype(jnp.float32)
    inverse_norm = lax.rsqrt(jnp.sum(query_float * query_float, -1, keepdims=True) + 1e-06)
    unit_float = query_float * inverse_norm
    unit_low = unit_float.astype(jnp.bfloat16)
    edge = from_behind(
        jnp.concatenate([unit_low[:, -GROUP:], sorted_value[:, -GROUP:]], -1), "seq", 1
    )
    key_unit = with_prior(unit_low, edge[..., :HEAD_DIM])
    key_value = with_prior(sorted_value, edge[..., HEAD_DIM:])
    query_groups = sorted_query.reshape(rounds, blocks, GROUP, heads_here, HEAD_DIM)

    def masked_scores():
        raw = (
            jnp.einsum(
                "rncha,rnkha->rnhck", query_groups, key_unit, preferred_element_type=jnp.float32
            )
            * scale
        )
        return jnp.where(
            itself[:, :, None], own_score, jnp.where(allowed[:, :, None], raw, masked_score)
        )

    scores = masked_scores()
    peak = jnp.max(scores, -1, keepdims=True)
    totals = peak + jnp.log(jnp.sum(jnp.exp(scores - peak), -1, keepdims=True))
    probs_low = jnp.exp(scores - totals).astype(jnp.bfloat16)
    round_out = jnp.einsum(
        "rnhck,rnkha->rncha", probs_low, key_value, preferred_element_type=jnp.float32
    ).astype(jnp.bfloat16)
    out_flat = round_out.reshape(rounds, rows, local_width)
    total_flat = jnp.transpose(totals[..., 0], (0, 1, 3, 2)).reshape(rounds, rows, heads_here)
    token_out = regroup_rows(fill(out_flat, source_block, recv_slot))[
        send_block, round_index, send_slot
    ].astype(jnp.float32)
    token_total = regroup_totals(fill(total_flat, source_block, recv_slot))[
        send_block, round_index, send_slot
    ]
    mix = jax.nn.softmax(token_total, axis=0)
    token_out4 = token_out.reshape(rounds, rows, heads_here, HEAD_DIM)
    attended_low = (
        jnp.sum(mix[..., None] * token_out4, 0).reshape(rows, local_width).astype(jnp.bfloat16)
    )
    sum_one = stream_one.astype(jnp.float32) + branch_sum(
        jnp.dot(attended_low, merge_full, preferred_element_type=jnp.float32)
    )
    normal_two, factor_two, normed_two = norm_forward(sum_one, second_gain, second_bias)
    rows_two = full_rows(normed_two.astype(jnp.bfloat16))
    expand_full, shrink_full = (
        lax.all_gather(expand_weight, "seq", axis=0, tiled=True),
        lax.all_gather(shrink_weight, "seq", axis=1, tiled=True),
    )
    hidden = jnp.dot(rows_two, expand_full, preferred_element_type=jnp.float32)
    active, gelu_pull = jax.vjp(partial(jax.nn.gelu, approximate=False), hidden)
    active_low = active.astype(jnp.bfloat16)
    sum_two = stream_two.astype(jnp.float32) + branch_sum(
        jnp.dot(active_low, shrink_full, preferred_element_type=jnp.float32)
    )
    grad_rows_two = full_rows(grad_two)
    grad_active = jnp.dot(grad_rows_two, shrink_full.T, preferred_element_type=jnp.float32)
    grad_hidden = gelu_pull(grad_active)[0].astype(jnp.bfloat16)
    grad_shrink = jnp.dot(active_low.T, grad_rows_two, preferred_element_type=jnp.float32)
    grad_expand = jnp.dot(rows_two.T, grad_hidden, preferred_element_type=jnp.float32)
    grad_normed_two = branch_sum(
        jnp.dot(grad_hidden, expand_full.T, preferred_element_type=jnp.float32)
    )
    extra_one, grad_second_gain, grad_second_bias = norm_backward(
        grad_normed_two, normal_two, factor_two, second_gain
    )
    total_one = grad_one.astype(jnp.float32) + extra_one
    total_low = total_one.astype(jnp.bfloat16)
    grad_rows_one = full_rows(total_low)
    grad_attended = jnp.dot(grad_rows_one, merge_full.T, preferred_element_type=jnp.float32).astype(
        jnp.bfloat16
    )
    grad_merge = jnp.dot(attended_low.T, grad_rows_one, preferred_element_type=jnp.float32)
    grad_float = grad_attended.astype(jnp.float32).reshape(rows, heads_here, HEAD_DIM)
    dots = jnp.sum(token_out4 * grad_float[None], -1)
    grad_total = mix * (dots - jnp.sum(mix * dots, 0, keepdims=True))
    grad_out_low = (
        (mix[..., None] * grad_float[None]).astype(jnp.bfloat16).reshape(rounds, rows, local_width)
    )
    sorted_grad_out = regroup_rows(fill(grad_out_low, send_block, send_slot))[
        source_block, round_index, recv_slot
    ]
    sorted_grad_total = regroup_totals(fill(grad_total, send_block, send_slot))[
        source_block, round_index, recv_slot
    ]
    grad_groups = sorted_grad_out.reshape(rounds, blocks, GROUP, heads_here, HEAD_DIM)
    total_grad_groups = jnp.transpose(
        sorted_grad_total.reshape(rounds, blocks, GROUP, heads_here), (0, 1, 3, 2)
    )[..., None]
    probs = jnp.exp(masked_scores() - totals)
    probs_again = probs.astype(jnp.bfloat16)
    grad_probs = jnp.einsum(
        "rncha,rnkha->rnhck", grad_groups, key_value, preferred_element_type=jnp.float32
    )
    grad_key_value = jnp.einsum(
        "rnhck,rncha->rnkha", probs_again, grad_groups, preferred_element_type=jnp.float32
    )
    inner = jnp.sum(probs * grad_probs, -1, keepdims=True)
    grad_scores = jnp.where(
        live[:, :, None], probs * (grad_probs - inner + total_grad_groups), 0.0
    ).astype(jnp.bfloat16)
    grad_query_groups = (
        jnp.einsum("rnhck,rnkha->rncha", grad_scores, key_unit, preferred_element_type=jnp.float32)
        * scale
    )
    grad_key_unit = (
        jnp.einsum(
            "rnhck,rncha->rnkha", grad_scores, query_groups, preferred_element_type=jnp.float32
        )
        * scale
    )
    edge_grad = from_behind(
        jnp.concatenate([grad_key_unit[:, 0, GROUP:], grad_key_value[:, 0, GROUP:]], -1).astype(
            jnp.bfloat16
        ),
        "seq",
        -1,
    ).astype(jnp.float32)

    def fold_keys(grad_keys, arriving):
        own = grad_keys[:, :, :GROUP]
        later = jnp.concatenate([grad_keys[:, 1:, GROUP:], arriving[:, None]], 1)
        return (own + later).reshape(rounds, rows, heads_here, HEAD_DIM)

    grad_unit = fold_keys(grad_key_unit, edge_grad[..., :HEAD_DIM])
    grad_sorted_value = fold_keys(grad_key_value, edge_grad[..., HEAD_DIM:])
    grad_sorted_query = grad_query_groups.reshape(
        rounds, rows, heads_here, HEAD_DIM
    ) + inverse_norm * (grad_unit - unit_float * jnp.sum(unit_float * grad_unit, -1, keepdims=True))
    moved_first, moved_second = regroup_pair(
        fill(grad_sorted_query.reshape(rounds, rows, local_width), source_block, recv_slot),
        fill(grad_sorted_value.reshape(rounds, rows, local_width), source_block, recv_slot),
    )
    token_grad_query = moved_first[send_block, round_index, send_slot]
    token_grad_value = moved_second[send_block, round_index, send_slot]
    grad_query_low = jnp.sum(token_grad_query, 0).astype(jnp.bfloat16)
    grad_value_low = jnp.sum(token_grad_value, 0).astype(jnp.bfloat16)
    grad_query_full = jnp.dot(rows_one.T, grad_query_low, preferred_element_type=jnp.float32)
    grad_value_full = jnp.dot(rows_one.T, grad_value_low, preferred_element_type=jnp.float32)
    grad_normed_one = branch_sum(
        jnp.dot(grad_query_low, query_full.T, preferred_element_type=jnp.float32)
        + jnp.dot(grad_value_low, value_full.T, preferred_element_type=jnp.float32)
    )
    extra_two, grad_first_gain, grad_first_bias = norm_backward(
        grad_normed_one, normal_one, factor_one, first_gain
    )
    input_grad_two = (grad_two.astype(jnp.float32) + extra_two).astype(jnp.bfloat16)
    query_part, value_part, merge_part, expand_part, shrink_part = (
        lax.psum_scatter(grad_query_full, "seq", scatter_dimension=0, tiled=True),
        lax.psum_scatter(grad_value_full, "seq", scatter_dimension=0, tiled=True),
        lax.psum_scatter(grad_merge, "seq", scatter_dimension=1, tiled=True),
        lax.psum_scatter(grad_expand, "seq", scatter_dimension=0, tiled=True),
        lax.psum_scatter(grad_shrink, "seq", scatter_dimension=1, tiled=True),
    )
    first_gain_sum, first_bias_sum, second_gain_sum, second_bias_sum = lax.psum(
        (grad_first_gain, grad_first_bias, grad_second_gain, grad_second_bias), "seq"
    )
    return (
        sum_one.astype(jnp.bfloat16),
        sum_two.astype(jnp.bfloat16),
        total_low,
        input_grad_two,
        query_part,
        value_part,
        merge_part,
        expand_part,
        shrink_part,
        first_gain_sum,
        first_bias_sum,
        second_gain_sum,
        second_bias_sum,
    )


def flip(index, bit):
    return index + bit - 2 * bit * ((index // bit) % 2)


def flipped(index, bits):
    for bit in (1, 2, 4):
        if bits & bit:
            index = flip(index, bit)
    return index


class Place:
    def __init__(self, turns):
        self.turns = turns
        self.seq, self.head = lax.axis_index("seq"), lax.axis_index("head")
        self.which, self.turn = self.seq // turns, self.seq % turns

    def peer(self, seq_bits, head_bits=0):
        return (flipped(self.seq, seq_bits), flipped(self.head, head_bits))

    def greet(self):
        peers = [self.peer(bits) for bits in range(1, 8)]
        peers += [self.peer(0, bits) for bits in range(1, 4)]
        barrier = pltpu.get_barrier_semaphore()
        for peer in peers:
            pl.semaphore_signal(barrier, inc=1, device_id=peer, device_id_type=MESH)
        pl.semaphore_wait(barrier, len(peers))


class Wires:
    def __init__(self, send, receive):
        self.send, self.receive, self.copies = send, receive, []

    def push(self, source, target, device):
        index = len(self.copies)
        copy = pltpu.make_async_remote_copy(
            src_ref=source,
            dst_ref=target,
            send_sem=self.send.at[index],
            recv_sem=self.receive.at[index],
            device_id=device,
            device_id_type=MESH,
        )
        copy.start()
        self.copies.append(copy)
        return copy

    def settle(self, copies):
        for copy in copies:
            copy.wait_send()
        done = [id(copy) for copy in copies]
        self.copies = [None if id(copy) in done else copy for copy in self.copies]

    def drain(self):
        self.settle([copy for copy in self.copies if copy is not None])


class SeqGather:
    lines = (6, 4, 2)

    def __init__(self, wires, place, slot):
        self.wires, self.place, self.slot = wires, place, slot

    def start(self, source, source_for=None):
        p, mine = self.place, self.slot(self.place.seq)
        self.arriving = {}
        for bits in self.lines:
            block = source if source_for is None else source_for(bits)
            self.arriving[bits] = self.wires.push(block, mine, p.peer(bits))
        self.beside = {0: self.wires.push(source, mine, p.peer(1))}

    def forward(self, bits):
        p = self.place
        self.arriving[bits].wait_recv()
        block = self.slot(flipped(p.seq, bits))
        self.beside[bits] = self.wires.push(block, block, p.peer(1))

    def land(self, bits):
        self.beside[bits].wait_recv()

    def settle(self):
        self.wires.settle([*self.arriving.values(), *self.beside.values()])

    def finish(self):
        for bits in self.beside:
            self.land(bits)
        self.settle()


class HeadGather:
    def __init__(self, wires, place, slot):
        self.wires, self.place, self.slot = wires, place, slot

    def start(self, source):
        p = self.place
        mine = self.slot(p.head)
        self.long = self.wires.push(source, mine, p.peer(0, 2))
        self.short = self.wires.push(source, mine, p.peer(0, 1))

    def relay(self):
        p = self.place
        self.long.wait_recv()
        moved = self.slot(flip(p.head, 2))
        self.last = self.wires.push(moved, moved, p.peer(0, 1))

    def finish(self):
        self.short.wait_recv()
        self.last.wait_recv()
        self.wires.settle([self.long, self.short, self.last])


def columns_at(ref, index, width):
    return ref.at[:, pl.ds(pl.multiple_of(index * width, width), width)]


def rows_at(ref, index, width):
    return ref.at[pl.ds(pl.multiple_of(index * width, width), width)]


def span(index, width):
    return pl.ds(pl.multiple_of(index * width, width), width)


def dot(left, right, contract=((1,), (0,))):
    return lax.dot_general(
        left, right, (contract, ((), ())), preferred_element_type=jnp.float32
    )


def diagonal(size):
    return lax.broadcasted_iota(jnp.int32, (size, size), 0) == lax.broadcasted_iota(
        jnp.int32, (size, size), 1
    )


def to_row(column):
    return jnp.sum(jnp.where(diagonal(column.shape[0]), column, 0.0), 0, keepdims=True)


def to_column(row):
    return jnp.sum(jnp.where(diagonal(row.shape[1]), row, 0.0), 1, keepdims=True)


def in_lanes(total):
    bf16, f32 = jnp.bfloat16, jnp.float32
    high = total.astype(bf16).astype(f32)
    middle = (total - high).astype(bf16).astype(f32)
    low = total - high - middle
    lane = lax.broadcasted_iota(jnp.int32, (total.shape[0], 128), 1)
    parts = jnp.where(lane == 0, high, jnp.where(lane == 1, middle, low))
    return jnp.where(lane < 3, parts, 0.0).astype(bf16)


class SeqScatter:
    def __init__(self, wires, place, piece, pair, line):
        self.wires, self.place, self.piece = wires, place, piece
        self.pair, self.line = pair, line

    def start(self):
        p = self.place
        self.beside = {}
        for bits in (6, 4, 2, 0):
            source = self.piece(flipped(p.seq, bits + 1))
            self.beside[bits] = self.wires.push(source, self.pair.at[bits // 2], p.peer(1))

    def along(self):
        p, f32 = self.place, jnp.float32
        self.coming = []
        for bits in (6, 4, 2):
            self.beside[bits].wait_recv()
            at = self.pair.at[bits // 2]
            mine = self.piece(flipped(p.seq, bits))[...]
            at[...] = (at[...].astype(f32) + mine.astype(f32)).astype(jnp.bfloat16)
            self.coming.append(self.wires.push(at, self.line.at[bits // 2 - 1], p.peer(bits)))

    def finish(self, target):
        p, f32 = self.place, jnp.float32
        self.beside[0].wait_recv()
        total = self.piece(p.seq)[...].astype(f32) + self.pair[0].astype(f32)
        for copy in self.coming:
            copy.wait_recv()
        for other in range(3):
            total += self.line[other].astype(f32)
        target[...] = total


class Phases:
    def __init__(self, r, turns):
        self.r, self.turns = r, turns
        self.place = Place(turns)
        self.wires = Wires(r.send, r.receive)
        self.rows, self.width = r.two.shape
        self.wide = r.rows_one.shape[1]
        self.count = self.wide // self.width
        self.devices = r.everyone.shape[0] // self.rows
        self.pair = self.devices // turns
        self.units = self.devices


    def spread_columns(self, ref, index):
        column = ref[span(index, self.rows), :].astype(jnp.int32)
        lane = lax.broadcasted_iota(jnp.int32, column.shape, 1)
        parts = [
            jnp.where(column == lane + 128 * i, 1.0, 0.0).astype(jnp.bfloat16)
            for i in range(self.rows // 128)
        ]
        return jnp.concatenate(parts, 1)

    def spread_rows(self, ref, index):
        row = ref[index]
        place = lax.broadcasted_iota(jnp.int32, (self.rows, self.rows), 0)
        return jnp.where(row == place, 1.0, 0.0).astype(jnp.bfloat16)

    def from_units(self, ref, table, index):
        first = index * self.units
        return jnp.concatenate([ref[table[first + unit]] for unit in range(self.units)], 0)

    def to_units(self, index, rows):
        first, step = index * self.units, self.rows // self.units
        for unit in range(self.units):
            self.r.mid[first + unit] = rows[unit * step : (unit + 1) * step].astype(jnp.bfloat16)

    def sort_chunk(self, source, index):
        r = self.r
        here = span(index, self.rows)
        self.to_units(index, dot(self.spread_columns(r.chunk_column, index), source[here, :]))

    def sorted_block(self, index):
        r = self.r
        return dot(
            self.spread_columns(r.block_column, index), self.from_units(r.mid, r.units, index)
        )

    def unsort_block(self, source, index):
        r = self.r
        here = span(index, self.rows)
        self.to_units(index, dot(self.spread_rows(r.block_row, index), source[here, :]))

    def unsorted_chunk(self, index):
        r = self.r
        return dot(
            self.spread_rows(r.chunk_row, index), self.from_units(r.mid, r.units_back, index)
        )

    def tables(self):
        r = self.r
        bf16, f32, i32 = jnp.bfloat16, jnp.float32, jnp.int32
        rows, lines = self.rows, self.rows // 128
        tokens = rows * self.devices
        most = -(-(self.devices * (rows // GROUP + 1) + 1) // 128) * 128

        def column_of(row):
            pieces = [to_column(row[:, i * 128 : (i + 1) * 128]) for i in range(lines)]
            return jnp.concatenate(pieces, 0)

        def row_of(column):
            pieces = [to_row(column[i * 128 : (i + 1) * 128]) for i in range(lines)]
            return jnp.concatenate(pieces, 1)

        def wide(column):
            return jnp.broadcast_to(column, (rows, 128)).astype(i32).astype(jnp.int16)

        value = lax.broadcasted_iota(i32, (most, rows), 0)

        def count(block, until):
            return until + jnp.sum(
                jnp.where(r.bucket[block] <= value, 1.0, 0.0), 1, keepdims=True
            )

        until = lax.fori_loop(0, self.devices, count, jnp.zeros((most, 1), f32)).astype(i32)

        def first(block, carry):
            order = r.order[block]
            lane = lax.broadcasted_iota(i32, (1, rows), 1)
            bucket = jnp.sum(
                jnp.where(until <= lane + block * rows, 1.0, 0.0), 0, keepdims=True
            )
            key = bucket * tokens + order.astype(f32)
            for i in range(lines):
                r.keys[block * lines + i] = key[:, i * 128 : (i + 1) * 128]
            chunk = order // rows
            place = (chunk * rows + lane).astype(f32)
            slot = jnp.sum(jnp.where(place < column_of(place), 1.0, 0.0), 1, keepdims=True)
            r.block_column[span(block, rows), :] = wide(slot)
            r.block_row[block] = row_of(slot).astype(i32)
            local = column_of((order - chunk * rows).astype(f32))
            high = jnp.floor(local * 0.0625)
            at = lax.broadcasted_iota(i32, (rows, 2 * HEAD_DIM), 1)
            parts = jnp.where(at == 0, high, jnp.where(at == 1, local - 16.0 * high, 0.0))
            r.round_rows[span(block, rows), :] = parts.astype(bf16)
            self.unsort_block(r.round_rows, block)
            return carry

        lax.fori_loop(0, self.devices, first, 0)

        def second(chunk, carry):
            parts = self.from_units(r.mid, r.units_back, chunk)[:, 0:128].astype(f32)
            token = 16.0 * parts[:, 0:1] + parts[:, 1:2]
            r.chunk_column[span(chunk, rows), :] = wide(token)
            r.chunk_row[chunk] = row_of(token).astype(i32)
            return carry

        lax.fori_loop(0, self.devices, second, 0)

    def codes(self, index):
        r = self.r
        tokens = self.rows * self.devices
        groups = tokens // 128
        low = lax.broadcasted_iota(jnp.int32, (1, 128), 1) < GROUP
        result = []
        for i in range(2):
            here = 2 * index + i
            keys, before = r.keys[here], r.keys[(here + groups - 1) % groups]
            query = to_column(keys)
            least = jnp.floor(query * (1.0 / tokens)) * tokens
            for half, window in enumerate((jnp.where(low, keys, before), keys)):
                at = slice(half * GROUP, (half + 1) * GROUP)
                allowed = (window <= query[at]) & (window >= least[at])
                result.append(
                    jnp.where(window == query[at], 1.0, jnp.where(allowed, 0.0, 2.0))
                )
        return jnp.concatenate(result, 0)

    def window(self, rows, block):
        before = rows[block * GROUP : (block + 1) * GROUP]
        own = rows[(block + 1) * GROUP : (block + 2) * GROUP]
        return jnp.concatenate([own, before] if block % 2 == 0 else [before, own], 0)

    def over_rows(self, ref):
        step = ref.shape[0] // self.devices
        return SeqGather(self.wires, self.place, lambda seq: rows_at(ref, seq, step))

    def over_columns(self, ref):
        step = ref.shape[1] // self.devices
        return SeqGather(self.wires, self.place, lambda seq: columns_at(ref, seq, step))

    def start_seq(self, gather, source):
        gather.start(source)
        gather.slot(self.place.seq)[...] = source[...]

    def start_head(self, gather, source):
        gather.start(source)
        gather.slot(self.place.head)[...] = source[...]

    def over_head(self, ref):
        return HeadGather(self.wires, self.place, lambda head: columns_at(ref, head, self.width))

    def project(self):
        r, place, wires = self.r, self.place, self.wires
        bf16, f32 = jnp.bfloat16, jnp.float32
        stream = self.over_head(r.two_full)
        small = self.over_head(r.params_full)
        self.start_head(stream, r.two)
        for row, item in enumerate((r.gain_one, r.bias_one, r.gain_two, r.bias_two)):
            r.params[row : row + 1, :] = item[...]
        r.params[4:8, :] = jnp.zeros((4, self.width), f32)
        self.start_head(small, r.params)
        query, value = self.over_rows(r.query_full), self.over_rows(r.value_full)
        self.start_seq(query, r.query)
        self.tables()
        for bits in SeqGather.lines:
            query.forward(bits)
        self.start_seq(value, r.value)
        small.relay()
        stream.relay()
        self.bulk()
        small.finish()
        stream.finish()

        def normalise(tile, carry):
            here = span(tile, 128)
            rows = r.two_full[here, :].astype(f32)
            center = jnp.mean(rows, 1, keepdims=True)
            offset = rows - center
            factor = lax.rsqrt(jnp.mean(offset * offset, 1, keepdims=True) + 1e-05)
            r.center_one[here, :] = jnp.broadcast_to(center, (128, 128))
            r.factor_one[here, :] = jnp.broadcast_to(factor, (128, 128))
            r.rows_one[here, :] = (
                offset * factor * r.params_full[0:1, :] + r.params_full[1:2, :]
            ).astype(bf16)
            return carry

        lax.fori_loop(0, self.rows // 128, normalise, 0)
        for bits in SeqGather.lines:
            value.forward(bits)
        self.tokens = [
            self.project_one(query, r.query_full, 0),
            self.project_one(value, r.value_full, 1),
        ]
        self.begin(self.merge)
        self.begin(self.expand[0])

    def project_one(self, weight, full, part):
        r, place = self.r, self.place
        weight.finish()

        def multiply(tile, carry):
            here = span(tile, 256)
            result = dot(r.rows_one[here, :], full[...]).astype(jnp.bfloat16)
            for which in range(self.pair):
                r.packed[which, part, here, :] = result[
                    :, which * HEAD_DIM : (which + 1) * HEAD_DIM
                ]
            return carry

        lax.fori_loop(0, self.rows // 256, multiply, 0)
        columns = pl.ds(part * HEAD_DIM, HEAD_DIM)
        tokens = SeqGather(
            self.wires,
            place,
            lambda seq: rows_at(r.everyone, seq, self.rows).at[:, columns],
        )
        mine = r.packed.at[place.which, part]
        tokens.start(
            mine, lambda bits: mine if bits < self.turns else r.packed.at[1 - place.which, part]
        )
        tokens.slot(place.seq)[...] = mine[...]
        return tokens

    def bulk(self):
        r, place = self.r, self.place
        my_rows = rows_at(r.merge_full, place.head, r.merge.shape[0])
        self.merge = SeqGather(
            self.wires, place, lambda seq: columns_at(my_rows, seq, r.merge.shape[1])
        )
        self.merge.source = r.merge
        self.expand, self.shrink = [], []
        for part in range(2):
            step, columns = r.expand.shape[0], r.expand.shape[1] // 2
            cut = pl.ds(part * columns, columns)
            gather = SeqGather(
                self.wires,
                place,
                lambda seq, cut=cut: rows_at(r.expand_full, seq, step).at[:, cut],
            )
            gather.source = r.expand.at[:, cut]
            self.expand.append(gather)
            rows, width = r.shrink.shape[0] // 2, r.shrink.shape[1]
            down = pl.ds(part * rows, rows)
            gather = SeqGather(
                self.wires,
                place,
                lambda seq, down=down: columns_at(r.shrink_full.at[down], seq, width),
            )
            gather.source = r.shrink.at[down]
            self.shrink.append(gather)
        self.one, self.grads = self.over_head(r.one_full), self.over_head(r.grad_full)

    def begin(self, gather):
        self.start_seq(gather, gather.source)

    def go_on(self, gather):
        for bits in (2, 6, 4):
            gather.forward(bits)

    def begin_streams(self):
        self.start_head(self.one, self.r.one)
        self.start_head(self.grads, self.r.grad_two)

    def begin_merge_rows(self):
        r, place = self.r, self.place
        self.merge.finish()
        self.heads = HeadGather(
            self.wires, place, lambda head: rows_at(r.merge_full, head, r.merge.shape[0])
        )
        self.heads.start(self.heads.slot(place.head))

    def sort_tokens(self):
        r, place = self.r, self.place
        bf16, f32 = jnp.bfloat16, jnp.float32
        self.sort_chunk(r.everyone, place.seq)
        for tokens in self.tokens:
            for bits in (2, 6, 4):
                tokens.forward(bits)
        self.begin(self.expand[1])
        self.begin_streams()
        self.go_on(self.merge)
        self.go_on(self.expand[0])
        for bits in (2, 6, 4):
            self.sort_chunk(r.everyone, flipped(place.seq, bits))
        for bits in (0, 2, 6, 4):
            for tokens in self.tokens:
                tokens.land(bits)
            self.sort_chunk(r.everyone, flipped(place.seq, bits + 1))
        for tokens in self.tokens:
            tokens.settle()

        def second(block, carry):
            rows = self.sorted_block(block)
            here = span(block, self.rows)
            later = pl.ds(pl.multiple_of(block * self.rows + GROUP, GROUP), self.rows)
            query = rows[:, :HEAD_DIM]
            r.sorted_query[here, :] = query.astype(bf16)
            factor = lax.rsqrt(jnp.sum(query * query, 1, keepdims=True) + 1e-06)
            r.unit[later, :] = (query * factor).astype(bf16)
            r.key_value[later, :] = rows[:, HEAD_DIM:].astype(bf16)
            return carry

        lax.fori_loop(0, self.devices, second, 0)
        last = pl.ds(self.devices * self.rows, GROUP)
        r.unit[0:GROUP, :] = r.unit[last, :]
        r.key_value[0:GROUP, :] = r.key_value[last, :]

    def attend(self):
        r = self.r
        bf16, f32 = jnp.bfloat16, jnp.float32
        scale = HEAD_DIM ** (-0.5)
        some = 4 * GROUP

        def group(index, carry):
            here = span(index, some)
            longer = pl.ds(pl.multiple_of(index * some, some), some + GROUP)
            query, unit, value = r.sorted_query[here, :], r.unit[longer, :], r.key_value[longer, :]
            raw = [
                dot(query[i * GROUP : (i + 1) * GROUP], self.window(unit, i), ((1,), (1,)))
                for i in range(4)
            ]
            code = self.codes(index)
            scores = jnp.where(
                code == 0.0,
                jnp.concatenate(raw, 0) * scale,
                jnp.where(code == 1.0, own_score, masked_score),
            )
            peak = jnp.max(scores, 1, keepdims=True)
            power = jnp.exp(scores - peak)
            total = jnp.sum(power, 1, keepdims=True)
            probs = power * (1.0 / total)
            r.probs[here, :] = probs
            probs = probs.astype(bf16)
            result = [
                dot(probs[i * GROUP : (i + 1) * GROUP], self.window(value, i)) for i in range(4)
            ]
            r.round_rows[here, :HEAD_DIM] = jnp.concatenate(result, 0).astype(bf16)
            r.round_rows[here, HEAD_DIM:] = in_lanes(peak + jnp.log(total))
            return carry

        lax.fori_loop(0, self.devices * self.rows // some, group, 0)

    def return_rows(self):
        r, place, wires = self.r, self.place, self.wires
        bf16, f32 = jnp.bfloat16, jnp.float32

        def first(block, carry):
            self.unsort_block(r.round_rows, block)
            return carry

        lax.fori_loop(0, self.devices, first, 0)
        coming = []
        for half in (1 - place.which, place.which):
            arriving = []
            for bits in (3, 1, 2, 0):
                turn = flipped(place.turn, bits)
                rows = self.unsorted_chunk(half * self.turns + turn)
                total = jnp.sum(rows[:, HEAD_DIM:], 1, keepdims=True)
                lines = [to_row(total[i : i + 128]) for i in range(0, self.rows, 128)]
                total = jnp.concatenate(lines, 0)
                rows = rows[:, :HEAD_DIM].astype(bf16)
                if not bits:
                    r.outs[place.turn, half] = rows
                    r.totals[place.turn, half] = total
                    continue
                r.out_send[bits - 1, half] = rows
                r.total_send[bits - 1, half] = total
                for source, target in ((r.total_send, r.totals), (r.out_send, r.outs)):
                    arriving.append(
                        wires.push(
                            source.at[bits - 1, half],
                            target.at[place.turn, half],
                            place.peer(bits),
                        )
                    )
            coming.append(arriving)
        self.rounds_coming = coming

    def mix_half(self, half):
        r = self.r
        bf16, f32 = jnp.bfloat16, jnp.float32
        totals = [r.totals[turn, half] for turn in range(self.turns)]
        peak = totals[0]
        for total in totals[1:]:
            peak = jnp.maximum(peak, total)
        power = [jnp.exp(total - peak) for total in totals]
        whole = sum(power[1:], power[0])
        for turn in range(self.turns):
            r.mix_rows[turn, half] = power[turn] / whole

        def combine(part, carry):
            here = span(part, 128)
            attended = jnp.zeros((128, HEAD_DIM), f32)
            for turn in range(self.turns):
                mix = to_column(r.mix_rows[turn, half, pl.ds(part, 1), :])
                mix = jnp.broadcast_to(mix, (128, HEAD_DIM))
                r.mix[turn, half, here, :] = mix
                attended += mix * r.outs[turn, half, here, :].astype(f32)
            r.attended[half, here, :] = attended.astype(bf16)
            return carry

        lax.fori_loop(0, self.rows // 128, combine, 0)

    def mix_rounds(self):
        r, place, wires = self.r, self.place, self.wires

        def columns(head, which):
            return columns_at(r.attended_full, head * self.pair + which, HEAD_DIM)

        def gather(which):
            return HeadGather(wires, place, lambda head: columns(head, which))

        mine = columns(place.head, place.which)
        for copy in self.rounds_coming[0]:
            copy.wait_recv()
        self.mix_half(1 - place.which)
        swap = wires.push(r.attended.at[1 - place.which], mine, place.peer(4))
        for copy in self.rounds_coming[1]:
            copy.wait_recv()
        self.mix_half(place.which)
        own, other = gather(place.which), gather(1 - place.which)
        own.start(r.attended.at[place.which])
        mine[...] = r.attended[place.which]
        swap.wait_recv()
        other.start(other.slot(place.head))
        own.relay()
        other.relay()
        own.finish()
        other.finish()
        wires.settle([copy for arriving in self.rounds_coming for copy in arriving])


    def feed_forward(self):
        r, place, wires = self.r, self.place, self.wires
        bf16, f32 = jnp.bfloat16, jnp.float32
        tile_rows = self.rows // 2
        self.parts_two = []
        for tile in range(2):
            here = pl.ds(tile * tile_rows, tile_rows)
            total = r.one_full[here, :].astype(f32) + dot(r.attended_full[here, :], r.merge_full[...])
            center = jnp.mean(total, 1, keepdims=True)
            offset = total - center
            factor = lax.rsqrt(jnp.mean(offset * offset, 1, keepdims=True) + 1e-05)
            normal = offset * factor
            r.tall[...] = total
            r.result_one[here, :] = columns_at(r.tall, place.head, self.width)[...].astype(bf16)
            r.tall[...] = normal
            r.normal_two[here, :] = columns_at(r.tall, place.head, self.width)[...]
            r.factor_two[here, :] = jnp.broadcast_to(factor, (tile_rows, 128))
            rows = (normal * r.params_full[2:3, :] + r.params_full[3:4, :]).astype(bf16)
            r.rows_two[here, :] = rows
            hidden = dot(rows, r.expand_full[...])
            below = 0.5 * (1.0 + lax.erf(hidden * (0.5**0.5)))
            r.active[here, :] = (hidden * below).astype(bf16)
            slope = below + hidden * jnp.exp(-0.5 * hidden * hidden) * ((2.0 * jnp.pi) ** -0.5)
            grad = dot(r.grad_full[here, :], r.shrink_full[...], ((1,), (1,)))
            grad = (grad * slope).astype(bf16)
            r.grad_hidden[here, :] = grad
            part = dot(grad, r.expand_full[...], ((1,), (1,)))
            self.send_part(
                tile, part, r.tall[...], r.params_full[2:3, :], r.part_two, r.stat_two,
                r.parts_two, self.parts_two,
            )
        self.send_stats(r.stat_two, r.stats_two, self.parts_two)

    def send_part(self, tile, part, normal, gain, part_ref, stat_ref, target, copies):
        tile_rows = part.shape[0]
        here = pl.ds(tile * tile_rows, tile_rows)
        scaled = part * gain
        first = jnp.sum(scaled, 1, keepdims=True)
        second = jnp.sum(scaled * normal, 1, keepdims=True)
        lines = tile_rows // 128
        for line in range(lines):
            at = slice(line * 128, (line + 1) * 128)
            row = tile * lines + line
            stat_ref[row : row + 1, :] = to_row(first[at])
            row += self.rows // 128
            stat_ref[row : row + 1, :] = to_row(second[at])
        part_ref[here, :] = part.astype(jnp.bfloat16)
        for bits in (2, 3, 1):
            device = self.place.peer(0, bits)
            source = columns_at(part_ref.at[here], device[1], self.width)
            copies.append(self.wires.push(source, target.at[bits - 1, here], device))

    def send_stats(self, stat_ref, target, copies):
        for bits in (2, 3, 1):
            device = self.place.peer(0, bits)
            copies.append(self.wires.push(stat_ref, target.at[bits - 1], device))

    def norm_back(self, part_ref, parts, stat_ref, stats, normal_at, factor_ref, gain, finish):
        f32 = jnp.float32
        lines = self.rows // 128

        def piece(line, carry):
            here = span(line, 128)
            grad = columns_at(part_ref.at[here], self.place.head, self.width)[...].astype(f32)
            first, second = stat_ref[pl.ds(line, 1), :], stat_ref[pl.ds(line + lines, 1), :]
            for other in range(3):
                grad += parts[other, here, :].astype(f32)
                first += stats[other, pl.ds(line, 1), :]
                second += stats[other, pl.ds(line + lines, 1), :]
            normal = normal_at(here)
            first, second = to_column(first) / self.wide, to_column(second) / self.wide
            finish(here, factor_ref[here, 0:1] * (grad * gain - first - normal * second))
            gains, biases = carry
            return (
                gains + jnp.sum(grad * normal, 0, keepdims=True),
                biases + jnp.sum(grad, 0, keepdims=True),
            )

        zero = jnp.zeros((1, self.width), f32)
        return lax.fori_loop(0, lines, piece, (zero, zero))

    def my_params(self, row):
        return columns_at(self.r.params_full, self.place.head, self.width)[row : row + 1, :]

    def feed_back(self):
        r, place, wires = self.r, self.place, self.wires
        bf16, f32 = jnp.bfloat16, jnp.float32
        self.weights(r.rows_two, r.grad_hidden, r.grad_expand)
        self.expand_out = SeqScatter(
            wires, place, lambda seq: rows_at(r.grad_expand, seq, r.expand.shape[0]),
            r.expand_pair, r.expand_line,
        )
        for copy in self.parts_two:
            copy.wait_recv()
        wires.settle(self.parts_two)

        def finish(here, change):
            total = r.grad_one[here, :].astype(f32) + change
            r.input_grad_one[here, :] = total.astype(bf16)

        gains, biases = self.norm_back(
            r.part_two, r.parts_two, r.stat_two, r.stats_two,
            lambda here: r.normal_two[here, :], r.factor_two, self.my_params(2), finish,
        )
        r.norm_send[2:3, :], r.norm_send[3:4, :] = gains, biases
        gather = self.over_head(r.grad_rows_one)
        self.start_head(gather, r.input_grad_one)
        self.expand_out.start()

        def feed(tile, carry):
            here = span(tile, 256)
            r.feed[here, :] = dot(r.active[here, :], r.shrink_full[...]).astype(bf16)
            return carry

        lax.fori_loop(0, self.rows // 256, feed, 0)
        self.weights(r.active, r.grad_full, r.grad_shrink)
        self.shrink_out = SeqScatter(
            wires, place, lambda seq: columns_at(r.grad_shrink, seq, r.shrink.shape[1]),
            r.shrink_pair, r.shrink_line,
        )
        gather.relay()
        gather.finish()

    def weights(self, left, right, target):
        step = min(256, left.shape[1])

        def piece(index, carry):
            columns = span(index, step)
            result = dot(left[:, columns], right[...], ((0,), (0,)))
            target[columns, :] = result.astype(jnp.bfloat16)
            return carry

        lax.fori_loop(0, left.shape[1] // step, piece, 0)

    def send_feed(self):
        r = self.r
        self.feeds = []
        for bits in (2, 3, 1):
            device = self.place.peer(0, bits)
            source = columns_at(r.feed, device[1], self.width)
            self.feeds.append(self.wires.push(source, r.feeds.at[bits - 1], device))

    def finish_feed(self):
        r = self.r
        f32 = jnp.float32
        for copy in self.feeds:
            copy.wait_recv()
        total = r.two[...].astype(f32)
        total += columns_at(r.feed, self.place.head, self.width)[...].astype(f32)
        for other in range(3):
            total += r.feeds[other].astype(f32)
        r.result_two[...] = total.astype(jnp.bfloat16)


    def grad_rounds(self):
        r, place, wires = self.r, self.place, self.wires
        bf16, f32 = jnp.bfloat16, jnp.float32
        my_rows = rows_at(r.merge_full, place.head, r.merge.shape[0])

        def attended(tile, carry):
            here = span(tile, 256)
            grad = dot(r.grad_rows_one[here, :], my_rows[...], ((1,), (1,))).astype(bf16)
            for which in range(self.pair):
                r.grad_heads[which, here, :] = grad[:, which * HEAD_DIM : (which + 1) * HEAD_DIM]
            return carry

        lax.fori_loop(0, self.rows // 256, attended, 0)
        mine = r.grad_attended.at[place.which]
        swap = wires.push(r.grad_heads.at[1 - place.which], mine, place.peer(4))
        mine[...] = r.grad_heads[place.which]
        lines = self.rows // 128

        def spread(half, carry):
            def piece(part, carry):
                here = span(part, 128)
                grad = r.grad_attended[half, here, :].astype(f32)
                turns = [flipped(place.turn, bits) for bits in range(self.turns)]
                mixes = [r.mix[turn, half, here, :] for turn in turns]
                dots = [
                    jnp.sum(r.outs[turn, half, here, :].astype(f32) * grad, 1, keepdims=True)
                    for turn in turns
                ]
                mean = sum(mix[:, 0:1] * value for mix, value in zip(mixes, dots))
                for bits in range(self.turns):
                    change = to_row(mixes[bits][:, 0:1] * (dots[bits] - mean))
                    rows = (mixes[bits] * grad).astype(bf16)
                    if bits:
                        r.grad_send[bits - 1, half, here, :] = rows
                        r.grad_total_send[bits - 1, half, pl.ds(part, 1), :] = change
                    else:
                        r.grad_outs[place.turn, half, here, :] = rows
                        r.grad_totals[place.turn, half, pl.ds(part, 1), :] = change
                return carry

            return lax.fori_loop(0, lines, piece, carry)

        self.grads_coming = {bits: [] for bits in (3, 1, 2)}

        def send(half):
            for bits in (3, 1, 2):
                for source, target in (
                    (r.grad_total_send, r.grad_totals),
                    (r.grad_send, r.grad_outs),
                ):
                    self.grads_coming[bits].append(
                        wires.push(
                            source.at[bits - 1, half],
                            target.at[place.turn, half],
                            place.peer(bits),
                        )
                    )

        spread(place.which, 0)
        send(place.which)
        self.weights(columns_at(r.attended_full, place.head, self.width), r.grad_rows_one, r.grad_merge)
        swap.wait_recv()
        spread(1 - place.which, 0)
        send(1 - place.which)
        self.merge_out = SeqScatter(
            wires, place, lambda seq: columns_at(r.grad_merge, seq, r.merge.shape[1]),
            r.merge_pair, r.merge_line,
        )

    def sort_grads(self):
        r, place = self.r, self.place
        bf16 = jnp.bfloat16
        lines = self.rows // 128
        for bits in (0, 1, 2, 3):
            turn = flipped(place.turn, bits)
            if bits:
                for copy in self.grads_coming[bits]:
                    copy.wait_recv()

            def stage(half, carry, turn=turn):
                chunk = half * self.turns + turn
                r.everyone[span(chunk, self.rows), :HEAD_DIM] = r.grad_outs[turn, half]

                def piece(part, carry):
                    total = to_column(r.grad_totals[turn, half, pl.ds(part, 1), :])
                    r.everyone[span(chunk * lines + part, 128), HEAD_DIM:] = in_lanes(total)
                    return carry

                lax.fori_loop(0, lines, piece, 0)
                self.sort_chunk(r.everyone, chunk)
                return carry

            lax.fori_loop(0, self.pair, stage, 0)

        def second(block, carry):
            r.round_rows[span(block, self.rows), :] = self.sorted_block(block).astype(bf16)
            return carry

        lax.fori_loop(0, self.devices, second, 0)

    def attend_back(self):
        r = self.r
        bf16, f32 = jnp.bfloat16, jnp.float32
        scale = HEAD_DIM ** (-0.5)
        some = 4 * GROUP
        r.grad_unit[0:GROUP, :] = jnp.zeros((GROUP, HEAD_DIM), f32)
        r.grad_value[0:GROUP, :] = jnp.zeros((GROUP, HEAD_DIM), f32)

        def one(rows, block):
            return rows[block * GROUP : (block + 1) * GROUP]

        def fold(pieces):
            owns = [piece[:GROUP] if i % 2 == 0 else piece[GROUP:] for i, piece in enumerate(pieces)]
            befores = [piece[GROUP:] if i % 2 == 0 else piece[:GROUP] for i, piece in enumerate(pieces)]
            middle = [owns[i] + befores[i + 1] for i in range(3)]
            return befores[0], jnp.concatenate(middle + [owns[3]], 0)

        def group(index, carry):
            here = span(index, some)
            longer = pl.ds(pl.multiple_of(index * some, some), some + GROUP)
            before = pl.ds(pl.multiple_of(index * some, some), GROUP)
            after = pl.ds(pl.multiple_of(index * some + GROUP, GROUP), some)
            query, unit, value = r.sorted_query[here, :], r.unit[longer, :], r.key_value[longer, :]
            grad = r.round_rows[here, :HEAD_DIM]
            total = jnp.sum(r.round_rows[here, HEAD_DIM:].astype(f32), 1, keepdims=True)
            probs = r.probs[here, :]
            low = probs.astype(bf16)
            live = jnp.where(self.codes(index) == 0.0, probs, 0.0)
            grad_probs = jnp.concatenate(
                [dot(one(grad, i), self.window(value, i), ((1,), (1,))) for i in range(4)], 0
            )
            inner = jnp.sum(probs * grad_probs, 1, keepdims=True)
            scores = (live * (grad_probs - inner + total)).astype(bf16)
            r.probs[here, :] = (
                jnp.concatenate([dot(one(scores, i), self.window(unit, i)) for i in range(4)], 0) * scale
            )
            for target, left, right, factor in (
                (r.grad_unit, scores, query, scale),
                (r.grad_value, low, grad, 1.0),
            ):
                first, rest = fold(
                    [dot(one(left, i), one(right, i), ((0,), (0,))) * factor for i in range(4)]
                )
                target[before, :] += first
                target[after, :] = rest
            return carry

        lax.fori_loop(0, self.devices * self.rows // some, group, 0)
        last = pl.ds(self.devices * self.rows, GROUP)
        r.grad_unit[last, :] += r.grad_unit[0:GROUP, :]
        r.grad_value[last, :] += r.grad_value[0:GROUP, :]

        def whole(index, carry):
            here = span(index, some)
            after = pl.ds(pl.multiple_of(index * some + GROUP, GROUP), some)
            query = r.sorted_query[here, :].astype(f32)
            factor = lax.rsqrt(jnp.sum(query * query, 1, keepdims=True) + 1e-06)
            unit = query * factor
            grad = r.grad_unit[after, :]
            along = jnp.sum(unit * grad, 1, keepdims=True)
            grad = r.probs[here, :] + factor * (grad - unit * along)
            r.round_rows[here, :HEAD_DIM] = grad.astype(bf16)
            r.round_rows[here, HEAD_DIM:] = r.grad_value[after, :].astype(bf16)
            return carry

        lax.fori_loop(0, self.devices * self.rows // some, whole, 0)

    def return_grads(self):
        r, place, wires = self.r, self.place, self.wires
        bf16, f32 = jnp.bfloat16, jnp.float32

        def first(block, carry):
            self.unsort_block(r.round_rows, block)
            return carry

        lax.fori_loop(0, self.devices, first, 0)
        coming = []
        for kind, half in enumerate((1 - place.which, place.which)):
            for bits in (3, 1, 2, 0):
                chunk = half * self.turns + flipped(place.turn, bits)
                rows = self.unsorted_chunk(chunk).astype(bf16)
                if bits:
                    r.everyone[pl.ds(((bits - 1) * 2 + kind) * self.rows, self.rows), :] = rows
                else:
                    r.grad_pairs[place.turn, kind] = rows
            for part in (1, 0):
                columns = pl.ds(part * HEAD_DIM, HEAD_DIM)
                arriving = []
                for bits in (3, 1, 2):
                    rows = pl.ds(((bits - 1) * 2 + kind) * self.rows, self.rows)
                    arriving.append(
                        wires.push(
                            r.everyone.at[rows, columns],
                            r.grad_pairs.at[place.turn, kind, :, columns],
                            place.peer(bits),
                        )
                    )
                coming.append((kind, part, columns, arriving))
        swaps = []
        for kind, part, columns, arriving in coming:
            for copy in arriving:
                copy.wait_recv()
            target = r.grad_key if part else r.grad_query
            mine = columns_at(target, place.which, HEAD_DIM)
            total = r.grad_pairs[0, kind, :, columns].astype(f32)
            for turn in range(1, self.turns):
                total += r.grad_pairs[turn, kind, :, columns].astype(f32)
            if kind == 0:
                r.grad_pair[part] = total.astype(bf16)
                swaps.append(wires.push(r.grad_pair.at[part], mine, place.peer(4)))
            else:
                mine[...] = total.astype(bf16)
                swaps[1 - part].wait_recv()
                if part:
                    self.value_weights()

    def value_weights(self):
        r = self.r
        self.weights(r.rows_one, r.grad_key, r.grad_value_full)
        self.value_out = SeqScatter(
            self.wires, self.place,
            lambda seq: rows_at(r.grad_value_full, seq, r.value.shape[0]),
            r.value_pair, r.value_line,
        )
        self.value_out.start()

    def project_back(self):
        r, place, wires = self.r, self.place, self.wires
        bf16, f32 = jnp.bfloat16, jnp.float32
        self.weights(r.rows_one, r.grad_query, r.grad_query_full)
        self.query_out = SeqScatter(
            wires, place, lambda seq: rows_at(r.grad_query_full, seq, r.query.shape[0]),
            r.query_pair, r.query_line,
        )
        self.query_out.start()
        copies = []
        tile_rows = self.rows // 2
        for tile in range(2):
            here = pl.ds(tile * tile_rows, tile_rows)
            part = dot(r.grad_query[here, :], r.query_full[...], ((1,), (1,)))
            part += dot(r.grad_key[here, :], r.value_full[...], ((1,), (1,)))
            normal = (r.two_full[here, :].astype(f32) - r.center_one[here, 0:1]) * r.factor_one[
                here, 0:1
            ]
            self.send_part(
                tile, part, normal, r.params_full[0:1, :], r.part_one, r.stat_one,
                r.parts_one, copies,
            )
        self.send_stats(r.stat_one, r.stats_one, copies)
        self.value_out.along()
        for copy in copies:
            copy.wait_recv()

        def normal_at(here):
            rows = columns_at(r.two_full.at[here], place.head, self.width)[...].astype(f32)
            return (rows - r.center_one[here, 0:1]) * r.factor_one[here, 0:1]

        def finish(here, change):
            total = r.grad_two[here, :].astype(f32) + change
            r.input_grad_two[here, :] = total.astype(bf16)

        gains, biases = self.norm_back(
            r.part_one, r.parts_one, r.stat_one, r.stats_one, normal_at, r.factor_one,
            self.my_params(0), finish,
        )
        r.norm_send[0:1, :], r.norm_send[1:2, :] = gains, biases
        norms = [
            wires.push(r.norm_send, r.norms.at[bits - 1], place.peer(bits)) for bits in range(1, 8)
        ]
        self.query_out.along()
        self.expand_out.finish(r.expand_part)
        self.shrink_out.finish(r.shrink_part)
        self.merge_out.finish(r.merge_part)
        self.finish_feed()
        total = r.norm_send[...]
        for bits, copy in enumerate(norms):
            copy.wait_recv()
            total += r.norms[bits]
        r.norm_grads[...] = total
        self.query_out.finish(r.query_part)
        self.value_out.finish(r.value_part)


def on_device(names, turns, *refs):
    r = SimpleNamespace(**dict(zip(names, refs)))
    r.feed, r.grad_expand, r.grad_shrink = r.one_full, r.expand_full, r.shrink_full
    r.grad_pair, r.part_one, r.grad_send = r.packed.at[0], r.part_two, r.out_send
    steps = Phases(r, turns)
    steps.place.greet()
    steps.project()
    steps.sort_tokens()
    steps.go_on(steps.expand[1])
    steps.begin(steps.shrink[0])
    steps.attend()
    steps.begin(steps.shrink[1])
    steps.begin_merge_rows()
    steps.return_rows()
    steps.go_on(steps.shrink[0])
    steps.mix_rounds()
    steps.one.relay()
    steps.grads.relay()
    steps.heads.relay()
    steps.go_on(steps.shrink[1])
    steps.one.finish()
    steps.grads.finish()
    steps.heads.finish()
    steps.expand[0].finish()
    steps.expand[1].finish()
    steps.shrink[0].finish()
    steps.shrink[1].finish()
    steps.feed_forward()
    steps.feed_back()
    steps.expand_out.along()
    steps.grad_rounds()
    steps.send_feed()
    steps.sort_grads()
    steps.shrink_out.start()
    steps.merge_out.start()
    steps.attend_back()
    steps.shrink_out.along()
    steps.merge_out.along()
    steps.return_grads()
    steps.project_back()
    steps.wires.drain()
    assert len(steps.wires.copies) <= r.send.shape[0]


def whole(turns, arguments, tables):
    bf16, f32 = jnp.bfloat16, jnp.float32
    heads, devices = lax.axis_size("head"), lax.axis_size("seq")
    pair = devices // turns
    rows, width = arguments["two"].shape
    tokens, wide = devices * rows, heads * width
    hidden = arguments["expand"].shape[1]
    lines = rows // 128
    shape = {name: value.shape for name, value in arguments.items()}
    results = dict(
        result_one=((rows, width), bf16),
        result_two=((rows, width), bf16),
        input_grad_one=((rows, width), bf16),
        input_grad_two=((rows, width), bf16),
        query_part=(shape["query"], f32),
        value_part=(shape["value"], f32),
        merge_part=(shape["merge"], f32),
        expand_part=(shape["expand"], f32),
        shrink_part=(shape["shrink"], f32),
        norm_grads=((8, width), f32),
    )
    scratch = dict(
        params=((8, width), f32),
        keys=((tokens // 128, 1, 128), f32),
        block_row=((devices, 1, rows), jnp.int32),
        block_column=((tokens, 128), jnp.int16),
        chunk_row=((devices, 1, rows), jnp.int32),
        chunk_column=((tokens, 128), jnp.int16),
        sorted_query=((tokens, HEAD_DIM), bf16),
        unit=((tokens + GROUP, HEAD_DIM), bf16),
        key_value=((tokens + GROUP, HEAD_DIM), bf16),
        probs=((tokens, 2 * GROUP), f32),
        outs=((turns, pair, rows, HEAD_DIM), bf16),
        mix=((turns, pair, rows, HEAD_DIM), f32),
        rows_one=((rows, wide), bf16),
        center_one=((rows, 128), f32),
        factor_one=((rows, 128), f32),
        query_full=((wide, width), bf16),
        value_full=((wide, width), bf16),
        merge_full=((wide, wide), bf16),
        expand_full=((wide, hidden), bf16),
        shrink_full=((hidden, wide), bf16),
        one_full=((rows, wide), bf16),
        two_full=((rows, wide), bf16),
        grad_full=((rows, wide), bf16),
        attended_full=((rows, wide), bf16),
        everyone=((tokens, 2 * HEAD_DIM), bf16),
        mid=((devices * devices, rows // devices, 2 * HEAD_DIM), bf16),
        params_full=((8, wide), f32),
        packed=((pair, 2, rows, HEAD_DIM), bf16),
        round_rows=((tokens, 2 * HEAD_DIM), bf16),
        out_send=((turns - 1, pair, rows, HEAD_DIM), bf16),
        total_send=((turns - 1, pair, lines, 128), f32),
        totals=((turns, pair, lines, 128), f32),
        mix_rows=((turns, pair, lines, 128), f32),
        attended=((pair, rows, HEAD_DIM), bf16),
        tall=((rows // 2, wide), f32),
        normal_two=((rows, width), f32),
        factor_two=((rows, 128), f32),
        rows_two=((rows, wide), bf16),
        active=((rows, hidden), bf16),
        grad_hidden=((rows, hidden), bf16),
        part_two=((rows, wide), bf16),
        stat_two=((2 * lines, 128), f32),
        parts_two=((heads - 1, rows, width), bf16),
        stats_two=((heads - 1, 2 * lines, 128), f32),
        stat_one=((2 * lines, 128), f32),
        parts_one=((heads - 1, rows, width), bf16),
        stats_one=((heads - 1, 2 * lines, 128), f32),
        feeds=((heads - 1, rows, width), bf16),
        grad_rows_one=((rows, wide), bf16),
        grad_heads=((pair, rows, HEAD_DIM), bf16),
        grad_attended=((pair, rows, HEAD_DIM), bf16),
        grad_total_send=((turns - 1, pair, lines, 128), f32),
        grad_outs=((turns, pair, rows, HEAD_DIM), bf16),
        grad_totals=((turns, pair, lines, 128), f32),
        grad_unit=((tokens + GROUP, HEAD_DIM), f32),
        grad_value=((tokens + GROUP, HEAD_DIM), f32),
        grad_pairs=((turns, pair, rows, 2 * HEAD_DIM), bf16),
        grad_query=((rows, width), bf16),
        grad_key=((rows, width), bf16),
        norm_send=((8, width), f32),
        norms=((devices - 1, 8, width), f32),
    )
    for name, full in (
        ("query", (wide, width)),
        ("value", (wide, width)),
        ("merge", (width, wide)),
        ("expand", (wide, hidden)),
        ("shrink", (hidden, wide)),
    ):
        own = "grad_" + name + ("_full" if name in ("query", "value") else "")
        if name not in ("expand", "shrink"):
            scratch[own] = (full, bf16)
        scratch[name + "_pair"] = ((devices // 2,) + shape[name], bf16)
        scratch[name + "_line"] = ((devices // 2 - 1,) + shape[name], bf16)
    wires = dict(send=224, receive=224)
    vmem = pl.BlockSpec(memory_space=pltpu.VMEM)
    smem = pl.BlockSpec(memory_space=pltpu.SMEM)
    names = [*arguments, *tables, *results, *scratch, *wires]
    out = pl.pallas_call(
        partial(on_device, names, turns),
        out_shape=[jax.ShapeDtypeStruct(*item) for item in results.values()],
        in_specs=[vmem] * len(arguments)
        + [smem if name.startswith("units") else vmem for name in tables],
        out_specs=[vmem] * len(results),
        scratch_shapes=[pltpu.VMEM(*item) for item in scratch.values()]
        + [pltpu.SemaphoreType.DMA((number,)) for number in wires.values()],
        compiler_params=pltpu.CompilerParams(
            collective_id=0, has_side_effects=True, vmem_limit_bytes=63 << 20
        ),
    )(*arguments.values(), *tables.values())
    return SimpleNamespace(**dict(zip(results, out)))


def round_tables(order, bucket, devices, rows):
    i32 = jnp.int32
    unit = rows // devices
    order, bucket = order.reshape(devices, 1, rows), bucket.reshape(devices, 1, rows)
    each = jnp.arange(devices, dtype=i32)
    share = jnp.sum((order // rows == each[None, :, None]).astype(i32), -1)
    before = each[:, None] < each[None, :]
    in_block = jnp.sum(jnp.where(before[None], share[:, :, None], 0), 1)
    in_chunk = jnp.sum(jnp.where(before[:, :, None], share[:, None, :], 0), 0)
    start = each * unit

    def find(offset, share, other):
        ends = offset + share
        segment = jnp.sum((ends[:, None, :] <= start[None, :, None]).astype(i32), -1)
        chosen = (segment[:, :, None] == each).astype(i32)
        move = jnp.sum(chosen * (other - offset)[:, None, :], -1)
        return ((segment * rows + start[None] + move) // unit).reshape(-1)

    return dict(
        order=order,
        bucket=bucket,
        units=find(in_block, share, in_chunk),
        units_back=find(in_chunk.T, share.T, in_block.T),
    )


def by_rounds(
    stream_one,
    stream_two,
    grad_one,
    grad_two,
    query_weight,
    value_weight,
    merge_weight,
    expand_weight,
    shrink_weight,
    first_gain,
    first_bias,
    second_gain,
    second_bias,
    bucket_ids,
    sort_order,
):
    devices, place = lax.axis_size("seq"), lax.axis_index("seq")
    rounds = sort_order.shape[0]
    turn = place % rounds
    order = lax.dynamic_slice_in_dim(sort_order, turn, 1, 0)[0]
    bucket = lax.dynamic_slice_in_dim(bucket_ids, turn, 1, 0)[0]
    arguments = dict(
        one=stream_one,
        two=stream_two,
        grad_one=grad_one,
        grad_two=grad_two,
        query=query_weight,
        value=value_weight,
        merge=merge_weight,
        expand=expand_weight,
        shrink=shrink_weight,
        gain_one=first_gain[None],
        bias_one=first_bias[None],
        gain_two=second_gain[None],
        bias_two=second_bias[None],
    )
    k = whole(rounds, arguments, round_tables(order, bucket, devices, stream_one.shape[0]))
    return (
        k.result_one,
        k.result_two,
        k.input_grad_one,
        k.input_grad_two,
        k.query_part,
        k.value_part,
        k.merge_part,
        k.expand_part,
        k.shrink_part,
        k.norm_grads[0],
        k.norm_grads[1],
        k.norm_grads[2],
        k.norm_grads[3],
    )


def solution(mesh):
    placed = (
        P("seq", "head"),
        P("seq", "head"),
        P("seq", "head"),
        P("seq", "head"),
        P("seq", "head"),
        P("seq", "head"),
        P("head", "seq"),
        P("seq", "head"),
        P("head", "seq"),
        P("head"),
        P("head"),
        P("head"),
        P("head"),
        P(),
        P(),
    )

    def local(*arguments):
        rounds = arguments[-1].shape[0]
        if mesh.shape["seq"] * mesh.shape["head"] == rounds * HEADS:
            return by_rounds(*arguments)
        return by_blocks(*arguments)

    return jax.shard_map(
        local,
        mesh=mesh,
        in_specs=placed,
        out_specs=(
            P("seq", "head"),
            P("seq", "head"),
            P("seq", "head"),
            P("seq", "head"),
            P("seq", "head"),
            P("seq", "head"),
            P("head", "seq"),
            P("seq", "head"),
            P("head", "seq"),
            P("head"),
            P("head"),
            P("head"),
            P("head"),
        ),
        check_vma=False,
    )
```

```python
from functools import partial
from types import SimpleNamespace

import jax
import jax.numpy as jnp
from jax import lax
from jax.experimental import pallas as pl
from jax.experimental.pallas import tpu as pltpu
from jax.sharding import PartitionSpec as P

HEADS = 8
HEAD_DIM = 128
GROUP = 64
MESH = pl.DeviceIdType.MESH


masked_score = -1000000000.0
own_score = -100000.0


def as_sent(shard):

    def short(part):
        return part.astype(jnp.bfloat16) if part.dtype == jnp.float32 else part

    return jax.tree.map(short, shard)


def from_behind(block, axis, distance):
    devices = range(lax.axis_size(axis))
    route = [(i - distance, i) for i in devices if i - distance in devices]
    return lax.ppermute(block, axis, route)


def row_sums(first, second):
    return lax.psum((first, second), "head")


def full_rows(part):
    return lax.all_gather(part, "head", axis=1, tiled=True)


def branch_sum(part):
    return lax.psum_scatter(part, "head", scatter_dimension=1, tiled=True)


def norm_forward(value, gain, shift):
    width = value.shape[1] * lax.axis_size("head")
    total, square = row_sums(
        jnp.sum(value, 1, keepdims=True), jnp.sum(value * value, 1, keepdims=True)
    )
    center = total / width
    spread = square / width - center * center
    factor = lax.rsqrt(spread + 1e-05)
    normal = (value - center) * factor
    return (normal, factor, normal * gain + shift)


def norm_backward(grad, normal, factor, gain):
    width = grad.shape[1] * lax.axis_size("head")
    scaled = grad * gain
    first, second = row_sums(
        jnp.sum(scaled, 1, keepdims=True), jnp.sum(scaled * normal, 1, keepdims=True)
    )
    result = factor * (scaled - first / width - normal * (second / width))
    return (result, jnp.sum(grad * normal, 0), jnp.sum(grad, 0))


def regroup_rows(buffer):
    turns = []
    for turn in range(buffer.shape[1]):
        turns.append(
            lax.all_to_all(buffer[:, turn], "seq", split_axis=0, concat_axis=0, tiled=True)
        )
    result = jnp.stack(turns, 1)
    return result


def regroup_totals(buffer):
    moved = lax.all_to_all(
        buffer.reshape(buffer.shape[0], -1, buffer.shape[3]),
        "seq",
        split_axis=0,
        concat_axis=0,
        tiled=True,
    )
    return moved.reshape(buffer.shape)


def regroup_pair(first, second):
    firsts = []
    seconds = []
    for turn in range(first.shape[1]):
        moved_first, moved_second = (
            lax.all_to_all(as_sent(first[:, turn]), "seq", split_axis=0, concat_axis=0, tiled=True),
            lax.all_to_all(
                as_sent(second[:, turn]), "seq", split_axis=0, concat_axis=0, tiled=True
            ),
        )
        firsts.append(moved_first)
        seconds.append(moved_second)
    result = (jnp.stack(firsts, 1), jnp.stack(seconds, 1))
    return result


def by_blocks(
    stream_one,
    stream_two,
    grad_one,
    grad_two,
    query_weight,
    value_weight,
    merge_weight,
    expand_weight,
    shrink_weight,
    first_gain,
    first_bias,
    second_gain,
    second_bias,
    bucket_ids,
    sort_order,
):
    devices = lax.axis_size("seq")
    place = lax.axis_index("seq")
    rows = stream_one.shape[0]
    rounds = sort_order.shape[0]
    capacity = 2 * rows // devices
    blocks = rows // GROUP
    heads_here = HEADS // lax.axis_size("head")
    local_width = heads_here * HEAD_DIM
    scale = HEAD_DIM ** (-0.5)
    round_index = jnp.arange(rounds, dtype=jnp.int32)[:, None]
    counter = jnp.arange(rows, dtype=jnp.int32)

    def invert(line):
        return jnp.zeros_like(line).at[line].set(jnp.arange(line.shape[0], dtype=jnp.int32))

    inverse = jax.vmap(invert)(sort_order)
    my_sorted = lax.dynamic_slice_in_dim(inverse, place * rows, rows, 1)
    send_block = my_sorted // rows
    same_block = send_block[:, :, None] == send_block[:, None, :]
    send_slot = jnp.sum(
        (same_block & (my_sorted[:, None, :] < my_sorted[:, :, None])).astype(jnp.int32), -1
    )
    block_tokens = lax.dynamic_slice_in_dim(sort_order, place * rows, rows, 1)
    source_block = block_tokens // rows
    earlier = counter[None, :] < counter[:, None]
    recv_slot = jnp.sum(
        ((source_block[:, :, None] == source_block[:, None, :]) & earlier[None]).astype(jnp.int32),
        -1,
    )
    query_bucket = jnp.take_along_axis(bucket_ids, block_tokens, 1)
    prior_start = (place - 1) % devices * rows + rows - GROUP
    prior_tokens = lax.dynamic_slice_in_dim(sort_order, prior_start, GROUP, 1)
    prior_bucket = jnp.take_along_axis(bucket_ids, prior_tokens, 1)

    def with_prior(own, prior):
        pieces = own.reshape((rounds, blocks, GROUP) + own.shape[2:])
        before = jnp.concatenate([prior[:, None], pieces[:, :-1]], 1)
        return jnp.concatenate([pieces, before], 2)

    query_place = block_tokens.reshape(rounds, blocks, GROUP)
    key_place = with_prior(block_tokens, prior_tokens)
    key_bucket = with_prior(query_bucket, prior_bucket)
    allowed = (key_place[:, :, None, :] <= query_place[:, :, :, None]) & (
        key_bucket[:, :, None, :] == query_bucket.reshape(rounds, blocks, GROUP)[:, :, :, None]
    )
    itself = key_place[:, :, None, :] == query_place[:, :, :, None]
    live = allowed & jnp.logical_not(itself)

    def fill(values, block, slot):
        empty = jnp.zeros((devices, rounds, capacity, values.shape[-1]), values.dtype)
        return empty.at[block, round_index, slot].set(values)

    normal_one, factor_one, normed_one = norm_forward(
        stream_two.astype(jnp.float32), first_gain, first_bias
    )
    rows_one = full_rows(normed_one.astype(jnp.bfloat16))
    query_full, value_full, merge_full = (
        lax.all_gather(query_weight, "seq", axis=0, tiled=True),
        lax.all_gather(value_weight, "seq", axis=0, tiled=True),
        lax.all_gather(merge_weight, "seq", axis=1, tiled=True),
    )
    queries = jnp.dot(rows_one, query_full, preferred_element_type=jnp.float32).astype(jnp.bfloat16)
    values = jnp.dot(rows_one, value_full, preferred_element_type=jnp.float32).astype(jnp.bfloat16)
    packed = jnp.concatenate([queries, values], 1)
    outgoing = fill(jnp.broadcast_to(packed[None], (rounds,) + packed.shape), send_block, send_slot)
    incoming = regroup_rows(outgoing)
    sorted_rows = incoming[source_block, round_index, recv_slot]
    sorted_query = sorted_rows[:, :, :local_width].reshape(rounds, rows, heads_here, HEAD_DIM)
    sorted_value = sorted_rows[:, :, local_width:].reshape(rounds, rows, heads_here, HEAD_DIM)
    query_float = sorted_query.astype(jnp.float32)
    inverse_norm = lax.rsqrt(jnp.sum(query_float * query_float, -1, keepdims=True) + 1e-06)
    unit_float = query_float * inverse_norm
    unit_low = unit_float.astype(jnp.bfloat16)
    edge = from_behind(
        jnp.concatenate([unit_low[:, -GROUP:], sorted_value[:, -GROUP:]], -1), "seq", 1
    )
    key_unit = with_prior(unit_low, edge[..., :HEAD_DIM])
    key_value = with_prior(sorted_value, edge[..., HEAD_DIM:])
    query_groups = sorted_query.reshape(rounds, blocks, GROUP, heads_here, HEAD_DIM)

    def masked_scores():
        raw = (
            jnp.einsum(
                "rncha,rnkha->rnhck", query_groups, key_unit, preferred_element_type=jnp.float32
            )
            * scale
        )
        return jnp.where(
            itself[:, :, None], own_score, jnp.where(allowed[:, :, None], raw, masked_score)
        )

    scores = masked_scores()
    peak = jnp.max(scores, -1, keepdims=True)
    totals = peak + jnp.log(jnp.sum(jnp.exp(scores - peak), -1, keepdims=True))
    probs_low = jnp.exp(scores - totals).astype(jnp.bfloat16)
    round_out = jnp.einsum(
        "rnhck,rnkha->rncha", probs_low, key_value, preferred_element_type=jnp.float32
    ).astype(jnp.bfloat16)
    out_flat = round_out.reshape(rounds, rows, local_width)
    total_flat = jnp.transpose(totals[..., 0], (0, 1, 3, 2)).reshape(rounds, rows, heads_here)
    token_out = regroup_rows(fill(out_flat, source_block, recv_slot))[
        send_block, round_index, send_slot
    ].astype(jnp.float32)
    token_total = regroup_totals(fill(total_flat, source_block, recv_slot))[
        send_block, round_index, send_slot
    ]
    mix = jax.nn.softmax(token_total, axis=0)
    token_out4 = token_out.reshape(rounds, rows, heads_here, HEAD_DIM)
    attended_low = (
        jnp.sum(mix[..., None] * token_out4, 0).reshape(rows, local_width).astype(jnp.bfloat16)
    )
    sum_one = stream_one.astype(jnp.float32) + branch_sum(
        jnp.dot(attended_low, merge_full, preferred_element_type=jnp.float32)
    )
    normal_two, factor_two, normed_two = norm_forward(sum_one, second_gain, second_bias)
    rows_two = full_rows(normed_two.astype(jnp.bfloat16))
    expand_full, shrink_full = (
        lax.all_gather(expand_weight, "seq", axis=0, tiled=True),
        lax.all_gather(shrink_weight, "seq", axis=1, tiled=True),
    )
    hidden = jnp.dot(rows_two, expand_full, preferred_element_type=jnp.float32)
    active, gelu_pull = jax.vjp(partial(jax.nn.gelu, approximate=False), hidden)
    active_low = active.astype(jnp.bfloat16)
    sum_two = stream_two.astype(jnp.float32) + branch_sum(
        jnp.dot(active_low, shrink_full, preferred_element_type=jnp.float32)
    )
    grad_rows_two = full_rows(grad_two)
    grad_active = jnp.dot(grad_rows_two, shrink_full.T, preferred_element_type=jnp.float32)
    grad_hidden = gelu_pull(grad_active)[0].astype(jnp.bfloat16)
    grad_shrink = jnp.dot(active_low.T, grad_rows_two, preferred_element_type=jnp.float32)
    grad_expand = jnp.dot(rows_two.T, grad_hidden, preferred_element_type=jnp.float32)
    grad_normed_two = branch_sum(
        jnp.dot(grad_hidden, expand_full.T, preferred_element_type=jnp.float32)
    )
    extra_one, grad_second_gain, grad_second_bias = norm_backward(
        grad_normed_two, normal_two, factor_two, second_gain
    )
    total_one = grad_one.astype(jnp.float32) + extra_one
    total_low = total_one.astype(jnp.bfloat16)
    grad_rows_one = full_rows(total_low)
    grad_attended = jnp.dot(grad_rows_one, merge_full.T, preferred_element_type=jnp.float32).astype(
        jnp.bfloat16
    )
    grad_merge = jnp.dot(attended_low.T, grad_rows_one, preferred_element_type=jnp.float32)
    grad_float = grad_attended.astype(jnp.float32).reshape(rows, heads_here, HEAD_DIM)
    dots = jnp.sum(token_out4 * grad_float[None], -1)
    grad_total = mix * (dots - jnp.sum(mix * dots, 0, keepdims=True))
    grad_out_low = (
        (mix[..., None] * grad_float[None]).astype(jnp.bfloat16).reshape(rounds, rows, local_width)
    )
    sorted_grad_out = regroup_rows(fill(grad_out_low, send_block, send_slot))[
        source_block, round_index, recv_slot
    ]
    sorted_grad_total = regroup_totals(fill(grad_total, send_block, send_slot))[
        source_block, round_index, recv_slot
    ]
    grad_groups = sorted_grad_out.reshape(rounds, blocks, GROUP, heads_here, HEAD_DIM)
    total_grad_groups = jnp.transpose(
        sorted_grad_total.reshape(rounds, blocks, GROUP, heads_here), (0, 1, 3, 2)
    )[..., None]
    probs = jnp.exp(masked_scores() - totals)
    probs_again = probs.astype(jnp.bfloat16)
    grad_probs = jnp.einsum(
        "rncha,rnkha->rnhck", grad_groups, key_value, preferred_element_type=jnp.float32
    )
    grad_key_value = jnp.einsum(
        "rnhck,rncha->rnkha", probs_again, grad_groups, preferred_element_type=jnp.float32
    )
    inner = jnp.sum(probs * grad_probs, -1, keepdims=True)
    grad_scores = jnp.where(
        live[:, :, None], probs * (grad_probs - inner + total_grad_groups), 0.0
    ).astype(jnp.bfloat16)
    grad_query_groups = (
        jnp.einsum("rnhck,rnkha->rncha", grad_scores, key_unit, preferred_element_type=jnp.float32)
        * scale
    )
    grad_key_unit = (
        jnp.einsum(
            "rnhck,rncha->rnkha", grad_scores, query_groups, preferred_element_type=jnp.float32
        )
        * scale
    )
    edge_grad = from_behind(
        jnp.concatenate([grad_key_unit[:, 0, GROUP:], grad_key_value[:, 0, GROUP:]], -1).astype(
            jnp.bfloat16
        ),
        "seq",
        -1,
    ).astype(jnp.float32)

    def fold_keys(grad_keys, arriving):
        own = grad_keys[:, :, :GROUP]
        later = jnp.concatenate([grad_keys[:, 1:, GROUP:], arriving[:, None]], 1)
        return (own + later).reshape(rounds, rows, heads_here, HEAD_DIM)

    grad_unit = fold_keys(grad_key_unit, edge_grad[..., :HEAD_DIM])
    grad_sorted_value = fold_keys(grad_key_value, edge_grad[..., HEAD_DIM:])
    grad_sorted_query = grad_query_groups.reshape(
        rounds, rows, heads_here, HEAD_DIM
    ) + inverse_norm * (grad_unit - unit_float * jnp.sum(unit_float * grad_unit, -1, keepdims=True))
    moved_first, moved_second = regroup_pair(
        fill(grad_sorted_query.reshape(rounds, rows, local_width), source_block, recv_slot),
        fill(grad_sorted_value.reshape(rounds, rows, local_width), source_block, recv_slot),
    )
    token_grad_query = moved_first[send_block, round_index, send_slot]
    token_grad_value = moved_second[send_block, round_index, send_slot]
    grad_query_low = jnp.sum(token_grad_query, 0).astype(jnp.bfloat16)
    grad_value_low = jnp.sum(token_grad_value, 0).astype(jnp.bfloat16)
    grad_query_full = jnp.dot(rows_one.T, grad_query_low, preferred_element_type=jnp.float32)
    grad_value_full = jnp.dot(rows_one.T, grad_value_low, preferred_element_type=jnp.float32)
    grad_normed_one = branch_sum(
        jnp.dot(grad_query_low, query_full.T, preferred_element_type=jnp.float32)
        + jnp.dot(grad_value_low, value_full.T, preferred_element_type=jnp.float32)
    )
    extra_two, grad_first_gain, grad_first_bias = norm_backward(
        grad_normed_one, normal_one, factor_one, first_gain
    )
    input_grad_two = (grad_two.astype(jnp.float32) + extra_two).astype(jnp.bfloat16)
    query_part, value_part, merge_part, expand_part, shrink_part = (
        lax.psum_scatter(grad_query_full, "seq", scatter_dimension=0, tiled=True),
        lax.psum_scatter(grad_value_full, "seq", scatter_dimension=0, tiled=True),
        lax.psum_scatter(grad_merge, "seq", scatter_dimension=1, tiled=True),
        lax.psum_scatter(grad_expand, "seq", scatter_dimension=0, tiled=True),
        lax.psum_scatter(grad_shrink, "seq", scatter_dimension=1, tiled=True),
    )
    first_gain_sum, first_bias_sum, second_gain_sum, second_bias_sum = lax.psum(
        (grad_first_gain, grad_first_bias, grad_second_gain, grad_second_bias), "seq"
    )
    return (
        sum_one.astype(jnp.bfloat16),
        sum_two.astype(jnp.bfloat16),
        total_low,
        input_grad_two,
        query_part,
        value_part,
        merge_part,
        expand_part,
        shrink_part,
        first_gain_sum,
        first_bias_sum,
        second_gain_sum,
        second_bias_sum,
    )


def flip(index, bit):
    return index + bit - 2 * bit * ((index // bit) % 2)


def flipped(index, bits):
    for bit in (1, 2, 4):
        if bits & bit:
            index = flip(index, bit)
    return index


class Place:
    def __init__(self):
        self.seq, self.head = lax.axis_index("seq"), lax.axis_index("head")
        self.line, self.side = self.seq // 2, self.seq % 2
        self.pair, self.core = self.head // 2, self.head % 2
        self.turn = self.side * 2 + self.core
        self.home = self.line // 2 == self.core
        self.away = self.line // 2 != self.core

    def peer(self, seq_bits, head_bits=0):
        return (flipped(self.seq, seq_bits), flipped(self.head, head_bits))

    def member(self, bits):
        return self.peer(bits // 2, bits % 2)

    def chunk(self, turn, half):
        return (2 * (turn % 2) + half) * 2 + turn // 2

    def greet(self):
        peers = [self.peer(bits) for bits in range(1, 8)]
        peers += [self.peer(0, bits) for bits in range(1, 4)]
        peers += [self.peer(bits, 1) for bits in (1, 2, 4, 6)]
        barrier = pltpu.get_barrier_semaphore()
        for peer in peers:
            pl.semaphore_signal(barrier, inc=1, device_id=peer, device_id_type=MESH)
        pl.semaphore_wait(barrier, len(peers))


class Copy:
    def __init__(self, copy, starts, lands):
        self.copy, self.starts, self.lands = copy, starts, lands
        self.when(starts, copy.start)

    def when(self, condition, act):
        if condition is None:
            act()
        else:
            pl.when(condition)(act)

    def wait_recv(self):
        self.when(self.lands, self.copy.wait_recv)

    def wait_send(self):
        self.when(self.starts, self.copy.wait_send)


class Wires:
    def __init__(self, send, receive):
        self.send, self.receive, self.copies = send, receive, []

    def push(self, source, target, device, starts=None, lands=None):
        index = len(self.copies)
        copy = pltpu.make_async_remote_copy(
            src_ref=source,
            dst_ref=target,
            send_sem=self.send.at[index],
            recv_sem=self.receive.at[index],
            device_id=device,
            device_id_type=MESH,
        )
        self.copies.append(Copy(copy, starts, lands))
        return self.copies[-1]

    def settle(self, copies):
        for copy in copies:
            copy.wait_send()
        done = [id(copy) for copy in copies]
        self.copies = [None if id(copy) in done else copy for copy in self.copies]

    def drain(self):
        self.settle([copy for copy in self.copies if copy is not None])


class Spread:
    def __init__(self, wires, place):
        self.wires, self.place, self.copies = wires, place, []

    def start(self, source_at, target):
        p = self.place
        for bits, starts in ((4, p.away), (6, p.away), (2, p.home)):
            seq = flipped(p.seq, bits)
            head = p.head - p.core + p.line // 2
            copy = self.wires.push(source_at(seq // 2), target, (seq, head), starts, starts)
            self.copies.append(copy)

    def finish(self):
        for copy in self.copies:
            copy.wait_recv()


class TokenGather:
    def __init__(self, wires, place, everyone, rows):
        self.wires, self.place, self.everyone, self.rows = wires, place, everyone, rows
        self.line = {2: [], 4: [], 6: []}
        self.own = []

    def slot(self, seq, part):
        return columns_at(rows_at(self.everyone, seq, self.rows), part, HEAD_DIM)

    def start(self, packed, part):
        p = self.place
        mine = self.slot(p.seq, part)
        for bits, starts in ((4, p.away), (6, p.away), (2, p.home)):
            seq = flipped(p.seq, bits)
            self.line[bits].append(
                self.wires.push(
                    packed.at[(seq // 2) % 2, part],
                    mine,
                    (seq, p.head - p.core + part),
                    starts,
                    p.core == part,
                )
            )
        source = packed.at[p.line % 2, part]
        self.own.append(self.wires.push(source, mine, p.peer(0, 1), p.home, p.away))

        @pl.when(p.home)
        def _():
            mine[...] = source[...]

    def pass_own(self):
        p = self.place
        for copy in self.own:
            copy.wait_recv()
        block = self.slot(p.seq, p.core)
        self.beside = {0: self.wires.push(block, block, p.peer(1))}
        self.shared = {}

    def forward(self, bits):
        p = self.place
        for copy in self.line[bits]:
            copy.wait_recv()
        block = self.slot(flipped(p.seq, bits), p.core)
        self.beside[bits] = self.wires.push(block, block, p.peer(1))
        self.shared[bits] = self.wires.push(block, block, p.peer(0, 1))

    def share(self, bits):
        p = self.place
        self.beside[bits].wait_recv()
        block = self.slot(flipped(p.seq, bits + 1), p.core)
        self.shared[bits + 1] = self.wires.push(block, block, p.peer(0, 1))

    def land(self, bits):
        self.shared[bits].wait_recv()

    def settle(self):
        lines = [copy for copies in self.line.values() for copy in copies]
        self.wires.settle(lines + self.own + [*self.beside.values(), *self.shared.values()])


class SeqGather:
    def __init__(self, wires, place, slot):
        self.wires, self.place, self.slot = wires, place, slot

    def start(self, source, for_far=None):
        p, mine = self.place, self.slot(self.place.seq)
        far = source if for_far is None else for_far
        self.arriving = {4: self.wires.push(far, mine, p.peer(4))}
        self.arriving[2] = self.wires.push(source, mine, p.peer(2))
        self.beside = {0: self.wires.push(source, mine, p.peer(1))}

    def forward(self, bits):
        p = self.place
        self.arriving[bits].wait_recv()
        block = self.slot(flipped(p.seq, bits))
        if bits == 4:
            self.arriving[6] = self.wires.push(block, block, p.peer(2))
        self.beside[bits] = self.wires.push(block, block, p.peer(1))

    def land(self, bits):
        self.beside[bits].wait_recv()

    def settle(self):
        self.wires.settle([*self.arriving.values(), *self.beside.values()])

    def finish(self):
        for bits in self.beside:
            self.land(bits)
        self.settle()


class PairGather:
    def __init__(self, wires, place, slot, both):
        self.wires, self.place, self.slot, self.both = wires, place, slot, both

    def start(self, source):
        p = self.place
        self.first = self.wires.push(source, self.slot(p.seq), p.peer(1))

    def along(self):
        p = self.place
        self.first.wait_recv()
        pair = self.both(p.seq // 2)
        self.far = self.wires.push(pair, pair, p.peer(4))
        self.near = self.wires.push(pair, pair, p.peer(2))

    def forward(self):
        p = self.place
        self.far.wait_recv()
        pair = self.both(flip(p.seq, 4) // 2)
        self.last = self.wires.push(pair, pair, p.peer(2))

    def finish(self):
        self.near.wait_recv()
        self.last.wait_recv()
        self.wires.settle([self.first, self.far, self.near, self.last])


class HeadGather:
    def __init__(self, wires, place, slot):
        self.wires, self.place, self.slot = wires, place, slot

    def start(self, source):
        p = self.place
        mine = self.slot(p.head)
        self.long = self.wires.push(source, mine, p.peer(0, 2))
        self.short = self.wires.push(source, mine, p.peer(0, 1))

    def relay(self):
        p = self.place
        self.long.wait_recv()
        moved = self.slot(flip(p.head, 2))
        self.last = self.wires.push(moved, moved, p.peer(0, 1))

    def finish(self):
        self.short.wait_recv()
        self.last.wait_recv()
        self.wires.settle([self.long, self.short, self.last])


def columns_at(ref, index, width):
    return ref.at[:, pl.ds(pl.multiple_of(index * width, width), width)]


def rows_at(ref, index, width):
    return ref.at[pl.ds(pl.multiple_of(index * width, width), width)]


def span(index, width):
    return pl.ds(pl.multiple_of(index * width, width), width)


def dot(left, right, contract=((1,), (0,))):
    return lax.dot_general(
        left, right, (contract, ((), ())), preferred_element_type=jnp.float32
    )


def diagonal(size):
    return lax.broadcasted_iota(jnp.int32, (size, size), 0) == lax.broadcasted_iota(
        jnp.int32, (size, size), 1
    )


def to_row(column):
    return jnp.sum(jnp.where(diagonal(column.shape[0]), column, 0.0), 0, keepdims=True)


def to_column(row):
    return jnp.sum(jnp.where(diagonal(row.shape[1]), row, 0.0), 1, keepdims=True)


def in_lanes(total):
    bf16, f32 = jnp.bfloat16, jnp.float32
    high = total.astype(bf16).astype(f32)
    middle = (total - high).astype(bf16).astype(f32)
    low = total - high - middle
    lane = lax.broadcasted_iota(jnp.int32, (total.shape[0], 128), 1)
    parts = jnp.where(lane == 0, high, jnp.where(lane == 1, middle, low))
    return jnp.where(lane < 3, parts, 0.0).astype(bf16)


class SeqScatter:
    def __init__(self, wires, place, piece, pair, line):
        self.wires, self.place, self.piece = wires, place, piece
        self.pair, self.line = pair, line

    def start(self):
        p = self.place
        self.beside = {}
        for bits in (6, 2, 4, 0):
            source = self.piece(flipped(p.seq, bits + 1))
            self.beside[bits] = self.wires.push(source, self.pair.at[bits // 2], p.peer(1))

    def add(self, bits, more=None):
        at, f32 = self.pair.at[bits // 2], jnp.float32
        self.beside[bits].wait_recv()
        mine = self.piece(flipped(self.place.seq, bits))[...]
        total = at[...].astype(f32) + mine.astype(f32)
        if more is not None:
            total += more[...].astype(f32)
        at[...] = total.astype(jnp.bfloat16)
        return at

    def along(self):
        device = self.place.peer(2)
        self.shares = self.wires.push(self.add(6), self.line.at[0], device)
        self.near = self.wires.push(self.add(2), self.line.at[1], device)

    def across(self):
        self.shares.wait_recv()
        total = self.add(4, self.line.at[0])
        self.far = self.wires.push(total, self.line.at[2], self.place.peer(4))

    def finish(self, target):
        p, f32 = self.place, jnp.float32
        self.beside[0].wait_recv()
        total = self.piece(p.seq)[...].astype(f32) + self.pair.at[0][...].astype(f32)
        self.near.wait_recv()
        total += self.line.at[1][...].astype(f32)
        self.far.wait_recv()
        target[...] = total + self.line.at[2][...].astype(f32)


class Phases:
    def __init__(self, r, turns):
        self.r, self.turns = r, turns
        self.place = Place()
        self.wires = Wires(r.send, r.receive)
        self.rows, self.width = r.two.shape
        self.wide = r.rows_one.shape[1]
        self.count = self.wide // self.width
        self.devices = r.everyone.shape[0] // self.rows
        self.pair = self.devices // turns
        self.units = self.devices


    def spread_columns(self, ref, index):
        column = ref[span(index, self.rows), :].astype(jnp.int32)
        lane = lax.broadcasted_iota(jnp.int32, column.shape, 1)
        parts = [
            jnp.where(column == lane + 128 * i, 1.0, 0.0).astype(jnp.bfloat16)
            for i in range(self.rows // 128)
        ]
        return jnp.concatenate(parts, 1)

    def spread_rows(self, ref, index):
        row = ref[index]
        place = lax.broadcasted_iota(jnp.int32, (self.rows, self.rows), 0)
        return jnp.where(row == place, 1.0, 0.0).astype(jnp.bfloat16)

    def from_units(self, ref, table, index):
        first = index * self.units
        return jnp.concatenate([ref[table[first + unit]] for unit in range(self.units)], 0)

    def to_units(self, index, rows):
        first, step = index * self.units, self.rows // self.units
        for unit in range(self.units):
            self.r.mid[first + unit] = rows[unit * step : (unit + 1) * step].astype(jnp.bfloat16)

    def sort_chunk(self, source, index):
        r = self.r
        here = span(index, self.rows)
        self.to_units(index, dot(self.spread_columns(r.chunk_column, index), source[here, :]))

    def sorted_block(self, index):
        r = self.r
        return dot(
            self.spread_columns(r.block_column, index), self.from_units(r.mid, r.units, index)
        )

    def unsort_block(self, source, index):
        r = self.r
        here = span(index, self.rows)
        self.to_units(index, dot(self.spread_rows(r.block_row, index), source[here, :]))

    def unsorted_chunk(self, index):
        r = self.r
        return dot(
            self.spread_rows(r.chunk_row, index), self.from_units(r.mid, r.units_back, index)
        )

    def column_of(self, row):
        pieces = [to_column(row[:, i : i + 128]) for i in range(0, self.rows, 128)]
        return jnp.concatenate(pieces, 0)

    def row_of(self, column):
        pieces = [to_row(column[i : i + 128]) for i in range(0, self.rows, 128)]
        return jnp.concatenate(pieces, 1)

    def wide_column(self, column):
        return jnp.broadcast_to(column, (self.rows, 128)).astype(jnp.int32).astype(jnp.int16)

    def bucket_tables(self):
        r = self.r
        f32, i32 = jnp.float32, jnp.int32
        rows = self.rows
        most = -(-(self.devices * (rows // GROUP + 1) + 1) // 128) * 128

        value = lax.broadcasted_iota(i32, (most, rows), 0)

        def count(block, until):
            return until + jnp.sum(
                jnp.where(r.bucket[block] <= value, 1.0, 0.0), 1, keepdims=True
            )

        until = lax.fori_loop(0, self.devices, count, jnp.zeros((most, 1), f32))
        r.until[...] = jnp.broadcast_to(until, (most, 128))

    def block_tables(self, start, stop):
        r = self.r
        bf16, f32, i32 = jnp.bfloat16, jnp.float32, jnp.int32
        rows, lines = self.rows, self.rows // 128
        tokens = rows * self.devices

        def first(block, carry):
            order = r.order[block]
            until = r.until[:, 0:1].astype(i32)
            lane = lax.broadcasted_iota(i32, (1, rows), 1)
            bucket = jnp.sum(
                jnp.where(until <= lane + block * rows, 1.0, 0.0), 0, keepdims=True
            )
            key = bucket * tokens + order.astype(f32)
            for i in range(lines):
                r.keys[block * lines + i] = key[:, i * 128 : (i + 1) * 128]
            chunk = order // rows
            place = (chunk * rows + lane).astype(f32)
            slot = jnp.sum(jnp.where(place < self.column_of(place), 1.0, 0.0), 1, keepdims=True)
            r.block_column[span(block, rows), :] = self.wide_column(slot)
            r.block_row[block] = self.row_of(slot).astype(i32)
            local = self.column_of((order - chunk * rows).astype(f32))
            high = jnp.floor(local * 0.0625)
            at = lax.broadcasted_iota(i32, (rows, 2 * HEAD_DIM), 1)
            parts = jnp.where(at == 0, high, jnp.where(at == 1, local - 16.0 * high, 0.0))
            r.round_rows[span(block, rows), :] = parts.astype(bf16)
            self.unsort_block(r.round_rows, block)
            return carry

        lax.fori_loop(start, stop, first, 0)

    def chunk_tables(self):
        r = self.r
        f32, i32 = jnp.float32, jnp.int32
        rows = self.rows

        def second(chunk, carry):
            parts = self.from_units(r.mid, r.units_back, chunk)[:, 0:128].astype(f32)
            token = 16.0 * parts[:, 0:1] + parts[:, 1:2]
            r.chunk_column[span(chunk, rows), :] = self.wide_column(token)
            r.chunk_row[chunk] = self.row_of(token).astype(i32)
            return carry

        lax.fori_loop(0, self.devices, second, 0)

    def codes(self, index):
        r = self.r
        tokens = self.rows * self.devices
        groups = tokens // 128
        low = lax.broadcasted_iota(jnp.int32, (1, 128), 1) < GROUP
        result = []
        for i in range(2):
            here = 2 * index + i
            keys, before = r.keys[here], r.keys[(here + groups - 1) % groups]
            query = to_column(keys)
            least = jnp.floor(query * (1.0 / tokens)) * tokens
            for half, window in enumerate((jnp.where(low, keys, before), keys)):
                at = slice(half * GROUP, (half + 1) * GROUP)
                allowed = (window <= query[at]) & (window >= least[at])
                result.append(
                    jnp.where(window == query[at], 1.0, jnp.where(allowed, 0.0, 2.0))
                )
        return jnp.concatenate(result, 0)

    def window(self, rows, block):
        before = rows[block * GROUP : (block + 1) * GROUP]
        own = rows[(block + 1) * GROUP : (block + 2) * GROUP]
        return jnp.concatenate([own, before] if block % 2 == 0 else [before, own], 0)

    def over_rows(self, ref):
        step = ref.shape[0] // self.devices
        return SeqGather(self.wires, self.place, lambda seq: rows_at(ref, seq, step))

    def over_columns(self, ref):
        step = ref.shape[1] // self.devices
        return SeqGather(self.wires, self.place, lambda seq: columns_at(ref, seq, step))

    def start_seq(self, gather, source):
        gather.start(source)
        gather.slot(self.place.seq)[...] = source[...]

    def start_head(self, gather, source):
        gather.start(source)
        gather.slot(self.place.head)[...] = source[...]

    def over_head(self, ref):
        return HeadGather(self.wires, self.place, lambda head: columns_at(ref, head, self.width))

    def project(self):
        r, place, wires = self.r, self.place, self.wires
        bf16, f32 = jnp.bfloat16, jnp.float32
        stream = self.over_head(r.two_full)
        small = self.over_head(r.params_full)
        self.start_head(stream, r.two)
        for row, item in enumerate((r.gain_one, r.bias_one, r.gain_two, r.bias_two)):
            r.params[row : row + 1, :] = item[...]
        r.params[4:8, :] = jnp.zeros((4, self.width), f32)
        self.start_head(small, r.params)
        query, value = self.over_rows(r.query_full), self.over_rows(r.value_full)
        self.start_seq(query, r.query)
        self.start_seq(value, r.value)
        self.bulk()
        self.begin(self.expand[0])
        self.bucket_tables()
        for weight in (query, value):
            for bits in (4, 2):
                weight.forward(bits)
        small.relay()
        stream.relay()
        query.forward(6)
        value.forward(6)
        small.finish()
        stream.finish()

        def normalise(tile, carry):
            here = span(tile, 128)
            rows = r.two_full[here, :].astype(f32)
            center = jnp.mean(rows, 1, keepdims=True)
            offset = rows - center
            factor = lax.rsqrt(jnp.mean(offset * offset, 1, keepdims=True) + 1e-05)
            r.center_one[here, :] = jnp.broadcast_to(center, (128, 128))
            r.factor_one[here, :] = jnp.broadcast_to(factor, (128, 128))
            r.rows_one[here, :] = (
                offset * factor * r.params_full[0:1, :] + r.params_full[1:2, :]
            ).astype(bf16)
            return carry

        lax.fori_loop(0, self.rows // 128, normalise, 0)
        self.tokens = TokenGather(self.wires, place, r.everyone, self.rows)
        self.project_one(query, r.query_full, 0)
        self.project_one(value, r.value_full, 1)
        self.begin(self.merge)

    def project_one(self, weight, full, part):
        r = self.r
        weight.finish()

        def multiply(tile, carry):
            here = span(tile, 256)
            result = dot(r.rows_one[here, :], full[...]).astype(jnp.bfloat16)
            for which in range(self.pair):
                r.packed[which, part, here, :] = result[
                    :, which * HEAD_DIM : (which + 1) * HEAD_DIM
                ]
            return carry

        lax.fori_loop(0, self.rows // 256, multiply, 0)
        self.tokens.start(r.packed, part)

    def bulk(self):
        r, place = self.r, self.place
        my_rows = rows_at(r.merge_full, place.head, r.merge.shape[0])
        self.merge = SeqGather(
            self.wires, place, lambda seq: columns_at(my_rows, seq, r.merge.shape[1])
        )
        self.merge.source = r.merge
        self.expand, self.shrink = [], []
        for part in range(2):
            step, columns = r.expand.shape[0], r.expand.shape[1] // 2
            cut = pl.ds(part * columns, columns)
            slot = lambda seq, cut=cut: rows_at(r.expand_full, seq, step).at[:, cut]
            if part:
                gather = SeqGather(self.wires, place, slot)
            else:
                both = lambda pair: rows_at(r.expand_full, pair, 2 * step).at[:, 0:columns]
                gather = PairGather(self.wires, place, slot, both)
            gather.source = r.expand.at[:, cut]
            self.expand.append(gather)
            rows, width = r.shrink.shape[0] // 2, r.shrink.shape[1]
            down = pl.ds(part * rows, rows)
            gather = SeqGather(
                self.wires,
                place,
                lambda seq, down=down: columns_at(r.shrink_full.at[down], seq, width),
            )
            gather.source = r.shrink.at[down]
            self.shrink.append(gather)
        self.one, self.grads = self.over_head(r.one_full), self.over_head(r.grad_full)

    def begin(self, gather):
        self.start_seq(gather, gather.source)

    def go_on(self, gather):
        for bits in (4, 2, 6):
            gather.forward(bits)

    def begin_streams(self):
        self.start_head(self.one, self.r.one)
        self.start_head(self.grads, self.r.grad_two)

    def begin_merge_rows(self):
        r, place = self.r, self.place
        self.merge.finish()
        self.heads = HeadGather(
            self.wires, place, lambda head: rows_at(r.merge_full, head, r.merge.shape[0])
        )
        self.heads.start(self.heads.slot(place.head))

    def sort_tokens(self):
        r, place = self.r, self.place
        bf16, f32 = jnp.bfloat16, jnp.float32
        tokens = self.tokens
        half = self.devices // 2
        self.block_tables(0, half)
        tokens.pass_own()
        self.block_tables(half, self.devices)
        for bits in (2, 4, 6):
            tokens.forward(bits)
        self.expand[0].along()
        self.begin_streams()
        self.begin(self.expand[1])
        self.chunk_tables()
        self.sort_chunk(r.everyone, place.seq)
        for bits in (2, 4, 6):
            tokens.land(bits)
            self.sort_chunk(r.everyone, flipped(place.seq, bits))
        for bits in (0, 2, 4, 6):
            tokens.share(bits)
        for bits in (0, 2, 4, 6):
            tokens.land(bits + 1)
            self.sort_chunk(r.everyone, flipped(place.seq, bits + 1))
        tokens.settle()

        def second(block, carry):
            rows = self.sorted_block(block)
            here = span(block, self.rows)
            later = pl.ds(pl.multiple_of(block * self.rows + GROUP, GROUP), self.rows)
            query = rows[:, :HEAD_DIM]
            r.sorted_query[here, :] = query.astype(bf16)
            factor = lax.rsqrt(jnp.sum(query * query, 1, keepdims=True) + 1e-06)
            r.unit[later, :] = (query * factor).astype(bf16)
            r.key_value[later, :] = rows[:, HEAD_DIM:].astype(bf16)
            return carry

        lax.fori_loop(0, self.devices, second, 0)
        last = pl.ds(self.devices * self.rows, GROUP)
        r.unit[0:GROUP, :] = r.unit[last, :]
        r.key_value[0:GROUP, :] = r.key_value[last, :]

    def attend(self):
        r = self.r
        bf16, f32 = jnp.bfloat16, jnp.float32
        scale = HEAD_DIM ** (-0.5)
        some = 4 * GROUP

        def group(index, carry):
            here = span(index, some)
            longer = pl.ds(pl.multiple_of(index * some, some), some + GROUP)
            query, unit, value = r.sorted_query[here, :], r.unit[longer, :], r.key_value[longer, :]
            raw = [
                dot(query[i * GROUP : (i + 1) * GROUP], self.window(unit, i), ((1,), (1,)))
                for i in range(4)
            ]
            code = self.codes(index)
            scores = jnp.where(
                code == 0.0,
                jnp.concatenate(raw, 0) * scale,
                jnp.where(code == 1.0, own_score, masked_score),
            )
            peak = jnp.max(scores, 1, keepdims=True)
            power = jnp.exp(scores - peak)
            total = jnp.sum(power, 1, keepdims=True)
            probs = power * (1.0 / total)
            r.probs[here, :] = probs
            probs = probs.astype(bf16)
            result = [
                dot(probs[i * GROUP : (i + 1) * GROUP], self.window(value, i)) for i in range(4)
            ]
            r.round_rows[here, :HEAD_DIM] = jnp.concatenate(result, 0).astype(bf16)
            r.round_rows[here, HEAD_DIM:] = in_lanes(peak + jnp.log(total))
            return carry

        lax.fori_loop(0, self.devices * self.rows // some, group, 0)

    def return_rows(self):
        r, place, wires = self.r, self.place, self.wires
        bf16, f32 = jnp.bfloat16, jnp.float32

        def first(block, carry):
            self.unsort_block(r.round_rows, block)
            return carry

        lax.fori_loop(0, self.devices, first, 0)
        coming = []
        for half in range(self.pair):
            arriving = []
            for bits in (3, 2, 1, 0):
                turn = flipped(place.turn, bits)
                rows = self.unsorted_chunk(place.chunk(turn, half))
                total = jnp.sum(rows[:, HEAD_DIM:], 1, keepdims=True)
                lines = [to_row(total[i : i + 128]) for i in range(0, self.rows, 128)]
                total = jnp.concatenate(lines, 0)
                rows = rows[:, :HEAD_DIM].astype(bf16)
                if not bits:
                    r.outs[place.turn, half] = rows
                    r.totals[place.turn, half] = total
                    continue
                r.out_send[bits - 1, half] = rows
                r.total_send[bits - 1, half] = total
                for source, target in ((r.total_send, r.totals), (r.out_send, r.outs)):
                    arriving.append(
                        wires.push(
                            source.at[bits - 1, half],
                            target.at[place.turn, half],
                            place.member(bits),
                        )
                    )
            coming.append(arriving)
        self.rounds_coming = coming

    def mix_half(self, half):
        r = self.r
        bf16, f32 = jnp.bfloat16, jnp.float32
        totals = [r.totals[turn, half] for turn in range(self.turns)]
        peak = totals[0]
        for total in totals[1:]:
            peak = jnp.maximum(peak, total)
        power = [jnp.exp(total - peak) for total in totals]
        whole = sum(power[1:], power[0])
        for turn in range(self.turns):
            r.mix_rows[turn, half] = power[turn] / whole

        def combine(part, carry):
            here = span(part, 128)
            attended = jnp.zeros((128, HEAD_DIM), f32)
            for turn in range(self.turns):
                mix = to_column(r.mix_rows[turn, half, pl.ds(part, 1), :])
                mix = jnp.broadcast_to(mix, (128, HEAD_DIM))
                r.mix[turn, half, here, :] = mix
                attended += mix * r.outs[turn, half, here, :].astype(f32)
            r.attended[half, here, :] = attended.astype(bf16)
            return carry

        lax.fori_loop(0, self.rows // 128, combine, 0)

    def mix_rounds(self):
        r, place, wires = self.r, self.place, self.wires

        for half in range(self.pair):
            for copy in self.rounds_coming[half]:
                copy.wait_recv()
            self.mix_half(half)
        mine = columns_at(r.attended_full, place.pair * 4 + place.line, HEAD_DIM)
        back = Spread(wires, place)
        back.start(lambda line: r.attended.at[line % 2], mine)

        @pl.when(place.home)
        def _():
            mine[...] = r.attended[place.line % 2]

        back.finish()
        gather = self.over_head(r.attended_full)
        gather.start(gather.slot(place.head))
        gather.relay()
        gather.finish()
        wires.settle([copy for arriving in self.rounds_coming for copy in arriving])


    def normalise_sum(self):
        r, place = self.r, self.place
        bf16, f32 = jnp.bfloat16, jnp.float32
        tile_rows = self.rows // 2
        for tile in range(2):
            here = pl.ds(tile * tile_rows, tile_rows)
            total = r.one_full[here, :].astype(f32) + dot(r.attended_full[here, :], r.merge_full[...])
            center = jnp.mean(total, 1, keepdims=True)
            offset = total - center
            factor = lax.rsqrt(jnp.mean(offset * offset, 1, keepdims=True) + 1e-05)
            normal = offset * factor
            r.tall[here, :] = total
            mine = columns_at(r.tall.at[here], place.head, self.width)
            r.result_one[here, :] = mine[...].astype(bf16)
            r.tall[here, :] = normal
            r.normal_two[here, :] = mine[...]
            r.factor_two[here, :] = jnp.broadcast_to(factor, (tile_rows, 128))
            r.rows_two[here, :] = (normal * r.params_full[2:3, :] + r.params_full[3:4, :]).astype(
                bf16
            )

    def feed_half(self, half, tile):
        r = self.r
        bf16 = jnp.bfloat16
        tile_rows, step = self.rows // 2, r.active.shape[1] // 2
        here, units = pl.ds(tile * tile_rows, tile_rows), pl.ds(half * step, step)
        hidden = dot(r.rows_two[here, :], r.expand_full[:, units])
        below = 0.5 * (1.0 + lax.erf(hidden * (0.5**0.5)))
        r.active[here, units] = (hidden * below).astype(bf16)
        slope = below + hidden * jnp.exp(-0.5 * hidden * hidden) * ((2.0 * jnp.pi) ** -0.5)
        grad = dot(r.grad_full[here, :], r.shrink_full[units, :], ((1,), (1,)))
        r.grad_hidden[here, units] = (grad * slope).astype(bf16)

    def shrink_grads(self, half):
        r = self.r
        step = r.active.shape[1] // 2
        units = pl.ds(half * step, step)
        self.weights(r.active.at[:, units], r.grad_full, r.grad_shrink.at[units])
        width = r.shrink.shape[1]
        scatter = SeqScatter(
            self.wires, self.place,
            lambda seq: columns_at(r.grad_shrink.at[units], seq, width),
            r.shrink_pair.at[:, units], r.shrink_line.at[:, units],
        )
        scatter.start()
        self.shrink_out.append(scatter)

    def feed_forward(self):
        r, place, wires = self.r, self.place, self.wires
        self.parts_two, self.shrink_out = [], []
        tile_rows = self.rows // 2
        self.normalise_sum()
        self.expand[0].finish()
        self.shrink[0].finish()
        for tile in range(2):
            self.feed_half(0, tile)
        self.shrink_grads(0)
        self.expand[1].finish()
        self.shrink[1].finish()
        for tile in range(2):
            here = pl.ds(tile * tile_rows, tile_rows)
            self.feed_half(1, tile)
            part = dot(r.grad_hidden[here, :], r.expand_full[...], ((1,), (1,)))
            self.send_part(
                tile, part, r.tall[here, :], r.params_full[2:3, :], r.part_two, r.stat_two,
                r.parts_two, self.parts_two,
            )
        for tile in range(2):
            self.relay_part(tile, r.part_two, r.parts_two, self.parts_two)
        self.send_stats(r.stat_two, r.stats_two, self.parts_two)
        self.shrink_grads(1)

    def send_part(self, tile, part, normal, gain, part_ref, stat_ref, target, copies):
        tile_rows = part.shape[0]
        here = pl.ds(tile * tile_rows, tile_rows)
        scaled = part * gain
        first = jnp.sum(scaled, 1, keepdims=True)
        second = jnp.sum(scaled * normal, 1, keepdims=True)
        lines = tile_rows // 128
        for line in range(lines):
            at = slice(line * 128, (line + 1) * 128)
            row = tile * lines + line
            stat_ref[row : row + 1, :] = to_row(first[at])
            row += self.rows // 128
            stat_ref[row : row + 1, :] = to_row(second[at])
        part_ref[here, :] = part.astype(jnp.bfloat16)
        twin = self.place.peer(0, 1)
        for slot, head in ((1, flip(twin[1], 2)), (0, twin[1])):
            source = columns_at(part_ref.at[here], head, self.width)
            copies.append(self.wires.push(source, target.at[slot, here], twin))

    def relay_part(self, tile, part_ref, target, copies):
        tile_rows = self.rows // 2
        here = pl.ds(tile * tile_rows, tile_rows)
        far = self.place.peer(0, 2)
        copies[2 * tile].wait_recv()
        mine = columns_at(part_ref.at[here], far[1], self.width)[...].astype(jnp.float32)
        total = mine + target[1, here, :].astype(jnp.float32)
        target[1, here, :] = total.astype(jnp.bfloat16)
        copies.append(self.wires.push(target.at[1, here], target.at[2, here], far))

    def send_stats(self, stat_ref, target, copies):
        for bits in (2, 3, 1):
            device = self.place.peer(0, bits)
            copies.append(self.wires.push(stat_ref, target.at[bits - 1], device))

    def norm_back(self, part_ref, parts, stat_ref, stats, normal_at, factor_ref, gain, finish):
        f32 = jnp.float32
        lines = self.rows // 128

        def piece(line, carry):
            here = span(line, 128)
            grad = columns_at(part_ref.at[here], self.place.head, self.width)[...].astype(f32)
            first, second = stat_ref[pl.ds(line, 1), :], stat_ref[pl.ds(line + lines, 1), :]
            for other in range(3):
                if other != 1:
                    grad += parts[other, here, :].astype(f32)
                first += stats[other, pl.ds(line, 1), :]
                second += stats[other, pl.ds(line + lines, 1), :]
            normal = normal_at(here)
            first, second = to_column(first) / self.wide, to_column(second) / self.wide
            finish(here, factor_ref[here, 0:1] * (grad * gain - first - normal * second))
            gains, biases = carry
            return (
                gains + jnp.sum(grad * normal, 0, keepdims=True),
                biases + jnp.sum(grad, 0, keepdims=True),
            )

        zero = jnp.zeros((1, self.width), f32)
        return lax.fori_loop(0, lines, piece, (zero, zero))

    def my_params(self, row):
        return columns_at(self.r.params_full, self.place.head, self.width)[row : row + 1, :]

    def feed_back(self):
        r, place, wires = self.r, self.place, self.wires
        bf16, f32 = jnp.bfloat16, jnp.float32
        self.weights(r.rows_two, r.grad_hidden, r.grad_expand)
        self.expand_out = SeqScatter(
            wires, place, lambda seq: rows_at(r.grad_expand, seq, r.expand.shape[0]),
            r.expand_pair, r.expand_line,
        )
        self.expand_out.start()
        for copy in self.parts_two[1:2] + self.parts_two[3:]:
            copy.wait_recv()
        wires.settle(self.parts_two)

        def finish(here, change):
            total = r.grad_one[here, :].astype(f32) + change
            r.input_grad_one[here, :] = total.astype(bf16)

        gains, biases = self.norm_back(
            r.part_two, r.parts_two, r.stat_two, r.stats_two,
            lambda here: r.normal_two[here, :], r.factor_two, self.my_params(2), finish,
        )
        r.norm_send[2:3, :], r.norm_send[3:4, :] = gains, biases
        gather = self.over_head(r.grad_rows_one)
        self.start_head(gather, r.input_grad_one)
        gather.relay()

        def feed(tile, carry):
            here = span(tile, 256)
            r.feed[here, :] = dot(r.active[here, :], r.shrink_full[...]).astype(bf16)
            return carry

        lax.fori_loop(0, self.rows // 256, feed, 0)
        gather.finish()

    def weights(self, left, right, target):
        step = min(256, left.shape[1])

        def piece(index, carry):
            columns = span(index, step)
            result = dot(left[:, columns], right[...], ((0,), (0,)))
            target[columns, :] = result.astype(jnp.bfloat16)
            return carry

        lax.fori_loop(0, left.shape[1] // step, piece, 0)

    def send_feed(self):
        r = self.r
        self.feeds = []
        for bits in (2, 3, 1):
            device = self.place.peer(0, bits)
            source = columns_at(r.feed, device[1], self.width)
            self.feeds.append(self.wires.push(source, r.feeds.at[bits - 1], device))

    def finish_feed(self):
        r = self.r
        f32 = jnp.float32
        for copy in self.feeds:
            copy.wait_recv()
        total = r.two[...].astype(f32)
        total += columns_at(r.feed, self.place.head, self.width)[...].astype(f32)
        for other in range(3):
            total += r.feeds[other].astype(f32)
        r.result_two[...] = total.astype(jnp.bfloat16)


    def grad_rounds(self):
        r, place, wires = self.r, self.place, self.wires
        bf16, f32 = jnp.bfloat16, jnp.float32
        my_rows = rows_at(r.merge_full, place.head, r.merge.shape[0])

        def attended(tile, carry):
            here = span(tile, 256)
            grad = dot(r.grad_rows_one[here, :], my_rows[...], ((1,), (1,))).astype(bf16)
            for which in range(self.pair):
                r.grad_heads[which, here, :] = grad[:, which * HEAD_DIM : (which + 1) * HEAD_DIM]
            return carry

        lax.fori_loop(0, self.rows // 256, attended, 0)
        mine = r.grad_attended.at[place.line % 2]
        there = Spread(wires, place)
        there.start(lambda line: r.grad_heads.at[line % 2], mine)

        @pl.when(place.home)
        def _():
            mine[...] = r.grad_heads[place.line % 2]

        lines = self.rows // 128

        def spread(half, carry):
            def piece(part, carry):
                here = span(part, 128)
                grad = r.grad_attended[half, here, :].astype(f32)
                turns = [flipped(place.turn, bits) for bits in range(self.turns)]
                mixes = [r.mix[turn, half, here, :] for turn in turns]
                dots = [
                    jnp.sum(r.outs[turn, half, here, :].astype(f32) * grad, 1, keepdims=True)
                    for turn in turns
                ]
                mean = sum(mix[:, 0:1] * value for mix, value in zip(mixes, dots))
                for bits in range(self.turns):
                    change = to_row(mixes[bits][:, 0:1] * (dots[bits] - mean))
                    rows = (mixes[bits] * grad).astype(bf16)
                    if bits:
                        r.grad_send[bits - 1, half, here, :] = rows
                        r.grad_total_send[bits - 1, half, pl.ds(part, 1), :] = change
                    else:
                        r.grad_outs[place.turn, half, here, :] = rows
                        r.grad_totals[place.turn, half, pl.ds(part, 1), :] = change
                return carry

            return lax.fori_loop(0, lines, piece, carry)

        self.grads_coming = {bits: [] for bits in (3, 1, 2)}

        def send(half):
            for bits in (3, 1, 2):
                for source, target in (
                    (r.grad_total_send, r.grad_totals),
                    (r.grad_send, r.grad_outs),
                ):
                    self.grads_coming[bits].append(
                        wires.push(
                            source.at[bits - 1, half],
                            target.at[place.turn, half],
                            place.member(bits),
                        )
                    )

        for scatter in self.shrink_out:
            scatter.along()
        self.weights(columns_at(r.attended_full, place.head, self.width), r.grad_rows_one, r.grad_merge)
        there.finish()
        for half in range(self.pair):
            spread(half, 0)
            send(half)
        self.merge_out = SeqScatter(
            wires, place, lambda seq: columns_at(r.grad_merge, seq, r.merge.shape[1]),
            r.merge_pair, r.merge_line,
        )

    def sort_grads(self):
        r, place = self.r, self.place
        bf16 = jnp.bfloat16
        lines = self.rows // 128
        for bits in (0, 1, 2, 3):
            turn = flipped(place.turn, bits)
            if bits:
                for copy in self.grads_coming[bits]:
                    copy.wait_recv()

            def stage(half, carry, turn=turn):
                chunk = self.place.chunk(turn, half)
                r.everyone[span(chunk, self.rows), :HEAD_DIM] = r.grad_outs[turn, half]

                def piece(part, carry):
                    total = to_column(r.grad_totals[turn, half, pl.ds(part, 1), :])
                    r.everyone[span(chunk * lines + part, 128), HEAD_DIM:] = in_lanes(total)
                    return carry

                lax.fori_loop(0, lines, piece, 0)
                self.sort_chunk(r.everyone, chunk)
                return carry

            lax.fori_loop(0, self.pair, stage, 0)
        self.merge_out.start()
        for scatter in self.shrink_out:
            scatter.across()

        def second(block, carry):
            r.round_rows[span(block, self.rows), :] = self.sorted_block(block).astype(bf16)
            return carry

        lax.fori_loop(0, self.devices, second, 0)

    def attend_back(self):
        r = self.r
        bf16, f32 = jnp.bfloat16, jnp.float32
        scale = HEAD_DIM ** (-0.5)
        some = 4 * GROUP
        r.grad_unit[0:GROUP, :] = jnp.zeros((GROUP, HEAD_DIM), f32)
        r.grad_value[0:GROUP, :] = jnp.zeros((GROUP, HEAD_DIM), f32)

        def one(rows, block):
            return rows[block * GROUP : (block + 1) * GROUP]

        def fold(pieces):
            owns = [piece[:GROUP] if i % 2 == 0 else piece[GROUP:] for i, piece in enumerate(pieces)]
            befores = [piece[GROUP:] if i % 2 == 0 else piece[:GROUP] for i, piece in enumerate(pieces)]
            middle = [owns[i] + befores[i + 1] for i in range(3)]
            return befores[0], jnp.concatenate(middle + [owns[3]], 0)

        def group(index, carry):
            here = span(index, some)
            longer = pl.ds(pl.multiple_of(index * some, some), some + GROUP)
            before = pl.ds(pl.multiple_of(index * some, some), GROUP)
            after = pl.ds(pl.multiple_of(index * some + GROUP, GROUP), some)
            query, unit, value = r.sorted_query[here, :], r.unit[longer, :], r.key_value[longer, :]
            grad = r.round_rows[here, :HEAD_DIM]
            total = jnp.sum(r.round_rows[here, HEAD_DIM:].astype(f32), 1, keepdims=True)
            probs = r.probs[here, :]
            low = probs.astype(bf16)
            live = jnp.where(self.codes(index) == 0.0, probs, 0.0)
            grad_probs = jnp.concatenate(
                [dot(one(grad, i), self.window(value, i), ((1,), (1,))) for i in range(4)], 0
            )
            inner = jnp.sum(probs * grad_probs, 1, keepdims=True)
            scores = (live * (grad_probs - inner + total)).astype(bf16)
            r.probs[here, :] = (
                jnp.concatenate([dot(one(scores, i), self.window(unit, i)) for i in range(4)], 0) * scale
            )
            for target, left, right, factor in (
                (r.grad_unit, scores, query, scale),
                (r.grad_value, low, grad, 1.0),
            ):
                first, rest = fold(
                    [dot(one(left, i), one(right, i), ((0,), (0,))) * factor for i in range(4)]
                )
                target[before, :] += first
                target[after, :] = rest
            return carry

        lax.fori_loop(0, self.devices * self.rows // some, group, 0)
        last = pl.ds(self.devices * self.rows, GROUP)
        r.grad_unit[last, :] += r.grad_unit[0:GROUP, :]
        r.grad_value[last, :] += r.grad_value[0:GROUP, :]

        def whole(index, carry):
            here = span(index, some)
            after = pl.ds(pl.multiple_of(index * some + GROUP, GROUP), some)
            query = r.sorted_query[here, :].astype(f32)
            factor = lax.rsqrt(jnp.sum(query * query, 1, keepdims=True) + 1e-06)
            unit = query * factor
            grad = r.grad_unit[after, :]
            along = jnp.sum(unit * grad, 1, keepdims=True)
            grad = r.probs[here, :] + factor * (grad - unit * along)
            r.round_rows[here, :HEAD_DIM] = grad.astype(bf16)
            r.round_rows[here, HEAD_DIM:] = r.grad_value[after, :].astype(bf16)
            return carry

        lax.fori_loop(0, self.devices * self.rows // some, whole, 0)

    def return_grads(self):
        r, place, wires = self.r, self.place, self.wires
        bf16, f32 = jnp.bfloat16, jnp.float32

        def first(block, carry):
            self.unsort_block(r.round_rows, block)
            return carry

        lax.fori_loop(0, self.devices, first, 0)
        self.backs = {}

        def rows_for(bits, half):
            return self.unsorted_chunk(place.chunk(flipped(place.turn, bits), half)).astype(bf16)

        def block(slot, half):
            return pl.ds((slot * 2 + half) * self.rows, self.rows)

        for bits in (3, 1, 2, 0):
            for half in range(self.pair):
                r.everyone[block(bits, half), :] = rows_for(bits, half)
        parts = {part: pl.ds(part * HEAD_DIM, HEAD_DIM) for part in (1, 0)}
        both = self.pair * self.rows
        shares, sides = {}, {}
        for part, columns in parts.items():
            for bits in (3, 1):
                source = r.everyone.at[pl.ds(bits * both, both), columns]
                shares[part, bits] = wires.push(
                    source, r.grad_pairs.at[bits // 2, :, columns], place.peer(0, 1)
                )
        for part, columns in parts.items():
            shares[part, 3].wait_recv()
            total = r.everyone[pl.ds(2 * both, both), columns].astype(f32)
            total += r.grad_pairs[1, :, columns].astype(f32)
            r.grad_pairs[1, :, columns] = total.astype(bf16)
            sides[part] = wires.push(
                r.grad_pairs.at[1, :, columns], r.grad_pairs.at[2, :, columns], place.peer(1)
            )
        for part, columns in parts.items():
            shares[part, 1].wait_recv()
            sides[part].wait_recv()
            for half in range(self.pair):
                rows = pl.ds(half * self.rows, self.rows)
                total = r.everyone[block(0, half), columns].astype(f32)
                total += r.grad_pairs[0, rows, columns].astype(f32)
                total += r.grad_pairs[2, rows, columns].astype(f32)
                r.grad_pair[part, half] = total.astype(bf16)
            target = r.grad_key if part else r.grad_query
            mine = columns_at(target, place.line % 2, HEAD_DIM)
            back = Spread(wires, place)
            back.start(lambda line, part=part: r.grad_pair.at[part, line % 2], mine)
            pl.when(place.home)(partial(self.keep_grad, mine, part))
            self.backs[part] = back
        self.backs[1].finish()
        self.value_weights()
        self.backs[0].finish()

    def keep_grad(self, mine, part):
        mine[...] = self.r.grad_pair[part, self.place.line % 2]

    def value_weights(self):
        r = self.r
        self.weights(r.rows_one, r.grad_key, r.grad_value_full)
        self.value_out = SeqScatter(
            self.wires, self.place,
            lambda seq: rows_at(r.grad_value_full, seq, r.value.shape[0]),
            r.value_pair, r.value_line,
        )
        self.value_out.start()

    def project_back(self):
        r, place, wires = self.r, self.place, self.wires
        bf16, f32 = jnp.bfloat16, jnp.float32
        self.weights(r.rows_one, r.grad_query, r.grad_query_full)
        self.query_out = SeqScatter(
            wires, place, lambda seq: rows_at(r.grad_query_full, seq, r.query.shape[0]),
            r.query_pair, r.query_line,
        )
        self.query_out.start()
        copies = []
        tile_rows = self.rows // 2
        for tile in range(2):
            here = pl.ds(tile * tile_rows, tile_rows)
            part = dot(r.grad_query[here, :], r.query_full[...], ((1,), (1,)))
            part += dot(r.grad_key[here, :], r.value_full[...], ((1,), (1,)))
            normal = (r.two_full[here, :].astype(f32) - r.center_one[here, 0:1]) * r.factor_one[
                here, 0:1
            ]
            self.send_part(
                tile, part, normal, r.params_full[0:1, :], r.part_one, r.stat_one,
                r.parts_one, copies,
            )
        for tile in range(2):
            self.relay_part(tile, r.part_one, r.parts_one, copies)
        self.send_stats(r.stat_one, r.stats_one, copies)
        self.value_out.along()
        self.query_out.along()
        for copy in copies[1:2] + copies[3:]:
            copy.wait_recv()

        def normal_at(here):
            rows = columns_at(r.two_full.at[here], place.head, self.width)[...].astype(f32)
            return (rows - r.center_one[here, 0:1]) * r.factor_one[here, 0:1]

        def finish(here, change):
            total = r.grad_two[here, :].astype(f32) + change
            r.input_grad_two[here, :] = total.astype(bf16)

        gains, biases = self.norm_back(
            r.part_one, r.parts_one, r.stat_one, r.stats_one, normal_at, r.factor_one,
            self.my_params(0), finish,
        )
        r.norm_send[0:1, :], r.norm_send[1:2, :] = gains, biases
        norms = [
            wires.push(r.norm_send, r.norms.at[bits - 1], place.peer(bits)) for bits in range(1, 8)
        ]
        self.value_out.across()
        self.query_out.across()
        self.expand_out.finish(r.expand_part)
        step = r.shrink.shape[0] // 2
        for half, scatter in enumerate(self.shrink_out):
            scatter.finish(r.shrink_part.at[pl.ds(half * step, step)])
        self.merge_out.finish(r.merge_part)
        self.finish_feed()
        total = r.norm_send[...]
        for bits, copy in enumerate(norms):
            copy.wait_recv()
            total += r.norms[bits]
        r.norm_grads[...] = total
        self.query_out.finish(r.query_part)
        self.value_out.finish(r.value_part)


def on_device(names, turns, *refs):
    r = SimpleNamespace(**dict(zip(names, refs)))
    r.feed, r.grad_expand = r.one_full, r.expand_full
    r.grad_pair, r.part_one, r.grad_send = r.packed, r.part_two, r.out_send
    steps = Phases(r, turns)
    steps.place.greet()
    steps.project()
    steps.sort_tokens()
    steps.go_on(steps.merge)
    steps.expand[0].forward()
    steps.begin(steps.shrink[0])
    steps.attend()
    steps.go_on(steps.expand[1])
    steps.return_rows()
    steps.begin_merge_rows()
    steps.begin(steps.shrink[1])
    steps.mix_rounds()
    steps.go_on(steps.shrink[0])
    steps.one.relay()
    steps.grads.relay()
    steps.heads.relay()
    steps.go_on(steps.shrink[1])
    steps.one.finish()
    steps.grads.finish()
    steps.heads.finish()
    steps.feed_forward()
    steps.feed_back()
    steps.grad_rounds()
    steps.send_feed()
    steps.sort_grads()
    steps.expand_out.along()
    steps.attend_back()
    steps.expand_out.across()
    steps.merge_out.along()
    steps.return_grads()
    steps.merge_out.across()
    steps.project_back()
    steps.wires.drain()
    assert len(steps.wires.copies) <= r.send.shape[0]


def whole(turns, arguments, tables):
    bf16, f32 = jnp.bfloat16, jnp.float32
    heads, devices = lax.axis_size("head"), lax.axis_size("seq")
    pair = devices // turns
    rows, width = arguments["two"].shape
    tokens, wide = devices * rows, heads * width
    hidden = arguments["expand"].shape[1]
    lines = rows // 128
    shape = {name: value.shape for name, value in arguments.items()}
    results = dict(
        result_one=((rows, width), bf16),
        result_two=((rows, width), bf16),
        input_grad_one=((rows, width), bf16),
        input_grad_two=((rows, width), bf16),
        query_part=(shape["query"], f32),
        value_part=(shape["value"], f32),
        merge_part=(shape["merge"], f32),
        expand_part=(shape["expand"], f32),
        shrink_part=(shape["shrink"], f32),
        norm_grads=((8, width), f32),
    )
    scratch = dict(
        params=((8, width), f32),
        keys=((tokens // 128, 1, 128), f32),
        until=((-(-(devices * (rows // GROUP + 1) + 1) // 128) * 128, 128), f32),
        block_row=((devices, 1, rows), jnp.int32),
        block_column=((tokens, 128), jnp.int16),
        chunk_row=((devices, 1, rows), jnp.int32),
        chunk_column=((tokens, 128), jnp.int16),
        sorted_query=((tokens, HEAD_DIM), bf16),
        unit=((tokens + GROUP, HEAD_DIM), bf16),
        key_value=((tokens + GROUP, HEAD_DIM), bf16),
        probs=((tokens, 2 * GROUP), f32),
        outs=((turns, pair, rows, HEAD_DIM), bf16),
        mix=((turns, pair, rows, HEAD_DIM), f32),
        rows_one=((rows, wide), bf16),
        center_one=((rows, 128), f32),
        factor_one=((rows, 128), f32),
        query_full=((wide, width), bf16),
        value_full=((wide, width), bf16),
        merge_full=((wide, wide), bf16),
        expand_full=((wide, hidden), bf16),
        shrink_full=((hidden, wide), bf16),
        one_full=((rows, wide), bf16),
        two_full=((rows, wide), bf16),
        grad_full=((rows, wide), bf16),
        attended_full=((rows, wide), bf16),
        everyone=((tokens, 2 * HEAD_DIM), bf16),
        mid=((devices * devices, rows // devices, 2 * HEAD_DIM), bf16),
        params_full=((8, wide), f32),
        packed=((pair, 2, rows, HEAD_DIM), bf16),
        round_rows=((tokens, 2 * HEAD_DIM), bf16),
        out_send=((turns - 1, pair, rows, HEAD_DIM), bf16),
        total_send=((turns - 1, pair, lines, 128), f32),
        totals=((turns, pair, lines, 128), f32),
        mix_rows=((turns, pair, lines, 128), f32),
        attended=((pair, rows, HEAD_DIM), bf16),
        tall=((rows, wide), f32),
        normal_two=((rows, width), f32),
        factor_two=((rows, 128), f32),
        rows_two=((rows, wide), bf16),
        active=((rows, hidden), bf16),
        grad_hidden=((rows, hidden), bf16),
        part_two=((rows, wide), bf16),
        stat_two=((2 * lines, 128), f32),
        parts_two=((heads - 1, rows, width), bf16),
        stats_two=((heads - 1, 2 * lines, 128), f32),
        stat_one=((2 * lines, 128), f32),
        parts_one=((heads - 1, rows, width), bf16),
        stats_one=((heads - 1, 2 * lines, 128), f32),
        feeds=((heads - 1, rows, width), bf16),
        grad_rows_one=((rows, wide), bf16),
        grad_heads=((pair, rows, HEAD_DIM), bf16),
        grad_attended=((pair, rows, HEAD_DIM), bf16),
        grad_total_send=((turns - 1, pair, lines, 128), f32),
        grad_outs=((turns, pair, rows, HEAD_DIM), bf16),
        grad_totals=((turns, pair, lines, 128), f32),
        grad_unit=((tokens + GROUP, HEAD_DIM), f32),
        grad_value=((tokens + GROUP, HEAD_DIM), f32),
        grad_pairs=((3, pair * rows, 2 * HEAD_DIM), bf16),
        grad_query=((rows, width), bf16),
        grad_key=((rows, width), bf16),
        norm_send=((8, width), f32),
        norms=((devices - 1, 8, width), f32),
    )
    for name, full in (
        ("query", (wide, width)),
        ("value", (wide, width)),
        ("merge", (width, wide)),
        ("expand", (wide, hidden)),
        ("shrink", (hidden, wide)),
    ):
        own = "grad_" + name + ("_full" if name in ("query", "value") else "")
        if name != "expand":
            scratch[own] = (full, bf16)
        scratch[name + "_pair"] = ((devices // 2,) + shape[name], bf16)
        scratch[name + "_line"] = ((devices // 2 - 1,) + shape[name], bf16)
    wires = dict(send=224, receive=224)
    vmem = pl.BlockSpec(memory_space=pltpu.VMEM)
    smem = pl.BlockSpec(memory_space=pltpu.SMEM)
    names = [*arguments, *tables, *results, *scratch, *wires]
    out = pl.pallas_call(
        partial(on_device, names, turns),
        out_shape=[jax.ShapeDtypeStruct(*item) for item in results.values()],
        in_specs=[vmem] * len(arguments)
        + [smem if name.startswith("units") else vmem for name in tables],
        out_specs=[vmem] * len(results),
        scratch_shapes=[pltpu.VMEM(*item) for item in scratch.values()]
        + [pltpu.SemaphoreType.DMA((number,)) for number in wires.values()],
        compiler_params=pltpu.CompilerParams(
            collective_id=0, has_side_effects=True, vmem_limit_bytes=63 << 20
        ),
    )(*arguments.values(), *tables.values())
    return SimpleNamespace(**dict(zip(results, out)))


def round_tables(order, bucket, devices, rows):
    i32 = jnp.int32
    unit = rows // devices
    order, bucket = order.reshape(devices, 1, rows), bucket.reshape(devices, 1, rows)
    each = jnp.arange(devices, dtype=i32)
    share = jnp.sum((order // rows == each[None, :, None]).astype(i32), -1)
    before = each[:, None] < each[None, :]
    in_block = jnp.sum(jnp.where(before[None], share[:, :, None], 0), 1)
    in_chunk = jnp.sum(jnp.where(before[:, :, None], share[:, None, :], 0), 0)
    start = each * unit

    def find(offset, share, other):
        ends = offset + share
        segment = jnp.sum((ends[:, None, :] <= start[None, :, None]).astype(i32), -1)
        chosen = (segment[:, :, None] == each).astype(i32)
        move = jnp.sum(chosen * (other - offset)[:, None, :], -1)
        return ((segment * rows + start[None] + move) // unit).reshape(-1)

    return dict(
        order=order,
        bucket=bucket,
        units=find(in_block, share, in_chunk),
        units_back=find(in_chunk.T, share.T, in_block.T),
    )


def by_rounds(
    stream_one,
    stream_two,
    grad_one,
    grad_two,
    query_weight,
    value_weight,
    merge_weight,
    expand_weight,
    shrink_weight,
    first_gain,
    first_bias,
    second_gain,
    second_bias,
    bucket_ids,
    sort_order,
):
    devices, rounds = lax.axis_size("seq"), sort_order.shape[0]
    turn = lax.axis_index("seq") % 2 * 2 + lax.axis_index("head") % 2
    order = lax.dynamic_slice_in_dim(sort_order, turn, 1, 0)[0]
    bucket = lax.dynamic_slice_in_dim(bucket_ids, turn, 1, 0)[0]
    arguments = dict(
        one=stream_one,
        two=stream_two,
        grad_one=grad_one,
        grad_two=grad_two,
        query=query_weight,
        value=value_weight,
        merge=merge_weight,
        expand=expand_weight,
        shrink=shrink_weight,
        gain_one=first_gain[None],
        bias_one=first_bias[None],
        gain_two=second_gain[None],
        bias_two=second_bias[None],
    )
    k = whole(rounds, arguments, round_tables(order, bucket, devices, stream_one.shape[0]))
    return (
        k.result_one,
        k.result_two,
        k.input_grad_one,
        k.input_grad_two,
        k.query_part,
        k.value_part,
        k.merge_part,
        k.expand_part,
        k.shrink_part,
        k.norm_grads[0],
        k.norm_grads[1],
        k.norm_grads[2],
        k.norm_grads[3],
    )


def solution(mesh):
    placed = (
        P("seq", "head"),
        P("seq", "head"),
        P("seq", "head"),
        P("seq", "head"),
        P("seq", "head"),
        P("seq", "head"),
        P("head", "seq"),
        P("seq", "head"),
        P("head", "seq"),
        P("head"),
        P("head"),
        P("head"),
        P("head"),
        P(),
        P(),
    )

    def local(*arguments):
        rounds = arguments[-1].shape[0]
        if mesh.shape["seq"] == HEADS == 2 * rounds and mesh.shape["head"] == rounds:
            return by_rounds(*arguments)
        return by_blocks(*arguments)

    return jax.shard_map(
        local,
        mesh=mesh,
        in_specs=placed,
        out_specs=(
            P("seq", "head"),
            P("seq", "head"),
            P("seq", "head"),
            P("seq", "head"),
            P("seq", "head"),
            P("seq", "head"),
            P("head", "seq"),
            P("seq", "head"),
            P("head", "seq"),
            P("head"),
            P("head"),
            P("head"),
            P("head"),
        ),
        check_vma=False,
    )
```

```python
from functools import partial
from types import SimpleNamespace

import jax
import jax.numpy as jnp
from jax import lax
from jax.experimental import pallas as pl
from jax.experimental.pallas import tpu as pltpu
from jax.sharding import PartitionSpec as P

HEADS = 8
HEAD_DIM = 128
GROUP = 64
MESH = pl.DeviceIdType.MESH


masked_score = -1000000000.0
own_score = -100000.0


def as_sent(shard):

    def short(part):
        return part.astype(jnp.bfloat16) if part.dtype == jnp.float32 else part

    return jax.tree.map(short, shard)


def from_behind(block, axis, distance):
    devices = range(lax.axis_size(axis))
    route = [(i - distance, i) for i in devices if i - distance in devices]
    return lax.ppermute(block, axis, route)


def row_sums(first, second):
    return lax.psum((first, second), "head")


def full_rows(part):
    return lax.all_gather(part, "head", axis=1, tiled=True)


def branch_sum(part):
    return lax.psum_scatter(part, "head", scatter_dimension=1, tiled=True)


def norm_forward(value, gain, shift):
    width = value.shape[1] * lax.axis_size("head")
    total, square = row_sums(
        jnp.sum(value, 1, keepdims=True), jnp.sum(value * value, 1, keepdims=True)
    )
    center = total / width
    spread = square / width - center * center
    factor = lax.rsqrt(spread + 1e-05)
    normal = (value - center) * factor
    return (normal, factor, normal * gain + shift)


def norm_backward(grad, normal, factor, gain):
    width = grad.shape[1] * lax.axis_size("head")
    scaled = grad * gain
    first, second = row_sums(
        jnp.sum(scaled, 1, keepdims=True), jnp.sum(scaled * normal, 1, keepdims=True)
    )
    result = factor * (scaled - first / width - normal * (second / width))
    return (result, jnp.sum(grad * normal, 0), jnp.sum(grad, 0))


def regroup_rows(buffer):
    turns = []
    for turn in range(buffer.shape[1]):
        turns.append(
            lax.all_to_all(buffer[:, turn], "seq", split_axis=0, concat_axis=0, tiled=True)
        )
    result = jnp.stack(turns, 1)
    return result


def regroup_totals(buffer):
    moved = lax.all_to_all(
        buffer.reshape(buffer.shape[0], -1, buffer.shape[3]),
        "seq",
        split_axis=0,
        concat_axis=0,
        tiled=True,
    )
    return moved.reshape(buffer.shape)


def regroup_pair(first, second):
    firsts = []
    seconds = []
    for turn in range(first.shape[1]):
        moved_first, moved_second = (
            lax.all_to_all(as_sent(first[:, turn]), "seq", split_axis=0, concat_axis=0, tiled=True),
            lax.all_to_all(
                as_sent(second[:, turn]), "seq", split_axis=0, concat_axis=0, tiled=True
            ),
        )
        firsts.append(moved_first)
        seconds.append(moved_second)
    result = (jnp.stack(firsts, 1), jnp.stack(seconds, 1))
    return result


def by_blocks(
    stream_one,
    stream_two,
    grad_one,
    grad_two,
    query_weight,
    value_weight,
    merge_weight,
    expand_weight,
    shrink_weight,
    first_gain,
    first_bias,
    second_gain,
    second_bias,
    bucket_ids,
    sort_order,
):
    devices = lax.axis_size("seq")
    place = lax.axis_index("seq")
    rows = stream_one.shape[0]
    rounds = sort_order.shape[0]
    capacity = 2 * rows // devices
    blocks = rows // GROUP
    heads_here = HEADS // lax.axis_size("head")
    local_width = heads_here * HEAD_DIM
    scale = HEAD_DIM ** (-0.5)
    round_index = jnp.arange(rounds, dtype=jnp.int32)[:, None]
    counter = jnp.arange(rows, dtype=jnp.int32)

    def invert(line):
        return jnp.zeros_like(line).at[line].set(jnp.arange(line.shape[0], dtype=jnp.int32))

    inverse = jax.vmap(invert)(sort_order)
    my_sorted = lax.dynamic_slice_in_dim(inverse, place * rows, rows, 1)
    send_block = my_sorted // rows
    same_block = send_block[:, :, None] == send_block[:, None, :]
    send_slot = jnp.sum(
        (same_block & (my_sorted[:, None, :] < my_sorted[:, :, None])).astype(jnp.int32), -1
    )
    block_tokens = lax.dynamic_slice_in_dim(sort_order, place * rows, rows, 1)
    source_block = block_tokens // rows
    earlier = counter[None, :] < counter[:, None]
    recv_slot = jnp.sum(
        ((source_block[:, :, None] == source_block[:, None, :]) & earlier[None]).astype(jnp.int32),
        -1,
    )
    query_bucket = jnp.take_along_axis(bucket_ids, block_tokens, 1)
    prior_start = (place - 1) % devices * rows + rows - GROUP
    prior_tokens = lax.dynamic_slice_in_dim(sort_order, prior_start, GROUP, 1)
    prior_bucket = jnp.take_along_axis(bucket_ids, prior_tokens, 1)

    def with_prior(own, prior):
        pieces = own.reshape((rounds, blocks, GROUP) + own.shape[2:])
        before = jnp.concatenate([prior[:, None], pieces[:, :-1]], 1)
        return jnp.concatenate([pieces, before], 2)

    query_place = block_tokens.reshape(rounds, blocks, GROUP)
    key_place = with_prior(block_tokens, prior_tokens)
    key_bucket = with_prior(query_bucket, prior_bucket)
    allowed = (key_place[:, :, None, :] <= query_place[:, :, :, None]) & (
        key_bucket[:, :, None, :] == query_bucket.reshape(rounds, blocks, GROUP)[:, :, :, None]
    )
    itself = key_place[:, :, None, :] == query_place[:, :, :, None]
    live = allowed & jnp.logical_not(itself)

    def fill(values, block, slot):
        empty = jnp.zeros((devices, rounds, capacity, values.shape[-1]), values.dtype)
        return empty.at[block, round_index, slot].set(values)

    normal_one, factor_one, normed_one = norm_forward(
        stream_two.astype(jnp.float32), first_gain, first_bias
    )
    rows_one = full_rows(normed_one.astype(jnp.bfloat16))
    query_full, value_full, merge_full = (
        lax.all_gather(query_weight, "seq", axis=0, tiled=True),
        lax.all_gather(value_weight, "seq", axis=0, tiled=True),
        lax.all_gather(merge_weight, "seq", axis=1, tiled=True),
    )
    queries = jnp.dot(rows_one, query_full, preferred_element_type=jnp.float32).astype(jnp.bfloat16)
    values = jnp.dot(rows_one, value_full, preferred_element_type=jnp.float32).astype(jnp.bfloat16)
    packed = jnp.concatenate([queries, values], 1)
    outgoing = fill(jnp.broadcast_to(packed[None], (rounds,) + packed.shape), send_block, send_slot)
    incoming = regroup_rows(outgoing)
    sorted_rows = incoming[source_block, round_index, recv_slot]
    sorted_query = sorted_rows[:, :, :local_width].reshape(rounds, rows, heads_here, HEAD_DIM)
    sorted_value = sorted_rows[:, :, local_width:].reshape(rounds, rows, heads_here, HEAD_DIM)
    query_float = sorted_query.astype(jnp.float32)
    inverse_norm = lax.rsqrt(jnp.sum(query_float * query_float, -1, keepdims=True) + 1e-06)
    unit_float = query_float * inverse_norm
    unit_low = unit_float.astype(jnp.bfloat16)
    edge = from_behind(
        jnp.concatenate([unit_low[:, -GROUP:], sorted_value[:, -GROUP:]], -1), "seq", 1
    )
    key_unit = with_prior(unit_low, edge[..., :HEAD_DIM])
    key_value = with_prior(sorted_value, edge[..., HEAD_DIM:])
    query_groups = sorted_query.reshape(rounds, blocks, GROUP, heads_here, HEAD_DIM)

    def masked_scores():
        raw = (
            jnp.einsum(
                "rncha,rnkha->rnhck", query_groups, key_unit, preferred_element_type=jnp.float32
            )
            * scale
        )
        return jnp.where(
            itself[:, :, None], own_score, jnp.where(allowed[:, :, None], raw, masked_score)
        )

    scores = masked_scores()
    peak = jnp.max(scores, -1, keepdims=True)
    totals = peak + jnp.log(jnp.sum(jnp.exp(scores - peak), -1, keepdims=True))
    probs_low = jnp.exp(scores - totals).astype(jnp.bfloat16)
    round_out = jnp.einsum(
        "rnhck,rnkha->rncha", probs_low, key_value, preferred_element_type=jnp.float32
    ).astype(jnp.bfloat16)
    out_flat = round_out.reshape(rounds, rows, local_width)
    total_flat = jnp.transpose(totals[..., 0], (0, 1, 3, 2)).reshape(rounds, rows, heads_here)
    token_out = regroup_rows(fill(out_flat, source_block, recv_slot))[
        send_block, round_index, send_slot
    ].astype(jnp.float32)
    token_total = regroup_totals(fill(total_flat, source_block, recv_slot))[
        send_block, round_index, send_slot
    ]
    mix = jax.nn.softmax(token_total, axis=0)
    token_out4 = token_out.reshape(rounds, rows, heads_here, HEAD_DIM)
    attended_low = (
        jnp.sum(mix[..., None] * token_out4, 0).reshape(rows, local_width).astype(jnp.bfloat16)
    )
    sum_one = stream_one.astype(jnp.float32) + branch_sum(
        jnp.dot(attended_low, merge_full, preferred_element_type=jnp.float32)
    )
    normal_two, factor_two, normed_two = norm_forward(sum_one, second_gain, second_bias)
    rows_two = full_rows(normed_two.astype(jnp.bfloat16))
    expand_full, shrink_full = (
        lax.all_gather(expand_weight, "seq", axis=0, tiled=True),
        lax.all_gather(shrink_weight, "seq", axis=1, tiled=True),
    )
    hidden = jnp.dot(rows_two, expand_full, preferred_element_type=jnp.float32)
    active, gelu_pull = jax.vjp(partial(jax.nn.gelu, approximate=False), hidden)
    active_low = active.astype(jnp.bfloat16)
    sum_two = stream_two.astype(jnp.float32) + branch_sum(
        jnp.dot(active_low, shrink_full, preferred_element_type=jnp.float32)
    )
    grad_rows_two = full_rows(grad_two)
    grad_active = jnp.dot(grad_rows_two, shrink_full.T, preferred_element_type=jnp.float32)
    grad_hidden = gelu_pull(grad_active)[0].astype(jnp.bfloat16)
    grad_shrink = jnp.dot(active_low.T, grad_rows_two, preferred_element_type=jnp.float32)
    grad_expand = jnp.dot(rows_two.T, grad_hidden, preferred_element_type=jnp.float32)
    grad_normed_two = branch_sum(
        jnp.dot(grad_hidden, expand_full.T, preferred_element_type=jnp.float32)
    )
    extra_one, grad_second_gain, grad_second_bias = norm_backward(
        grad_normed_two, normal_two, factor_two, second_gain
    )
    total_one = grad_one.astype(jnp.float32) + extra_one
    total_low = total_one.astype(jnp.bfloat16)
    grad_rows_one = full_rows(total_low)
    grad_attended = jnp.dot(grad_rows_one, merge_full.T, preferred_element_type=jnp.float32).astype(
        jnp.bfloat16
    )
    grad_merge = jnp.dot(attended_low.T, grad_rows_one, preferred_element_type=jnp.float32)
    grad_float = grad_attended.astype(jnp.float32).reshape(rows, heads_here, HEAD_DIM)
    dots = jnp.sum(token_out4 * grad_float[None], -1)
    grad_total = mix * (dots - jnp.sum(mix * dots, 0, keepdims=True))
    grad_out_low = (
        (mix[..., None] * grad_float[None]).astype(jnp.bfloat16).reshape(rounds, rows, local_width)
    )
    sorted_grad_out = regroup_rows(fill(grad_out_low, send_block, send_slot))[
        source_block, round_index, recv_slot
    ]
    sorted_grad_total = regroup_totals(fill(grad_total, send_block, send_slot))[
        source_block, round_index, recv_slot
    ]
    grad_groups = sorted_grad_out.reshape(rounds, blocks, GROUP, heads_here, HEAD_DIM)
    total_grad_groups = jnp.transpose(
        sorted_grad_total.reshape(rounds, blocks, GROUP, heads_here), (0, 1, 3, 2)
    )[..., None]
    probs = jnp.exp(masked_scores() - totals)
    probs_again = probs.astype(jnp.bfloat16)
    grad_probs = jnp.einsum(
        "rncha,rnkha->rnhck", grad_groups, key_value, preferred_element_type=jnp.float32
    )
    grad_key_value = jnp.einsum(
        "rnhck,rncha->rnkha", probs_again, grad_groups, preferred_element_type=jnp.float32
    )
    inner = jnp.sum(probs * grad_probs, -1, keepdims=True)
    grad_scores = jnp.where(
        live[:, :, None], probs * (grad_probs - inner + total_grad_groups), 0.0
    ).astype(jnp.bfloat16)
    grad_query_groups = (
        jnp.einsum("rnhck,rnkha->rncha", grad_scores, key_unit, preferred_element_type=jnp.float32)
        * scale
    )
    grad_key_unit = (
        jnp.einsum(
            "rnhck,rncha->rnkha", grad_scores, query_groups, preferred_element_type=jnp.float32
        )
        * scale
    )
    edge_grad = from_behind(
        jnp.concatenate([grad_key_unit[:, 0, GROUP:], grad_key_value[:, 0, GROUP:]], -1).astype(
            jnp.bfloat16
        ),
        "seq",
        -1,
    ).astype(jnp.float32)

    def fold_keys(grad_keys, arriving):
        own = grad_keys[:, :, :GROUP]
        later = jnp.concatenate([grad_keys[:, 1:, GROUP:], arriving[:, None]], 1)
        return (own + later).reshape(rounds, rows, heads_here, HEAD_DIM)

    grad_unit = fold_keys(grad_key_unit, edge_grad[..., :HEAD_DIM])
    grad_sorted_value = fold_keys(grad_key_value, edge_grad[..., HEAD_DIM:])
    grad_sorted_query = grad_query_groups.reshape(
        rounds, rows, heads_here, HEAD_DIM
    ) + inverse_norm * (grad_unit - unit_float * jnp.sum(unit_float * grad_unit, -1, keepdims=True))
    moved_first, moved_second = regroup_pair(
        fill(grad_sorted_query.reshape(rounds, rows, local_width), source_block, recv_slot),
        fill(grad_sorted_value.reshape(rounds, rows, local_width), source_block, recv_slot),
    )
    token_grad_query = moved_first[send_block, round_index, send_slot]
    token_grad_value = moved_second[send_block, round_index, send_slot]
    grad_query_low = jnp.sum(token_grad_query, 0).astype(jnp.bfloat16)
    grad_value_low = jnp.sum(token_grad_value, 0).astype(jnp.bfloat16)
    grad_query_full = jnp.dot(rows_one.T, grad_query_low, preferred_element_type=jnp.float32)
    grad_value_full = jnp.dot(rows_one.T, grad_value_low, preferred_element_type=jnp.float32)
    grad_normed_one = branch_sum(
        jnp.dot(grad_query_low, query_full.T, preferred_element_type=jnp.float32)
        + jnp.dot(grad_value_low, value_full.T, preferred_element_type=jnp.float32)
    )
    extra_two, grad_first_gain, grad_first_bias = norm_backward(
        grad_normed_one, normal_one, factor_one, first_gain
    )
    input_grad_two = (grad_two.astype(jnp.float32) + extra_two).astype(jnp.bfloat16)
    query_part, value_part, merge_part, expand_part, shrink_part = (
        lax.psum_scatter(grad_query_full, "seq", scatter_dimension=0, tiled=True),
        lax.psum_scatter(grad_value_full, "seq", scatter_dimension=0, tiled=True),
        lax.psum_scatter(grad_merge, "seq", scatter_dimension=1, tiled=True),
        lax.psum_scatter(grad_expand, "seq", scatter_dimension=0, tiled=True),
        lax.psum_scatter(grad_shrink, "seq", scatter_dimension=1, tiled=True),
    )
    first_gain_sum, first_bias_sum, second_gain_sum, second_bias_sum = lax.psum(
        (grad_first_gain, grad_first_bias, grad_second_gain, grad_second_bias), "seq"
    )
    return (
        sum_one.astype(jnp.bfloat16),
        sum_two.astype(jnp.bfloat16),
        total_low,
        input_grad_two,
        query_part,
        value_part,
        merge_part,
        expand_part,
        shrink_part,
        first_gain_sum,
        first_bias_sum,
        second_gain_sum,
        second_bias_sum,
    )


def flip(index, bit):
    return index + bit - 2 * bit * ((index // bit) % 2)


def flipped(index, bits):
    for bit in (1, 2, 4):
        if bits & bit:
            index = flip(index, bit)
    return index


class Place:
    def __init__(self):
        self.seq, self.head = lax.axis_index("seq"), lax.axis_index("head")
        self.line, self.side = self.seq // 2, self.seq % 2
        self.pair, self.core = self.head // 2, self.head % 2
        self.turn = self.side * 2 + self.core
        self.home = self.line // 2 == self.core
        self.away = self.line // 2 != self.core

    def peer(self, seq_bits, head_bits=0):
        return (flipped(self.seq, seq_bits), flipped(self.head, head_bits))

    def member(self, bits):
        return self.peer(bits // 2, bits % 2)

    def chunk(self, turn, half):
        return (2 * (turn % 2) + half) * 2 + turn // 2

    def greet(self):
        peers = [self.peer(bits) for bits in range(1, 8)]
        peers += [self.peer(0, bits) for bits in range(1, 4)]
        peers += [self.peer(bits, 1) for bits in (1, 2, 4, 6)]
        barrier = pltpu.get_barrier_semaphore()
        for peer in peers:
            pl.semaphore_signal(barrier, inc=1, device_id=peer, device_id_type=MESH)
        pl.semaphore_wait(barrier, len(peers))


class Copy:
    def __init__(self, copy, starts, lands):
        self.copy, self.starts, self.lands = copy, starts, lands
        self.when(starts, copy.start)

    def when(self, condition, act):
        if condition is None:
            act()
        else:
            pl.when(condition)(act)

    def wait_recv(self):
        self.when(self.lands, self.copy.wait_recv)

    def wait_send(self):
        self.when(self.starts, self.copy.wait_send)


class Wires:
    def __init__(self, send, receive):
        self.send, self.receive, self.copies = send, receive, []

    def push(self, source, target, device, starts=None, lands=None):
        index = len(self.copies)
        copy = pltpu.make_async_remote_copy(
            src_ref=source,
            dst_ref=target,
            send_sem=self.send.at[index],
            recv_sem=self.receive.at[index],
            device_id=device,
            device_id_type=MESH,
        )
        self.copies.append(Copy(copy, starts, lands))
        return self.copies[-1]

    def settle(self, copies):
        for copy in copies:
            copy.wait_send()
        done = [id(copy) for copy in copies]
        self.copies = [None if id(copy) in done else copy for copy in self.copies]

    def drain(self):
        self.settle([copy for copy in self.copies if copy is not None])


class Spread:
    def __init__(self, wires, place):
        self.wires, self.place, self.copies = wires, place, []

    def start(self, source_at, target):
        p = self.place
        for bits, starts in ((4, p.away), (6, p.away), (2, p.home)):
            seq = flipped(p.seq, bits)
            head = p.head - p.core + p.line // 2
            copy = self.wires.push(source_at(seq // 2), target, (seq, head), starts, starts)
            self.copies.append(copy)

    def finish(self):
        for copy in self.copies:
            copy.wait_recv()


class TokenGather:
    def __init__(self, wires, place, everyone, rows):
        self.wires, self.place, self.everyone, self.rows = wires, place, everyone, rows
        self.line = {2: [], 4: [], 6: []}
        self.own = []

    def slot(self, seq, part):
        return columns_at(rows_at(self.everyone, seq, self.rows), part, HEAD_DIM)

    def start(self, packed, part):
        p = self.place
        mine = self.slot(p.seq, part)
        for bits, starts in ((4, p.away), (6, p.away), (2, p.home)):
            seq = flipped(p.seq, bits)
            self.line[bits].append(
                self.wires.push(
                    packed.at[(seq // 2) % 2, part],
                    mine,
                    (seq, p.head - p.core + part),
                    starts,
                    p.core == part,
                )
            )
        source = packed.at[p.line % 2, part]
        self.own.append(self.wires.push(source, mine, p.peer(0, 1), p.home, p.away))

        @pl.when(p.home)
        def _():
            mine[...] = source[...]

    def pass_own(self):
        p = self.place
        for copy in self.own:
            copy.wait_recv()
        block = self.slot(p.seq, p.core)
        self.beside = {0: self.wires.push(block, block, p.peer(1))}
        self.shared = {}

    def forward(self, bits):
        p = self.place
        for copy in self.line[bits]:
            copy.wait_recv()
        block = self.slot(flipped(p.seq, bits), p.core)
        self.beside[bits] = self.wires.push(block, block, p.peer(1))
        self.shared[bits] = self.wires.push(block, block, p.peer(0, 1))

    def share(self, bits):
        p = self.place
        self.beside[bits].wait_recv()
        block = self.slot(flipped(p.seq, bits + 1), p.core)
        self.shared[bits + 1] = self.wires.push(block, block, p.peer(0, 1))

    def land(self, bits):
        self.shared[bits].wait_recv()

    def settle(self):
        lines = [copy for copies in self.line.values() for copy in copies]
        self.wires.settle(lines + self.own + [*self.beside.values(), *self.shared.values()])


class SeqGather:
    def __init__(self, wires, place, slot):
        self.wires, self.place, self.slot = wires, place, slot

    def start(self, source, for_far=None):
        p, mine = self.place, self.slot(self.place.seq)
        far = source if for_far is None else for_far
        self.arriving = {4: self.wires.push(far, mine, p.peer(4))}
        self.arriving[2] = self.wires.push(source, mine, p.peer(2))
        self.beside = {0: self.wires.push(source, mine, p.peer(1))}

    def forward(self, bits):
        p = self.place
        self.arriving[bits].wait_recv()
        block = self.slot(flipped(p.seq, bits))
        if bits == 4:
            self.arriving[6] = self.wires.push(block, block, p.peer(2))
        self.beside[bits] = self.wires.push(block, block, p.peer(1))

    def land(self, bits):
        self.beside[bits].wait_recv()

    def settle(self):
        self.wires.settle([*self.arriving.values(), *self.beside.values()])

    def finish(self):
        for bits in self.beside:
            self.land(bits)
        self.settle()


class PairGather:
    def __init__(self, wires, place, slot, both):
        self.wires, self.place, self.slot, self.both = wires, place, slot, both

    def start(self, source):
        p = self.place
        self.first = self.wires.push(source, self.slot(p.seq), p.peer(1))

    def along(self):
        p = self.place
        self.first.wait_recv()
        pair = self.both(p.seq // 2)
        self.far = self.wires.push(pair, pair, p.peer(4))
        self.near = self.wires.push(pair, pair, p.peer(2))

    def forward(self):
        p = self.place
        self.far.wait_recv()
        pair = self.both(flip(p.seq, 4) // 2)
        self.last = self.wires.push(pair, pair, p.peer(2))

    def finish(self):
        self.near.wait_recv()
        self.last.wait_recv()
        self.wires.settle([self.first, self.far, self.near, self.last])


class HeadGather:
    def __init__(self, wires, place, slot):
        self.wires, self.place, self.slot = wires, place, slot

    def start(self, source):
        p = self.place
        mine = self.slot(p.head)
        self.long = self.wires.push(source, mine, p.peer(0, 2))
        self.short = self.wires.push(source, mine, p.peer(0, 1))

    def relay(self):
        p = self.place
        self.long.wait_recv()
        moved = self.slot(flip(p.head, 2))
        self.last = self.wires.push(moved, moved, p.peer(0, 1))

    def finish(self):
        self.short.wait_recv()
        self.last.wait_recv()
        self.wires.settle([self.long, self.short, self.last])


def columns_at(ref, index, width):
    return ref.at[:, pl.ds(pl.multiple_of(index * width, width), width)]


def rows_at(ref, index, width):
    return ref.at[pl.ds(pl.multiple_of(index * width, width), width)]


def span(index, width):
    return pl.ds(pl.multiple_of(index * width, width), width)


def dot(left, right, contract=((1,), (0,))):
    return lax.dot_general(
        left, right, (contract, ((), ())), preferred_element_type=jnp.float32
    )


def diagonal(size):
    return lax.broadcasted_iota(jnp.int32, (size, size), 0) == lax.broadcasted_iota(
        jnp.int32, (size, size), 1
    )


def to_row(column):
    return jnp.sum(jnp.where(diagonal(column.shape[0]), column, 0.0), 0, keepdims=True)


def to_column(row):
    return jnp.sum(jnp.where(diagonal(row.shape[1]), row, 0.0), 1, keepdims=True)


def in_lanes(total):
    bf16, f32 = jnp.bfloat16, jnp.float32
    high = total.astype(bf16).astype(f32)
    middle = (total - high).astype(bf16).astype(f32)
    low = total - high - middle
    lane = lax.broadcasted_iota(jnp.int32, (total.shape[0], 128), 1)
    parts = jnp.where(lane == 0, high, jnp.where(lane == 1, middle, low))
    return jnp.where(lane < 3, parts, 0.0).astype(bf16)


class SeqScatter:
    def __init__(self, wires, place, piece, pair, line):
        self.wires, self.place, self.piece = wires, place, piece
        self.pair, self.line = pair, line

    def start(self):
        p = self.place
        self.beside = {}
        for bits in (6, 2, 4, 0):
            source = self.piece(flipped(p.seq, bits + 1))
            self.beside[bits] = self.wires.push(source, self.pair.at[bits // 2], p.peer(1))

    def add(self, bits, more=None):
        at, f32 = self.pair.at[bits // 2], jnp.float32
        self.beside[bits].wait_recv()
        mine = self.piece(flipped(self.place.seq, bits))[...]
        total = at[...].astype(f32) + mine.astype(f32)
        if more is not None:
            total += more[...].astype(f32)
        at[...] = total.astype(jnp.bfloat16)
        return at

    def along(self):
        device = self.place.peer(2)
        self.shares = self.wires.push(self.add(6), self.line.at[0], device)
        self.near = self.wires.push(self.add(2), self.line.at[1], device)

    def across(self):
        self.shares.wait_recv()
        total = self.add(4, self.line.at[0])
        self.far = self.wires.push(total, self.line.at[2], self.place.peer(4))

    def finish(self, target):
        p, f32 = self.place, jnp.float32
        self.beside[0].wait_recv()
        total = self.piece(p.seq)[...].astype(f32) + self.pair.at[0][...].astype(f32)
        self.near.wait_recv()
        total += self.line.at[1][...].astype(f32)
        self.far.wait_recv()
        target[...] = total + self.line.at[2][...].astype(f32)


class Phases:
    def __init__(self, r, turns):
        self.r, self.turns = r, turns
        self.place = Place()
        self.wires = Wires(r.send, r.receive)
        self.rows, self.width = r.two.shape
        self.wide = r.rows_one.shape[1]
        self.count = self.wide // self.width
        self.devices = r.everyone.shape[0] // self.rows
        self.pair = self.devices // turns
        self.units = self.devices


    def spread_columns(self, ref, index):
        column = ref[span(index, self.rows), :].astype(jnp.int32)
        lane = lax.broadcasted_iota(jnp.int32, column.shape, 1)
        parts = [
            jnp.where(column == lane + 128 * i, 1.0, 0.0).astype(jnp.bfloat16)
            for i in range(self.rows // 128)
        ]
        return jnp.concatenate(parts, 1)

    def spread_rows(self, ref, index):
        row = ref[index]
        place = lax.broadcasted_iota(jnp.int32, (self.rows, self.rows), 0)
        return jnp.where(row == place, 1.0, 0.0).astype(jnp.bfloat16)

    def from_units(self, ref, table, index):
        return jnp.concatenate([ref[table[index, unit]] for unit in range(self.units)], 0)

    def to_units(self, index, rows):
        first, step = index * self.units, self.rows // self.units
        for unit in range(self.units):
            self.r.mid[first + unit] = rows[unit * step : (unit + 1) * step].astype(jnp.bfloat16)

    def sort_chunk(self, source, index):
        r = self.r
        here = span(index, self.rows)
        self.to_units(index, dot(self.spread_columns(r.chunk_column, index), source[here, :]))

    def sorted_block(self, index):
        r = self.r
        return dot(
            self.spread_columns(r.block_column, index), self.from_units(r.mid, r.units, index)
        )

    def unsort_block(self, source, index):
        r = self.r
        here = span(index, self.rows)
        self.to_units(index, dot(self.spread_rows(r.block_row, index), source[here, :]))

    def unsorted_chunk(self, index):
        r = self.r
        return dot(
            self.spread_rows(r.chunk_row, index), self.from_units(r.mid, r.units_back, index)
        )

    def column_of(self, row):
        pieces = [to_column(row[:, i : i + 128]) for i in range(0, self.rows, 128)]
        return jnp.concatenate(pieces, 0)

    def row_of(self, column):
        pieces = [to_row(column[i : i + 128]) for i in range(0, self.rows, 128)]
        return jnp.concatenate(pieces, 1)

    def wide_column(self, column):
        return jnp.broadcast_to(column, (self.rows, 128)).astype(jnp.int32).astype(jnp.int16)

    def line_of(self, ref, block):
        return ref[pl.ds(self.place.turn, 1), span(block, self.rows)]

    def unit_tables(self):
        r = self.r
        bf16, f32, i32 = jnp.bfloat16, jnp.float32, jnp.int32
        unit = self.rows // self.units
        row = lax.broadcasted_iota(i32, (128, 128), 0)
        column = lax.broadcasted_iota(i32, (128, 128), 1)
        by_chunk = r.shares[...].astype(bf16)
        by_block = dot(by_chunk, jnp.where(row == column, 1.0, 0.0).astype(bf16)[:8], ((0,), (0,)))
        by_block = by_block[:8].astype(bf16)
        earlier = jnp.where(row < column, 1.0, 0.0).astype(bf16)
        below = jnp.where(row > column, 1.0, 0.0).astype(bf16)[:8, :8]
        start = (column[:8] * unit).astype(f32)

        def find(share, offset, other):
            segment, move = jnp.zeros((8, 128), f32), jnp.zeros((8, 128), f32)
            ends = offset + share.astype(f32)
            for i in range(self.units):
                segment += jnp.where(ends[:, i : i + 1] <= start, 1.0, 0.0)
            for i in range(self.units):
                shift = (other - offset)[:, i : i + 1]
                move += jnp.where(segment == float(i), shift, 0.0)
            place = ((segment * self.rows + start + move) * (1.0 / unit)).astype(i32)
            return jnp.clip(place, 0, self.units * self.units - 1)

        in_chunk, in_block = dot(by_chunk, earlier), dot(below, by_chunk)
        r.unit_rows[1] = find(by_chunk, in_chunk, in_block)
        r.unit_rows[0] = find(by_block, dot(by_block, earlier), dot(below, by_block))
        copies = [
            pltpu.make_async_copy(r.unit_rows.at[i], target, r.local.at[i])
            for i, target in enumerate((r.units, r.units_back))
        ]
        for copy in copies:
            copy.start()
        for copy in copies:
            copy.wait()

    def bucket_tables(self):
        r = self.r
        f32, i32 = jnp.float32, jnp.int32
        rows = self.rows
        most = -(-(self.devices * (rows // GROUP + 1) + 1) // 128) * 128

        value = lax.broadcasted_iota(i32, (most, rows), 0)

        def count(block, until):
            return until + jnp.sum(
                jnp.where(self.line_of(r.bucket, block) <= value, 1.0, 0.0), 1, keepdims=True
            )

        until = lax.fori_loop(0, self.devices, count, jnp.zeros((most, 1), f32))
        r.until[...] = jnp.broadcast_to(until, (most, 128))

    def block_tables(self, start, stop):
        r = self.r
        bf16, f32, i32 = jnp.bfloat16, jnp.float32, jnp.int32
        rows, lines = self.rows, self.rows // 128
        tokens = rows * self.devices

        def first(block, carry):
            order = self.line_of(r.order, block)
            until = r.until[:, 0:1].astype(i32)
            lane = lax.broadcasted_iota(i32, (1, rows), 1)
            bucket = jnp.sum(
                jnp.where(until <= lane + block * rows, 1.0, 0.0), 0, keepdims=True
            )
            key = bucket * tokens + order.astype(f32)
            for i in range(lines):
                r.keys[block * lines + i] = key[:, i * 128 : (i + 1) * 128]
            chunk = order // rows
            each = lax.broadcasted_iota(i32, (8, rows), 0)
            share = jnp.sum(jnp.where(chunk == each, 1.0, 0.0), 1, keepdims=True)
            at = lax.broadcasted_iota(i32, (8, 128), 1)
            r.shares[...] += jnp.where(at == block, share, 0.0)
            place = (chunk * rows + lane).astype(f32)
            slot = jnp.sum(jnp.where(place < self.column_of(place), 1.0, 0.0), 1, keepdims=True)
            r.block_column[span(block, rows), :] = self.wide_column(slot)
            r.block_row[block] = self.row_of(slot).astype(i32)
            local = self.column_of((order - chunk * rows).astype(f32))
            high = jnp.floor(local * 0.0625)
            at = lax.broadcasted_iota(i32, (rows, 2 * HEAD_DIM), 1)
            parts = jnp.where(at == 0, high, jnp.where(at == 1, local - 16.0 * high, 0.0))
            r.round_rows[span(block, rows), :] = parts.astype(bf16)
            self.unsort_block(r.round_rows, block)
            return carry

        lax.fori_loop(start, stop, first, 0)

    def chunk_tables(self):
        r = self.r
        f32, i32 = jnp.float32, jnp.int32
        rows = self.rows

        def second(chunk, carry):
            parts = self.from_units(r.mid, r.units_back, chunk)[:, 0:128].astype(f32)
            token = 16.0 * parts[:, 0:1] + parts[:, 1:2]
            r.chunk_column[span(chunk, rows), :] = self.wide_column(token)
            r.chunk_row[chunk] = self.row_of(token).astype(i32)
            return carry

        lax.fori_loop(0, self.devices, second, 0)

    def codes(self, index):
        r = self.r
        tokens = self.rows * self.devices
        groups = tokens // 128
        low = lax.broadcasted_iota(jnp.int32, (1, 128), 1) < GROUP
        result = []
        for i in range(2):
            here = 2 * index + i
            keys, before = r.keys[here], r.keys[(here + groups - 1) % groups]
            query = to_column(keys)
            least = jnp.floor(query * (1.0 / tokens)) * tokens
            for half, window in enumerate((jnp.where(low, keys, before), keys)):
                at = slice(half * GROUP, (half + 1) * GROUP)
                allowed = (window <= query[at]) & (window >= least[at])
                result.append(
                    jnp.where(window == query[at], 1.0, jnp.where(allowed, 0.0, 2.0))
                )
        return jnp.concatenate(result, 0)

    def window(self, rows, block):
        before = rows[block * GROUP : (block + 1) * GROUP]
        own = rows[(block + 1) * GROUP : (block + 2) * GROUP]
        return jnp.concatenate([own, before] if block % 2 == 0 else [before, own], 0)

    def over_rows(self, ref):
        step = ref.shape[0] // self.devices
        return SeqGather(self.wires, self.place, lambda seq: rows_at(ref, seq, step))

    def over_columns(self, ref):
        step = ref.shape[1] // self.devices
        return SeqGather(self.wires, self.place, lambda seq: columns_at(ref, seq, step))

    def start_seq(self, gather, source):
        gather.start(source)
        gather.slot(self.place.seq)[...] = source[...]

    def start_head(self, gather, source):
        gather.start(source)
        gather.slot(self.place.head)[...] = source[...]

    def over_head(self, ref):
        return HeadGather(self.wires, self.place, lambda head: columns_at(ref, head, self.width))

    def project(self):
        r, place, wires = self.r, self.place, self.wires
        bf16, f32 = jnp.bfloat16, jnp.float32
        stream = self.over_head(r.two_full)
        small = self.over_head(r.params_full)
        self.start_head(stream, r.two)
        for row, item in enumerate((r.gain_one, r.bias_one, r.gain_two, r.bias_two)):
            r.params[row : row + 1, :] = item[...]
        r.params[4:8, :] = jnp.zeros((4, self.width), f32)
        self.start_head(small, r.params)
        query, value = self.over_rows(r.query_full), self.over_rows(r.value_full)
        self.start_seq(query, r.query)
        self.start_seq(value, r.value)
        self.bulk()
        self.begin(self.expand[0])
        r.shares[...] = jnp.zeros_like(r.shares)
        self.bucket_tables()
        for weight in (query, value):
            for bits in (4, 2):
                weight.forward(bits)
        self.begin(self.expand[1])
        small.relay()
        stream.relay()
        query.forward(6)
        value.forward(6)
        small.finish()
        stream.finish()

        def normalise(tile, carry):
            here = span(tile, 128)
            rows = r.two_full[here, :].astype(f32)
            center = jnp.mean(rows, 1, keepdims=True)
            offset = rows - center
            factor = lax.rsqrt(jnp.mean(offset * offset, 1, keepdims=True) + 1e-05)
            r.center_one[here, :] = jnp.broadcast_to(center, (128, 128))
            r.factor_one[here, :] = jnp.broadcast_to(factor, (128, 128))
            r.rows_one[here, :] = (
                offset * factor * r.params_full[0:1, :] + r.params_full[1:2, :]
            ).astype(bf16)
            return carry

        lax.fori_loop(0, self.rows // 128, normalise, 0)
        self.tokens = TokenGather(self.wires, place, r.everyone, self.rows)
        self.project_one(query, r.query_full, 0)
        self.project_one(value, r.value_full, 1)
        self.begin(self.merge)

    def project_one(self, weight, full, part):
        r = self.r
        weight.finish()

        def multiply(tile, carry):
            here = span(tile, 256)
            result = dot(r.rows_one[here, :], full[...]).astype(jnp.bfloat16)
            for which in range(self.pair):
                r.packed[which, part, here, :] = result[
                    :, which * HEAD_DIM : (which + 1) * HEAD_DIM
                ]
            return carry

        lax.fori_loop(0, self.rows // 256, multiply, 0)
        self.tokens.start(r.packed, part)

    def bulk(self):
        r, place = self.r, self.place
        my_rows = rows_at(r.merge_full, place.head, r.merge.shape[0])
        self.merge = SeqGather(
            self.wires, place, lambda seq: columns_at(my_rows, seq, r.merge.shape[1])
        )
        self.merge.source = r.merge
        self.expand, self.shrink = [], []
        for part in range(2):
            step, columns = r.expand.shape[0], r.expand.shape[1] // 2
            cut = pl.ds(part * columns, columns)
            slot = lambda seq, cut=cut: rows_at(r.expand_full, seq, step).at[:, cut]
            if part:
                gather = SeqGather(self.wires, place, slot)
            else:
                both = lambda pair: rows_at(r.expand_full, pair, 2 * step).at[:, 0:columns]
                gather = PairGather(self.wires, place, slot, both)
            gather.source = r.expand.at[:, cut]
            self.expand.append(gather)
            rows, width = r.shrink.shape[0] // 2, r.shrink.shape[1]
            down = pl.ds(part * rows, rows)
            gather = SeqGather(
                self.wires,
                place,
                lambda seq, down=down: columns_at(r.shrink_full.at[down], seq, width),
            )
            gather.source = r.shrink.at[down]
            self.shrink.append(gather)
        self.one, self.grads = self.over_head(r.one_full), self.over_head(r.grad_full)

    def begin(self, gather):
        self.start_seq(gather, gather.source)

    def go_on(self, gather):
        for bits in (4, 2, 6):
            gather.forward(bits)

    def begin_streams(self):
        self.start_head(self.one, self.r.one)
        self.start_head(self.grads, self.r.grad_two)

    def begin_merge_rows(self):
        r, place = self.r, self.place
        self.merge.finish()
        self.heads = HeadGather(
            self.wires, place, lambda head: rows_at(r.merge_full, head, r.merge.shape[0])
        )
        self.heads.start(self.heads.slot(place.head))

    def sort_tokens(self):
        r, place = self.r, self.place
        bf16, f32 = jnp.bfloat16, jnp.float32
        tokens = self.tokens
        half = self.devices // 2
        self.block_tables(0, half)
        tokens.pass_own()
        self.block_tables(half, self.devices)
        for bits in (2, 4, 6):
            tokens.forward(bits)
        self.go_on(self.expand[1])
        self.expand[0].along()
        self.begin_streams()
        self.begin(self.shrink[0])
        self.unit_tables()
        self.chunk_tables()
        self.sort_chunk(r.everyone, place.seq)
        for bits in (2, 4, 6):
            tokens.land(bits)
            self.sort_chunk(r.everyone, flipped(place.seq, bits))
        for bits in (0, 2, 4, 6):
            tokens.share(bits)
        for bits in (0, 2, 4, 6):
            tokens.land(bits + 1)
            self.sort_chunk(r.everyone, flipped(place.seq, bits + 1))
        tokens.settle()

        def second(block, carry):
            rows = self.sorted_block(block)
            here = span(block, self.rows)
            later = pl.ds(pl.multiple_of(block * self.rows + GROUP, GROUP), self.rows)
            query = rows[:, :HEAD_DIM]
            r.sorted_query[here, :] = query.astype(bf16)
            factor = lax.rsqrt(jnp.sum(query * query, 1, keepdims=True) + 1e-06)
            r.unit[later, :] = (query * factor).astype(bf16)
            r.key_value[later, :] = rows[:, HEAD_DIM:].astype(bf16)
            return carry

        lax.fori_loop(0, self.devices, second, 0)
        last = pl.ds(self.devices * self.rows, GROUP)
        r.unit[0:GROUP, :] = r.unit[last, :]
        r.key_value[0:GROUP, :] = r.key_value[last, :]

    def attend(self):
        r = self.r
        bf16, f32 = jnp.bfloat16, jnp.float32
        scale = HEAD_DIM ** (-0.5)
        some = 4 * GROUP

        def group(index, carry):
            here = span(index, some)
            longer = pl.ds(pl.multiple_of(index * some, some), some + GROUP)
            query, unit, value = r.sorted_query[here, :], r.unit[longer, :], r.key_value[longer, :]
            raw = [
                dot(query[i * GROUP : (i + 1) * GROUP], self.window(unit, i), ((1,), (1,)))
                for i in range(4)
            ]
            code = self.codes(index)
            scores = jnp.where(
                code == 0.0,
                jnp.concatenate(raw, 0) * scale,
                jnp.where(code == 1.0, own_score, masked_score),
            )
            peak = jnp.max(scores, 1, keepdims=True)
            power = jnp.exp(scores - peak)
            total = jnp.sum(power, 1, keepdims=True)
            probs = power * (1.0 / total)
            r.probs[here, :] = probs
            probs = probs.astype(bf16)
            result = [
                dot(probs[i * GROUP : (i + 1) * GROUP], self.window(value, i)) for i in range(4)
            ]
            r.round_rows[here, :HEAD_DIM] = jnp.concatenate(result, 0).astype(bf16)
            r.round_rows[here, HEAD_DIM:] = in_lanes(peak + jnp.log(total))
            return carry

        lax.fori_loop(0, self.devices * self.rows // some, group, 0)

    def return_rows(self):
        r, place, wires = self.r, self.place, self.wires
        bf16, f32 = jnp.bfloat16, jnp.float32

        def first(block, carry):
            self.unsort_block(r.round_rows, block)
            return carry

        lax.fori_loop(0, self.devices, first, 0)
        coming = []
        for half in range(self.pair):
            arriving = []
            for bits in (3, 2, 1, 0):
                turn = flipped(place.turn, bits)
                rows = self.unsorted_chunk(place.chunk(turn, half))
                total = jnp.sum(rows[:, HEAD_DIM:], 1, keepdims=True)
                lines = [to_row(total[i : i + 128]) for i in range(0, self.rows, 128)]
                total = jnp.concatenate(lines, 0)
                rows = rows[:, :HEAD_DIM].astype(bf16)
                if not bits:
                    r.outs[place.turn, half] = rows
                    r.totals[place.turn, half] = total
                    continue
                r.out_send[bits - 1, half] = rows
                r.total_send[bits - 1, half] = total
                for source, target in ((r.total_send, r.totals), (r.out_send, r.outs)):
                    arriving.append(
                        wires.push(
                            source.at[bits - 1, half],
                            target.at[place.turn, half],
                            place.member(bits),
                        )
                    )
            coming.append(arriving)
        self.rounds_coming = coming

    def mix_half(self, half):
        r = self.r
        bf16, f32 = jnp.bfloat16, jnp.float32
        totals = [r.totals[turn, half] for turn in range(self.turns)]
        peak = totals[0]
        for total in totals[1:]:
            peak = jnp.maximum(peak, total)
        power = [jnp.exp(total - peak) for total in totals]
        whole = sum(power[1:], power[0])
        for turn in range(self.turns):
            r.mix_rows[turn, half] = power[turn] / whole

        def combine(part, carry):
            here = span(part, 128)
            attended = jnp.zeros((128, HEAD_DIM), f32)
            for turn in range(self.turns):
                mix = to_column(r.mix_rows[turn, half, pl.ds(part, 1), :])
                mix = jnp.broadcast_to(mix, (128, HEAD_DIM))
                r.mix[turn, half, here, :] = mix
                attended += mix * r.outs[turn, half, here, :].astype(f32)
            r.attended[half, here, :] = attended.astype(bf16)
            return carry

        lax.fori_loop(0, self.rows // 128, combine, 0)

    def mix_rounds(self):
        r, place, wires = self.r, self.place, self.wires

        for half in range(self.pair):
            for copy in self.rounds_coming[half]:
                copy.wait_recv()
            self.mix_half(half)
        mine = columns_at(r.attended_full, place.pair * 4 + place.line, HEAD_DIM)
        back = Spread(wires, place)
        back.start(lambda line: r.attended.at[line % 2], mine)

        @pl.when(place.home)
        def _():
            mine[...] = r.attended[place.line % 2]

        back.finish()
        gather = self.over_head(r.attended_full)
        gather.start(gather.slot(place.head))
        gather.relay()
        gather.finish()
        wires.settle([copy for arriving in self.rounds_coming for copy in arriving])


    def normalise_sum(self):
        r, place = self.r, self.place
        bf16, f32 = jnp.bfloat16, jnp.float32
        tile_rows = self.rows // 2
        for tile in range(2):
            here = pl.ds(tile * tile_rows, tile_rows)
            total = r.one_full[here, :].astype(f32) + dot(r.attended_full[here, :], r.merge_full[...])
            center = jnp.mean(total, 1, keepdims=True)
            offset = total - center
            factor = lax.rsqrt(jnp.mean(offset * offset, 1, keepdims=True) + 1e-05)
            normal = offset * factor
            r.tall[here, :] = total
            mine = columns_at(r.tall.at[here], place.head, self.width)
            r.result_one[here, :] = mine[...].astype(bf16)
            r.tall[here, :] = normal
            r.normal_two[here, :] = mine[...]
            r.factor_two[here, :] = jnp.broadcast_to(factor, (tile_rows, 128))
            r.rows_two[here, :] = (normal * r.params_full[2:3, :] + r.params_full[3:4, :]).astype(
                bf16
            )

    def feed_half(self, half, tile):
        r = self.r
        bf16 = jnp.bfloat16
        tile_rows, step = self.rows // 2, r.active.shape[1] // 2
        here, units = pl.ds(tile * tile_rows, tile_rows), pl.ds(half * step, step)
        hidden = dot(r.rows_two[here, :], r.expand_full[:, units])
        below = 0.5 * (1.0 + lax.erf(hidden * (0.5**0.5)))
        r.active[here, units] = (hidden * below).astype(bf16)
        slope = below + hidden * jnp.exp(-0.5 * hidden * hidden) * ((2.0 * jnp.pi) ** -0.5)
        grad = dot(r.grad_full[here, :], r.shrink_full[units, :], ((1,), (1,)))
        r.grad_hidden[here, units] = (grad * slope).astype(bf16)

    def shrink_grads(self, half):
        r = self.r
        step = r.active.shape[1] // 2
        units = pl.ds(half * step, step)
        self.weights(r.active.at[:, units], r.grad_full, r.grad_shrink.at[units])
        width = r.shrink.shape[1]
        scatter = SeqScatter(
            self.wires, self.place,
            lambda seq: columns_at(r.grad_shrink.at[units], seq, width),
            r.shrink_pair.at[:, units], r.shrink_line.at[:, units],
        )
        scatter.start()
        self.shrink_out.append(scatter)

    def feed_forward(self):
        r, place, wires = self.r, self.place, self.wires
        self.parts_two, self.shrink_out = [], []
        tile_rows = self.rows // 2
        self.normalise_sum()
        self.expand[0].finish()
        self.shrink[0].finish()
        for tile in range(2):
            self.feed_half(0, tile)
        self.shrink_grads(0)
        self.expand[1].finish()
        self.shrink[1].finish()
        for tile in range(2):
            here = pl.ds(tile * tile_rows, tile_rows)
            self.feed_half(1, tile)
            part = dot(r.grad_hidden[here, :], r.expand_full[...], ((1,), (1,)))
            self.send_part(
                tile, part, r.tall[here, :], r.params_full[2:3, :], r.part_two, r.stat_two,
                r.parts_two, self.parts_two,
            )
        for tile in range(2):
            self.relay_part(tile, r.part_two, r.parts_two, self.parts_two)
        self.send_stats(r.stat_two, r.stats_two, self.parts_two)
        self.shrink_grads(1)

    def send_part(self, tile, part, normal, gain, part_ref, stat_ref, target, copies):
        tile_rows = part.shape[0]
        here = pl.ds(tile * tile_rows, tile_rows)
        scaled = part * gain
        first = jnp.sum(scaled, 1, keepdims=True)
        second = jnp.sum(scaled * normal, 1, keepdims=True)
        lines = tile_rows // 128
        for line in range(lines):
            at = slice(line * 128, (line + 1) * 128)
            row = tile * lines + line
            stat_ref[row : row + 1, :] = to_row(first[at])
            row += self.rows // 128
            stat_ref[row : row + 1, :] = to_row(second[at])
        part_ref[here, :] = part.astype(jnp.bfloat16)
        twin = self.place.peer(0, 1)
        for slot, head in ((1, flip(twin[1], 2)), (0, twin[1])):
            source = columns_at(part_ref.at[here], head, self.width)
            copies.append(self.wires.push(source, target.at[slot, here], twin))

    def relay_part(self, tile, part_ref, target, copies):
        tile_rows = self.rows // 2
        here = pl.ds(tile * tile_rows, tile_rows)
        far = self.place.peer(0, 2)
        copies[2 * tile].wait_recv()
        mine = columns_at(part_ref.at[here], far[1], self.width)[...].astype(jnp.float32)
        total = mine + target[1, here, :].astype(jnp.float32)
        target[1, here, :] = total.astype(jnp.bfloat16)
        copies.append(self.wires.push(target.at[1, here], target.at[2, here], far))

    def send_stats(self, stat_ref, target, copies):
        for bits in (2, 3, 1):
            device = self.place.peer(0, bits)
            copies.append(self.wires.push(stat_ref, target.at[bits - 1], device))

    def norm_back(self, part_ref, parts, stat_ref, stats, normal_at, factor_ref, gain, finish):
        f32 = jnp.float32
        lines = self.rows // 128

        def piece(line, carry):
            here = span(line, 128)
            grad = columns_at(part_ref.at[here], self.place.head, self.width)[...].astype(f32)
            first, second = stat_ref[pl.ds(line, 1), :], stat_ref[pl.ds(line + lines, 1), :]
            for other in range(3):
                if other != 1:
                    grad += parts[other, here, :].astype(f32)
                first += stats[other, pl.ds(line, 1), :]
                second += stats[other, pl.ds(line + lines, 1), :]
            normal = normal_at(here)
            first, second = to_column(first) / self.wide, to_column(second) / self.wide
            finish(here, factor_ref[here, 0:1] * (grad * gain - first - normal * second))
            gains, biases = carry
            return (
                gains + jnp.sum(grad * normal, 0, keepdims=True),
                biases + jnp.sum(grad, 0, keepdims=True),
            )

        zero = jnp.zeros((1, self.width), f32)
        return lax.fori_loop(0, lines, piece, (zero, zero))

    def my_params(self, row):
        return columns_at(self.r.params_full, self.place.head, self.width)[row : row + 1, :]

    def feed_back(self):
        r, place, wires = self.r, self.place, self.wires
        bf16, f32 = jnp.bfloat16, jnp.float32
        self.weights(r.rows_two, r.grad_hidden, r.grad_expand)
        rows, half = r.expand.shape[0], r.expand.shape[1] // 2
        self.expand_out = []
        for cut in (pl.ds(0, half), pl.ds(half, half)):
            self.expand_out.append(
                SeqScatter(
                    wires, place,
                    lambda seq, cut=cut: rows_at(r.grad_expand, seq, rows).at[:, cut],
                    r.expand_pair.at[:, :, cut], r.expand_line.at[:, :, cut],
                )
            )
        self.expand_out[0].start()
        for copy in self.parts_two[1:2] + self.parts_two[3:]:
            copy.wait_recv()
        wires.settle(self.parts_two)

        def finish(here, change):
            total = r.grad_one[here, :].astype(f32) + change
            r.input_grad_one[here, :] = total.astype(bf16)

        gains, biases = self.norm_back(
            r.part_two, r.parts_two, r.stat_two, r.stats_two,
            lambda here: r.normal_two[here, :], r.factor_two, self.my_params(2), finish,
        )
        r.norm_send[2:3, :], r.norm_send[3:4, :] = gains, biases
        gather = self.over_head(r.grad_rows_one)
        self.start_head(gather, r.input_grad_one)
        gather.relay()

        def feed(tile, carry):
            here = span(tile, 256)
            r.feed[here, :] = dot(r.active[here, :], r.shrink_full[...]).astype(bf16)
            return carry

        lax.fori_loop(0, self.rows // 256, feed, 0)
        gather.finish()

    def weights(self, left, right, target):
        step = min(256, left.shape[1])

        def piece(index, carry):
            columns = span(index, step)
            result = dot(left[:, columns], right[...], ((0,), (0,)))
            target[columns, :] = result.astype(jnp.bfloat16)
            return carry

        lax.fori_loop(0, left.shape[1] // step, piece, 0)

    def send_feed(self):
        r = self.r
        self.feeds = []
        for bits in (2, 3, 1):
            device = self.place.peer(0, bits)
            source = columns_at(r.feed, device[1], self.width)
            self.feeds.append(self.wires.push(source, r.feeds.at[bits - 1], device))

    def finish_feed(self):
        r = self.r
        f32 = jnp.float32
        for copy in self.feeds:
            copy.wait_recv()
        total = r.two[...].astype(f32)
        total += columns_at(r.feed, self.place.head, self.width)[...].astype(f32)
        for other in range(3):
            total += r.feeds[other].astype(f32)
        r.result_two[...] = total.astype(jnp.bfloat16)


    def grad_rounds(self):
        r, place, wires = self.r, self.place, self.wires
        bf16, f32 = jnp.bfloat16, jnp.float32
        my_rows = rows_at(r.merge_full, place.head, r.merge.shape[0])

        def attended(tile, carry):
            here = span(tile, 256)
            grad = dot(r.grad_rows_one[here, :], my_rows[...], ((1,), (1,))).astype(bf16)
            for which in range(self.pair):
                r.grad_heads[which, here, :] = grad[:, which * HEAD_DIM : (which + 1) * HEAD_DIM]
            return carry

        lax.fori_loop(0, self.rows // 256, attended, 0)
        mine = r.grad_attended.at[place.line % 2]
        there = Spread(wires, place)
        there.start(lambda line: r.grad_heads.at[line % 2], mine)

        @pl.when(place.home)
        def _():
            mine[...] = r.grad_heads[place.line % 2]

        lines = self.rows // 128

        def spread(half, carry):
            def piece(part, carry):
                here = span(part, 128)
                grad = r.grad_attended[half, here, :].astype(f32)
                turns = [flipped(place.turn, bits) for bits in range(self.turns)]
                mixes = [r.mix[turn, half, here, :] for turn in turns]
                dots = [
                    jnp.sum(r.outs[turn, half, here, :].astype(f32) * grad, 1, keepdims=True)
                    for turn in turns
                ]
                mean = sum(mix[:, 0:1] * value for mix, value in zip(mixes, dots))
                for bits in range(self.turns):
                    change = to_row(mixes[bits][:, 0:1] * (dots[bits] - mean))
                    rows = (mixes[bits] * grad).astype(bf16)
                    if bits:
                        r.grad_send[bits - 1, half, here, :] = rows
                        r.grad_total_send[bits - 1, half, pl.ds(part, 1), :] = change
                    else:
                        r.grad_outs[place.turn, half, here, :] = rows
                        r.grad_totals[place.turn, half, pl.ds(part, 1), :] = change
                return carry

            return lax.fori_loop(0, lines, piece, carry)

        self.grads_coming = {bits: [] for bits in (3, 1, 2)}

        def send(half):
            for bits in (3, 1, 2):
                for source, target in (
                    (r.grad_total_send, r.grad_totals),
                    (r.grad_send, r.grad_outs),
                ):
                    self.grads_coming[bits].append(
                        wires.push(
                            source.at[bits - 1, half],
                            target.at[place.turn, half],
                            place.member(bits),
                        )
                    )

        for scatter in self.shrink_out:
            scatter.along()
        self.weights(columns_at(r.attended_full, place.head, self.width), r.grad_rows_one, r.grad_merge)
        there.finish()
        for half in range(self.pair):
            spread(half, 0)
            send(half)
        self.merge_out = SeqScatter(
            wires, place, lambda seq: columns_at(r.grad_merge, seq, r.merge.shape[1]),
            r.merge_pair, r.merge_line,
        )

    def sort_grads(self):
        r, place = self.r, self.place
        bf16 = jnp.bfloat16
        lines = self.rows // 128
        for bits in (0, 1, 2, 3):
            turn = flipped(place.turn, bits)
            if bits:
                for copy in self.grads_coming[bits]:
                    copy.wait_recv()

            def stage(half, carry, turn=turn):
                chunk = self.place.chunk(turn, half)
                r.everyone[span(chunk, self.rows), :HEAD_DIM] = r.grad_outs[turn, half]

                def piece(part, carry):
                    total = to_column(r.grad_totals[turn, half, pl.ds(part, 1), :])
                    r.everyone[span(chunk * lines + part, 128), HEAD_DIM:] = in_lanes(total)
                    return carry

                lax.fori_loop(0, lines, piece, 0)
                self.sort_chunk(r.everyone, chunk)
                return carry

            lax.fori_loop(0, self.pair, stage, 0)
        self.expand_out[1].start()
        self.merge_out.start()
        for scatter in self.shrink_out:
            scatter.across()

        def second(block, carry):
            r.round_rows[span(block, self.rows), :] = self.sorted_block(block).astype(bf16)
            return carry

        lax.fori_loop(0, self.devices, second, 0)

    def attend_back(self):
        r = self.r
        bf16, f32 = jnp.bfloat16, jnp.float32
        scale = HEAD_DIM ** (-0.5)
        some = 4 * GROUP
        r.grad_unit[0:GROUP, :] = jnp.zeros((GROUP, HEAD_DIM), f32)
        r.grad_value[0:GROUP, :] = jnp.zeros((GROUP, HEAD_DIM), f32)

        def one(rows, block):
            return rows[block * GROUP : (block + 1) * GROUP]

        def fold(pieces):
            owns = [piece[:GROUP] if i % 2 == 0 else piece[GROUP:] for i, piece in enumerate(pieces)]
            befores = [piece[GROUP:] if i % 2 == 0 else piece[:GROUP] for i, piece in enumerate(pieces)]
            middle = [owns[i] + befores[i + 1] for i in range(3)]
            return befores[0], jnp.concatenate(middle + [owns[3]], 0)

        def group(index, carry):
            here = span(index, some)
            longer = pl.ds(pl.multiple_of(index * some, some), some + GROUP)
            before = pl.ds(pl.multiple_of(index * some, some), GROUP)
            after = pl.ds(pl.multiple_of(index * some + GROUP, GROUP), some)
            query, unit, value = r.sorted_query[here, :], r.unit[longer, :], r.key_value[longer, :]
            grad = r.round_rows[here, :HEAD_DIM]
            total = jnp.sum(r.round_rows[here, HEAD_DIM:].astype(f32), 1, keepdims=True)
            probs = r.probs[here, :]
            low = probs.astype(bf16)
            live = jnp.where(self.codes(index) == 0.0, probs, 0.0)
            grad_probs = jnp.concatenate(
                [dot(one(grad, i), self.window(value, i), ((1,), (1,))) for i in range(4)], 0
            )
            inner = jnp.sum(probs * grad_probs, 1, keepdims=True)
            scores = (live * (grad_probs - inner + total)).astype(bf16)
            r.probs[here, :] = (
                jnp.concatenate([dot(one(scores, i), self.window(unit, i)) for i in range(4)], 0) * scale
            )
            for target, left, right, factor in (
                (r.grad_unit, scores, query, scale),
                (r.grad_value, low, grad, 1.0),
            ):
                first, rest = fold(
                    [dot(one(left, i), one(right, i), ((0,), (0,))) * factor for i in range(4)]
                )
                target[before, :] += first
                target[after, :] = rest
            return carry

        lax.fori_loop(0, self.devices * self.rows // some, group, 0)
        last = pl.ds(self.devices * self.rows, GROUP)
        r.grad_unit[last, :] += r.grad_unit[0:GROUP, :]
        r.grad_value[last, :] += r.grad_value[0:GROUP, :]

        def whole(index, carry):
            here = span(index, some)
            after = pl.ds(pl.multiple_of(index * some + GROUP, GROUP), some)
            query = r.sorted_query[here, :].astype(f32)
            factor = lax.rsqrt(jnp.sum(query * query, 1, keepdims=True) + 1e-06)
            unit = query * factor
            grad = r.grad_unit[after, :]
            along = jnp.sum(unit * grad, 1, keepdims=True)
            grad = r.probs[here, :] + factor * (grad - unit * along)
            r.round_rows[here, :HEAD_DIM] = grad.astype(bf16)
            r.round_rows[here, HEAD_DIM:] = r.grad_value[after, :].astype(bf16)
            return carry

        lax.fori_loop(0, self.devices * self.rows // some, whole, 0)

    def return_grads(self):
        r, place, wires = self.r, self.place, self.wires
        bf16, f32 = jnp.bfloat16, jnp.float32

        def first(block, carry):
            self.unsort_block(r.round_rows, block)
            return carry

        lax.fori_loop(0, self.devices, first, 0)
        self.backs = {}

        def rows_for(bits, half):
            return self.unsorted_chunk(place.chunk(flipped(place.turn, bits), half)).astype(bf16)

        def block(slot, half):
            return pl.ds((slot * 2 + half) * self.rows, self.rows)

        for bits in (3, 1, 2, 0):
            for half in range(self.pair):
                r.everyone[block(bits, half), :] = rows_for(bits, half)
        parts = {part: pl.ds(part * HEAD_DIM, HEAD_DIM) for part in (1, 0)}
        both = self.pair * self.rows
        shares, sides = {}, {}
        for part, columns in parts.items():
            for bits in (3, 1):
                source = r.everyone.at[pl.ds(bits * both, both), columns]
                shares[part, bits] = wires.push(
                    source, r.grad_pairs.at[bits // 2, :, columns], place.peer(0, 1)
                )
        for part, columns in parts.items():
            shares[part, 3].wait_recv()
            total = r.everyone[pl.ds(2 * both, both), columns].astype(f32)
            total += r.grad_pairs[1, :, columns].astype(f32)
            r.grad_pairs[1, :, columns] = total.astype(bf16)
            sides[part] = wires.push(
                r.grad_pairs.at[1, :, columns], r.grad_pairs.at[2, :, columns], place.peer(1)
            )
        for part, columns in parts.items():
            shares[part, 1].wait_recv()
            sides[part].wait_recv()
            for half in range(self.pair):
                rows = pl.ds(half * self.rows, self.rows)
                total = r.everyone[block(0, half), columns].astype(f32)
                total += r.grad_pairs[0, rows, columns].astype(f32)
                total += r.grad_pairs[2, rows, columns].astype(f32)
                r.grad_pair[part, half] = total.astype(bf16)
            target = r.grad_key if part else r.grad_query
            mine = columns_at(target, place.line % 2, HEAD_DIM)
            back = Spread(wires, place)
            back.start(lambda line, part=part: r.grad_pair.at[part, line % 2], mine)
            pl.when(place.home)(partial(self.keep_grad, mine, part))
            self.backs[part] = back
        self.backs[1].finish()
        self.value_weights()
        self.backs[0].finish()

    def keep_grad(self, mine, part):
        mine[...] = self.r.grad_pair[part, self.place.line % 2]

    def value_weights(self):
        r = self.r
        self.weights(r.rows_one, r.grad_key, r.grad_value_full)
        self.value_out = SeqScatter(
            self.wires, self.place,
            lambda seq: rows_at(r.grad_value_full, seq, r.value.shape[0]),
            r.value_pair, r.value_line,
        )
        self.value_out.start()

    def project_back(self):
        r, place, wires = self.r, self.place, self.wires
        bf16, f32 = jnp.bfloat16, jnp.float32
        self.weights(r.rows_one, r.grad_query, r.grad_query_full)
        self.query_out = SeqScatter(
            wires, place, lambda seq: rows_at(r.grad_query_full, seq, r.query.shape[0]),
            r.query_pair, r.query_line,
        )
        self.query_out.start()
        copies = []
        tile_rows = self.rows // 2
        for tile in range(2):
            here = pl.ds(tile * tile_rows, tile_rows)
            part = dot(r.grad_query[here, :], r.query_full[...], ((1,), (1,)))
            part += dot(r.grad_key[here, :], r.value_full[...], ((1,), (1,)))
            normal = (r.two_full[here, :].astype(f32) - r.center_one[here, 0:1]) * r.factor_one[
                here, 0:1
            ]
            self.send_part(
                tile, part, normal, r.params_full[0:1, :], r.part_one, r.stat_one,
                r.parts_one, copies,
            )
        for tile in range(2):
            self.relay_part(tile, r.part_one, r.parts_one, copies)
        self.send_stats(r.stat_one, r.stats_one, copies)
        self.value_out.along()
        self.query_out.along()
        for copy in copies[1:2] + copies[3:]:
            copy.wait_recv()

        def normal_at(here):
            rows = columns_at(r.two_full.at[here], place.head, self.width)[...].astype(f32)
            return (rows - r.center_one[here, 0:1]) * r.factor_one[here, 0:1]

        def finish(here, change):
            total = r.grad_two[here, :].astype(f32) + change
            r.input_grad_two[here, :] = total.astype(bf16)

        gains, biases = self.norm_back(
            r.part_one, r.parts_one, r.stat_one, r.stats_one, normal_at, r.factor_one,
            self.my_params(0), finish,
        )
        r.norm_send[0:1, :], r.norm_send[1:2, :] = gains, biases
        norms = [
            wires.push(r.norm_send, r.norms.at[bits - 1], place.peer(bits)) for bits in range(1, 8)
        ]
        self.value_out.across()
        self.query_out.across()
        half = r.expand.shape[1] // 2
        for part, scatter in enumerate(self.expand_out):
            scatter.finish(r.expand_part.at[:, pl.ds(part * half, half)])
        step = r.shrink.shape[0] // 2
        for half, scatter in enumerate(self.shrink_out):
            scatter.finish(r.shrink_part.at[pl.ds(half * step, step)])
        self.merge_out.finish(r.merge_part)
        self.finish_feed()
        total = r.norm_send[...]
        for bits, copy in enumerate(norms):
            copy.wait_recv()
            total += r.norms[bits]
        r.norm_grads[...] = total
        self.query_out.finish(r.query_part)
        self.value_out.finish(r.value_part)


def on_device(names, turns, *refs):
    r = SimpleNamespace(**dict(zip(names, refs)))
    r.result_one, r.result_two, r.input_grad_one, r.input_grad_two = (
        r.streams.at[i] for i in range(4)
    )
    r.query_part, r.value_part = r.projections.at[0], r.projections.at[1]
    merge_rows, shrink_rows = r.merge.shape[0], r.shrink.shape[0]
    r.merge_part = r.columns.at[pl.ds(0, merge_rows)]
    r.shrink_part = r.columns.at[pl.ds(merge_rows, shrink_rows)]
    r.feed, r.grad_expand = r.one_full, r.expand_full
    r.grad_pair, r.part_one, r.grad_send = r.packed, r.part_two, r.out_send
    steps = Phases(r, turns)
    steps.place.greet()
    steps.project()
    steps.sort_tokens()
    steps.go_on(steps.merge)
    steps.expand[0].forward()
    steps.begin(steps.shrink[1])
    steps.attend()
    steps.return_rows()
    steps.go_on(steps.shrink[0])
    steps.begin_merge_rows()
    steps.mix_rounds()
    steps.go_on(steps.shrink[1])
    steps.one.relay()
    steps.grads.relay()
    steps.heads.relay()
    steps.one.finish()
    steps.grads.finish()
    steps.heads.finish()
    steps.feed_forward()
    steps.feed_back()
    steps.grad_rounds()
    steps.send_feed()
    steps.sort_grads()
    steps.expand_out[0].along()
    steps.attend_back()
    steps.expand_out[0].across()
    steps.expand_out[1].along()
    steps.merge_out.along()
    steps.return_grads()
    steps.expand_out[1].across()
    steps.merge_out.across()
    steps.project_back()
    steps.wires.drain()
    assert len(steps.wires.copies) <= r.send.shape[0]


def whole(turns, arguments):
    bf16, f32 = jnp.bfloat16, jnp.float32
    heads, devices = lax.axis_size("head"), lax.axis_size("seq")
    pair = devices // turns
    rows, width = arguments["two"].shape
    tokens, wide = devices * rows, heads * width
    hidden = arguments["expand"].shape[1]
    lines = rows // 128
    shape = {name: value.shape for name, value in arguments.items()}
    results = dict(
        streams=((4, rows, width), bf16),
        projections=((2,) + shape["query"], f32),
        expand_part=(shape["expand"], f32),
        columns=((shape["merge"][0] + shape["shrink"][0], shape["merge"][1]), f32),
        norm_grads=((8, width), f32),
    )
    scratch = dict(
        params=((8, width), f32),
        keys=((tokens // 128, 1, 128), f32),
        shares=((8, 128), f32),
        unit_rows=((2, 8, 128), jnp.int32),
        until=((-(-(devices * (rows // GROUP + 1) + 1) // 128) * 128, 128), f32),
        block_row=((devices, 1, rows), jnp.int32),
        block_column=((tokens, 128), jnp.int16),
        chunk_row=((devices, 1, rows), jnp.int32),
        chunk_column=((tokens, 128), jnp.int16),
        sorted_query=((tokens, HEAD_DIM), bf16),
        unit=((tokens + GROUP, HEAD_DIM), bf16),
        key_value=((tokens + GROUP, HEAD_DIM), bf16),
        probs=((tokens, 2 * GROUP), f32),
        outs=((turns, pair, rows, HEAD_DIM), bf16),
        mix=((turns, pair, rows, HEAD_DIM), f32),
        rows_one=((rows, wide), bf16),
        center_one=((rows, 128), f32),
        factor_one=((rows, 128), f32),
        query_full=((wide, width), bf16),
        value_full=((wide, width), bf16),
        merge_full=((wide, wide), bf16),
        expand_full=((wide, hidden), bf16),
        shrink_full=((hidden, wide), bf16),
        one_full=((rows, wide), bf16),
        two_full=((rows, wide), bf16),
        grad_full=((rows, wide), bf16),
        attended_full=((rows, wide), bf16),
        everyone=((tokens, 2 * HEAD_DIM), bf16),
        mid=((devices * devices, rows // devices, 2 * HEAD_DIM), bf16),
        params_full=((8, wide), f32),
        packed=((pair, 2, rows, HEAD_DIM), bf16),
        round_rows=((tokens, 2 * HEAD_DIM), bf16),
        out_send=((turns - 1, pair, rows, HEAD_DIM), bf16),
        total_send=((turns - 1, pair, lines, 128), f32),
        totals=((turns, pair, lines, 128), f32),
        mix_rows=((turns, pair, lines, 128), f32),
        attended=((pair, rows, HEAD_DIM), bf16),
        tall=((rows, wide), f32),
        normal_two=((rows, width), f32),
        factor_two=((rows, 128), f32),
        rows_two=((rows, wide), bf16),
        active=((rows, hidden), bf16),
        grad_hidden=((rows, hidden), bf16),
        part_two=((rows, wide), bf16),
        stat_two=((2 * lines, 128), f32),
        parts_two=((heads - 1, rows, width), bf16),
        stats_two=((heads - 1, 2 * lines, 128), f32),
        stat_one=((2 * lines, 128), f32),
        parts_one=((heads - 1, rows, width), bf16),
        stats_one=((heads - 1, 2 * lines, 128), f32),
        feeds=((heads - 1, rows, width), bf16),
        grad_rows_one=((rows, wide), bf16),
        grad_heads=((pair, rows, HEAD_DIM), bf16),
        grad_attended=((pair, rows, HEAD_DIM), bf16),
        grad_total_send=((turns - 1, pair, lines, 128), f32),
        grad_outs=((turns, pair, rows, HEAD_DIM), bf16),
        grad_totals=((turns, pair, lines, 128), f32),
        grad_unit=((tokens + GROUP, HEAD_DIM), f32),
        grad_value=((tokens + GROUP, HEAD_DIM), f32),
        grad_pairs=((3, pair * rows, 2 * HEAD_DIM), bf16),
        grad_query=((rows, width), bf16),
        grad_key=((rows, width), bf16),
        norm_send=((8, width), f32),
        norms=((devices - 1, 8, width), f32),
    )
    for name, full in (
        ("query", (wide, width)),
        ("value", (wide, width)),
        ("merge", (width, wide)),
        ("expand", (wide, hidden)),
        ("shrink", (hidden, wide)),
    ):
        own = "grad_" + name + ("_full" if name in ("query", "value") else "")
        if name != "expand":
            scratch[own] = (full, bf16)
        scratch[name + "_pair"] = ((devices // 2,) + shape[name], bf16)
        scratch[name + "_line"] = ((devices // 2 - 1,) + shape[name], bf16)
    wires = dict(send=224, receive=224, local=2)
    vmem = pl.BlockSpec(memory_space=pltpu.VMEM)
    tables = dict(units=(8, 128), units_back=(8, 128))
    names = [*arguments, *results, *scratch, *tables, *wires]
    out = pl.pallas_call(
        partial(on_device, names, turns),
        out_shape=[jax.ShapeDtypeStruct(*item) for item in results.values()],
        in_specs=[vmem] * len(arguments),
        out_specs=[vmem] * len(results),
        scratch_shapes=[pltpu.VMEM(*item) for item in scratch.values()]
        + [pltpu.SMEM(item, jnp.int32) for item in tables.values()]
        + [pltpu.SemaphoreType.DMA((number,)) for number in wires.values()],
        compiler_params=pltpu.CompilerParams(
            collective_id=0, has_side_effects=True, vmem_limit_bytes=63 << 20
        ),
    )(*arguments.values())
    return SimpleNamespace(**dict(zip(results, out)))


def by_rounds(
    stream_one,
    stream_two,
    grad_one,
    grad_two,
    query_weight,
    value_weight,
    merge_weight,
    expand_weight,
    shrink_weight,
    first_gain,
    first_bias,
    second_gain,
    second_bias,
    bucket_ids,
    sort_order,
):
    arguments = dict(
        one=stream_one,
        two=stream_two,
        grad_one=grad_one,
        grad_two=grad_two,
        query=query_weight,
        value=value_weight,
        merge=merge_weight,
        expand=expand_weight,
        shrink=shrink_weight,
        gain_one=first_gain[None],
        bias_one=first_bias[None],
        gain_two=second_gain[None],
        bias_two=second_bias[None],
        bucket=bucket_ids,
        order=sort_order,
    )
    k = whole(sort_order.shape[0], arguments)
    merge_rows = merge_weight.shape[0]
    return (
        *(k.streams[i] for i in range(4)),
        k.projections[0],
        k.projections[1],
        k.columns[:merge_rows],
        k.expand_part,
        k.columns[merge_rows:],
        *(k.norm_grads[i] for i in range(4)),
    )


def solution(mesh):
    placed = (
        P("seq", "head"),
        P("seq", "head"),
        P("seq", "head"),
        P("seq", "head"),
        P("seq", "head"),
        P("seq", "head"),
        P("head", "seq"),
        P("seq", "head"),
        P("head", "seq"),
        P("head"),
        P("head"),
        P("head"),
        P("head"),
        P(),
        P(),
    )

    def local(*arguments):
        rounds = arguments[-1].shape[0]
        if mesh.shape["seq"] == HEADS == 2 * rounds and mesh.shape["head"] == rounds:
            return by_rounds(*arguments)
        return by_blocks(*arguments)

    return jax.shard_map(
        local,
        mesh=mesh,
        in_specs=placed,
        out_specs=(
            P("seq", "head"),
            P("seq", "head"),
            P("seq", "head"),
            P("seq", "head"),
            P("seq", "head"),
            P("seq", "head"),
            P("head", "seq"),
            P("seq", "head"),
            P("head", "seq"),
            P("head"),
            P("head"),
            P("head"),
            P("head"),
        ),
        check_vma=False,
    )
```

```python
from functools import partial
from types import SimpleNamespace

import jax
import jax.numpy as jnp
from jax import lax
from jax.experimental import pallas as pl
from jax.experimental.pallas import tpu as pltpu
from jax.sharding import PartitionSpec as P

HEADS = 8
HEAD_DIM = 128
GROUP = 64
MESH = pl.DeviceIdType.MESH


masked_score = -1000000000.0
own_score = -100000.0


def as_sent(shard):

    def short(part):
        return part.astype(jnp.bfloat16) if part.dtype == jnp.float32 else part

    return jax.tree.map(short, shard)


def from_behind(block, axis, distance):
    devices = range(lax.axis_size(axis))
    route = [(i - distance, i) for i in devices if i - distance in devices]
    return lax.ppermute(block, axis, route)


def row_sums(first, second):
    return lax.psum((first, second), "head")


def full_rows(part):
    return lax.all_gather(part, "head", axis=1, tiled=True)


def branch_sum(part):
    return lax.psum_scatter(part, "head", scatter_dimension=1, tiled=True)


def norm_forward(value, gain, shift):
    width = value.shape[1] * lax.axis_size("head")
    total, square = row_sums(
        jnp.sum(value, 1, keepdims=True), jnp.sum(value * value, 1, keepdims=True)
    )
    center = total / width
    spread = square / width - center * center
    factor = lax.rsqrt(spread + 1e-05)
    normal = (value - center) * factor
    return (normal, factor, normal * gain + shift)


def norm_backward(grad, normal, factor, gain):
    width = grad.shape[1] * lax.axis_size("head")
    scaled = grad * gain
    first, second = row_sums(
        jnp.sum(scaled, 1, keepdims=True), jnp.sum(scaled * normal, 1, keepdims=True)
    )
    result = factor * (scaled - first / width - normal * (second / width))
    return (result, jnp.sum(grad * normal, 0), jnp.sum(grad, 0))


def regroup_rows(buffer):
    turns = []
    for turn in range(buffer.shape[1]):
        turns.append(
            lax.all_to_all(buffer[:, turn], "seq", split_axis=0, concat_axis=0, tiled=True)
        )
    result = jnp.stack(turns, 1)
    return result


def regroup_totals(buffer):
    moved = lax.all_to_all(
        buffer.reshape(buffer.shape[0], -1, buffer.shape[3]),
        "seq",
        split_axis=0,
        concat_axis=0,
        tiled=True,
    )
    return moved.reshape(buffer.shape)


def regroup_pair(first, second):
    firsts = []
    seconds = []
    for turn in range(first.shape[1]):
        moved_first, moved_second = (
            lax.all_to_all(as_sent(first[:, turn]), "seq", split_axis=0, concat_axis=0, tiled=True),
            lax.all_to_all(
                as_sent(second[:, turn]), "seq", split_axis=0, concat_axis=0, tiled=True
            ),
        )
        firsts.append(moved_first)
        seconds.append(moved_second)
    result = (jnp.stack(firsts, 1), jnp.stack(seconds, 1))
    return result


def by_blocks(
    stream_one,
    stream_two,
    grad_one,
    grad_two,
    query_weight,
    value_weight,
    merge_weight,
    expand_weight,
    shrink_weight,
    first_gain,
    first_bias,
    second_gain,
    second_bias,
    bucket_ids,
    sort_order,
):
    devices = lax.axis_size("seq")
    place = lax.axis_index("seq")
    rows = stream_one.shape[0]
    rounds = sort_order.shape[0]
    capacity = 2 * rows // devices
    blocks = rows // GROUP
    heads_here = HEADS // lax.axis_size("head")
    local_width = heads_here * HEAD_DIM
    scale = HEAD_DIM ** (-0.5)
    round_index = jnp.arange(rounds, dtype=jnp.int32)[:, None]
    counter = jnp.arange(rows, dtype=jnp.int32)

    def invert(line):
        return jnp.zeros_like(line).at[line].set(jnp.arange(line.shape[0], dtype=jnp.int32))

    inverse = jax.vmap(invert)(sort_order)
    my_sorted = lax.dynamic_slice_in_dim(inverse, place * rows, rows, 1)
    send_block = my_sorted // rows
    same_block = send_block[:, :, None] == send_block[:, None, :]
    send_slot = jnp.sum(
        (same_block & (my_sorted[:, None, :] < my_sorted[:, :, None])).astype(jnp.int32), -1
    )
    block_tokens = lax.dynamic_slice_in_dim(sort_order, place * rows, rows, 1)
    source_block = block_tokens // rows
    earlier = counter[None, :] < counter[:, None]
    recv_slot = jnp.sum(
        ((source_block[:, :, None] == source_block[:, None, :]) & earlier[None]).astype(jnp.int32),
        -1,
    )
    query_bucket = jnp.take_along_axis(bucket_ids, block_tokens, 1)
    prior_start = (place - 1) % devices * rows + rows - GROUP
    prior_tokens = lax.dynamic_slice_in_dim(sort_order, prior_start, GROUP, 1)
    prior_bucket = jnp.take_along_axis(bucket_ids, prior_tokens, 1)

    def with_prior(own, prior):
        pieces = own.reshape((rounds, blocks, GROUP) + own.shape[2:])
        before = jnp.concatenate([prior[:, None], pieces[:, :-1]], 1)
        return jnp.concatenate([pieces, before], 2)

    query_place = block_tokens.reshape(rounds, blocks, GROUP)
    key_place = with_prior(block_tokens, prior_tokens)
    key_bucket = with_prior(query_bucket, prior_bucket)
    allowed = (key_place[:, :, None, :] <= query_place[:, :, :, None]) & (
        key_bucket[:, :, None, :] == query_bucket.reshape(rounds, blocks, GROUP)[:, :, :, None]
    )
    itself = key_place[:, :, None, :] == query_place[:, :, :, None]
    live = allowed & jnp.logical_not(itself)

    def fill(values, block, slot):
        empty = jnp.zeros((devices, rounds, capacity, values.shape[-1]), values.dtype)
        return empty.at[block, round_index, slot].set(values)

    normal_one, factor_one, normed_one = norm_forward(
        stream_two.astype(jnp.float32), first_gain, first_bias
    )
    rows_one = full_rows(normed_one.astype(jnp.bfloat16))
    query_full, value_full, merge_full = (
        lax.all_gather(query_weight, "seq", axis=0, tiled=True),
        lax.all_gather(value_weight, "seq", axis=0, tiled=True),
        lax.all_gather(merge_weight, "seq", axis=1, tiled=True),
    )
    queries = jnp.dot(rows_one, query_full, preferred_element_type=jnp.float32).astype(jnp.bfloat16)
    values = jnp.dot(rows_one, value_full, preferred_element_type=jnp.float32).astype(jnp.bfloat16)
    packed = jnp.concatenate([queries, values], 1)
    outgoing = fill(jnp.broadcast_to(packed[None], (rounds,) + packed.shape), send_block, send_slot)
    incoming = regroup_rows(outgoing)
    sorted_rows = incoming[source_block, round_index, recv_slot]
    sorted_query = sorted_rows[:, :, :local_width].reshape(rounds, rows, heads_here, HEAD_DIM)
    sorted_value = sorted_rows[:, :, local_width:].reshape(rounds, rows, heads_here, HEAD_DIM)
    query_float = sorted_query.astype(jnp.float32)
    inverse_norm = lax.rsqrt(jnp.sum(query_float * query_float, -1, keepdims=True) + 1e-06)
    unit_float = query_float * inverse_norm
    unit_low = unit_float.astype(jnp.bfloat16)
    edge = from_behind(
        jnp.concatenate([unit_low[:, -GROUP:], sorted_value[:, -GROUP:]], -1), "seq", 1
    )
    key_unit = with_prior(unit_low, edge[..., :HEAD_DIM])
    key_value = with_prior(sorted_value, edge[..., HEAD_DIM:])
    query_groups = sorted_query.reshape(rounds, blocks, GROUP, heads_here, HEAD_DIM)

    def masked_scores():
        raw = (
            jnp.einsum(
                "rncha,rnkha->rnhck", query_groups, key_unit, preferred_element_type=jnp.float32
            )
            * scale
        )
        return jnp.where(
            itself[:, :, None], own_score, jnp.where(allowed[:, :, None], raw, masked_score)
        )

    scores = masked_scores()
    peak = jnp.max(scores, -1, keepdims=True)
    totals = peak + jnp.log(jnp.sum(jnp.exp(scores - peak), -1, keepdims=True))
    probs_low = jnp.exp(scores - totals).astype(jnp.bfloat16)
    round_out = jnp.einsum(
        "rnhck,rnkha->rncha", probs_low, key_value, preferred_element_type=jnp.float32
    ).astype(jnp.bfloat16)
    out_flat = round_out.reshape(rounds, rows, local_width)
    total_flat = jnp.transpose(totals[..., 0], (0, 1, 3, 2)).reshape(rounds, rows, heads_here)
    token_out = regroup_rows(fill(out_flat, source_block, recv_slot))[
        send_block, round_index, send_slot
    ].astype(jnp.float32)
    token_total = regroup_totals(fill(total_flat, source_block, recv_slot))[
        send_block, round_index, send_slot
    ]
    mix = jax.nn.softmax(token_total, axis=0)
    token_out4 = token_out.reshape(rounds, rows, heads_here, HEAD_DIM)
    attended_low = (
        jnp.sum(mix[..., None] * token_out4, 0).reshape(rows, local_width).astype(jnp.bfloat16)
    )
    sum_one = stream_one.astype(jnp.float32) + branch_sum(
        jnp.dot(attended_low, merge_full, preferred_element_type=jnp.float32)
    )
    normal_two, factor_two, normed_two = norm_forward(sum_one, second_gain, second_bias)
    rows_two = full_rows(normed_two.astype(jnp.bfloat16))
    expand_full, shrink_full = (
        lax.all_gather(expand_weight, "seq", axis=0, tiled=True),
        lax.all_gather(shrink_weight, "seq", axis=1, tiled=True),
    )
    hidden = jnp.dot(rows_two, expand_full, preferred_element_type=jnp.float32)
    active, gelu_pull = jax.vjp(partial(jax.nn.gelu, approximate=False), hidden)
    active_low = active.astype(jnp.bfloat16)
    sum_two = stream_two.astype(jnp.float32) + branch_sum(
        jnp.dot(active_low, shrink_full, preferred_element_type=jnp.float32)
    )
    grad_rows_two = full_rows(grad_two)
    grad_active = jnp.dot(grad_rows_two, shrink_full.T, preferred_element_type=jnp.float32)
    grad_hidden = gelu_pull(grad_active)[0].astype(jnp.bfloat16)
    grad_shrink = jnp.dot(active_low.T, grad_rows_two, preferred_element_type=jnp.float32)
    grad_expand = jnp.dot(rows_two.T, grad_hidden, preferred_element_type=jnp.float32)
    grad_normed_two = branch_sum(
        jnp.dot(grad_hidden, expand_full.T, preferred_element_type=jnp.float32)
    )
    extra_one, grad_second_gain, grad_second_bias = norm_backward(
        grad_normed_two, normal_two, factor_two, second_gain
    )
    total_one = grad_one.astype(jnp.float32) + extra_one
    total_low = total_one.astype(jnp.bfloat16)
    grad_rows_one = full_rows(total_low)
    grad_attended = jnp.dot(grad_rows_one, merge_full.T, preferred_element_type=jnp.float32).astype(
        jnp.bfloat16
    )
    grad_merge = jnp.dot(attended_low.T, grad_rows_one, preferred_element_type=jnp.float32)
    grad_float = grad_attended.astype(jnp.float32).reshape(rows, heads_here, HEAD_DIM)
    dots = jnp.sum(token_out4 * grad_float[None], -1)
    grad_total = mix * (dots - jnp.sum(mix * dots, 0, keepdims=True))
    grad_out_low = (
        (mix[..., None] * grad_float[None]).astype(jnp.bfloat16).reshape(rounds, rows, local_width)
    )
    sorted_grad_out = regroup_rows(fill(grad_out_low, send_block, send_slot))[
        source_block, round_index, recv_slot
    ]
    sorted_grad_total = regroup_totals(fill(grad_total, send_block, send_slot))[
        source_block, round_index, recv_slot
    ]
    grad_groups = sorted_grad_out.reshape(rounds, blocks, GROUP, heads_here, HEAD_DIM)
    total_grad_groups = jnp.transpose(
        sorted_grad_total.reshape(rounds, blocks, GROUP, heads_here), (0, 1, 3, 2)
    )[..., None]
    probs = jnp.exp(masked_scores() - totals)
    probs_again = probs.astype(jnp.bfloat16)
    grad_probs = jnp.einsum(
        "rncha,rnkha->rnhck", grad_groups, key_value, preferred_element_type=jnp.float32
    )
    grad_key_value = jnp.einsum(
        "rnhck,rncha->rnkha", probs_again, grad_groups, preferred_element_type=jnp.float32
    )
    inner = jnp.sum(probs * grad_probs, -1, keepdims=True)
    grad_scores = jnp.where(
        live[:, :, None], probs * (grad_probs - inner + total_grad_groups), 0.0
    ).astype(jnp.bfloat16)
    grad_query_groups = (
        jnp.einsum("rnhck,rnkha->rncha", grad_scores, key_unit, preferred_element_type=jnp.float32)
        * scale
    )
    grad_key_unit = (
        jnp.einsum(
            "rnhck,rncha->rnkha", grad_scores, query_groups, preferred_element_type=jnp.float32
        )
        * scale
    )
    edge_grad = from_behind(
        jnp.concatenate([grad_key_unit[:, 0, GROUP:], grad_key_value[:, 0, GROUP:]], -1).astype(
            jnp.bfloat16
        ),
        "seq",
        -1,
    ).astype(jnp.float32)

    def fold_keys(grad_keys, arriving):
        own = grad_keys[:, :, :GROUP]
        later = jnp.concatenate([grad_keys[:, 1:, GROUP:], arriving[:, None]], 1)
        return (own + later).reshape(rounds, rows, heads_here, HEAD_DIM)

    grad_unit = fold_keys(grad_key_unit, edge_grad[..., :HEAD_DIM])
    grad_sorted_value = fold_keys(grad_key_value, edge_grad[..., HEAD_DIM:])
    grad_sorted_query = grad_query_groups.reshape(
        rounds, rows, heads_here, HEAD_DIM
    ) + inverse_norm * (grad_unit - unit_float * jnp.sum(unit_float * grad_unit, -1, keepdims=True))
    moved_first, moved_second = regroup_pair(
        fill(grad_sorted_query.reshape(rounds, rows, local_width), source_block, recv_slot),
        fill(grad_sorted_value.reshape(rounds, rows, local_width), source_block, recv_slot),
    )
    token_grad_query = moved_first[send_block, round_index, send_slot]
    token_grad_value = moved_second[send_block, round_index, send_slot]
    grad_query_low = jnp.sum(token_grad_query, 0).astype(jnp.bfloat16)
    grad_value_low = jnp.sum(token_grad_value, 0).astype(jnp.bfloat16)
    grad_query_full = jnp.dot(rows_one.T, grad_query_low, preferred_element_type=jnp.float32)
    grad_value_full = jnp.dot(rows_one.T, grad_value_low, preferred_element_type=jnp.float32)
    grad_normed_one = branch_sum(
        jnp.dot(grad_query_low, query_full.T, preferred_element_type=jnp.float32)
        + jnp.dot(grad_value_low, value_full.T, preferred_element_type=jnp.float32)
    )
    extra_two, grad_first_gain, grad_first_bias = norm_backward(
        grad_normed_one, normal_one, factor_one, first_gain
    )
    input_grad_two = (grad_two.astype(jnp.float32) + extra_two).astype(jnp.bfloat16)
    query_part, value_part, merge_part, expand_part, shrink_part = (
        lax.psum_scatter(grad_query_full, "seq", scatter_dimension=0, tiled=True),
        lax.psum_scatter(grad_value_full, "seq", scatter_dimension=0, tiled=True),
        lax.psum_scatter(grad_merge, "seq", scatter_dimension=1, tiled=True),
        lax.psum_scatter(grad_expand, "seq", scatter_dimension=0, tiled=True),
        lax.psum_scatter(grad_shrink, "seq", scatter_dimension=1, tiled=True),
    )
    first_gain_sum, first_bias_sum, second_gain_sum, second_bias_sum = lax.psum(
        (grad_first_gain, grad_first_bias, grad_second_gain, grad_second_bias), "seq"
    )
    return (
        sum_one.astype(jnp.bfloat16),
        sum_two.astype(jnp.bfloat16),
        total_low,
        input_grad_two,
        query_part,
        value_part,
        merge_part,
        expand_part,
        shrink_part,
        first_gain_sum,
        first_bias_sum,
        second_gain_sum,
        second_bias_sum,
    )


def flip(index, bit):
    return index + bit - 2 * bit * ((index // bit) % 2)


def flipped(index, bits):
    for bit in (1, 2, 4):
        if bits & bit:
            index = flip(index, bit)
    return index


class Place:
    def __init__(self):
        self.seq, self.head = lax.axis_index("seq"), lax.axis_index("head")
        self.line, self.side = self.seq // 2, self.seq % 2
        self.pair, self.core = self.head // 2, self.head % 2
        self.turn = self.side * 2 + self.core
        self.home = self.line // 2 == self.core
        self.away = self.line // 2 != self.core

    def peer(self, seq_bits, head_bits=0):
        return (flipped(self.seq, seq_bits), flipped(self.head, head_bits))

    def member(self, bits):
        return self.peer(bits // 2, bits % 2)

    def chunk(self, turn, half):
        return (2 * (turn % 2) + half) * 2 + turn // 2

    def greet(self):
        peers = [self.peer(bits) for bits in range(1, 8)]
        peers += [self.peer(0, bits) for bits in range(1, 4)]
        peers += [self.peer(bits, 1) for bits in (1, 2, 4, 6)]
        barrier = pltpu.get_barrier_semaphore()
        for peer in peers:
            pl.semaphore_signal(barrier, inc=1, device_id=peer, device_id_type=MESH)
        return partial(pl.semaphore_wait, barrier, len(peers))


class Copy:
    def __init__(self, copy, starts, lands):
        self.copy, self.starts, self.lands = copy, starts, lands
        self.when(starts, copy.start)

    def when(self, condition, act):
        if condition is None:
            act()
        else:
            pl.when(condition)(act)

    def wait_recv(self):
        self.when(self.lands, self.copy.wait_recv)

    def wait_send(self):
        self.when(self.starts, self.copy.wait_send)


class Wires:
    def __init__(self, send, receive):
        self.send, self.receive, self.copies = send, receive, []

    def push(self, source, target, device, starts=None, lands=None):
        index = len(self.copies)
        copy = pltpu.make_async_remote_copy(
            src_ref=source,
            dst_ref=target,
            send_sem=self.send.at[index],
            recv_sem=self.receive.at[index],
            device_id=device,
            device_id_type=MESH,
        )
        self.copies.append(Copy(copy, starts, lands))
        return self.copies[-1]

    def settle(self, copies):
        for copy in copies:
            copy.wait_send()
        done = [id(copy) for copy in copies]
        self.copies = [None if id(copy) in done else copy for copy in self.copies]

    def drain(self):
        self.settle([copy for copy in self.copies if copy is not None])


class Spread:
    def __init__(self, wires, place):
        self.wires, self.place, self.copies = wires, place, []

    def start(self, source_at, target, half=None):
        p = self.place
        for bits, starts in ((4, p.away), (6, p.away), (2, p.home)):
            seq = flipped(p.seq, bits)
            head = p.head - p.core + p.line // 2
            lands = starts
            if half is not None:
                starts = jnp.logical_and(starts, (seq // 2) % 2 == half)
                lands = jnp.logical_and(lands, p.line % 2 == half)
            copy = self.wires.push(source_at(seq // 2), target, (seq, head), starts, lands)
            self.copies.append(copy)

    def finish(self):
        for copy in self.copies:
            copy.wait_recv()


class TokenGather:
    def __init__(self, wires, place, everyone, rows):
        self.wires, self.place, self.everyone, self.rows = wires, place, everyone, rows
        self.line = {2: [], 4: [], 6: []}
        self.own = []

    def slot(self, seq, part):
        return columns_at(rows_at(self.everyone, seq, self.rows), part, HEAD_DIM)

    def start(self, packed, part):
        p = self.place
        mine = self.slot(p.seq, part)
        for bits, starts in ((4, p.away), (6, p.away), (2, p.home)):
            seq = flipped(p.seq, bits)
            self.line[bits].append(
                self.wires.push(
                    packed.at[(seq // 2) % 2, part],
                    mine,
                    (seq, p.head - p.core + part),
                    starts,
                    p.core == part,
                )
            )
        source = packed.at[p.line % 2, part]
        self.own.append(self.wires.push(source, mine, p.peer(0, 1), p.home, p.away))

        @pl.when(p.home)
        def _():
            mine[...] = source[...]

    def pass_own(self):
        p = self.place
        for copy in self.own:
            copy.wait_recv()
        block = self.slot(p.seq, p.core)
        self.beside = {0: self.wires.push(block, block, p.peer(1))}
        self.shared = {}

    def forward(self, bits):
        p = self.place
        for copy in self.line[bits]:
            copy.wait_recv()
        block = self.slot(flipped(p.seq, bits), p.core)
        self.beside[bits] = self.wires.push(block, block, p.peer(1))
        self.shared[bits] = self.wires.push(block, block, p.peer(0, 1))

    def share(self, bits):
        p = self.place
        self.beside[bits].wait_recv()
        block = self.slot(flipped(p.seq, bits + 1), p.core)
        self.shared[bits + 1] = self.wires.push(block, block, p.peer(0, 1))

    def land(self, bits):
        self.shared[bits].wait_recv()

    def settle(self):
        lines = [copy for copies in self.line.values() for copy in copies]
        self.wires.settle(lines + self.own + [*self.beside.values(), *self.shared.values()])


class SeqGather:
    def __init__(self, wires, place, slot):
        self.wires, self.place, self.slot = wires, place, slot

    def start(self, source, for_far=None):
        p, mine = self.place, self.slot(self.place.seq)
        far = source if for_far is None else for_far
        self.arriving = {4: self.wires.push(far, mine, p.peer(4))}
        self.arriving[2] = self.wires.push(source, mine, p.peer(2))
        self.beside = {0: self.wires.push(source, mine, p.peer(1))}

    def forward(self, bits):
        p = self.place
        self.arriving[bits].wait_recv()
        block = self.slot(flipped(p.seq, bits))
        if bits == 4:
            self.arriving[6] = self.wires.push(block, block, p.peer(2))
        self.beside[bits] = self.wires.push(block, block, p.peer(1))

    def land(self, bits):
        self.beside[bits].wait_recv()

    def settle(self):
        self.wires.settle([*self.arriving.values(), *self.beside.values()])

    def finish(self):
        for bits in self.beside:
            self.land(bits)
        self.settle()


class PairGather:
    def __init__(self, wires, place, slot, both):
        self.wires, self.place, self.slot, self.both = wires, place, slot, both

    def start(self, source):
        p = self.place
        self.first = self.wires.push(source, self.slot(p.seq), p.peer(1))

    def along(self):
        p = self.place
        self.first.wait_recv()
        pair = self.both(p.seq // 2)
        self.far = self.wires.push(pair, pair, p.peer(4))
        self.near = self.wires.push(pair, pair, p.peer(2))

    def forward(self):
        p = self.place
        self.far.wait_recv()
        pair = self.both(flip(p.seq, 4) // 2)
        self.last = self.wires.push(pair, pair, p.peer(2))

    def finish(self):
        self.near.wait_recv()
        self.last.wait_recv()
        self.wires.settle([self.first, self.far, self.near, self.last])


class HeadGather:
    def __init__(self, wires, place, slot):
        self.wires, self.place, self.slot = wires, place, slot

    def start(self, source):
        p = self.place
        mine = self.slot(p.head)
        self.long = self.wires.push(source, mine, p.peer(0, 2))
        self.short = self.wires.push(source, mine, p.peer(0, 1))

    def relay(self):
        p = self.place
        self.long.wait_recv()
        moved = self.slot(flip(p.head, 2))
        self.last = self.wires.push(moved, moved, p.peer(0, 1))

    def finish(self):
        self.short.wait_recv()
        self.last.wait_recv()
        self.wires.settle([self.long, self.short, self.last])


def columns_at(ref, index, width):
    return ref.at[:, pl.ds(pl.multiple_of(index * width, width), width)]


def rows_at(ref, index, width):
    return ref.at[pl.ds(pl.multiple_of(index * width, width), width)]


def span(index, width):
    return pl.ds(pl.multiple_of(index * width, width), width)


def dot(left, right, contract=((1,), (0,))):
    return lax.dot_general(
        left, right, (contract, ((), ())), preferred_element_type=jnp.float32
    )


def diagonal(size):
    return lax.broadcasted_iota(jnp.int32, (size, size), 0) == lax.broadcasted_iota(
        jnp.int32, (size, size), 1
    )


def to_row(column):
    return jnp.sum(jnp.where(diagonal(column.shape[0]), column, 0.0), 0, keepdims=True)


def to_column(row):
    return jnp.sum(jnp.where(diagonal(row.shape[1]), row, 0.0), 1, keepdims=True)


def in_lanes(total):
    bf16, f32 = jnp.bfloat16, jnp.float32
    high = total.astype(bf16).astype(f32)
    middle = (total - high).astype(bf16).astype(f32)
    low = total - high - middle
    lane = lax.broadcasted_iota(jnp.int32, (total.shape[0], 128), 1)
    parts = jnp.where(lane == 0, high, jnp.where(lane == 1, middle, low))
    return jnp.where(lane < 3, parts, 0.0).astype(bf16)


class SeqScatter:
    def __init__(self, wires, place, piece, pair, line):
        self.wires, self.place, self.piece = wires, place, piece
        self.pair, self.line = pair, line

    def start(self):
        p = self.place
        self.beside = {}
        for bits in (6, 2, 4, 0):
            source = self.piece(flipped(p.seq, bits + 1))
            self.beside[bits] = self.wires.push(source, self.pair.at[bits // 2], p.peer(1))

    def add(self, bits, more=None):
        at, f32 = self.pair.at[bits // 2], jnp.float32
        self.beside[bits].wait_recv()
        mine = self.piece(flipped(self.place.seq, bits))[...]
        total = at[...].astype(f32) + mine.astype(f32)
        if more is not None:
            total += more[...].astype(f32)
        at[...] = total.astype(jnp.bfloat16)
        return at

    def along(self):
        device = self.place.peer(2)
        self.shares = self.wires.push(self.add(6), self.line.at[0], device)
        self.near = self.wires.push(self.add(2), self.line.at[1], device)

    def across(self):
        self.shares.wait_recv()
        total = self.add(4, self.line.at[0])
        self.far = self.wires.push(total, self.line.at[2], self.place.peer(4))

    def finish(self, target):
        p, f32 = self.place, jnp.float32
        self.beside[0].wait_recv()
        total = self.piece(p.seq)[...].astype(f32) + self.pair.at[0][...].astype(f32)
        self.near.wait_recv()
        total += self.line.at[1][...].astype(f32)
        self.far.wait_recv()
        target[...] = total + self.line.at[2][...].astype(f32)


class PairScatter:
    def __init__(self, wires, place, piece, both, line, pair):
        self.wires, self.place, self.piece, self.both = wires, place, piece, both
        self.line, self.pair = line, pair

    def start(self):
        p, device = self.place, self.place.peer(2)
        share, near = (self.both(flipped(p.seq, bits) // 2) for bits in (6, 2))
        self.shares = self.wires.push(share, self.line.at[0], device)
        self.near = self.wires.push(near, self.line.at[1], device)

    def across(self):
        p, f32 = self.place, jnp.float32
        self.shares.wait_recv()
        mine = self.both(flip(p.seq, 4) // 2)
        at = self.line.at[0]
        at[...] = (at[...].astype(f32) + mine[...].astype(f32)).astype(jnp.bfloat16)
        self.far = self.wires.push(at, self.line.at[2], p.peer(4))

    def side(self):
        p, f32 = self.place, jnp.float32
        self.near.wait_recv()
        self.far.wait_recv()
        mine = self.both(p.seq // 2)
        total = mine[...].astype(f32) + self.line.at[1][...].astype(f32)
        total += self.line.at[2][...].astype(f32)
        self.wires.settle([self.near])
        mine[...] = total.astype(jnp.bfloat16)
        self.last = self.wires.push(self.piece(flip(p.seq, 1)), self.pair, p.peer(1))

    def finish(self, target):
        self.last.wait_recv()
        f32 = jnp.float32
        target[...] = self.piece(self.place.seq)[...].astype(f32) + self.pair[...].astype(f32)


class Phases:
    def __init__(self, r, turns):
        self.r, self.turns = r, turns
        self.place = Place()
        self.wires = Wires(r.send, r.receive)
        self.rows, self.width = r.two.shape
        self.wide = r.rows_one.shape[1]
        self.count = self.wide // self.width
        self.devices = r.everyone.shape[0] // self.rows
        self.pair = self.devices // turns
        self.units = self.devices


    def spread_columns(self, ref, index):
        column = ref[span(index, self.rows), :].astype(jnp.int32)
        lane = lax.broadcasted_iota(jnp.int32, column.shape, 1)
        parts = [
            jnp.where(column == lane + 128 * i, 1.0, 0.0).astype(jnp.bfloat16)
            for i in range(self.rows // 128)
        ]
        return jnp.concatenate(parts, 1)

    def spread_rows(self, ref, index):
        row = ref[index]
        place = lax.broadcasted_iota(jnp.int32, (self.rows, self.rows), 0)
        return jnp.where(row == place, 1.0, 0.0).astype(jnp.bfloat16)

    def from_units(self, ref, table, index):
        return jnp.concatenate([ref[table[index, unit]] for unit in range(self.units)], 0)

    def to_units(self, index, rows):
        first, step = index * self.units, self.rows // self.units
        for unit in range(self.units):
            self.r.mid[first + unit] = rows[unit * step : (unit + 1) * step].astype(jnp.bfloat16)

    def sort_chunk(self, source, index):
        r = self.r
        here = span(index, self.rows)
        self.to_units(index, dot(self.spread_columns(r.chunk_column, index), source[here, :]))

    def sorted_block(self, index):
        r = self.r
        return dot(
            self.spread_columns(r.block_column, index), self.from_units(r.mid, r.units, index)
        )

    def unsort_block(self, source, index):
        r = self.r
        here = span(index, self.rows)
        self.to_units(index, dot(self.spread_rows(r.block_row, index), source[here, :]))

    def unsorted_chunk(self, index):
        r = self.r
        return dot(
            self.spread_rows(r.chunk_row, index), self.from_units(r.mid, r.units_back, index)
        )

    def column_of(self, row):
        pieces = [to_column(row[:, i : i + 128]) for i in range(0, self.rows, 128)]
        return jnp.concatenate(pieces, 0)

    def row_of(self, column):
        pieces = [to_row(column[i : i + 128]) for i in range(0, self.rows, 128)]
        return jnp.concatenate(pieces, 1)

    def wide_column(self, column):
        return jnp.broadcast_to(column, (self.rows, 128)).astype(jnp.int32).astype(jnp.int16)

    def line_of(self, ref, block):
        return ref[pl.ds(self.place.turn, 1), span(block, self.rows)]

    def unit_tables(self):
        r = self.r
        bf16, f32, i32 = jnp.bfloat16, jnp.float32, jnp.int32
        unit = self.rows // self.units
        row = lax.broadcasted_iota(i32, (128, 128), 0)
        column = lax.broadcasted_iota(i32, (128, 128), 1)
        by_chunk = r.shares[...].astype(bf16)
        by_block = dot(by_chunk, jnp.where(row == column, 1.0, 0.0).astype(bf16)[:8], ((0,), (0,)))
        by_block = by_block[:8].astype(bf16)
        earlier = jnp.where(row < column, 1.0, 0.0).astype(bf16)
        below = jnp.where(row > column, 1.0, 0.0).astype(bf16)[:8, :8]
        start = (column[:8] * unit).astype(f32)

        def find(share, offset, other):
            segment, move = jnp.zeros((8, 128), f32), jnp.zeros((8, 128), f32)
            ends = offset + share.astype(f32)
            for i in range(self.units):
                segment += jnp.where(ends[:, i : i + 1] <= start, 1.0, 0.0)
            for i in range(self.units):
                shift = (other - offset)[:, i : i + 1]
                move += jnp.where(segment == float(i), shift, 0.0)
            place = ((segment * self.rows + start + move) * (1.0 / unit)).astype(i32)
            return jnp.clip(place, 0, self.units * self.units - 1)

        in_chunk, in_block = dot(by_chunk, earlier), dot(below, by_chunk)
        r.unit_rows[1] = find(by_chunk, in_chunk, in_block)
        r.unit_rows[0] = find(by_block, dot(by_block, earlier), dot(below, by_block))
        copies = [
            pltpu.make_async_copy(r.unit_rows.at[i], target, r.local.at[i])
            for i, target in enumerate((r.units, r.units_back))
        ]
        for copy in copies:
            copy.start()
        for copy in copies:
            copy.wait()

    def bucket_tables(self):
        r = self.r
        f32, i32 = jnp.float32, jnp.int32
        rows = self.rows
        most = -(-(self.devices * (rows // GROUP + 1) + 1) // 128) * 128

        value = lax.broadcasted_iota(i32, (most, rows), 0)

        def count(block, until):
            return until + jnp.sum(
                jnp.where(self.line_of(r.bucket, block) <= value, 1.0, 0.0), 1, keepdims=True
            )

        until = lax.fori_loop(0, self.devices, count, jnp.zeros((most, 1), f32))
        r.until[...] = jnp.broadcast_to(until, (most, 128))

    def block_tables(self, start, stop):
        r = self.r
        bf16, f32, i32 = jnp.bfloat16, jnp.float32, jnp.int32
        rows, lines = self.rows, self.rows // 128
        tokens = rows * self.devices

        def first(block, carry):
            order = self.line_of(r.order, block)
            until = r.until[:, 0:1].astype(i32)
            lane = lax.broadcasted_iota(i32, (1, rows), 1)
            bucket = jnp.sum(
                jnp.where(until <= lane + block * rows, 1.0, 0.0), 0, keepdims=True
            )
            key = bucket * tokens + order.astype(f32)
            for i in range(lines):
                r.keys[block * lines + i] = key[:, i * 128 : (i + 1) * 128]
            chunk = order // rows
            each = lax.broadcasted_iota(i32, (8, rows), 0)
            share = jnp.sum(jnp.where(chunk == each, 1.0, 0.0), 1, keepdims=True)
            at = lax.broadcasted_iota(i32, (8, 128), 1)
            r.shares[...] += jnp.where(at == block, share, 0.0)
            place = (chunk * rows + lane).astype(f32)
            slot = jnp.sum(jnp.where(place < self.column_of(place), 1.0, 0.0), 1, keepdims=True)
            r.block_column[span(block, rows), :] = self.wide_column(slot)
            r.block_row[block] = self.row_of(slot).astype(i32)
            local = self.column_of((order - chunk * rows).astype(f32))
            high = jnp.floor(local * 0.0625)
            at = lax.broadcasted_iota(i32, (rows, 2 * HEAD_DIM), 1)
            parts = jnp.where(at == 0, high, jnp.where(at == 1, local - 16.0 * high, 0.0))
            r.round_rows[span(block, rows), :] = parts.astype(bf16)
            self.unsort_block(r.round_rows, block)
            return carry

        lax.fori_loop(start, stop, first, 0)

    def chunk_tables(self):
        r = self.r
        f32, i32 = jnp.float32, jnp.int32
        rows = self.rows

        def second(chunk, carry):
            parts = self.from_units(r.mid, r.units_back, chunk)[:, 0:128].astype(f32)
            token = 16.0 * parts[:, 0:1] + parts[:, 1:2]
            r.chunk_column[span(chunk, rows), :] = self.wide_column(token)
            r.chunk_row[chunk] = self.row_of(token).astype(i32)
            return carry

        lax.fori_loop(0, self.devices, second, 0)

    def codes(self, index):
        r = self.r
        tokens = self.rows * self.devices
        groups = tokens // 128
        low = lax.broadcasted_iota(jnp.int32, (1, 128), 1) < GROUP
        result = []
        for i in range(2):
            here = 2 * index + i
            keys, before = r.keys[here], r.keys[(here + groups - 1) % groups]
            query = to_column(keys)
            least = jnp.floor(query * (1.0 / tokens)) * tokens
            for half, window in enumerate((jnp.where(low, keys, before), keys)):
                at = slice(half * GROUP, (half + 1) * GROUP)
                allowed = (window <= query[at]) & (window >= least[at])
                result.append(
                    jnp.where(window == query[at], 1.0, jnp.where(allowed, 0.0, 2.0))
                )
        return jnp.concatenate(result, 0)

    def window(self, rows, block):
        before = rows[block * GROUP : (block + 1) * GROUP]
        own = rows[(block + 1) * GROUP : (block + 2) * GROUP]
        return jnp.concatenate([own, before] if block % 2 == 0 else [before, own], 0)

    def over_rows(self, ref):
        step = ref.shape[0] // self.devices
        return SeqGather(self.wires, self.place, lambda seq: rows_at(ref, seq, step))

    def over_columns(self, ref):
        step = ref.shape[1] // self.devices
        return SeqGather(self.wires, self.place, lambda seq: columns_at(ref, seq, step))

    def start_seq(self, gather, source):
        gather.start(source)
        gather.slot(self.place.seq)[...] = source[...]

    def start_head(self, gather, source):
        gather.start(source)
        gather.slot(self.place.head)[...] = source[...]

    def over_head(self, ref):
        return HeadGather(self.wires, self.place, lambda head: columns_at(ref, head, self.width))

    def project(self):
        r, place, wires = self.r, self.place, self.wires
        bf16, f32 = jnp.bfloat16, jnp.float32
        arrived = place.greet()
        half = self.devices // 2
        r.shares[...] = jnp.zeros_like(r.shares)
        self.bucket_tables()
        self.block_tables(0, half)
        arrived()
        stream = self.over_head(r.two_full)
        small = self.over_head(r.params_full)
        self.start_head(stream, r.two)
        for row, item in enumerate((r.gain_one, r.bias_one, r.gain_two, r.bias_two)):
            r.params[row : row + 1, :] = item[...]
        r.params[4:8, :] = jnp.zeros((4, self.width), f32)
        self.start_head(small, r.params)
        query, value = self.over_rows(r.query_full), self.over_rows(r.value_full)
        self.start_seq(query, r.query)
        self.start_seq(value, r.value)
        self.bulk()
        self.begin(self.merge)
        self.begin(self.expand[0])
        self.block_tables(half, self.devices)
        for weight in (query, value):
            for bits in (4, 2):
                weight.forward(bits)
        self.begin(self.expand[1])
        small.relay()
        stream.relay()
        query.forward(6)
        value.forward(6)
        small.finish()
        stream.finish()

        def normalise(tile, carry):
            here = span(tile, 128)
            rows = r.two_full[here, :].astype(f32)
            center = jnp.mean(rows, 1, keepdims=True)
            offset = rows - center
            factor = lax.rsqrt(jnp.mean(offset * offset, 1, keepdims=True) + 1e-05)
            r.center_one[here, :] = jnp.broadcast_to(center, (128, 128))
            r.factor_one[here, :] = jnp.broadcast_to(factor, (128, 128))
            r.rows_one[here, :] = (
                offset * factor * r.params_full[0:1, :] + r.params_full[1:2, :]
            ).astype(bf16)
            return carry

        lax.fori_loop(0, self.rows // 128, normalise, 0)
        self.tokens = TokenGather(self.wires, place, r.everyone, self.rows)
        self.project_one(query, r.query_full, 0)
        self.project_one(value, r.value_full, 1)

    def project_one(self, weight, full, part):
        r = self.r
        weight.finish()

        def multiply(tile, carry):
            here = span(tile, 256)
            result = dot(r.rows_one[here, :], full[...]).astype(jnp.bfloat16)
            for which in range(self.pair):
                r.packed[which, part, here, :] = result[
                    :, which * HEAD_DIM : (which + 1) * HEAD_DIM
                ]
            return carry

        lax.fori_loop(0, self.rows // 256, multiply, 0)
        self.tokens.start(r.packed, part)

    def bulk(self):
        r, place = self.r, self.place
        my_rows = rows_at(r.merge_full, place.head, r.merge.shape[0])
        self.merge = SeqGather(
            self.wires, place, lambda seq: columns_at(my_rows, seq, r.merge.shape[1])
        )
        self.merge.source = r.merge
        self.expand, self.shrink = [], []
        for part in range(2):
            step, columns = r.expand.shape[0], r.expand.shape[1] // 2
            cut = pl.ds(part * columns, columns)
            slot = lambda seq, cut=cut: rows_at(r.expand_full, seq, step).at[:, cut]
            if part:
                gather = SeqGather(self.wires, place, slot)
            else:
                both = lambda pair: rows_at(r.expand_full, pair, 2 * step).at[:, 0:columns]
                gather = PairGather(self.wires, place, slot, both)
            gather.source = r.expand.at[:, cut]
            self.expand.append(gather)
            rows, width = r.shrink.shape[0] // 2, r.shrink.shape[1]
            down = pl.ds(part * rows, rows)
            gather = SeqGather(
                self.wires,
                place,
                lambda seq, down=down: columns_at(r.shrink_full.at[down], seq, width),
            )
            gather.source = r.shrink.at[down]
            self.shrink.append(gather)
        self.one, self.grads = self.over_head(r.one_full), self.over_head(r.grad_full)

    def begin(self, gather):
        self.start_seq(gather, gather.source)

    def go_on(self, gather):
        for bits in (4, 2, 6):
            gather.forward(bits)

    def begin_streams(self):
        self.start_head(self.one, self.r.one)
        self.start_head(self.grads, self.r.grad_two)

    def begin_merge_rows(self):
        r, place = self.r, self.place
        self.merge.finish()
        self.heads = HeadGather(
            self.wires, place, lambda head: rows_at(r.merge_full, head, r.merge.shape[0])
        )
        self.heads.start(self.heads.slot(place.head))

    def sort_tokens(self):
        r, place = self.r, self.place
        bf16, f32 = jnp.bfloat16, jnp.float32
        tokens = self.tokens
        self.unit_tables()
        tokens.pass_own()
        for bits in (2, 4, 6):
            tokens.forward(bits)
        self.go_on(self.merge)
        self.go_on(self.expand[1])
        self.expand[0].along()
        self.begin_streams()
        self.begin(self.shrink[0])
        self.chunk_tables()
        self.sort_chunk(r.everyone, place.seq)
        for bits in (2, 4, 6):
            tokens.land(bits)
            self.sort_chunk(r.everyone, flipped(place.seq, bits))
        for bits in (0, 2, 4, 6):
            tokens.share(bits)
        for bits in (0, 2, 4, 6):
            tokens.land(bits + 1)
            self.sort_chunk(r.everyone, flipped(place.seq, bits + 1))
        tokens.settle()

        def second(block, carry):
            rows = self.sorted_block(block)
            here = span(block, self.rows)
            later = pl.ds(pl.multiple_of(block * self.rows + GROUP, GROUP), self.rows)
            query = rows[:, :HEAD_DIM]
            r.sorted_query[here, :] = query.astype(bf16)
            factor = lax.rsqrt(jnp.sum(query * query, 1, keepdims=True) + 1e-06)
            r.unit[later, :] = (query * factor).astype(bf16)
            r.key_value[later, :] = rows[:, HEAD_DIM:].astype(bf16)
            return carry

        lax.fori_loop(0, self.devices, second, 0)
        last = pl.ds(self.devices * self.rows, GROUP)
        r.unit[0:GROUP, :] = r.unit[last, :]
        r.key_value[0:GROUP, :] = r.key_value[last, :]

    def attend(self):
        r = self.r
        bf16, f32 = jnp.bfloat16, jnp.float32
        scale = HEAD_DIM ** (-0.5)
        some = 4 * GROUP

        def group(index, carry):
            here = span(index, some)
            longer = pl.ds(pl.multiple_of(index * some, some), some + GROUP)
            query, unit, value = r.sorted_query[here, :], r.unit[longer, :], r.key_value[longer, :]
            raw = [
                dot(query[i * GROUP : (i + 1) * GROUP], self.window(unit, i), ((1,), (1,)))
                for i in range(4)
            ]
            code = self.codes(index)
            scores = jnp.where(
                code == 0.0,
                jnp.concatenate(raw, 0) * scale,
                jnp.where(code == 1.0, own_score, masked_score),
            )
            peak = jnp.max(scores, 1, keepdims=True)
            power = jnp.exp(scores - peak)
            total = jnp.sum(power, 1, keepdims=True)
            probs = power * (1.0 / total)
            r.probs[here, :] = probs
            probs = probs.astype(bf16)
            result = [
                dot(probs[i * GROUP : (i + 1) * GROUP], self.window(value, i)) for i in range(4)
            ]
            r.round_rows[here, :HEAD_DIM] = jnp.concatenate(result, 0).astype(bf16)
            r.round_rows[here, HEAD_DIM:] = in_lanes(peak + jnp.log(total))
            return carry

        lax.fori_loop(0, self.devices * self.rows // some, group, 0)

    def return_rows(self):
        r, place, wires = self.r, self.place, self.wires
        bf16, f32 = jnp.bfloat16, jnp.float32

        def first(block, carry):
            self.unsort_block(r.round_rows, block)
            return carry

        lax.fori_loop(0, self.devices, first, 0)
        self.shares, self.sides = {}, []
        for half in range(self.pair):
            for bits in (3, 1, 2, 0):
                turn = flipped(place.turn, bits)
                rows = self.unsorted_chunk(place.chunk(turn, half))
                total = jnp.sum(rows[:, HEAD_DIM:], 1, keepdims=True)
                lines = [to_row(total[i : i + 128]) for i in range(0, self.rows, 128)]
                r.out[bits, half] = rows[:, :HEAD_DIM].astype(bf16)
                r.total[bits, half] = jnp.concatenate(lines, 0)
                if bits % 2:
                    self.shares[bits, half] = [
                        wires.push(
                            source.at[bits, half], target.at[bits // 2, half], place.peer(0, 1)
                        )
                        for source, target in ((r.total, r.share_total), (r.out, r.share))
                    ]
            for copy in self.shares[3, half]:
                copy.wait_recv()
            r.merged_total[half] = self.combine(
                (
                    (r.total.at[2, half], r.out.at[2, half]),
                    (r.share_total.at[1, half], r.share.at[1, half]),
                ),
                (r.merged.at[half],),
            )
            self.sides.append(
                [
                    wires.push(source.at[half], target.at[half], place.peer(1))
                    for source, target in ((r.merged_total, r.side_total), (r.merged, r.side))
                ]
            )

    def combine(self, terms, targets):
        f32 = jnp.float32
        totals = [total[...] for total, _ in terms]
        peak = totals[0]
        for total in totals[1:]:
            peak = jnp.maximum(peak, total)
        whole = peak + jnp.log(sum(jnp.exp(total - peak) for total in totals))
        for part in range(self.rows // 128):
            here = pl.ds(part * 128, 128)
            rows = jnp.zeros((128, HEAD_DIM), f32)
            for total, (_, out) in zip(totals, terms):
                mix = to_column(jnp.exp(total - whole)[part : part + 1, :])
                rows += mix * out[here, :].astype(f32)
            for target in targets:
                target[here, :] = rows.astype(target.dtype)
        return whole

    def mix_rounds(self):
        r, place, wires = self.r, self.place, self.wires
        mine = columns_at(r.attended_full, place.pair * 4 + place.line, HEAD_DIM)
        back = Spread(wires, place)
        self.wholes = []
        for half in range(self.pair):
            for copy in self.shares[1, half] + self.sides[half]:
                copy.wait_recv()
            r.whole_total[place.turn, half] = self.combine(
                (
                    (r.total.at[0, half], r.out.at[0, half]),
                    (r.share_total.at[0, half], r.share.at[0, half]),
                    (r.side_total.at[half], r.side.at[half]),
                ),
                (r.attended.at[half], r.attended_wide.at[half]),
            )
            back.start(lambda line: r.attended.at[line % 2], mine, half)
            whole = r.whole_total.at[place.turn, half]
            for bits in (1, 2, 3):
                self.wholes.append(wires.push(whole, whole, place.member(bits)))

        @pl.when(place.home)
        def _():
            mine[...] = r.attended[place.line % 2]

        back.finish()
        gather = self.over_head(r.attended_full)
        gather.start(gather.slot(place.head))
        gather.relay()
        gather.finish()


    def normalise_sum(self):
        r, place = self.r, self.place
        bf16, f32 = jnp.bfloat16, jnp.float32
        tile_rows = self.rows // 2
        for tile in range(2):
            here = pl.ds(tile * tile_rows, tile_rows)
            total = r.one_full[here, :].astype(f32) + dot(r.attended_full[here, :], r.merge_full[...])
            center = jnp.mean(total, 1, keepdims=True)
            offset = total - center
            factor = lax.rsqrt(jnp.mean(offset * offset, 1, keepdims=True) + 1e-05)
            normal = offset * factor
            r.tall[here, :] = total
            mine = columns_at(r.tall.at[here], place.head, self.width)
            r.result_one[here, :] = mine[...].astype(bf16)
            r.tall[here, :] = normal
            r.normal_two[here, :] = mine[...]
            r.factor_two[here, :] = jnp.broadcast_to(factor, (tile_rows, 128))
            r.rows_two[here, :] = (normal * r.params_full[2:3, :] + r.params_full[3:4, :]).astype(
                bf16
            )

    def feed_half(self, half, tile):
        r = self.r
        bf16 = jnp.bfloat16
        tile_rows, step = self.rows // 2, r.active.shape[1] // 2
        here, units = pl.ds(tile * tile_rows, tile_rows), pl.ds(half * step, step)
        hidden = dot(r.rows_two[here, :], r.expand_full[:, units])
        below = 0.5 * (1.0 + lax.erf(hidden * (0.5**0.5)))
        r.active[here, units] = (hidden * below).astype(bf16)
        slope = below + hidden * jnp.exp(-0.5 * hidden * hidden) * ((2.0 * jnp.pi) ** -0.5)
        grad = dot(r.grad_full[here, :], r.shrink_full[units, :], ((1,), (1,)))
        r.grad_hidden[here, units] = (grad * slope).astype(bf16)

    def shrink_grads(self, half):
        r = self.r
        step = r.active.shape[1] // 2
        units = pl.ds(half * step, step)
        self.weights(r.active.at[:, units], r.grad_full, r.grad_shrink.at[units])
        width = r.shrink.shape[1]
        scatter = SeqScatter(
            self.wires, self.place,
            lambda seq: columns_at(r.grad_shrink.at[units], seq, width),
            r.shrink_pair.at[:, units], r.shrink_line.at[:, units],
        )
        scatter.start()
        self.shrink_out.append(scatter)

    def feed_forward(self):
        r, place, wires = self.r, self.place, self.wires
        self.parts_two, self.shrink_out = [], []
        tile_rows = self.rows // 2
        self.normalise_sum()
        self.expand[0].finish()
        self.shrink[0].finish()
        for tile in range(2):
            self.feed_half(0, tile)
        self.shrink_grads(0)
        self.expand[1].finish()
        self.shrink[1].finish()
        for tile in range(2):
            here = pl.ds(tile * tile_rows, tile_rows)
            self.feed_half(1, tile)
            part = dot(r.grad_hidden[here, :], r.expand_full[...], ((1,), (1,)))
            self.send_part(
                tile, part, r.tall[here, :], r.params_full[2:3, :], r.part_two, r.stat_two,
                r.parts_two, self.parts_two,
            )
        for tile in range(2):
            self.relay_part(tile, r.part_two, r.parts_two, self.parts_two)
        self.send_stats(r.stat_two, r.stats_two, self.parts_two)
        self.shrink_grads(1)

    def send_part(self, tile, part, normal, gain, part_ref, stat_ref, target, copies):
        tile_rows = part.shape[0]
        here = pl.ds(tile * tile_rows, tile_rows)
        scaled = part * gain
        first = jnp.sum(scaled, 1, keepdims=True)
        second = jnp.sum(scaled * normal, 1, keepdims=True)
        lines = tile_rows // 128
        for line in range(lines):
            at = slice(line * 128, (line + 1) * 128)
            row = tile * lines + line
            stat_ref[row : row + 1, :] = to_row(first[at])
            row += self.rows // 128
            stat_ref[row : row + 1, :] = to_row(second[at])
        part_ref[here, :] = part.astype(jnp.bfloat16)
        twin = self.place.peer(0, 1)
        for slot, head in ((1, flip(twin[1], 2)), (0, twin[1])):
            source = columns_at(part_ref.at[here], head, self.width)
            copies.append(self.wires.push(source, target.at[slot, here], twin))

    def relay_part(self, tile, part_ref, target, copies):
        tile_rows = self.rows // 2
        here = pl.ds(tile * tile_rows, tile_rows)
        far = self.place.peer(0, 2)
        copies[2 * tile].wait_recv()
        mine = columns_at(part_ref.at[here], far[1], self.width)[...].astype(jnp.float32)
        total = mine + target[1, here, :].astype(jnp.float32)
        target[1, here, :] = total.astype(jnp.bfloat16)
        copies.append(self.wires.push(target.at[1, here], target.at[2, here], far))

    def send_stats(self, stat_ref, target, copies):
        for bits in (2, 3, 1):
            device = self.place.peer(0, bits)
            copies.append(self.wires.push(stat_ref, target.at[bits - 1], device))

    def norm_back(self, part_ref, parts, stat_ref, stats, normal_at, factor_ref, gain, finish):
        f32 = jnp.float32
        lines = self.rows // 128

        def piece(line, carry):
            here = span(line, 128)
            grad = columns_at(part_ref.at[here], self.place.head, self.width)[...].astype(f32)
            first, second = stat_ref[pl.ds(line, 1), :], stat_ref[pl.ds(line + lines, 1), :]
            for other in range(3):
                if other != 1:
                    grad += parts[other, here, :].astype(f32)
                first += stats[other, pl.ds(line, 1), :]
                second += stats[other, pl.ds(line + lines, 1), :]
            normal = normal_at(here)
            first, second = to_column(first) / self.wide, to_column(second) / self.wide
            finish(here, factor_ref[here, 0:1] * (grad * gain - first - normal * second))
            gains, biases = carry
            return (
                gains + jnp.sum(grad * normal, 0, keepdims=True),
                biases + jnp.sum(grad, 0, keepdims=True),
            )

        zero = jnp.zeros((1, self.width), f32)
        return lax.fori_loop(0, lines, piece, (zero, zero))

    def my_params(self, row):
        return columns_at(self.r.params_full, self.place.head, self.width)[row : row + 1, :]

    def feed_back(self):
        r, place, wires = self.r, self.place, self.wires
        bf16, f32 = jnp.bfloat16, jnp.float32
        self.weights(r.rows_two, r.grad_hidden, r.grad_expand)
        rows, half = r.expand.shape[0], r.expand.shape[1] // 2
        first, second = pl.ds(0, half), pl.ds(half, half)
        self.expand_out = [
            PairScatter(
                wires, place,
                lambda seq: rows_at(r.grad_expand, seq, rows).at[:, first],
                lambda pair: rows_at(r.grad_expand, pair, 2 * rows).at[:, first],
                r.expand_lines, r.expand_side,
            ),
            SeqScatter(
                wires, place,
                lambda seq: rows_at(r.grad_expand, seq, rows).at[:, second],
                r.expand_pair, r.expand_line,
            ),
        ]
        self.expand_out[0].start()
        for copy in self.parts_two[1:2] + self.parts_two[3:]:
            copy.wait_recv()
        wires.settle(self.parts_two)

        def finish(here, change):
            total = r.grad_one[here, :].astype(f32) + change
            r.input_grad_one[here, :] = total.astype(bf16)

        gains, biases = self.norm_back(
            r.part_two, r.parts_two, r.stat_two, r.stats_two,
            lambda here: r.normal_two[here, :], r.factor_two, self.my_params(2), finish,
        )
        r.norm_send[2:3, :], r.norm_send[3:4, :] = gains, biases
        gather = self.over_head(r.grad_rows_one)
        self.start_head(gather, r.input_grad_one)
        gather.relay()

        def feed(tile, carry):
            here = span(tile, 256)
            r.feed[here, :] = dot(r.active[here, :], r.shrink_full[...]).astype(bf16)
            return carry

        lax.fori_loop(0, self.rows // 256, feed, 0)
        gather.finish()

    def weights(self, left, right, target):
        step = min(256, left.shape[1])

        def piece(index, carry):
            columns = span(index, step)
            result = dot(left[:, columns], right[...], ((0,), (0,)))
            target[columns, :] = result.astype(jnp.bfloat16)
            return carry

        lax.fori_loop(0, left.shape[1] // step, piece, 0)

    def send_feed(self):
        r = self.r
        self.feeds = []
        for bits in (2, 3, 1):
            device = self.place.peer(0, bits)
            source = columns_at(r.feed, device[1], self.width)
            self.feeds.append(self.wires.push(source, r.feeds.at[bits - 1], device))

    def finish_feed(self):
        r = self.r
        f32 = jnp.float32
        for copy in self.feeds:
            copy.wait_recv()
        total = r.two[...].astype(f32)
        total += columns_at(r.feed, self.place.head, self.width)[...].astype(f32)
        for other in range(3):
            total += r.feeds[other].astype(f32)
        r.result_two[...] = total.astype(jnp.bfloat16)


    def grad_rounds(self):
        r, place, wires = self.r, self.place, self.wires
        bf16, f32 = jnp.bfloat16, jnp.float32
        my_rows = rows_at(r.merge_full, place.head, r.merge.shape[0])

        def attended(tile, carry):
            here = span(tile, 256)
            grad = dot(r.grad_rows_one[here, :], my_rows[...], ((1,), (1,))).astype(bf16)
            for which in range(self.pair):
                r.grad_heads[which, here, :] = grad[:, which * HEAD_DIM : (which + 1) * HEAD_DIM]
            return carry

        lax.fori_loop(0, self.rows // 256, attended, 0)
        mine = r.grad_attended.at[place.line % 2]
        there = Spread(wires, place)
        there.start(lambda line: r.grad_heads.at[line % 2], mine)

        @pl.when(place.home)
        def _():
            mine[...] = r.grad_heads[place.line % 2]

        for scatter in self.shrink_out:
            scatter.along()
        self.weights(columns_at(r.attended_full, place.head, self.width), r.grad_rows_one, r.grad_merge)
        there.finish()
        self.grads_coming = []
        for half in range(self.pair):
            for part in range(self.rows // 128):
                here = pl.ds(part * 128, 128)
                rows = r.attended_wide[half, here, :] * r.grad_attended[half, here, :].astype(f32)
                r.means[place.turn, half, part : part + 1, :] = to_row(
                    jnp.sum(rows, 1, keepdims=True)
                )
            own = [item.at[place.turn, half] for item in (r.means, r.grad_outs)]
            own[1][...] = r.grad_attended[half]
            self.grads_coming.append(
                {
                    2: [wires.push(item, item, place.peer(1)) for item in own],
                    1: [wires.push(item, item, place.peer(0, 1)) for item in own],
                }
            )
        self.merge_out = SeqScatter(
            wires, place, lambda seq: columns_at(r.grad_merge, seq, r.merge.shape[1]),
            r.merge_pair, r.merge_line,
        )

    def sort_grads(self):
        r, place = self.r, self.place
        bf16 = jnp.bfloat16
        f32 = jnp.float32
        lines = self.rows // 128
        for copy in self.wholes:
            copy.wait_recv()
        for bits in (0, 1, 2, 3):
            turn = flipped(place.turn, bits)
            for half, coming in enumerate(self.grads_coming):
                for copy in coming.get(bits, ()):
                    copy.wait_recv()
                if bits == 2:
                    items = [item.at[turn, half] for item in (r.means, r.grad_outs)]
                    coming[3] = [self.wires.push(item, item, place.peer(0, 1)) for item in items]
                chunk = place.chunk(turn, half)

                def piece(part, carry, turn=turn, half=half, bits=bits, chunk=chunk):
                    here, line = span(part, 128), pl.ds(part, 1)
                    grad = r.grad_outs[turn, half, here, :].astype(f32)
                    out = r.out[bits, half, here, :].astype(f32)
                    mix = to_column(
                        jnp.exp(r.total[bits, half, line, :] - r.whole_total[turn, half, line, :])
                    )
                    mean = to_column(r.means[turn, half, line, :])
                    dots = jnp.sum(out * grad, 1, keepdims=True)
                    rows = span(chunk * lines + part, 128)
                    r.everyone[rows, :HEAD_DIM] = (mix * grad).astype(bf16)
                    r.everyone[rows, HEAD_DIM:] = in_lanes(mix * (dots - mean))
                    return carry

                lax.fori_loop(0, lines, piece, 0)
                self.sort_chunk(r.everyone, chunk)
        self.expand_out[1].start()
        self.merge_out.start()
        for scatter in self.shrink_out:
            scatter.across()

        def second(block, carry):
            r.round_rows[span(block, self.rows), :] = self.sorted_block(block).astype(bf16)
            return carry

        lax.fori_loop(0, self.devices, second, 0)

    def attend_back(self):
        r = self.r
        bf16, f32 = jnp.bfloat16, jnp.float32
        scale = HEAD_DIM ** (-0.5)
        some = 4 * GROUP
        r.grad_unit[0:GROUP, :] = jnp.zeros((GROUP, HEAD_DIM), f32)
        r.grad_value[0:GROUP, :] = jnp.zeros((GROUP, HEAD_DIM), f32)

        def one(rows, block):
            return rows[block * GROUP : (block + 1) * GROUP]

        def fold(pieces):
            owns = [piece[:GROUP] if i % 2 == 0 else piece[GROUP:] for i, piece in enumerate(pieces)]
            befores = [piece[GROUP:] if i % 2 == 0 else piece[:GROUP] for i, piece in enumerate(pieces)]
            middle = [owns[i] + befores[i + 1] for i in range(3)]
            return befores[0], jnp.concatenate(middle + [owns[3]], 0)

        def group(index, carry):
            here = span(index, some)
            longer = pl.ds(pl.multiple_of(index * some, some), some + GROUP)
            before = pl.ds(pl.multiple_of(index * some, some), GROUP)
            after = pl.ds(pl.multiple_of(index * some + GROUP, GROUP), some)
            query, unit, value = r.sorted_query[here, :], r.unit[longer, :], r.key_value[longer, :]
            grad = r.round_rows[here, :HEAD_DIM]
            total = jnp.sum(r.round_rows[here, HEAD_DIM:].astype(f32), 1, keepdims=True)
            probs = r.probs[here, :]
            low = probs.astype(bf16)
            live = jnp.where(self.codes(index) == 0.0, probs, 0.0)
            grad_probs = jnp.concatenate(
                [dot(one(grad, i), self.window(value, i), ((1,), (1,))) for i in range(4)], 0
            )
            inner = jnp.sum(probs * grad_probs, 1, keepdims=True)
            scores = (live * (grad_probs - inner + total)).astype(bf16)
            r.probs[here, :] = (
                jnp.concatenate([dot(one(scores, i), self.window(unit, i)) for i in range(4)], 0) * scale
            )
            for target, left, right, factor in (
                (r.grad_unit, scores, query, scale),
                (r.grad_value, low, grad, 1.0),
            ):
                first, rest = fold(
                    [dot(one(left, i), one(right, i), ((0,), (0,))) * factor for i in range(4)]
                )
                target[before, :] += first
                target[after, :] = rest
            return carry

        lax.fori_loop(0, self.devices * self.rows // some, group, 0)
        last = pl.ds(self.devices * self.rows, GROUP)
        r.grad_unit[last, :] += r.grad_unit[0:GROUP, :]
        r.grad_value[last, :] += r.grad_value[0:GROUP, :]

        def whole(index, carry):
            here = span(index, some)
            after = pl.ds(pl.multiple_of(index * some + GROUP, GROUP), some)
            query = r.sorted_query[here, :].astype(f32)
            factor = lax.rsqrt(jnp.sum(query * query, 1, keepdims=True) + 1e-06)
            unit = query * factor
            grad = r.grad_unit[after, :]
            along = jnp.sum(unit * grad, 1, keepdims=True)
            grad = r.probs[here, :] + factor * (grad - unit * along)
            r.round_rows[here, :HEAD_DIM] = grad.astype(bf16)
            r.round_rows[here, HEAD_DIM:] = r.grad_value[after, :].astype(bf16)
            return carry

        lax.fori_loop(0, self.devices * self.rows // some, whole, 0)

    def return_grads(self):
        r, place, wires = self.r, self.place, self.wires
        bf16, f32 = jnp.bfloat16, jnp.float32

        def first(block, carry):
            self.unsort_block(r.round_rows, block)
            return carry

        lax.fori_loop(0, self.devices, first, 0)
        self.backs = {}

        def rows_for(bits, half):
            return self.unsorted_chunk(place.chunk(flipped(place.turn, bits), half)).astype(bf16)

        def block(slot, half):
            return pl.ds((slot * 2 + half) * self.rows, self.rows)

        for bits in (3, 1, 2, 0):
            for half in range(self.pair):
                r.everyone[block(bits, half), :] = rows_for(bits, half)
        parts = {part: pl.ds(part * HEAD_DIM, HEAD_DIM) for part in (1, 0)}
        both = self.pair * self.rows
        shares, sides = {}, {}
        for part, columns in parts.items():
            for bits in (3, 1):
                source = r.everyone.at[pl.ds(bits * both, both), columns]
                shares[part, bits] = wires.push(
                    source, r.grad_pairs.at[bits // 2, :, columns], place.peer(0, 1)
                )
        for part, columns in parts.items():
            shares[part, 3].wait_recv()
            total = r.everyone[pl.ds(2 * both, both), columns].astype(f32)
            total += r.grad_pairs[1, :, columns].astype(f32)
            r.grad_pairs[1, :, columns] = total.astype(bf16)
            sides[part] = wires.push(
                r.grad_pairs.at[1, :, columns], r.grad_pairs.at[2, :, columns], place.peer(1)
            )
        for part, columns in parts.items():
            shares[part, 1].wait_recv()
            sides[part].wait_recv()
            for half in range(self.pair):
                rows = pl.ds(half * self.rows, self.rows)
                total = r.everyone[block(0, half), columns].astype(f32)
                total += r.grad_pairs[0, rows, columns].astype(f32)
                total += r.grad_pairs[2, rows, columns].astype(f32)
                r.grad_pair[part, half] = total.astype(bf16)
            target = r.grad_key if part else r.grad_query
            mine = columns_at(target, place.line % 2, HEAD_DIM)
            back = Spread(wires, place)
            back.start(lambda line, part=part: r.grad_pair.at[part, line % 2], mine)
            pl.when(place.home)(partial(self.keep_grad, mine, part))
            self.backs[part] = back
        self.backs[1].finish()
        self.value_weights()
        self.backs[0].finish()

    def keep_grad(self, mine, part):
        mine[...] = self.r.grad_pair[part, self.place.line % 2]

    def value_weights(self):
        r = self.r
        self.weights(r.rows_one, r.grad_key, r.grad_value_full)
        self.value_out = SeqScatter(
            self.wires, self.place,
            lambda seq: rows_at(r.grad_value_full, seq, r.value.shape[0]),
            r.value_pair, r.value_line,
        )
        self.value_out.start()

    def project_back(self):
        r, place, wires = self.r, self.place, self.wires
        bf16, f32 = jnp.bfloat16, jnp.float32
        self.weights(r.rows_one, r.grad_query, r.grad_query_full)
        self.query_out = SeqScatter(
            wires, place, lambda seq: rows_at(r.grad_query_full, seq, r.query.shape[0]),
            r.query_pair, r.query_line,
        )
        self.query_out.start()
        copies = []
        tile_rows = self.rows // 2
        for tile in range(2):
            here = pl.ds(tile * tile_rows, tile_rows)
            part = dot(r.grad_query[here, :], r.query_full[...], ((1,), (1,)))
            part += dot(r.grad_key[here, :], r.value_full[...], ((1,), (1,)))
            normal = (r.two_full[here, :].astype(f32) - r.center_one[here, 0:1]) * r.factor_one[
                here, 0:1
            ]
            self.send_part(
                tile, part, normal, r.params_full[0:1, :], r.part_one, r.stat_one,
                r.parts_one, copies,
            )
        for tile in range(2):
            self.relay_part(tile, r.part_one, r.parts_one, copies)
        self.send_stats(r.stat_one, r.stats_one, copies)
        self.value_out.along()
        self.query_out.along()
        for copy in copies[1:2] + copies[3:]:
            copy.wait_recv()

        def normal_at(here):
            rows = columns_at(r.two_full.at[here], place.head, self.width)[...].astype(f32)
            return (rows - r.center_one[here, 0:1]) * r.factor_one[here, 0:1]

        def finish(here, change):
            total = r.grad_two[here, :].astype(f32) + change
            r.input_grad_two[here, :] = total.astype(bf16)

        gains, biases = self.norm_back(
            r.part_one, r.parts_one, r.stat_one, r.stats_one, normal_at, r.factor_one,
            self.my_params(0), finish,
        )
        r.norm_send[0:1, :], r.norm_send[1:2, :] = gains, biases
        norms = [
            wires.push(r.norm_send, r.norms.at[bits - 1], place.peer(bits)) for bits in range(1, 8)
        ]
        self.value_out.across()
        self.query_out.across()
        half = r.expand.shape[1] // 2
        for part, scatter in enumerate(self.expand_out):
            scatter.finish(r.expand_part.at[:, pl.ds(part * half, half)])
        step = r.shrink.shape[0] // 2
        for half, scatter in enumerate(self.shrink_out):
            scatter.finish(r.shrink_part.at[pl.ds(half * step, step)])
        self.merge_out.finish(r.merge_part)
        self.finish_feed()
        total = r.norm_send[...]
        for bits, copy in enumerate(norms):
            copy.wait_recv()
            total += r.norms[bits]
        r.norm_grads[...] = total
        self.query_out.finish(r.query_part)
        self.value_out.finish(r.value_part)


def on_device(names, turns, *refs):
    r = SimpleNamespace(**dict(zip(names, refs)))
    r.result_one, r.result_two, r.input_grad_one, r.input_grad_two = (
        r.streams.at[i] for i in range(4)
    )
    r.query_part, r.value_part = r.projections.at[0], r.projections.at[1]
    merge_rows, shrink_rows = r.merge.shape[0], r.shrink.shape[0]
    r.merge_part = r.columns.at[pl.ds(0, merge_rows)]
    r.shrink_part = r.columns.at[pl.ds(merge_rows, shrink_rows)]
    r.feed, r.grad_expand = r.one_full, r.expand_full
    r.grad_pair, r.part_one = r.packed, r.part_two
    steps = Phases(r, turns)
    steps.project()
    steps.sort_tokens()
    steps.begin_merge_rows()
    steps.expand[0].forward()
    steps.begin(steps.shrink[1])
    steps.attend()
    steps.return_rows()
    steps.heads.relay()
    steps.go_on(steps.shrink[0])
    steps.mix_rounds()
    steps.go_on(steps.shrink[1])
    steps.one.relay()
    steps.grads.relay()
    steps.one.finish()
    steps.grads.finish()
    steps.heads.finish()
    steps.feed_forward()
    steps.feed_back()
    steps.grad_rounds()
    steps.send_feed()
    steps.expand_out[0].across()
    steps.sort_grads()
    steps.expand_out[0].side()
    steps.attend_back()
    steps.expand_out[1].along()
    steps.merge_out.along()
    steps.return_grads()
    steps.expand_out[1].across()
    steps.merge_out.across()
    steps.project_back()
    steps.wires.drain()
    assert len(steps.wires.copies) <= r.send.shape[0]


def whole(turns, arguments):
    bf16, f32 = jnp.bfloat16, jnp.float32
    heads, devices = lax.axis_size("head"), lax.axis_size("seq")
    pair = devices // turns
    rows, width = arguments["two"].shape
    tokens, wide = devices * rows, heads * width
    hidden = arguments["expand"].shape[1]
    lines = rows // 128
    shape = {name: value.shape for name, value in arguments.items()}
    results = dict(
        streams=((4, rows, width), bf16),
        projections=((2,) + shape["query"], f32),
        expand_part=(shape["expand"], f32),
        columns=((shape["merge"][0] + shape["shrink"][0], shape["merge"][1]), f32),
        norm_grads=((8, width), f32),
    )
    scratch = dict(
        params=((8, width), f32),
        keys=((tokens // 128, 1, 128), f32),
        shares=((8, 128), f32),
        unit_rows=((2, 8, 128), jnp.int32),
        until=((-(-(devices * (rows // GROUP + 1) + 1) // 128) * 128, 128), f32),
        block_row=((devices, 1, rows), jnp.int32),
        block_column=((tokens, 128), jnp.int16),
        chunk_row=((devices, 1, rows), jnp.int32),
        chunk_column=((tokens, 128), jnp.int16),
        sorted_query=((tokens, HEAD_DIM), bf16),
        unit=((tokens + GROUP, HEAD_DIM), bf16),
        key_value=((tokens + GROUP, HEAD_DIM), bf16),
        probs=((tokens, 2 * GROUP), f32),
        rows_one=((rows, wide), bf16),
        center_one=((rows, 128), f32),
        factor_one=((rows, 128), f32),
        query_full=((wide, width), bf16),
        value_full=((wide, width), bf16),
        merge_full=((wide, wide), bf16),
        expand_full=((wide, hidden), bf16),
        shrink_full=((hidden, wide), bf16),
        one_full=((rows, wide), bf16),
        two_full=((rows, wide), bf16),
        grad_full=((rows, wide), bf16),
        attended_full=((rows, wide), bf16),
        everyone=((tokens, 2 * HEAD_DIM), bf16),
        mid=((devices * devices, rows // devices, 2 * HEAD_DIM), bf16),
        params_full=((8, wide), f32),
        packed=((pair, 2, rows, HEAD_DIM), bf16),
        round_rows=((tokens, 2 * HEAD_DIM), bf16),
        attended=((pair, rows, HEAD_DIM), bf16),
        attended_wide=((pair, rows, HEAD_DIM), f32),
        out=((turns, pair, rows, HEAD_DIM), bf16),
        total=((turns, pair, lines, 128), f32),
        share=((2, pair, rows, HEAD_DIM), bf16),
        share_total=((2, pair, lines, 128), f32),
        merged=((pair, rows, HEAD_DIM), bf16),
        merged_total=((pair, lines, 128), f32),
        side=((pair, rows, HEAD_DIM), bf16),
        side_total=((pair, lines, 128), f32),
        whole_total=((turns, pair, lines, 128), f32),
        means=((turns, pair, lines, 128), f32),
        tall=((rows, wide), f32),
        normal_two=((rows, width), f32),
        factor_two=((rows, 128), f32),
        rows_two=((rows, wide), bf16),
        active=((rows, hidden), bf16),
        grad_hidden=((rows, hidden), bf16),
        part_two=((rows, wide), bf16),
        stat_two=((2 * lines, 128), f32),
        parts_two=((heads - 1, rows, width), bf16),
        stats_two=((heads - 1, 2 * lines, 128), f32),
        stat_one=((2 * lines, 128), f32),
        parts_one=((heads - 1, rows, width), bf16),
        stats_one=((heads - 1, 2 * lines, 128), f32),
        feeds=((heads - 1, rows, width), bf16),
        grad_rows_one=((rows, wide), bf16),
        grad_heads=((pair, rows, HEAD_DIM), bf16),
        grad_attended=((pair, rows, HEAD_DIM), bf16),
        grad_outs=((turns, pair, rows, HEAD_DIM), bf16),
        grad_unit=((tokens + GROUP, HEAD_DIM), f32),
        grad_value=((tokens + GROUP, HEAD_DIM), f32),
        grad_pairs=((3, pair * rows, 2 * HEAD_DIM), bf16),
        grad_query=((rows, width), bf16),
        grad_key=((rows, width), bf16),
        expand_lines=((3, 2 * shape["expand"][0], hidden // 2), bf16),
        expand_side=((shape["expand"][0], hidden // 2), bf16),
        norm_send=((8, width), f32),
        norms=((devices - 1, 8, width), f32),
    )
    for name, full in (
        ("query", (wide, width)),
        ("value", (wide, width)),
        ("merge", (width, wide)),
        ("expand", (wide, hidden)),
        ("shrink", (hidden, wide)),
    ):
        own = "grad_" + name + ("_full" if name in ("query", "value") else "")
        if name != "expand":
            scratch[own] = (full, bf16)
        height, across = shape[name]
        if name == "expand":
            across = across // 2
        scratch[name + "_pair"] = ((devices // 2, height, across), bf16)
        scratch[name + "_line"] = ((devices // 2 - 1, height, across), bf16)
    wires = dict(send=224, receive=224, local=2)
    vmem = pl.BlockSpec(memory_space=pltpu.VMEM)
    tables = dict(units=(8, 128), units_back=(8, 128))
    names = [*arguments, *results, *scratch, *tables, *wires]
    out = pl.pallas_call(
        partial(on_device, names, turns),
        out_shape=[jax.ShapeDtypeStruct(*item) for item in results.values()],
        in_specs=[vmem] * len(arguments),
        out_specs=[vmem] * len(results),
        scratch_shapes=[pltpu.VMEM(*item) for item in scratch.values()]
        + [pltpu.SMEM(item, jnp.int32) for item in tables.values()]
        + [pltpu.SemaphoreType.DMA((number,)) for number in wires.values()],
        compiler_params=pltpu.CompilerParams(
            collective_id=0, has_side_effects=True, vmem_limit_bytes=63 << 20
        ),
    )(*arguments.values())
    return SimpleNamespace(**dict(zip(results, out)))


def by_rounds(
    stream_one,
    stream_two,
    grad_one,
    grad_two,
    query_weight,
    value_weight,
    merge_weight,
    expand_weight,
    shrink_weight,
    first_gain,
    first_bias,
    second_gain,
    second_bias,
    bucket_ids,
    sort_order,
):
    arguments = dict(
        one=stream_one,
        two=stream_two,
        grad_one=grad_one,
        grad_two=grad_two,
        query=query_weight,
        value=value_weight,
        merge=merge_weight,
        expand=expand_weight,
        shrink=shrink_weight,
        gain_one=first_gain[None],
        bias_one=first_bias[None],
        gain_two=second_gain[None],
        bias_two=second_bias[None],
        bucket=bucket_ids,
        order=sort_order,
    )
    k = whole(sort_order.shape[0], arguments)
    merge_rows = merge_weight.shape[0]
    return (
        *(k.streams[i] for i in range(4)),
        k.projections[0],
        k.projections[1],
        k.columns[:merge_rows],
        k.expand_part,
        k.columns[merge_rows:],
        *(k.norm_grads[i] for i in range(4)),
    )


def solution(mesh):
    placed = (
        P("seq", "head"),
        P("seq", "head"),
        P("seq", "head"),
        P("seq", "head"),
        P("seq", "head"),
        P("seq", "head"),
        P("head", "seq"),
        P("seq", "head"),
        P("head", "seq"),
        P("head"),
        P("head"),
        P("head"),
        P("head"),
        P(),
        P(),
    )

    def local(*arguments):
        rounds = arguments[-1].shape[0]
        if mesh.shape["seq"] == HEADS == 2 * rounds and mesh.shape["head"] == rounds:
            return by_rounds(*arguments)
        return by_blocks(*arguments)

    return jax.shard_map(
        local,
        mesh=mesh,
        in_specs=placed,
        out_specs=(
            P("seq", "head"),
            P("seq", "head"),
            P("seq", "head"),
            P("seq", "head"),
            P("seq", "head"),
            P("seq", "head"),
            P("head", "seq"),
            P("seq", "head"),
            P("head", "seq"),
            P("head"),
            P("head"),
            P("head"),
            P("head"),
        ),
        check_vma=False,
    )
```

```python
from functools import partial
from types import SimpleNamespace

import jax
import jax.numpy as jnp
from jax import lax
from jax.experimental import pallas as pl
from jax.experimental.pallas import tpu as pltpu
from jax.sharding import PartitionSpec as P

HEADS = 8
HEAD_DIM = 128
GROUP = 64
MESH = pl.DeviceIdType.MESH


masked_score = -1000000000.0
own_score = -100000.0


def as_sent(shard):

    def short(part):
        return part.astype(jnp.bfloat16) if part.dtype == jnp.float32 else part

    return jax.tree.map(short, shard)


def from_behind(block, axis, distance):
    devices = range(lax.axis_size(axis))
    route = [(i - distance, i) for i in devices if i - distance in devices]
    return lax.ppermute(block, axis, route)


def row_sums(first, second):
    return lax.psum((first, second), "head")


def full_rows(part):
    return lax.all_gather(part, "head", axis=1, tiled=True)


def branch_sum(part):
    return lax.psum_scatter(part, "head", scatter_dimension=1, tiled=True)


def norm_forward(value, gain, shift):
    width = value.shape[1] * lax.axis_size("head")
    total, square = row_sums(
        jnp.sum(value, 1, keepdims=True), jnp.sum(value * value, 1, keepdims=True)
    )
    center = total / width
    spread = square / width - center * center
    factor = lax.rsqrt(spread + 1e-05)
    normal = (value - center) * factor
    return (normal, factor, normal * gain + shift)


def norm_backward(grad, normal, factor, gain):
    width = grad.shape[1] * lax.axis_size("head")
    scaled = grad * gain
    first, second = row_sums(
        jnp.sum(scaled, 1, keepdims=True), jnp.sum(scaled * normal, 1, keepdims=True)
    )
    result = factor * (scaled - first / width - normal * (second / width))
    return (result, jnp.sum(grad * normal, 0), jnp.sum(grad, 0))


def regroup_rows(buffer):
    turns = []
    for turn in range(buffer.shape[1]):
        turns.append(
            lax.all_to_all(buffer[:, turn], "seq", split_axis=0, concat_axis=0, tiled=True)
        )
    result = jnp.stack(turns, 1)
    return result


def regroup_totals(buffer):
    moved = lax.all_to_all(
        buffer.reshape(buffer.shape[0], -1, buffer.shape[3]),
        "seq",
        split_axis=0,
        concat_axis=0,
        tiled=True,
    )
    return moved.reshape(buffer.shape)


def regroup_pair(first, second):
    firsts = []
    seconds = []
    for turn in range(first.shape[1]):
        moved_first, moved_second = (
            lax.all_to_all(as_sent(first[:, turn]), "seq", split_axis=0, concat_axis=0, tiled=True),
            lax.all_to_all(
                as_sent(second[:, turn]), "seq", split_axis=0, concat_axis=0, tiled=True
            ),
        )
        firsts.append(moved_first)
        seconds.append(moved_second)
    result = (jnp.stack(firsts, 1), jnp.stack(seconds, 1))
    return result


def by_blocks(
    stream_one,
    stream_two,
    grad_one,
    grad_two,
    query_weight,
    value_weight,
    merge_weight,
    expand_weight,
    shrink_weight,
    first_gain,
    first_bias,
    second_gain,
    second_bias,
    bucket_ids,
    sort_order,
):
    devices = lax.axis_size("seq")
    place = lax.axis_index("seq")
    rows = stream_one.shape[0]
    rounds = sort_order.shape[0]
    capacity = 2 * rows // devices
    blocks = rows // GROUP
    heads_here = HEADS // lax.axis_size("head")
    local_width = heads_here * HEAD_DIM
    scale = HEAD_DIM ** (-0.5)
    round_index = jnp.arange(rounds, dtype=jnp.int32)[:, None]
    counter = jnp.arange(rows, dtype=jnp.int32)

    def invert(line):
        return jnp.zeros_like(line).at[line].set(jnp.arange(line.shape[0], dtype=jnp.int32))

    inverse = jax.vmap(invert)(sort_order)
    my_sorted = lax.dynamic_slice_in_dim(inverse, place * rows, rows, 1)
    send_block = my_sorted // rows
    same_block = send_block[:, :, None] == send_block[:, None, :]
    send_slot = jnp.sum(
        (same_block & (my_sorted[:, None, :] < my_sorted[:, :, None])).astype(jnp.int32), -1
    )
    block_tokens = lax.dynamic_slice_in_dim(sort_order, place * rows, rows, 1)
    source_block = block_tokens // rows
    earlier = counter[None, :] < counter[:, None]
    recv_slot = jnp.sum(
        ((source_block[:, :, None] == source_block[:, None, :]) & earlier[None]).astype(jnp.int32),
        -1,
    )
    query_bucket = jnp.take_along_axis(bucket_ids, block_tokens, 1)
    prior_start = (place - 1) % devices * rows + rows - GROUP
    prior_tokens = lax.dynamic_slice_in_dim(sort_order, prior_start, GROUP, 1)
    prior_bucket = jnp.take_along_axis(bucket_ids, prior_tokens, 1)

    def with_prior(own, prior):
        pieces = own.reshape((rounds, blocks, GROUP) + own.shape[2:])
        before = jnp.concatenate([prior[:, None], pieces[:, :-1]], 1)
        return jnp.concatenate([pieces, before], 2)

    query_place = block_tokens.reshape(rounds, blocks, GROUP)
    key_place = with_prior(block_tokens, prior_tokens)
    key_bucket = with_prior(query_bucket, prior_bucket)
    allowed = (key_place[:, :, None, :] <= query_place[:, :, :, None]) & (
        key_bucket[:, :, None, :] == query_bucket.reshape(rounds, blocks, GROUP)[:, :, :, None]
    )
    itself = key_place[:, :, None, :] == query_place[:, :, :, None]
    live = allowed & jnp.logical_not(itself)

    def fill(values, block, slot):
        empty = jnp.zeros((devices, rounds, capacity, values.shape[-1]), values.dtype)
        return empty.at[block, round_index, slot].set(values)

    normal_one, factor_one, normed_one = norm_forward(
        stream_two.astype(jnp.float32), first_gain, first_bias
    )
    rows_one = full_rows(normed_one.astype(jnp.bfloat16))
    query_full, value_full, merge_full = (
        lax.all_gather(query_weight, "seq", axis=0, tiled=True),
        lax.all_gather(value_weight, "seq", axis=0, tiled=True),
        lax.all_gather(merge_weight, "seq", axis=1, tiled=True),
    )
    queries = jnp.dot(rows_one, query_full, preferred_element_type=jnp.float32).astype(jnp.bfloat16)
    values = jnp.dot(rows_one, value_full, preferred_element_type=jnp.float32).astype(jnp.bfloat16)
    packed = jnp.concatenate([queries, values], 1)
    outgoing = fill(jnp.broadcast_to(packed[None], (rounds,) + packed.shape), send_block, send_slot)
    incoming = regroup_rows(outgoing)
    sorted_rows = incoming[source_block, round_index, recv_slot]
    sorted_query = sorted_rows[:, :, :local_width].reshape(rounds, rows, heads_here, HEAD_DIM)
    sorted_value = sorted_rows[:, :, local_width:].reshape(rounds, rows, heads_here, HEAD_DIM)
    query_float = sorted_query.astype(jnp.float32)
    inverse_norm = lax.rsqrt(jnp.sum(query_float * query_float, -1, keepdims=True) + 1e-06)
    unit_float = query_float * inverse_norm
    unit_low = unit_float.astype(jnp.bfloat16)
    edge = from_behind(
        jnp.concatenate([unit_low[:, -GROUP:], sorted_value[:, -GROUP:]], -1), "seq", 1
    )
    key_unit = with_prior(unit_low, edge[..., :HEAD_DIM])
    key_value = with_prior(sorted_value, edge[..., HEAD_DIM:])
    query_groups = sorted_query.reshape(rounds, blocks, GROUP, heads_here, HEAD_DIM)

    def masked_scores():
        raw = (
            jnp.einsum(
                "rncha,rnkha->rnhck", query_groups, key_unit, preferred_element_type=jnp.float32
            )
            * scale
        )
        return jnp.where(
            itself[:, :, None], own_score, jnp.where(allowed[:, :, None], raw, masked_score)
        )

    scores = masked_scores()
    peak = jnp.max(scores, -1, keepdims=True)
    totals = peak + jnp.log(jnp.sum(jnp.exp(scores - peak), -1, keepdims=True))
    probs_low = jnp.exp(scores - totals).astype(jnp.bfloat16)
    round_out = jnp.einsum(
        "rnhck,rnkha->rncha", probs_low, key_value, preferred_element_type=jnp.float32
    ).astype(jnp.bfloat16)
    out_flat = round_out.reshape(rounds, rows, local_width)
    total_flat = jnp.transpose(totals[..., 0], (0, 1, 3, 2)).reshape(rounds, rows, heads_here)
    token_out = regroup_rows(fill(out_flat, source_block, recv_slot))[
        send_block, round_index, send_slot
    ].astype(jnp.float32)
    token_total = regroup_totals(fill(total_flat, source_block, recv_slot))[
        send_block, round_index, send_slot
    ]
    mix = jax.nn.softmax(token_total, axis=0)
    token_out4 = token_out.reshape(rounds, rows, heads_here, HEAD_DIM)
    attended_low = (
        jnp.sum(mix[..., None] * token_out4, 0).reshape(rows, local_width).astype(jnp.bfloat16)
    )
    sum_one = stream_one.astype(jnp.float32) + branch_sum(
        jnp.dot(attended_low, merge_full, preferred_element_type=jnp.float32)
    )
    normal_two, factor_two, normed_two = norm_forward(sum_one, second_gain, second_bias)
    rows_two = full_rows(normed_two.astype(jnp.bfloat16))
    expand_full, shrink_full = (
        lax.all_gather(expand_weight, "seq", axis=0, tiled=True),
        lax.all_gather(shrink_weight, "seq", axis=1, tiled=True),
    )
    hidden = jnp.dot(rows_two, expand_full, preferred_element_type=jnp.float32)
    active, gelu_pull = jax.vjp(partial(jax.nn.gelu, approximate=False), hidden)
    active_low = active.astype(jnp.bfloat16)
    sum_two = stream_two.astype(jnp.float32) + branch_sum(
        jnp.dot(active_low, shrink_full, preferred_element_type=jnp.float32)
    )
    grad_rows_two = full_rows(grad_two)
    grad_active = jnp.dot(grad_rows_two, shrink_full.T, preferred_element_type=jnp.float32)
    grad_hidden = gelu_pull(grad_active)[0].astype(jnp.bfloat16)
    grad_shrink = jnp.dot(active_low.T, grad_rows_two, preferred_element_type=jnp.float32)
    grad_expand = jnp.dot(rows_two.T, grad_hidden, preferred_element_type=jnp.float32)
    grad_normed_two = branch_sum(
        jnp.dot(grad_hidden, expand_full.T, preferred_element_type=jnp.float32)
    )
    extra_one, grad_second_gain, grad_second_bias = norm_backward(
        grad_normed_two, normal_two, factor_two, second_gain
    )
    total_one = grad_one.astype(jnp.float32) + extra_one
    total_low = total_one.astype(jnp.bfloat16)
    grad_rows_one = full_rows(total_low)
    grad_attended = jnp.dot(grad_rows_one, merge_full.T, preferred_element_type=jnp.float32).astype(
        jnp.bfloat16
    )
    grad_merge = jnp.dot(attended_low.T, grad_rows_one, preferred_element_type=jnp.float32)
    grad_float = grad_attended.astype(jnp.float32).reshape(rows, heads_here, HEAD_DIM)
    dots = jnp.sum(token_out4 * grad_float[None], -1)
    grad_total = mix * (dots - jnp.sum(mix * dots, 0, keepdims=True))
    grad_out_low = (
        (mix[..., None] * grad_float[None]).astype(jnp.bfloat16).reshape(rounds, rows, local_width)
    )
    sorted_grad_out = regroup_rows(fill(grad_out_low, send_block, send_slot))[
        source_block, round_index, recv_slot
    ]
    sorted_grad_total = regroup_totals(fill(grad_total, send_block, send_slot))[
        source_block, round_index, recv_slot
    ]
    grad_groups = sorted_grad_out.reshape(rounds, blocks, GROUP, heads_here, HEAD_DIM)
    total_grad_groups = jnp.transpose(
        sorted_grad_total.reshape(rounds, blocks, GROUP, heads_here), (0, 1, 3, 2)
    )[..., None]
    probs = jnp.exp(masked_scores() - totals)
    probs_again = probs.astype(jnp.bfloat16)
    grad_probs = jnp.einsum(
        "rncha,rnkha->rnhck", grad_groups, key_value, preferred_element_type=jnp.float32
    )
    grad_key_value = jnp.einsum(
        "rnhck,rncha->rnkha", probs_again, grad_groups, preferred_element_type=jnp.float32
    )
    inner = jnp.sum(probs * grad_probs, -1, keepdims=True)
    grad_scores = jnp.where(
        live[:, :, None], probs * (grad_probs - inner + total_grad_groups), 0.0
    ).astype(jnp.bfloat16)
    grad_query_groups = (
        jnp.einsum("rnhck,rnkha->rncha", grad_scores, key_unit, preferred_element_type=jnp.float32)
        * scale
    )
    grad_key_unit = (
        jnp.einsum(
            "rnhck,rncha->rnkha", grad_scores, query_groups, preferred_element_type=jnp.float32
        )
        * scale
    )
    edge_grad = from_behind(
        jnp.concatenate([grad_key_unit[:, 0, GROUP:], grad_key_value[:, 0, GROUP:]], -1).astype(
            jnp.bfloat16
        ),
        "seq",
        -1,
    ).astype(jnp.float32)

    def fold_keys(grad_keys, arriving):
        own = grad_keys[:, :, :GROUP]
        later = jnp.concatenate([grad_keys[:, 1:, GROUP:], arriving[:, None]], 1)
        return (own + later).reshape(rounds, rows, heads_here, HEAD_DIM)

    grad_unit = fold_keys(grad_key_unit, edge_grad[..., :HEAD_DIM])
    grad_sorted_value = fold_keys(grad_key_value, edge_grad[..., HEAD_DIM:])
    grad_sorted_query = grad_query_groups.reshape(
        rounds, rows, heads_here, HEAD_DIM
    ) + inverse_norm * (grad_unit - unit_float * jnp.sum(unit_float * grad_unit, -1, keepdims=True))
    moved_first, moved_second = regroup_pair(
        fill(grad_sorted_query.reshape(rounds, rows, local_width), source_block, recv_slot),
        fill(grad_sorted_value.reshape(rounds, rows, local_width), source_block, recv_slot),
    )
    token_grad_query = moved_first[send_block, round_index, send_slot]
    token_grad_value = moved_second[send_block, round_index, send_slot]
    grad_query_low = jnp.sum(token_grad_query, 0).astype(jnp.bfloat16)
    grad_value_low = jnp.sum(token_grad_value, 0).astype(jnp.bfloat16)
    grad_query_full = jnp.dot(rows_one.T, grad_query_low, preferred_element_type=jnp.float32)
    grad_value_full = jnp.dot(rows_one.T, grad_value_low, preferred_element_type=jnp.float32)
    grad_normed_one = branch_sum(
        jnp.dot(grad_query_low, query_full.T, preferred_element_type=jnp.float32)
        + jnp.dot(grad_value_low, value_full.T, preferred_element_type=jnp.float32)
    )
    extra_two, grad_first_gain, grad_first_bias = norm_backward(
        grad_normed_one, normal_one, factor_one, first_gain
    )
    input_grad_two = (grad_two.astype(jnp.float32) + extra_two).astype(jnp.bfloat16)
    query_part, value_part, merge_part, expand_part, shrink_part = (
        lax.psum_scatter(grad_query_full, "seq", scatter_dimension=0, tiled=True),
        lax.psum_scatter(grad_value_full, "seq", scatter_dimension=0, tiled=True),
        lax.psum_scatter(grad_merge, "seq", scatter_dimension=1, tiled=True),
        lax.psum_scatter(grad_expand, "seq", scatter_dimension=0, tiled=True),
        lax.psum_scatter(grad_shrink, "seq", scatter_dimension=1, tiled=True),
    )
    first_gain_sum, first_bias_sum, second_gain_sum, second_bias_sum = lax.psum(
        (grad_first_gain, grad_first_bias, grad_second_gain, grad_second_bias), "seq"
    )
    return (
        sum_one.astype(jnp.bfloat16),
        sum_two.astype(jnp.bfloat16),
        total_low,
        input_grad_two,
        query_part,
        value_part,
        merge_part,
        expand_part,
        shrink_part,
        first_gain_sum,
        first_bias_sum,
        second_gain_sum,
        second_bias_sum,
    )


def flip(index, bit):
    return index + bit - 2 * bit * ((index // bit) % 2)


def flipped(index, bits):
    for bit in (1, 2, 4):
        if bits & bit:
            index = flip(index, bit)
    return index


class Place:
    def __init__(self):
        self.seq, self.head = lax.axis_index("seq"), lax.axis_index("head")
        self.line, self.side = self.seq // 2, self.seq % 2
        self.pair, self.core = self.head // 2, self.head % 2
        self.turn = self.side * 2 + self.core
        self.home = self.line // 2 == self.core
        self.away = self.line // 2 != self.core

    def peer(self, seq_bits, head_bits=0):
        return (flipped(self.seq, seq_bits), flipped(self.head, head_bits))

    def member(self, bits):
        return self.peer(bits // 2, bits % 2)

    def chunk(self, turn, half):
        return (2 * (turn % 2) + half) * 2 + turn // 2

    def greet(self):
        peers = [self.peer(bits) for bits in range(1, 8)]
        peers += [self.peer(0, bits) for bits in range(1, 4)]
        peers += [self.peer(bits, 1) for bits in (1, 2, 4, 6)]
        barrier = pltpu.get_barrier_semaphore()
        for peer in peers:
            pl.semaphore_signal(barrier, inc=1, device_id=peer, device_id_type=MESH)
        return partial(pl.semaphore_wait, barrier, len(peers))


class Copy:
    def __init__(self, copy, starts, lands):
        self.copy, self.starts, self.lands = copy, starts, lands
        self.when(starts, copy.start)

    def when(self, condition, act):
        if condition is None:
            act()
        else:
            pl.when(condition)(act)

    def wait_recv(self):
        self.when(self.lands, self.copy.wait_recv)

    def wait_send(self):
        self.when(self.starts, self.copy.wait_send)


class Wires:
    def __init__(self, send, receive):
        self.send, self.receive, self.copies = send, receive, []

    def push(self, source, target, device, starts=None, lands=None):
        index = len(self.copies)
        copy = pltpu.make_async_remote_copy(
            src_ref=source,
            dst_ref=target,
            send_sem=self.send.at[index],
            recv_sem=self.receive.at[index],
            device_id=device,
            device_id_type=MESH,
        )
        self.copies.append(Copy(copy, starts, lands))
        return self.copies[-1]

    def settle(self, copies):
        for copy in copies:
            copy.wait_send()
        done = [id(copy) for copy in copies]
        self.copies = [None if id(copy) in done else copy for copy in self.copies]

    def drain(self):
        self.settle([copy for copy in self.copies if copy is not None])


class Spread:
    def __init__(self, wires, place):
        self.wires, self.place, self.copies = wires, place, []

    def start(self, source_at, target, half=None):
        p = self.place
        for bits, starts in ((4, p.away), (6, p.away), (2, p.home)):
            seq = flipped(p.seq, bits)
            head = p.head - p.core + p.line // 2
            lands = starts
            if half is not None:
                starts = jnp.logical_and(starts, (seq // 2) % 2 == half)
                lands = jnp.logical_and(lands, p.line % 2 == half)
            copy = self.wires.push(source_at(seq // 2), target, (seq, head), starts, lands)
            self.copies.append(copy)

    def finish(self):
        for copy in self.copies:
            copy.wait_recv()


class TokenGather:
    def __init__(self, wires, place, everyone, rows):
        self.wires, self.place, self.everyone, self.rows = wires, place, everyone, rows
        self.line = {2: [], 4: [], 6: []}
        self.own = []

    def slot(self, seq, part):
        return columns_at(rows_at(self.everyone, seq, self.rows), part, HEAD_DIM)

    def start(self, packed, part):
        p = self.place
        mine = self.slot(p.seq, part)
        for bits, starts in ((4, p.away), (6, p.away), (2, p.home)):
            seq = flipped(p.seq, bits)
            self.line[bits].append(
                self.wires.push(
                    packed.at[(seq // 2) % 2, part],
                    mine,
                    (seq, p.head - p.core + part),
                    starts,
                    p.core == part,
                )
            )
        source = packed.at[p.line % 2, part]
        self.own.append(self.wires.push(source, mine, p.peer(0, 1), p.home, p.away))

        @pl.when(p.home)
        def _():
            mine[...] = source[...]

    def pass_own(self):
        p = self.place
        for copy in self.own:
            copy.wait_recv()
        block = self.slot(p.seq, p.core)
        self.beside = {0: self.wires.push(block, block, p.peer(1))}
        self.shared = {}

    def forward(self, bits):
        p = self.place
        for copy in self.line[bits]:
            copy.wait_recv()
        block = self.slot(flipped(p.seq, bits), p.core)
        self.beside[bits] = self.wires.push(block, block, p.peer(1))
        self.shared[bits] = self.wires.push(block, block, p.peer(0, 1))

    def share(self, bits):
        p = self.place
        self.beside[bits].wait_recv()
        block = self.slot(flipped(p.seq, bits + 1), p.core)
        self.shared[bits + 1] = self.wires.push(block, block, p.peer(0, 1))

    def land(self, bits):
        self.shared[bits].wait_recv()

    def settle(self):
        lines = [copy for copies in self.line.values() for copy in copies]
        self.wires.settle(lines + self.own + [*self.beside.values(), *self.shared.values()])


class SeqGather:
    def __init__(self, wires, place, slot):
        self.wires, self.place, self.slot = wires, place, slot

    def start(self, source, for_far=None):
        p, mine = self.place, self.slot(self.place.seq)
        far = source if for_far is None else for_far
        self.arriving = {4: self.wires.push(far, mine, p.peer(4))}
        self.arriving[2] = self.wires.push(source, mine, p.peer(2))
        self.beside = {0: self.wires.push(source, mine, p.peer(1))}

    def forward(self, bits):
        p = self.place
        self.arriving[bits].wait_recv()
        block = self.slot(flipped(p.seq, bits))
        if bits == 4:
            self.arriving[6] = self.wires.push(block, block, p.peer(2))
        self.beside[bits] = self.wires.push(block, block, p.peer(1))

    def land(self, bits):
        self.beside[bits].wait_recv()

    def settle(self):
        self.wires.settle([*self.arriving.values(), *self.beside.values()])

    def finish(self):
        for bits in self.beside:
            self.land(bits)
        self.settle()


class PairGather:
    def __init__(self, wires, place, slot, both):
        self.wires, self.place, self.slot, self.both = wires, place, slot, both

    def start(self, source):
        p = self.place
        self.first = self.wires.push(source, self.slot(p.seq), p.peer(1))

    def along(self):
        p = self.place
        self.first.wait_recv()
        pair = self.both(p.seq // 2)
        self.far = self.wires.push(pair, pair, p.peer(4))
        self.near = self.wires.push(pair, pair, p.peer(2))

    def forward(self):
        p = self.place
        self.far.wait_recv()
        pair = self.both(flip(p.seq, 4) // 2)
        self.last = self.wires.push(pair, pair, p.peer(2))

    def finish(self):
        self.near.wait_recv()
        self.last.wait_recv()
        self.wires.settle([self.first, self.far, self.near, self.last])


class HeadGather:
    def __init__(self, wires, place, slot):
        self.wires, self.place, self.slot = wires, place, slot

    def start(self, source):
        p = self.place
        mine = self.slot(p.head)
        self.long = self.wires.push(source, mine, p.peer(0, 2))
        self.short = self.wires.push(source, mine, p.peer(0, 1))

    def relay(self):
        p = self.place
        self.long.wait_recv()
        moved = self.slot(flip(p.head, 2))
        self.last = self.wires.push(moved, moved, p.peer(0, 1))

    def finish(self):
        self.short.wait_recv()
        self.last.wait_recv()
        self.wires.settle([self.long, self.short, self.last])


def columns_at(ref, index, width):
    return ref.at[:, pl.ds(pl.multiple_of(index * width, width), width)]


def rows_at(ref, index, width):
    return ref.at[pl.ds(pl.multiple_of(index * width, width), width)]


def span(index, width):
    return pl.ds(pl.multiple_of(index * width, width), width)


def dot(left, right, contract=((1,), (0,))):
    return lax.dot_general(
        left, right, (contract, ((), ())), preferred_element_type=jnp.float32
    )


def diagonal(size):
    return lax.broadcasted_iota(jnp.int32, (size, size), 0) == lax.broadcasted_iota(
        jnp.int32, (size, size), 1
    )


def to_row(column):
    return jnp.sum(jnp.where(diagonal(column.shape[0]), column, 0.0), 0, keepdims=True)


def to_column(row):
    return jnp.sum(jnp.where(diagonal(row.shape[1]), row, 0.0), 1, keepdims=True)


def in_lanes(total):
    bf16, f32 = jnp.bfloat16, jnp.float32
    high = total.astype(bf16).astype(f32)
    middle = (total - high).astype(bf16).astype(f32)
    low = total - high - middle
    lane = lax.broadcasted_iota(jnp.int32, (total.shape[0], 128), 1)
    parts = jnp.where(lane == 0, high, jnp.where(lane == 1, middle, low))
    return jnp.where(lane < 3, parts, 0.0).astype(bf16)


class SeqScatter:
    def __init__(self, wires, place, piece, pair, line):
        self.wires, self.place, self.piece = wires, place, piece
        self.pair, self.line = pair, line

    def start(self):
        p = self.place
        self.beside = {}
        for bits in (6, 2, 4, 0):
            source = self.piece(flipped(p.seq, bits + 1))
            self.beside[bits] = self.wires.push(source, self.pair.at[bits // 2], p.peer(1))

    def add(self, bits, more=None):
        at, f32 = self.pair.at[bits // 2], jnp.float32
        self.beside[bits].wait_recv()
        mine = self.piece(flipped(self.place.seq, bits))[...]
        total = at[...].astype(f32) + mine.astype(f32)
        if more is not None:
            total += more[...].astype(f32)
        at[...] = total.astype(jnp.bfloat16)
        return at

    def along(self):
        device = self.place.peer(2)
        self.shares = self.wires.push(self.add(6), self.line.at[0], device)
        self.near = self.wires.push(self.add(2), self.line.at[1], device)

    def across(self):
        self.shares.wait_recv()
        total = self.add(4, self.line.at[0])
        self.far = self.wires.push(total, self.line.at[2], self.place.peer(4))

    def finish(self, target):
        p, f32 = self.place, jnp.float32
        self.beside[0].wait_recv()
        total = self.piece(p.seq)[...].astype(f32) + self.pair.at[0][...].astype(f32)
        self.near.wait_recv()
        total += self.line.at[1][...].astype(f32)
        self.far.wait_recv()
        target[...] = total + self.line.at[2][...].astype(f32)


class PairScatter:
    def __init__(self, wires, place, piece, both, line, pair):
        self.wires, self.place, self.piece, self.both = wires, place, piece, both
        self.line, self.pair = line, pair

    def start(self):
        p, device = self.place, self.place.peer(2)
        share, near = (self.both(flipped(p.seq, bits) // 2) for bits in (6, 2))
        self.shares = self.wires.push(share, self.line.at[0], device)
        self.near = self.wires.push(near, self.line.at[1], device)

    def across(self):
        p, f32 = self.place, jnp.float32
        self.shares.wait_recv()
        mine = self.both(flip(p.seq, 4) // 2)
        at = self.line.at[0]
        at[...] = (at[...].astype(f32) + mine[...].astype(f32)).astype(jnp.bfloat16)
        self.far = self.wires.push(at, self.line.at[2], p.peer(4))

    def side(self):
        p, f32 = self.place, jnp.float32
        self.near.wait_recv()
        self.far.wait_recv()
        mine = self.both(p.seq // 2)
        total = mine[...].astype(f32) + self.line.at[1][...].astype(f32)
        total += self.line.at[2][...].astype(f32)
        self.wires.settle([self.near])
        mine[...] = total.astype(jnp.bfloat16)
        self.last = self.wires.push(self.piece(flip(p.seq, 1)), self.pair, p.peer(1))

    def finish(self, target):
        self.last.wait_recv()
        f32 = jnp.float32
        target[...] = self.piece(self.place.seq)[...].astype(f32) + self.pair[...].astype(f32)


class Phases:
    def __init__(self, r, turns):
        self.r, self.turns = r, turns
        self.place = Place()
        self.wires = Wires(r.send, r.receive)
        self.rows, self.width = r.two.shape
        self.wide = r.rows_one.shape[1]
        self.count = self.wide // self.width
        self.devices = r.everyone.shape[0] // self.rows
        self.pair = self.devices // turns
        self.units = self.devices


    def spread_columns(self, ref, index):
        column = ref[span(index, self.rows), :].astype(jnp.int32)
        lane = lax.broadcasted_iota(jnp.int32, column.shape, 1)
        parts = [
            jnp.where(column == lane + 128 * i, 1.0, 0.0).astype(jnp.bfloat16)
            for i in range(self.rows // 128)
        ]
        return jnp.concatenate(parts, 1)

    def spread_rows(self, ref, index):
        row = ref[index]
        place = lax.broadcasted_iota(jnp.int32, (self.rows, self.rows), 0)
        return jnp.where(row == place, 1.0, 0.0).astype(jnp.bfloat16)

    def from_units(self, ref, table, index):
        return jnp.concatenate([ref[table[index, unit]] for unit in range(self.units)], 0)

    def to_units(self, index, rows):
        first, step = index * self.units, self.rows // self.units
        for unit in range(self.units):
            self.r.mid[first + unit] = rows[unit * step : (unit + 1) * step].astype(jnp.bfloat16)

    def sort_chunk(self, source, index):
        r = self.r
        here = span(index, self.rows)
        self.to_units(index, dot(self.spread_columns(r.chunk_column, index), source[here, :]))

    def sorted_block(self, index):
        r = self.r
        return dot(
            self.spread_columns(r.block_column, index), self.from_units(r.mid, r.units, index)
        )

    def unsort_block(self, source, index):
        r = self.r
        here = span(index, self.rows)
        self.to_units(index, dot(self.spread_rows(r.block_row, index), source[here, :]))

    def unsorted_chunk(self, index):
        r = self.r
        return dot(
            self.spread_rows(r.chunk_row, index), self.from_units(r.mid, r.units_back, index)
        )

    def column_of(self, row):
        pieces = [to_column(row[:, i : i + 128]) for i in range(0, self.rows, 128)]
        return jnp.concatenate(pieces, 0)

    def row_of(self, column):
        pieces = [to_row(column[i : i + 128]) for i in range(0, self.rows, 128)]
        return jnp.concatenate(pieces, 1)

    def wide_column(self, column):
        return jnp.broadcast_to(column, (self.rows, 128)).astype(jnp.int32).astype(jnp.int16)

    def line_of(self, ref, block):
        return ref[pl.ds(self.place.turn, 1), span(block, self.rows)]

    def unit_tables(self):
        r = self.r
        bf16, f32, i32 = jnp.bfloat16, jnp.float32, jnp.int32
        unit = self.rows // self.units
        row = lax.broadcasted_iota(i32, (128, 128), 0)
        column = lax.broadcasted_iota(i32, (128, 128), 1)
        by_chunk = r.shares[...].astype(bf16)
        by_block = dot(by_chunk, jnp.where(row == column, 1.0, 0.0).astype(bf16)[:8], ((0,), (0,)))
        by_block = by_block[:8].astype(bf16)
        earlier = jnp.where(row < column, 1.0, 0.0).astype(bf16)
        below = jnp.where(row > column, 1.0, 0.0).astype(bf16)[:8, :8]
        start = (column[:8] * unit).astype(f32)

        def find(share, offset, other):
            segment, move = jnp.zeros((8, 128), f32), jnp.zeros((8, 128), f32)
            ends = offset + share.astype(f32)
            for i in range(self.units):
                segment += jnp.where(ends[:, i : i + 1] <= start, 1.0, 0.0)
            for i in range(self.units):
                shift = (other - offset)[:, i : i + 1]
                move += jnp.where(segment == float(i), shift, 0.0)
            place = ((segment * self.rows + start + move) * (1.0 / unit)).astype(i32)
            return jnp.clip(place, 0, self.units * self.units - 1)

        in_chunk, in_block = dot(by_chunk, earlier), dot(below, by_chunk)
        r.unit_rows[1] = find(by_chunk, in_chunk, in_block)
        r.unit_rows[0] = find(by_block, dot(by_block, earlier), dot(below, by_block))
        copies = [
            pltpu.make_async_copy(r.unit_rows.at[i], target, r.local.at[i])
            for i, target in enumerate((r.units, r.units_back))
        ]
        for copy in copies:
            copy.start()
        for copy in copies:
            copy.wait()

    def bucket_tables(self):
        r = self.r
        f32, i32 = jnp.float32, jnp.int32
        rows = self.rows
        most = -(-(self.devices * (rows // GROUP + 1) + 1) // 128) * 128

        value = lax.broadcasted_iota(i32, (most, rows), 0)

        def count(block, until):
            return until + jnp.sum(
                jnp.where(self.line_of(r.bucket, block) <= value, 1.0, 0.0), 1, keepdims=True
            )

        until = lax.fori_loop(0, self.devices, count, jnp.zeros((most, 1), f32))
        r.until[...] = jnp.broadcast_to(until, (most, 128))

    def block_tables(self, start, stop):
        r = self.r
        bf16, f32, i32 = jnp.bfloat16, jnp.float32, jnp.int32
        rows, lines = self.rows, self.rows // 128
        tokens = rows * self.devices

        def first(block, carry):
            order = self.line_of(r.order, block)
            until = r.until[:, 0:1].astype(i32)
            lane = lax.broadcasted_iota(i32, (1, rows), 1)
            bucket = jnp.sum(
                jnp.where(until <= lane + block * rows, 1.0, 0.0), 0, keepdims=True
            )
            key = bucket * tokens + order.astype(f32)
            for i in range(lines):
                r.keys[block * lines + i] = key[:, i * 128 : (i + 1) * 128]
            chunk = order // rows
            each = lax.broadcasted_iota(i32, (8, rows), 0)
            share = jnp.sum(jnp.where(chunk == each, 1.0, 0.0), 1, keepdims=True)
            at = lax.broadcasted_iota(i32, (8, 128), 1)
            r.shares[...] += jnp.where(at == block, share, 0.0)
            place = (chunk * rows + lane).astype(f32)
            slot = jnp.sum(jnp.where(place < self.column_of(place), 1.0, 0.0), 1, keepdims=True)
            r.block_column[span(block, rows), :] = self.wide_column(slot)
            r.block_row[block] = self.row_of(slot).astype(i32)
            local = self.column_of((order - chunk * rows).astype(f32))
            high = jnp.floor(local * 0.0625)
            at = lax.broadcasted_iota(i32, (rows, 2 * HEAD_DIM), 1)
            parts = jnp.where(at == 0, high, jnp.where(at == 1, local - 16.0 * high, 0.0))
            r.round_rows[span(block, rows), :] = parts.astype(bf16)
            self.unsort_block(r.round_rows, block)
            return carry

        lax.fori_loop(start, stop, first, 0)

    def chunk_tables(self):
        r = self.r
        f32, i32 = jnp.float32, jnp.int32
        rows = self.rows

        def second(chunk, carry):
            parts = self.from_units(r.mid, r.units_back, chunk)[:, 0:128].astype(f32)
            token = 16.0 * parts[:, 0:1] + parts[:, 1:2]
            r.chunk_column[span(chunk, rows), :] = self.wide_column(token)
            r.chunk_row[chunk] = self.row_of(token).astype(i32)
            return carry

        lax.fori_loop(0, self.devices, second, 0, unroll=2)

    def codes(self, index):
        r = self.r
        tokens = self.rows * self.devices
        groups = tokens // 128
        low = lax.broadcasted_iota(jnp.int32, (1, 128), 1) < GROUP
        result = []
        for i in range(2):
            here = 2 * index + i
            keys, before = r.keys[here], r.keys[(here + groups - 1) % groups]
            query = to_column(keys)
            least = jnp.floor(query * (1.0 / tokens)) * tokens
            for half, window in enumerate((jnp.where(low, keys, before), keys)):
                at = slice(half * GROUP, (half + 1) * GROUP)
                allowed = (window <= query[at]) & (window >= least[at])
                result.append(
                    jnp.where(window == query[at], 1.0, jnp.where(allowed, 0.0, 2.0))
                )
        return jnp.concatenate(result, 0)

    def window(self, rows, block):
        before = rows[block * GROUP : (block + 1) * GROUP]
        own = rows[(block + 1) * GROUP : (block + 2) * GROUP]
        return jnp.concatenate([own, before] if block % 2 == 0 else [before, own], 0)

    def over_rows(self, ref):
        step = ref.shape[0] // self.devices
        return SeqGather(self.wires, self.place, lambda seq: rows_at(ref, seq, step))

    def over_columns(self, ref):
        step = ref.shape[1] // self.devices
        return SeqGather(self.wires, self.place, lambda seq: columns_at(ref, seq, step))

    def start_seq(self, gather, source):
        gather.start(source)
        gather.slot(self.place.seq)[...] = source[...]

    def start_head(self, gather, source):
        gather.start(source)
        gather.slot(self.place.head)[...] = source[...]

    def over_head(self, ref):
        return HeadGather(self.wires, self.place, lambda head: columns_at(ref, head, self.width))

    def project(self):
        r, place, wires = self.r, self.place, self.wires
        bf16, f32 = jnp.bfloat16, jnp.float32
        arrived = place.greet()
        half = self.devices // 2
        r.shares[...] = jnp.zeros_like(r.shares)
        self.bucket_tables()
        self.block_tables(0, half)
        arrived()
        stream = self.over_head(r.two_full)
        small = self.over_head(r.params_full)
        self.start_head(stream, r.two)
        for row, item in enumerate((r.gain_one, r.bias_one, r.gain_two, r.bias_two)):
            r.params[row : row + 1, :] = item[...]
        r.params[4:8, :] = jnp.zeros((4, self.width), f32)
        self.start_head(small, r.params)
        query, value = self.over_rows(r.query_full), self.over_rows(r.value_full)
        self.start_seq(query, r.query)
        self.start_seq(value, r.value)
        self.bulk()
        self.begin(self.merge)
        self.begin(self.expand[0])
        self.block_tables(half, self.devices)
        for weight in (query, value):
            for bits in (4, 2):
                weight.forward(bits)
        self.begin(self.expand[1])
        small.relay()
        stream.relay()
        query.forward(6)
        value.forward(6)
        small.finish()
        stream.finish()

        def normalise(tile, carry):
            here = span(tile, 128)
            rows = r.two_full[here, :].astype(f32)
            center = jnp.mean(rows, 1, keepdims=True)
            offset = rows - center
            factor = lax.rsqrt(jnp.mean(offset * offset, 1, keepdims=True) + 1e-05)
            r.center_one[here, :] = jnp.broadcast_to(center, (128, 128))
            r.factor_one[here, :] = jnp.broadcast_to(factor, (128, 128))
            r.rows_one[here, :] = (
                offset * factor * r.params_full[0:1, :] + r.params_full[1:2, :]
            ).astype(bf16)
            return carry

        lax.fori_loop(0, self.rows // 128, normalise, 0)
        self.tokens = TokenGather(self.wires, place, r.everyone, self.rows)
        self.project_one(query, r.query_full, 0)
        self.project_one(value, r.value_full, 1)

    def project_one(self, weight, full, part):
        r = self.r
        weight.finish()

        def multiply(tile, carry):
            here = span(tile, 256)
            result = dot(r.rows_one[here, :], full[...]).astype(jnp.bfloat16)
            for which in range(self.pair):
                r.packed[which, part, here, :] = result[
                    :, which * HEAD_DIM : (which + 1) * HEAD_DIM
                ]
            return carry

        lax.fori_loop(0, self.rows // 256, multiply, 0)
        self.tokens.start(r.packed, part)

    def bulk(self):
        r, place = self.r, self.place
        my_rows = rows_at(r.merge_full, place.head, r.merge.shape[0])
        self.merge = SeqGather(
            self.wires, place, lambda seq: columns_at(my_rows, seq, r.merge.shape[1])
        )
        self.merge.source = r.merge
        self.expand, self.shrink = [], []
        for part in range(2):
            step, columns = r.expand.shape[0], r.expand.shape[1] // 2
            cut = pl.ds(part * columns, columns)
            slot = lambda seq, cut=cut: rows_at(r.expand_full, seq, step).at[:, cut]
            if part:
                gather = SeqGather(self.wires, place, slot)
            else:
                both = lambda pair: rows_at(r.expand_full, pair, 2 * step).at[:, 0:columns]
                gather = PairGather(self.wires, place, slot, both)
            gather.source = r.expand.at[:, cut]
            self.expand.append(gather)
            rows, width = r.shrink.shape[0] // 2, r.shrink.shape[1]
            down = pl.ds(part * rows, rows)
            gather = SeqGather(
                self.wires,
                place,
                lambda seq, down=down: columns_at(r.shrink_full.at[down], seq, width),
            )
            gather.source = r.shrink.at[down]
            self.shrink.append(gather)
        self.one, self.grads = self.over_head(r.one_full), self.over_head(r.grad_full)

    def begin(self, gather):
        self.start_seq(gather, gather.source)

    def go_on(self, gather):
        for bits in (4, 2, 6):
            gather.forward(bits)

    def begin_streams(self):
        self.start_head(self.one, self.r.one)
        self.start_head(self.grads, self.r.grad_two)

    def begin_merge_rows(self):
        r, place = self.r, self.place
        self.merge.finish()
        self.heads = HeadGather(
            self.wires, place, lambda head: rows_at(r.merge_full, head, r.merge.shape[0])
        )
        self.heads.start(self.heads.slot(place.head))

    def sort_tokens(self):
        r, place = self.r, self.place
        bf16, f32 = jnp.bfloat16, jnp.float32
        tokens = self.tokens
        self.unit_tables()
        tokens.pass_own()
        for bits in (2, 4, 6):
            tokens.forward(bits)
        self.go_on(self.merge)
        self.go_on(self.expand[1])
        self.expand[0].along()
        self.begin_streams()
        self.begin(self.shrink[0])
        self.chunk_tables()
        self.sort_chunk(r.everyone, place.seq)
        for bits in (2, 4, 6):
            tokens.land(bits)
            self.sort_chunk(r.everyone, flipped(place.seq, bits))
        for bits in (0, 2, 4, 6):
            tokens.share(bits)
        for bits in (0, 2, 4, 6):
            tokens.land(bits + 1)
            self.sort_chunk(r.everyone, flipped(place.seq, bits + 1))
        tokens.settle()

        def second(block, carry):
            rows = self.sorted_block(block)
            here = span(block, self.rows)
            later = pl.ds(pl.multiple_of(block * self.rows + GROUP, GROUP), self.rows)
            query = rows[:, :HEAD_DIM]
            r.sorted_query[here, :] = query.astype(bf16)
            factor = lax.rsqrt(jnp.sum(query * query, 1, keepdims=True) + 1e-06)
            r.unit[later, :] = (query * factor).astype(bf16)
            r.key_value[later, :] = rows[:, HEAD_DIM:].astype(bf16)
            return carry

        lax.fori_loop(0, self.devices, second, 0, unroll=2)
        last = pl.ds(self.devices * self.rows, GROUP)
        r.unit[0:GROUP, :] = r.unit[last, :]
        r.key_value[0:GROUP, :] = r.key_value[last, :]

    def attend(self):
        r = self.r
        bf16, f32 = jnp.bfloat16, jnp.float32
        scale = HEAD_DIM ** (-0.5)
        some = 4 * GROUP

        def group(index, carry):
            here = span(index, some)
            longer = pl.ds(pl.multiple_of(index * some, some), some + GROUP)
            query, unit, value = r.sorted_query[here, :], r.unit[longer, :], r.key_value[longer, :]
            raw = [
                dot(query[i * GROUP : (i + 1) * GROUP], self.window(unit, i), ((1,), (1,)))
                for i in range(4)
            ]
            code = self.codes(index)
            scores = jnp.where(
                code == 0.0,
                jnp.concatenate(raw, 0) * scale,
                jnp.where(code == 1.0, own_score, masked_score),
            )
            peak = jnp.max(scores, 1, keepdims=True)
            power = jnp.exp(scores - peak)
            total = jnp.sum(power, 1, keepdims=True)
            probs = power * (1.0 / total)
            r.probs[here, :] = probs
            probs = probs.astype(bf16)
            result = [
                dot(probs[i * GROUP : (i + 1) * GROUP], self.window(value, i)) for i in range(4)
            ]
            r.round_rows[here, :HEAD_DIM] = jnp.concatenate(result, 0).astype(bf16)
            r.round_rows[here, HEAD_DIM:] = in_lanes(peak + jnp.log(total))
            return carry

        lax.fori_loop(0, self.devices * self.rows // some, group, 0, unroll=2)

    def return_rows(self):
        r, place, wires = self.r, self.place, self.wires
        bf16, f32 = jnp.bfloat16, jnp.float32

        def first(block, carry):
            self.unsort_block(r.round_rows, block)
            return carry

        lax.fori_loop(0, self.devices, first, 0, unroll=2)
        self.shares, self.sides = {}, []
        for half in range(self.pair):
            for bits in (3, 1, 2, 0):
                turn = flipped(place.turn, bits)
                rows = self.unsorted_chunk(place.chunk(turn, half))
                total = jnp.sum(rows[:, HEAD_DIM:], 1, keepdims=True)
                lines = [to_row(total[i : i + 128]) for i in range(0, self.rows, 128)]
                r.out[bits, half] = rows[:, :HEAD_DIM].astype(bf16)
                r.total[bits, half] = jnp.concatenate(lines, 0)
                if bits % 2:
                    self.shares[bits, half] = [
                        wires.push(
                            source.at[bits, half], target.at[bits // 2, half], place.peer(0, 1)
                        )
                        for source, target in ((r.total, r.share_total), (r.out, r.share))
                    ]
            for copy in self.shares[3, half]:
                copy.wait_recv()
            r.merged_total[half] = self.combine(
                (
                    (r.total.at[2, half], r.out.at[2, half]),
                    (r.share_total.at[1, half], r.share.at[1, half]),
                ),
                (r.merged.at[half],),
            )
            self.sides.append(
                [
                    wires.push(source.at[half], target.at[half], place.peer(1))
                    for source, target in ((r.merged_total, r.side_total), (r.merged, r.side))
                ]
            )

    def combine(self, terms, targets):
        f32 = jnp.float32
        totals = [total[...] for total, _ in terms]
        peak = totals[0]
        for total in totals[1:]:
            peak = jnp.maximum(peak, total)
        whole = peak + jnp.log(sum(jnp.exp(total - peak) for total in totals))
        for part in range(self.rows // 128):
            here = pl.ds(part * 128, 128)
            rows = jnp.zeros((128, HEAD_DIM), f32)
            for total, (_, out) in zip(totals, terms):
                mix = to_column(jnp.exp(total - whole)[part : part + 1, :])
                rows += mix * out[here, :].astype(f32)
            for target in targets:
                target[here, :] = rows.astype(target.dtype)
        return whole

    def mix_rounds(self):
        r, place, wires = self.r, self.place, self.wires
        mine = columns_at(r.attended_full, place.pair * 4 + place.line, HEAD_DIM)
        back = Spread(wires, place)
        self.wholes = []
        for half in range(self.pair):
            for copy in self.shares[1, half] + self.sides[half]:
                copy.wait_recv()
            r.whole_total[place.turn, half] = self.combine(
                (
                    (r.total.at[0, half], r.out.at[0, half]),
                    (r.share_total.at[0, half], r.share.at[0, half]),
                    (r.side_total.at[half], r.side.at[half]),
                ),
                (r.attended.at[half], r.attended_wide.at[half]),
            )
            back.start(lambda line: r.attended.at[line % 2], mine, half)
            whole = r.whole_total.at[place.turn, half]
            for bits in (1, 2, 3):
                self.wholes.append(wires.push(whole, whole, place.member(bits)))

        @pl.when(place.home)
        def _():
            mine[...] = r.attended[place.line % 2]

        back.finish()
        gather = self.over_head(r.attended_full)
        gather.start(gather.slot(place.head))
        gather.relay()
        gather.finish()


    def normalise_sum(self):
        r, place = self.r, self.place
        bf16, f32 = jnp.bfloat16, jnp.float32
        tile_rows = self.rows // 2
        for tile in range(2):
            here = pl.ds(tile * tile_rows, tile_rows)
            total = r.one_full[here, :].astype(f32) + dot(r.attended_full[here, :], r.merge_full[...])
            center = jnp.mean(total, 1, keepdims=True)
            offset = total - center
            factor = lax.rsqrt(jnp.mean(offset * offset, 1, keepdims=True) + 1e-05)
            normal = offset * factor
            r.tall[here, :] = total
            mine = columns_at(r.tall.at[here], place.head, self.width)
            r.result_one[here, :] = mine[...].astype(bf16)
            r.tall[here, :] = normal
            r.normal_two[here, :] = mine[...]
            r.factor_two[here, :] = jnp.broadcast_to(factor, (tile_rows, 128))
            r.rows_two[here, :] = (normal * r.params_full[2:3, :] + r.params_full[3:4, :]).astype(
                bf16
            )

    def feed_half(self, half, tile):
        r = self.r
        bf16 = jnp.bfloat16
        tile_rows, step = self.rows // 2, r.active.shape[1] // 2
        here, units = pl.ds(tile * tile_rows, tile_rows), pl.ds(half * step, step)
        hidden = dot(r.rows_two[here, :], r.expand_full[:, units])
        below = 0.5 * (1.0 + lax.erf(hidden * (0.5**0.5)))
        r.active[here, units] = (hidden * below).astype(bf16)
        slope = below + hidden * jnp.exp(-0.5 * hidden * hidden) * ((2.0 * jnp.pi) ** -0.5)
        grad = dot(r.grad_full[here, :], r.shrink_full[units, :], ((1,), (1,)))
        r.grad_hidden[here, units] = (grad * slope).astype(bf16)

    def shrink_grads(self, half):
        r = self.r
        step = r.active.shape[1] // 2
        units = pl.ds(half * step, step)
        self.weights(r.active.at[:, units], r.grad_full, r.grad_shrink.at[units])
        width = r.shrink.shape[1]
        scatter = SeqScatter(
            self.wires, self.place,
            lambda seq: columns_at(r.grad_shrink.at[units], seq, width),
            r.shrink_pair.at[:, units], r.shrink_line.at[:, units],
        )
        scatter.start()
        self.shrink_out.append(scatter)

    def feed_forward(self):
        r, place, wires = self.r, self.place, self.wires
        self.parts_two, self.shrink_out = [], []
        tile_rows = self.rows // 2
        self.normalise_sum()
        self.expand[0].finish()
        self.shrink[0].finish()
        for tile in range(2):
            self.feed_half(0, tile)
        self.shrink_grads(0)
        self.expand[1].finish()
        self.shrink[1].finish()
        for tile in range(2):
            here = pl.ds(tile * tile_rows, tile_rows)
            self.feed_half(1, tile)
            part = dot(r.grad_hidden[here, :], r.expand_full[...], ((1,), (1,)))
            self.send_part(
                tile, part, r.tall[here, :], r.params_full[2:3, :], r.part_two, r.stat_two,
                r.parts_two, self.parts_two,
            )
        for tile in range(2):
            self.relay_part(tile, r.part_two, r.parts_two, self.parts_two)
        self.send_stats(r.stat_two, r.stats_two, self.parts_two)
        self.shrink_grads(1)

    def send_part(self, tile, part, normal, gain, part_ref, stat_ref, target, copies):
        tile_rows = part.shape[0]
        here = pl.ds(tile * tile_rows, tile_rows)
        scaled = part * gain
        first = jnp.sum(scaled, 1, keepdims=True)
        second = jnp.sum(scaled * normal, 1, keepdims=True)
        lines = tile_rows // 128
        for line in range(lines):
            at = slice(line * 128, (line + 1) * 128)
            row = tile * lines + line
            stat_ref[row : row + 1, :] = to_row(first[at])
            row += self.rows // 128
            stat_ref[row : row + 1, :] = to_row(second[at])
        part_ref[here, :] = part.astype(jnp.bfloat16)
        twin = self.place.peer(0, 1)
        for slot, head in ((1, flip(twin[1], 2)), (0, twin[1])):
            source = columns_at(part_ref.at[here], head, self.width)
            copies.append(self.wires.push(source, target.at[slot, here], twin))

    def relay_part(self, tile, part_ref, target, copies):
        tile_rows = self.rows // 2
        here = pl.ds(tile * tile_rows, tile_rows)
        far = self.place.peer(0, 2)
        copies[2 * tile].wait_recv()
        mine = columns_at(part_ref.at[here], far[1], self.width)[...].astype(jnp.float32)
        total = mine + target[1, here, :].astype(jnp.float32)
        target[1, here, :] = total.astype(jnp.bfloat16)
        copies.append(self.wires.push(target.at[1, here], target.at[2, here], far))

    def send_stats(self, stat_ref, target, copies):
        for bits in (2, 3, 1):
            device = self.place.peer(0, bits)
            copies.append(self.wires.push(stat_ref, target.at[bits - 1], device))

    def norm_back(self, part_ref, parts, stat_ref, stats, normal_at, factor_ref, gain, finish):
        f32 = jnp.float32
        lines = self.rows // 128

        def piece(line, carry):
            here = span(line, 128)
            grad = columns_at(part_ref.at[here], self.place.head, self.width)[...].astype(f32)
            first, second = stat_ref[pl.ds(line, 1), :], stat_ref[pl.ds(line + lines, 1), :]
            for other in range(3):
                if other != 1:
                    grad += parts[other, here, :].astype(f32)
                first += stats[other, pl.ds(line, 1), :]
                second += stats[other, pl.ds(line + lines, 1), :]
            normal = normal_at(here)
            first, second = to_column(first) / self.wide, to_column(second) / self.wide
            finish(here, factor_ref[here, 0:1] * (grad * gain - first - normal * second))
            gains, biases = carry
            return (
                gains + jnp.sum(grad * normal, 0, keepdims=True),
                biases + jnp.sum(grad, 0, keepdims=True),
            )

        zero = jnp.zeros((1, self.width), f32)
        return lax.fori_loop(0, lines, piece, (zero, zero))

    def my_params(self, row):
        return columns_at(self.r.params_full, self.place.head, self.width)[row : row + 1, :]

    def feed_back(self):
        r, place, wires = self.r, self.place, self.wires
        bf16, f32 = jnp.bfloat16, jnp.float32
        self.weights(r.rows_two, r.grad_hidden, r.grad_expand)
        rows, half = r.expand.shape[0], r.expand.shape[1] // 2
        first, second = pl.ds(0, half), pl.ds(half, half)
        self.expand_out = [
            PairScatter(
                wires, place,
                lambda seq: rows_at(r.grad_expand, seq, rows).at[:, first],
                lambda pair: rows_at(r.grad_expand, pair, 2 * rows).at[:, first],
                r.expand_lines, r.expand_side,
            ),
            SeqScatter(
                wires, place,
                lambda seq: rows_at(r.grad_expand, seq, rows).at[:, second],
                r.expand_pair, r.expand_line,
            ),
        ]
        self.expand_out[0].start()
        for copy in self.parts_two[1:2] + self.parts_two[3:]:
            copy.wait_recv()
        wires.settle(self.parts_two)

        def finish(here, change):
            total = r.grad_one[here, :].astype(f32) + change
            r.input_grad_one[here, :] = total.astype(bf16)

        gains, biases = self.norm_back(
            r.part_two, r.parts_two, r.stat_two, r.stats_two,
            lambda here: r.normal_two[here, :], r.factor_two, self.my_params(2), finish,
        )
        r.norm_send[2:3, :], r.norm_send[3:4, :] = gains, biases
        gather = self.over_head(r.grad_rows_one)
        self.start_head(gather, r.input_grad_one)
        gather.relay()

        def feed(tile, carry):
            here = span(tile, 256)
            r.feed[here, :] = dot(r.active[here, :], r.shrink_full[...]).astype(bf16)
            return carry

        lax.fori_loop(0, self.rows // 256, feed, 0)
        gather.finish()

    def weights(self, left, right, target):
        step = min(256, left.shape[1])

        def piece(index, carry):
            columns = span(index, step)
            result = dot(left[:, columns], right[...], ((0,), (0,)))
            target[columns, :] = result.astype(jnp.bfloat16)
            return carry

        lax.fori_loop(0, left.shape[1] // step, piece, 0)

    def send_feed(self):
        r = self.r
        self.feeds = []
        for bits in (2, 3, 1):
            device = self.place.peer(0, bits)
            source = columns_at(r.feed, device[1], self.width)
            self.feeds.append(self.wires.push(source, r.feeds.at[bits - 1], device))

    def finish_feed(self):
        r = self.r
        f32 = jnp.float32
        for copy in self.feeds:
            copy.wait_recv()
        total = r.two[...].astype(f32)
        total += columns_at(r.feed, self.place.head, self.width)[...].astype(f32)
        for other in range(3):
            total += r.feeds[other].astype(f32)
        r.result_two[...] = total.astype(jnp.bfloat16)


    def grad_rounds(self):
        r, place, wires = self.r, self.place, self.wires
        bf16, f32 = jnp.bfloat16, jnp.float32
        my_rows = rows_at(r.merge_full, place.head, r.merge.shape[0])

        def attended(tile, carry):
            here = span(tile, 256)
            grad = dot(r.grad_rows_one[here, :], my_rows[...], ((1,), (1,))).astype(bf16)
            for which in range(self.pair):
                r.grad_heads[which, here, :] = grad[:, which * HEAD_DIM : (which + 1) * HEAD_DIM]
            return carry

        lax.fori_loop(0, self.rows // 256, attended, 0)
        mine = r.grad_attended.at[place.line % 2]
        there = Spread(wires, place)
        there.start(lambda line: r.grad_heads.at[line % 2], mine)

        @pl.when(place.home)
        def _():
            mine[...] = r.grad_heads[place.line % 2]

        self.shrink_out[0].along()
        self.weights(columns_at(r.attended_full, place.head, self.width), r.grad_rows_one, r.grad_merge)
        there.finish()
        self.grads_coming = []
        for half in range(self.pair):
            for part in range(self.rows // 128):
                here = pl.ds(part * 128, 128)
                rows = r.attended_wide[half, here, :] * r.grad_attended[half, here, :].astype(f32)
                r.means[place.turn, half, part : part + 1, :] = to_row(
                    jnp.sum(rows, 1, keepdims=True)
                )
            own = [item.at[place.turn, half] for item in (r.means, r.grad_outs)]
            own[1][...] = r.grad_attended[half]
            self.grads_coming.append(
                {
                    2: [wires.push(item, item, place.peer(1)) for item in own],
                    1: [wires.push(item, item, place.peer(0, 1)) for item in own],
                }
            )
        self.shrink_out[1].along()
        self.merge_out = SeqScatter(
            wires, place, lambda seq: columns_at(r.grad_merge, seq, r.merge.shape[1]),
            r.merge_pair, r.merge_line,
        )

    def sort_grads(self):
        r, place = self.r, self.place
        bf16 = jnp.bfloat16
        f32 = jnp.float32
        lines = self.rows // 128
        for copy in self.wholes:
            copy.wait_recv()
        for bits in (0, 1, 2, 3):
            turn = flipped(place.turn, bits)
            for half, coming in enumerate(self.grads_coming):
                for copy in coming.get(bits, ()):
                    copy.wait_recv()
                if bits == 2:
                    items = [item.at[turn, half] for item in (r.means, r.grad_outs)]
                    coming[3] = [self.wires.push(item, item, place.peer(0, 1)) for item in items]
                chunk = place.chunk(turn, half)

                def piece(part, carry, turn=turn, half=half, bits=bits, chunk=chunk):
                    here, line = span(part, 128), pl.ds(part, 1)
                    grad = r.grad_outs[turn, half, here, :].astype(f32)
                    out = r.out[bits, half, here, :].astype(f32)
                    mix = to_column(
                        jnp.exp(r.total[bits, half, line, :] - r.whole_total[turn, half, line, :])
                    )
                    mean = to_column(r.means[turn, half, line, :])
                    dots = jnp.sum(out * grad, 1, keepdims=True)
                    rows = span(chunk * lines + part, 128)
                    r.everyone[rows, :HEAD_DIM] = (mix * grad).astype(bf16)
                    r.everyone[rows, HEAD_DIM:] = in_lanes(mix * (dots - mean))
                    return carry

                lax.fori_loop(0, lines, piece, 0)
                self.sort_chunk(r.everyone, chunk)
        self.expand_out[1].start()
        self.merge_out.start()
        for scatter in self.shrink_out:
            scatter.across()

        def second(block, carry):
            r.round_rows[span(block, self.rows), :] = self.sorted_block(block).astype(bf16)
            return carry

        lax.fori_loop(0, self.devices, second, 0, unroll=2)

    def attend_back(self):
        r = self.r
        bf16, f32 = jnp.bfloat16, jnp.float32
        scale = HEAD_DIM ** (-0.5)
        some = 4 * GROUP
        r.grad_unit[0:GROUP, :] = jnp.zeros((GROUP, HEAD_DIM), f32)
        r.grad_value[0:GROUP, :] = jnp.zeros((GROUP, HEAD_DIM), f32)

        def one(rows, block):
            return rows[block * GROUP : (block + 1) * GROUP]

        def fold(pieces):
            owns = [piece[:GROUP] if i % 2 == 0 else piece[GROUP:] for i, piece in enumerate(pieces)]
            befores = [piece[GROUP:] if i % 2 == 0 else piece[:GROUP] for i, piece in enumerate(pieces)]
            middle = [owns[i] + befores[i + 1] for i in range(3)]
            return befores[0], jnp.concatenate(middle + [owns[3]], 0)

        def group(index, carry):
            here = span(index, some)
            longer = pl.ds(pl.multiple_of(index * some, some), some + GROUP)
            before = pl.ds(pl.multiple_of(index * some, some), GROUP)
            after = pl.ds(pl.multiple_of(index * some + GROUP, GROUP), some)
            query, unit, value = r.sorted_query[here, :], r.unit[longer, :], r.key_value[longer, :]
            grad = r.round_rows[here, :HEAD_DIM]
            total = jnp.sum(r.round_rows[here, HEAD_DIM:].astype(f32), 1, keepdims=True)
            probs = r.probs[here, :]
            low = probs.astype(bf16)
            live = jnp.where(self.codes(index) == 0.0, probs, 0.0)
            grad_probs = jnp.concatenate(
                [dot(one(grad, i), self.window(value, i), ((1,), (1,))) for i in range(4)], 0
            )
            inner = jnp.sum(probs * grad_probs, 1, keepdims=True)
            scores = (live * (grad_probs - inner + total)).astype(bf16)
            r.probs[here, :] = (
                jnp.concatenate([dot(one(scores, i), self.window(unit, i)) for i in range(4)], 0) * scale
            )
            for target, left, right, factor in (
                (r.grad_unit, scores, query, scale),
                (r.grad_value, low, grad, 1.0),
            ):
                first, rest = fold(
                    [dot(one(left, i), one(right, i), ((0,), (0,))) * factor for i in range(4)]
                )
                target[before, :] += first
                target[after, :] = rest
            return carry

        lax.fori_loop(0, self.devices * self.rows // some, group, 0, unroll=2)
        last = pl.ds(self.devices * self.rows, GROUP)
        r.grad_unit[last, :] += r.grad_unit[0:GROUP, :]
        r.grad_value[last, :] += r.grad_value[0:GROUP, :]

        def whole(index, carry):
            here = span(index, some)
            after = pl.ds(pl.multiple_of(index * some + GROUP, GROUP), some)
            query = r.sorted_query[here, :].astype(f32)
            factor = lax.rsqrt(jnp.sum(query * query, 1, keepdims=True) + 1e-06)
            unit = query * factor
            grad = r.grad_unit[after, :]
            along = jnp.sum(unit * grad, 1, keepdims=True)
            grad = r.probs[here, :] + factor * (grad - unit * along)
            r.round_rows[here, :HEAD_DIM] = grad.astype(bf16)
            r.round_rows[here, HEAD_DIM:] = r.grad_value[after, :].astype(bf16)
            return carry

        lax.fori_loop(0, self.devices * self.rows // some, whole, 0, unroll=2)

    def return_grads(self):
        r, place, wires = self.r, self.place, self.wires
        bf16, f32 = jnp.bfloat16, jnp.float32

        def first(block, carry):
            self.unsort_block(r.round_rows, block)
            return carry

        lax.fori_loop(0, self.devices, first, 0, unroll=2)
        self.backs = {}

        def rows_for(bits, half):
            return self.unsorted_chunk(place.chunk(flipped(place.turn, bits), half)).astype(bf16)

        def block(slot, half):
            return pl.ds((slot * 2 + half) * self.rows, self.rows)

        for bits in (3, 1, 2, 0):
            for half in range(self.pair):
                r.everyone[block(bits, half), :] = rows_for(bits, half)
        parts = {part: pl.ds(part * HEAD_DIM, HEAD_DIM) for part in (1, 0)}
        both = self.pair * self.rows
        shares, sides = {}, {}
        for part, columns in parts.items():
            for bits in (3, 1):
                source = r.everyone.at[pl.ds(bits * both, both), columns]
                shares[part, bits] = wires.push(
                    source, r.grad_pairs.at[bits // 2, :, columns], place.peer(0, 1)
                )
        for part, columns in parts.items():
            shares[part, 3].wait_recv()
            total = r.everyone[pl.ds(2 * both, both), columns].astype(f32)
            total += r.grad_pairs[1, :, columns].astype(f32)
            r.grad_pairs[1, :, columns] = total.astype(bf16)
            sides[part] = wires.push(
                r.grad_pairs.at[1, :, columns], r.grad_pairs.at[2, :, columns], place.peer(1)
            )
        for part, columns in parts.items():
            shares[part, 1].wait_recv()
            sides[part].wait_recv()
            for half in range(self.pair):
                rows = pl.ds(half * self.rows, self.rows)
                total = r.everyone[block(0, half), columns].astype(f32)
                total += r.grad_pairs[0, rows, columns].astype(f32)
                total += r.grad_pairs[2, rows, columns].astype(f32)
                r.grad_pair[part, half] = total.astype(bf16)
            target = r.grad_key if part else r.grad_query
            mine = columns_at(target, place.line % 2, HEAD_DIM)
            back = Spread(wires, place)
            back.start(lambda line, part=part: r.grad_pair.at[part, line % 2], mine)
            pl.when(place.home)(partial(self.keep_grad, mine, part))
            self.backs[part] = back
        self.backs[1].finish()
        self.value_weights()
        self.backs[0].finish()

    def keep_grad(self, mine, part):
        mine[...] = self.r.grad_pair[part, self.place.line % 2]

    def value_weights(self):
        r = self.r
        self.weights(r.rows_one, r.grad_key, r.grad_value_full)
        self.value_out = SeqScatter(
            self.wires, self.place,
            lambda seq: rows_at(r.grad_value_full, seq, r.value.shape[0]),
            r.value_pair, r.value_line,
        )
        self.value_out.start()

    def project_back(self):
        r, place, wires = self.r, self.place, self.wires
        bf16, f32 = jnp.bfloat16, jnp.float32
        self.weights(r.rows_one, r.grad_query, r.grad_query_full)
        self.query_out = SeqScatter(
            wires, place, lambda seq: rows_at(r.grad_query_full, seq, r.query.shape[0]),
            r.query_pair, r.query_line,
        )
        self.query_out.start()
        copies = []
        tile_rows = self.rows // 2
        for tile in range(2):
            here = pl.ds(tile * tile_rows, tile_rows)
            part = dot(r.grad_query[here, :], r.query_full[...], ((1,), (1,)))
            part += dot(r.grad_key[here, :], r.value_full[...], ((1,), (1,)))
            normal = (r.two_full[here, :].astype(f32) - r.center_one[here, 0:1]) * r.factor_one[
                here, 0:1
            ]
            self.send_part(
                tile, part, normal, r.params_full[0:1, :], r.part_one, r.stat_one,
                r.parts_one, copies,
            )
        for tile in range(2):
            self.relay_part(tile, r.part_one, r.parts_one, copies)
        self.send_stats(r.stat_one, r.stats_one, copies)
        self.value_out.along()
        self.query_out.along()
        for copy in copies[1:2] + copies[3:]:
            copy.wait_recv()

        def normal_at(here):
            rows = columns_at(r.two_full.at[here], place.head, self.width)[...].astype(f32)
            return (rows - r.center_one[here, 0:1]) * r.factor_one[here, 0:1]

        def finish(here, change):
            total = r.grad_two[here, :].astype(f32) + change
            r.input_grad_two[here, :] = total.astype(bf16)

        gains, biases = self.norm_back(
            r.part_one, r.parts_one, r.stat_one, r.stats_one, normal_at, r.factor_one,
            self.my_params(0), finish,
        )
        r.norm_send[0:1, :], r.norm_send[1:2, :] = gains, biases
        norms = [
            wires.push(r.norm_send, r.norms.at[bits - 1], place.peer(bits)) for bits in range(1, 8)
        ]
        self.value_out.across()
        self.query_out.across()
        half = r.expand.shape[1] // 2
        for part, scatter in enumerate(self.expand_out):
            scatter.finish(r.expand_part.at[:, pl.ds(part * half, half)])
        step = r.shrink.shape[0] // 2
        for half, scatter in enumerate(self.shrink_out):
            scatter.finish(r.shrink_part.at[pl.ds(half * step, step)])
        self.merge_out.finish(r.merge_part)
        self.finish_feed()
        total = r.norm_send[...]
        for bits, copy in enumerate(norms):
            copy.wait_recv()
            total += r.norms[bits]
        r.norm_grads[...] = total
        self.query_out.finish(r.query_part)
        self.value_out.finish(r.value_part)


def on_device(names, turns, *refs):
    r = SimpleNamespace(**dict(zip(names, refs)))
    r.result_one, r.result_two, r.input_grad_one, r.input_grad_two = (
        r.streams.at[i] for i in range(4)
    )
    r.query_part, r.value_part = r.projections.at[0], r.projections.at[1]
    merge_rows, shrink_rows = r.merge.shape[0], r.shrink.shape[0]
    r.merge_part = r.columns.at[pl.ds(0, merge_rows)]
    r.shrink_part = r.columns.at[pl.ds(merge_rows, shrink_rows)]
    r.feed, r.grad_expand = r.one_full, r.expand_full
    r.grad_pair, r.part_one = r.packed, r.part_two
    steps = Phases(r, turns)
    steps.project()
    steps.sort_tokens()
    steps.begin_merge_rows()
    steps.expand[0].forward()
    steps.begin(steps.shrink[1])
    steps.attend()
    steps.return_rows()
    steps.heads.relay()
    steps.go_on(steps.shrink[0])
    steps.mix_rounds()
    steps.go_on(steps.shrink[1])
    steps.one.relay()
    steps.grads.relay()
    steps.one.finish()
    steps.grads.finish()
    steps.heads.finish()
    steps.feed_forward()
    steps.feed_back()
    steps.grad_rounds()
    steps.send_feed()
    steps.expand_out[0].across()
    steps.sort_grads()
    steps.expand_out[0].side()
    steps.attend_back()
    steps.expand_out[1].along()
    steps.merge_out.along()
    steps.return_grads()
    steps.expand_out[1].across()
    steps.merge_out.across()
    steps.project_back()
    steps.wires.drain()
    assert len(steps.wires.copies) <= r.send.shape[0]


def whole(turns, arguments):
    bf16, f32 = jnp.bfloat16, jnp.float32
    heads, devices = lax.axis_size("head"), lax.axis_size("seq")
    pair = devices // turns
    rows, width = arguments["two"].shape
    tokens, wide = devices * rows, heads * width
    hidden = arguments["expand"].shape[1]
    lines = rows // 128
    shape = {name: value.shape for name, value in arguments.items()}
    results = dict(
        streams=((4, rows, width), bf16),
        projections=((2,) + shape["query"], f32),
        expand_part=(shape["expand"], f32),
        columns=((shape["merge"][0] + shape["shrink"][0], shape["merge"][1]), f32),
        norm_grads=((8, width), f32),
    )
    scratch = dict(
        params=((8, width), f32),
        keys=((tokens // 128, 1, 128), f32),
        shares=((8, 128), f32),
        unit_rows=((2, 8, 128), jnp.int32),
        until=((-(-(devices * (rows // GROUP + 1) + 1) // 128) * 128, 128), f32),
        block_row=((devices, 1, rows), jnp.int32),
        block_column=((tokens, 128), jnp.int16),
        chunk_row=((devices, 1, rows), jnp.int32),
        chunk_column=((tokens, 128), jnp.int16),
        sorted_query=((tokens, HEAD_DIM), bf16),
        unit=((tokens + GROUP, HEAD_DIM), bf16),
        key_value=((tokens + GROUP, HEAD_DIM), bf16),
        probs=((tokens, 2 * GROUP), f32),
        rows_one=((rows, wide), bf16),
        center_one=((rows, 128), f32),
        factor_one=((rows, 128), f32),
        query_full=((wide, width), bf16),
        value_full=((wide, width), bf16),
        merge_full=((wide, wide), bf16),
        expand_full=((wide, hidden), bf16),
        shrink_full=((hidden, wide), bf16),
        one_full=((rows, wide), bf16),
        two_full=((rows, wide), bf16),
        grad_full=((rows, wide), bf16),
        attended_full=((rows, wide), bf16),
        everyone=((tokens, 2 * HEAD_DIM), bf16),
        mid=((devices * devices, rows // devices, 2 * HEAD_DIM), bf16),
        params_full=((8, wide), f32),
        packed=((pair, 2, rows, HEAD_DIM), bf16),
        round_rows=((tokens, 2 * HEAD_DIM), bf16),
        attended=((pair, rows, HEAD_DIM), bf16),
        attended_wide=((pair, rows, HEAD_DIM), f32),
        out=((turns, pair, rows, HEAD_DIM), bf16),
        total=((turns, pair, lines, 128), f32),
        share=((2, pair, rows, HEAD_DIM), bf16),
        share_total=((2, pair, lines, 128), f32),
        merged=((pair, rows, HEAD_DIM), bf16),
        merged_total=((pair, lines, 128), f32),
        side=((pair, rows, HEAD_DIM), bf16),
        side_total=((pair, lines, 128), f32),
        whole_total=((turns, pair, lines, 128), f32),
        means=((turns, pair, lines, 128), f32),
        tall=((rows, wide), f32),
        normal_two=((rows, width), f32),
        factor_two=((rows, 128), f32),
        rows_two=((rows, wide), bf16),
        active=((rows, hidden), bf16),
        grad_hidden=((rows, hidden), bf16),
        part_two=((rows, wide), bf16),
        stat_two=((2 * lines, 128), f32),
        parts_two=((heads - 1, rows, width), bf16),
        stats_two=((heads - 1, 2 * lines, 128), f32),
        stat_one=((2 * lines, 128), f32),
        parts_one=((heads - 1, rows, width), bf16),
        stats_one=((heads - 1, 2 * lines, 128), f32),
        feeds=((heads - 1, rows, width), bf16),
        grad_rows_one=((rows, wide), bf16),
        grad_heads=((pair, rows, HEAD_DIM), bf16),
        grad_attended=((pair, rows, HEAD_DIM), bf16),
        grad_outs=((turns, pair, rows, HEAD_DIM), bf16),
        grad_unit=((tokens + GROUP, HEAD_DIM), f32),
        grad_value=((tokens + GROUP, HEAD_DIM), f32),
        grad_pairs=((3, pair * rows, 2 * HEAD_DIM), bf16),
        grad_query=((rows, width), bf16),
        grad_key=((rows, width), bf16),
        expand_lines=((3, 2 * shape["expand"][0], hidden // 2), bf16),
        expand_side=((shape["expand"][0], hidden // 2), bf16),
        norm_send=((8, width), f32),
        norms=((devices - 1, 8, width), f32),
    )
    for name, full in (
        ("query", (wide, width)),
        ("value", (wide, width)),
        ("merge", (width, wide)),
        ("expand", (wide, hidden)),
        ("shrink", (hidden, wide)),
    ):
        own = "grad_" + name + ("_full" if name in ("query", "value") else "")
        if name != "expand":
            scratch[own] = (full, bf16)
        height, across = shape[name]
        if name == "expand":
            across = across // 2
        scratch[name + "_pair"] = ((devices // 2, height, across), bf16)
        scratch[name + "_line"] = ((devices // 2 - 1, height, across), bf16)
    wires = dict(send=224, receive=224, local=2)
    vmem = pl.BlockSpec(memory_space=pltpu.VMEM)
    tables = dict(units=(8, 128), units_back=(8, 128))
    names = [*arguments, *results, *scratch, *tables, *wires]
    out = pl.pallas_call(
        partial(on_device, names, turns),
        out_shape=[jax.ShapeDtypeStruct(*item) for item in results.values()],
        in_specs=[vmem] * len(arguments),
        out_specs=[vmem] * len(results),
        scratch_shapes=[pltpu.VMEM(*item) for item in scratch.values()]
        + [pltpu.SMEM(item, jnp.int32) for item in tables.values()]
        + [pltpu.SemaphoreType.DMA((number,)) for number in wires.values()],
        compiler_params=pltpu.CompilerParams(
            collective_id=0, has_side_effects=True, vmem_limit_bytes=63 << 20
        ),
    )(*arguments.values())
    return SimpleNamespace(**dict(zip(results, out)))


def by_rounds(
    stream_one,
    stream_two,
    grad_one,
    grad_two,
    query_weight,
    value_weight,
    merge_weight,
    expand_weight,
    shrink_weight,
    first_gain,
    first_bias,
    second_gain,
    second_bias,
    bucket_ids,
    sort_order,
):
    arguments = dict(
        one=stream_one,
        two=stream_two,
        grad_one=grad_one,
        grad_two=grad_two,
        query=query_weight,
        value=value_weight,
        merge=merge_weight,
        expand=expand_weight,
        shrink=shrink_weight,
        gain_one=first_gain[None],
        bias_one=first_bias[None],
        gain_two=second_gain[None],
        bias_two=second_bias[None],
        bucket=bucket_ids,
        order=sort_order,
    )
    k = whole(sort_order.shape[0], arguments)
    merge_rows = merge_weight.shape[0]
    return (
        *(k.streams[i] for i in range(4)),
        k.projections[0],
        k.projections[1],
        k.columns[:merge_rows],
        k.expand_part,
        k.columns[merge_rows:],
        *(k.norm_grads[i] for i in range(4)),
    )


def solution(mesh):
    placed = (
        P("seq", "head"),
        P("seq", "head"),
        P("seq", "head"),
        P("seq", "head"),
        P("seq", "head"),
        P("seq", "head"),
        P("head", "seq"),
        P("seq", "head"),
        P("head", "seq"),
        P("head"),
        P("head"),
        P("head"),
        P("head"),
        P(),
        P(),
    )

    def local(*arguments):
        rounds = arguments[-1].shape[0]
        if mesh.shape["seq"] == HEADS == 2 * rounds and mesh.shape["head"] == rounds:
            return by_rounds(*arguments)
        return by_blocks(*arguments)

    return jax.shard_map(
        local,
        mesh=mesh,
        in_specs=placed,
        out_specs=(
            P("seq", "head"),
            P("seq", "head"),
            P("seq", "head"),
            P("seq", "head"),
            P("seq", "head"),
            P("seq", "head"),
            P("head", "seq"),
            P("seq", "head"),
            P("head", "seq"),
            P("head"),
            P("head"),
            P("head"),
            P("head"),
        ),
        check_vma=False,
    )
```

```python
from functools import partial
from types import SimpleNamespace

import jax
import jax.numpy as jnp
from jax import lax
from jax.experimental import pallas as pl
from jax.experimental.pallas import tpu as pltpu
from jax.sharding import PartitionSpec as P

HEADS = 8
HEAD_DIM = 128
GROUP = 64
MESH = pl.DeviceIdType.MESH


masked_score = -1000000000.0
own_score = -100000.0


def as_sent(shard):

    def short(part):
        return part.astype(jnp.bfloat16) if part.dtype == jnp.float32 else part

    return jax.tree.map(short, shard)


def from_behind(block, axis, distance):
    devices = range(lax.axis_size(axis))
    route = [(i - distance, i) for i in devices if i - distance in devices]
    return lax.ppermute(block, axis, route)


def row_sums(first, second):
    return lax.psum((first, second), "head")


def full_rows(part):
    return lax.all_gather(part, "head", axis=1, tiled=True)


def branch_sum(part):
    return lax.psum_scatter(part, "head", scatter_dimension=1, tiled=True)


def norm_forward(value, gain, shift):
    width = value.shape[1] * lax.axis_size("head")
    total, square = row_sums(
        jnp.sum(value, 1, keepdims=True), jnp.sum(value * value, 1, keepdims=True)
    )
    center = total / width
    spread = square / width - center * center
    factor = lax.rsqrt(spread + 1e-05)
    normal = (value - center) * factor
    return (normal, factor, normal * gain + shift)


def norm_backward(grad, normal, factor, gain):
    width = grad.shape[1] * lax.axis_size("head")
    scaled = grad * gain
    first, second = row_sums(
        jnp.sum(scaled, 1, keepdims=True), jnp.sum(scaled * normal, 1, keepdims=True)
    )
    result = factor * (scaled - first / width - normal * (second / width))
    return (result, jnp.sum(grad * normal, 0), jnp.sum(grad, 0))


def regroup_rows(buffer):
    turns = []
    for turn in range(buffer.shape[1]):
        turns.append(
            lax.all_to_all(buffer[:, turn], "seq", split_axis=0, concat_axis=0, tiled=True)
        )
    result = jnp.stack(turns, 1)
    return result


def regroup_totals(buffer):
    moved = lax.all_to_all(
        buffer.reshape(buffer.shape[0], -1, buffer.shape[3]),
        "seq",
        split_axis=0,
        concat_axis=0,
        tiled=True,
    )
    return moved.reshape(buffer.shape)


def regroup_pair(first, second):
    firsts = []
    seconds = []
    for turn in range(first.shape[1]):
        moved_first, moved_second = (
            lax.all_to_all(as_sent(first[:, turn]), "seq", split_axis=0, concat_axis=0, tiled=True),
            lax.all_to_all(
                as_sent(second[:, turn]), "seq", split_axis=0, concat_axis=0, tiled=True
            ),
        )
        firsts.append(moved_first)
        seconds.append(moved_second)
    result = (jnp.stack(firsts, 1), jnp.stack(seconds, 1))
    return result


def by_blocks(
    stream_one,
    stream_two,
    grad_one,
    grad_two,
    query_weight,
    value_weight,
    merge_weight,
    expand_weight,
    shrink_weight,
    first_gain,
    first_bias,
    second_gain,
    second_bias,
    bucket_ids,
    sort_order,
):
    devices = lax.axis_size("seq")
    place = lax.axis_index("seq")
    rows = stream_one.shape[0]
    rounds = sort_order.shape[0]
    capacity = 2 * rows // devices
    blocks = rows // GROUP
    heads_here = HEADS // lax.axis_size("head")
    local_width = heads_here * HEAD_DIM
    scale = HEAD_DIM ** (-0.5)
    round_index = jnp.arange(rounds, dtype=jnp.int32)[:, None]
    counter = jnp.arange(rows, dtype=jnp.int32)

    def invert(line):
        return jnp.zeros_like(line).at[line].set(jnp.arange(line.shape[0], dtype=jnp.int32))

    inverse = jax.vmap(invert)(sort_order)
    my_sorted = lax.dynamic_slice_in_dim(inverse, place * rows, rows, 1)
    send_block = my_sorted // rows
    same_block = send_block[:, :, None] == send_block[:, None, :]
    send_slot = jnp.sum(
        (same_block & (my_sorted[:, None, :] < my_sorted[:, :, None])).astype(jnp.int32), -1
    )
    block_tokens = lax.dynamic_slice_in_dim(sort_order, place * rows, rows, 1)
    source_block = block_tokens // rows
    earlier = counter[None, :] < counter[:, None]
    recv_slot = jnp.sum(
        ((source_block[:, :, None] == source_block[:, None, :]) & earlier[None]).astype(jnp.int32),
        -1,
    )
    query_bucket = jnp.take_along_axis(bucket_ids, block_tokens, 1)
    prior_start = (place - 1) % devices * rows + rows - GROUP
    prior_tokens = lax.dynamic_slice_in_dim(sort_order, prior_start, GROUP, 1)
    prior_bucket = jnp.take_along_axis(bucket_ids, prior_tokens, 1)

    def with_prior(own, prior):
        pieces = own.reshape((rounds, blocks, GROUP) + own.shape[2:])
        before = jnp.concatenate([prior[:, None], pieces[:, :-1]], 1)
        return jnp.concatenate([pieces, before], 2)

    query_place = block_tokens.reshape(rounds, blocks, GROUP)
    key_place = with_prior(block_tokens, prior_tokens)
    key_bucket = with_prior(query_bucket, prior_bucket)
    allowed = (key_place[:, :, None, :] <= query_place[:, :, :, None]) & (
        key_bucket[:, :, None, :] == query_bucket.reshape(rounds, blocks, GROUP)[:, :, :, None]
    )
    itself = key_place[:, :, None, :] == query_place[:, :, :, None]
    live = allowed & jnp.logical_not(itself)

    def fill(values, block, slot):
        empty = jnp.zeros((devices, rounds, capacity, values.shape[-1]), values.dtype)
        return empty.at[block, round_index, slot].set(values)

    normal_one, factor_one, normed_one = norm_forward(
        stream_two.astype(jnp.float32), first_gain, first_bias
    )
    rows_one = full_rows(normed_one.astype(jnp.bfloat16))
    query_full, value_full, merge_full = (
        lax.all_gather(query_weight, "seq", axis=0, tiled=True),
        lax.all_gather(value_weight, "seq", axis=0, tiled=True),
        lax.all_gather(merge_weight, "seq", axis=1, tiled=True),
    )
    queries = jnp.dot(rows_one, query_full, preferred_element_type=jnp.float32).astype(jnp.bfloat16)
    values = jnp.dot(rows_one, value_full, preferred_element_type=jnp.float32).astype(jnp.bfloat16)
    packed = jnp.concatenate([queries, values], 1)
    outgoing = fill(jnp.broadcast_to(packed[None], (rounds,) + packed.shape), send_block, send_slot)
    incoming = regroup_rows(outgoing)
    sorted_rows = incoming[source_block, round_index, recv_slot]
    sorted_query = sorted_rows[:, :, :local_width].reshape(rounds, rows, heads_here, HEAD_DIM)
    sorted_value = sorted_rows[:, :, local_width:].reshape(rounds, rows, heads_here, HEAD_DIM)
    query_float = sorted_query.astype(jnp.float32)
    inverse_norm = lax.rsqrt(jnp.sum(query_float * query_float, -1, keepdims=True) + 1e-06)
    unit_float = query_float * inverse_norm
    unit_low = unit_float.astype(jnp.bfloat16)
    edge = from_behind(
        jnp.concatenate([unit_low[:, -GROUP:], sorted_value[:, -GROUP:]], -1), "seq", 1
    )
    key_unit = with_prior(unit_low, edge[..., :HEAD_DIM])
    key_value = with_prior(sorted_value, edge[..., HEAD_DIM:])
    query_groups = sorted_query.reshape(rounds, blocks, GROUP, heads_here, HEAD_DIM)

    def masked_scores():
        raw = (
            jnp.einsum(
                "rncha,rnkha->rnhck", query_groups, key_unit, preferred_element_type=jnp.float32
            )
            * scale
        )
        return jnp.where(
            itself[:, :, None], own_score, jnp.where(allowed[:, :, None], raw, masked_score)
        )

    scores = masked_scores()
    peak = jnp.max(scores, -1, keepdims=True)
    totals = peak + jnp.log(jnp.sum(jnp.exp(scores - peak), -1, keepdims=True))
    probs_low = jnp.exp(scores - totals).astype(jnp.bfloat16)
    round_out = jnp.einsum(
        "rnhck,rnkha->rncha", probs_low, key_value, preferred_element_type=jnp.float32
    ).astype(jnp.bfloat16)
    out_flat = round_out.reshape(rounds, rows, local_width)
    total_flat = jnp.transpose(totals[..., 0], (0, 1, 3, 2)).reshape(rounds, rows, heads_here)
    token_out = regroup_rows(fill(out_flat, source_block, recv_slot))[
        send_block, round_index, send_slot
    ].astype(jnp.float32)
    token_total = regroup_totals(fill(total_flat, source_block, recv_slot))[
        send_block, round_index, send_slot
    ]
    mix = jax.nn.softmax(token_total, axis=0)
    token_out4 = token_out.reshape(rounds, rows, heads_here, HEAD_DIM)
    attended_low = (
        jnp.sum(mix[..., None] * token_out4, 0).reshape(rows, local_width).astype(jnp.bfloat16)
    )
    sum_one = stream_one.astype(jnp.float32) + branch_sum(
        jnp.dot(attended_low, merge_full, preferred_element_type=jnp.float32)
    )
    normal_two, factor_two, normed_two = norm_forward(sum_one, second_gain, second_bias)
    rows_two = full_rows(normed_two.astype(jnp.bfloat16))
    expand_full, shrink_full = (
        lax.all_gather(expand_weight, "seq", axis=0, tiled=True),
        lax.all_gather(shrink_weight, "seq", axis=1, tiled=True),
    )
    hidden = jnp.dot(rows_two, expand_full, preferred_element_type=jnp.float32)
    active, gelu_pull = jax.vjp(partial(jax.nn.gelu, approximate=False), hidden)
    active_low = active.astype(jnp.bfloat16)
    sum_two = stream_two.astype(jnp.float32) + branch_sum(
        jnp.dot(active_low, shrink_full, preferred_element_type=jnp.float32)
    )
    grad_rows_two = full_rows(grad_two)
    grad_active = jnp.dot(grad_rows_two, shrink_full.T, preferred_element_type=jnp.float32)
    grad_hidden = gelu_pull(grad_active)[0].astype(jnp.bfloat16)
    grad_shrink = jnp.dot(active_low.T, grad_rows_two, preferred_element_type=jnp.float32)
    grad_expand = jnp.dot(rows_two.T, grad_hidden, preferred_element_type=jnp.float32)
    grad_normed_two = branch_sum(
        jnp.dot(grad_hidden, expand_full.T, preferred_element_type=jnp.float32)
    )
    extra_one, grad_second_gain, grad_second_bias = norm_backward(
        grad_normed_two, normal_two, factor_two, second_gain
    )
    total_one = grad_one.astype(jnp.float32) + extra_one
    total_low = total_one.astype(jnp.bfloat16)
    grad_rows_one = full_rows(total_low)
    grad_attended = jnp.dot(grad_rows_one, merge_full.T, preferred_element_type=jnp.float32).astype(
        jnp.bfloat16
    )
    grad_merge = jnp.dot(attended_low.T, grad_rows_one, preferred_element_type=jnp.float32)
    grad_float = grad_attended.astype(jnp.float32).reshape(rows, heads_here, HEAD_DIM)
    dots = jnp.sum(token_out4 * grad_float[None], -1)
    grad_total = mix * (dots - jnp.sum(mix * dots, 0, keepdims=True))
    grad_out_low = (
        (mix[..., None] * grad_float[None]).astype(jnp.bfloat16).reshape(rounds, rows, local_width)
    )
    sorted_grad_out = regroup_rows(fill(grad_out_low, send_block, send_slot))[
        source_block, round_index, recv_slot
    ]
    sorted_grad_total = regroup_totals(fill(grad_total, send_block, send_slot))[
        source_block, round_index, recv_slot
    ]
    grad_groups = sorted_grad_out.reshape(rounds, blocks, GROUP, heads_here, HEAD_DIM)
    total_grad_groups = jnp.transpose(
        sorted_grad_total.reshape(rounds, blocks, GROUP, heads_here), (0, 1, 3, 2)
    )[..., None]
    probs = jnp.exp(masked_scores() - totals)
    probs_again = probs.astype(jnp.bfloat16)
    grad_probs = jnp.einsum(
        "rncha,rnkha->rnhck", grad_groups, key_value, preferred_element_type=jnp.float32
    )
    grad_key_value = jnp.einsum(
        "rnhck,rncha->rnkha", probs_again, grad_groups, preferred_element_type=jnp.float32
    )
    inner = jnp.sum(probs * grad_probs, -1, keepdims=True)
    grad_scores = jnp.where(
        live[:, :, None], probs * (grad_probs - inner + total_grad_groups), 0.0
    ).astype(jnp.bfloat16)
    grad_query_groups = (
        jnp.einsum("rnhck,rnkha->rncha", grad_scores, key_unit, preferred_element_type=jnp.float32)
        * scale
    )
    grad_key_unit = (
        jnp.einsum(
            "rnhck,rncha->rnkha", grad_scores, query_groups, preferred_element_type=jnp.float32
        )
        * scale
    )
    edge_grad = from_behind(
        jnp.concatenate([grad_key_unit[:, 0, GROUP:], grad_key_value[:, 0, GROUP:]], -1).astype(
            jnp.bfloat16
        ),
        "seq",
        -1,
    ).astype(jnp.float32)

    def fold_keys(grad_keys, arriving):
        own = grad_keys[:, :, :GROUP]
        later = jnp.concatenate([grad_keys[:, 1:, GROUP:], arriving[:, None]], 1)
        return (own + later).reshape(rounds, rows, heads_here, HEAD_DIM)

    grad_unit = fold_keys(grad_key_unit, edge_grad[..., :HEAD_DIM])
    grad_sorted_value = fold_keys(grad_key_value, edge_grad[..., HEAD_DIM:])
    grad_sorted_query = grad_query_groups.reshape(
        rounds, rows, heads_here, HEAD_DIM
    ) + inverse_norm * (grad_unit - unit_float * jnp.sum(unit_float * grad_unit, -1, keepdims=True))
    moved_first, moved_second = regroup_pair(
        fill(grad_sorted_query.reshape(rounds, rows, local_width), source_block, recv_slot),
        fill(grad_sorted_value.reshape(rounds, rows, local_width), source_block, recv_slot),
    )
    token_grad_query = moved_first[send_block, round_index, send_slot]
    token_grad_value = moved_second[send_block, round_index, send_slot]
    grad_query_low = jnp.sum(token_grad_query, 0).astype(jnp.bfloat16)
    grad_value_low = jnp.sum(token_grad_value, 0).astype(jnp.bfloat16)
    grad_query_full = jnp.dot(rows_one.T, grad_query_low, preferred_element_type=jnp.float32)
    grad_value_full = jnp.dot(rows_one.T, grad_value_low, preferred_element_type=jnp.float32)
    grad_normed_one = branch_sum(
        jnp.dot(grad_query_low, query_full.T, preferred_element_type=jnp.float32)
        + jnp.dot(grad_value_low, value_full.T, preferred_element_type=jnp.float32)
    )
    extra_two, grad_first_gain, grad_first_bias = norm_backward(
        grad_normed_one, normal_one, factor_one, first_gain
    )
    input_grad_two = (grad_two.astype(jnp.float32) + extra_two).astype(jnp.bfloat16)
    query_part, value_part, merge_part, expand_part, shrink_part = (
        lax.psum_scatter(grad_query_full, "seq", scatter_dimension=0, tiled=True),
        lax.psum_scatter(grad_value_full, "seq", scatter_dimension=0, tiled=True),
        lax.psum_scatter(grad_merge, "seq", scatter_dimension=1, tiled=True),
        lax.psum_scatter(grad_expand, "seq", scatter_dimension=0, tiled=True),
        lax.psum_scatter(grad_shrink, "seq", scatter_dimension=1, tiled=True),
    )
    first_gain_sum, first_bias_sum, second_gain_sum, second_bias_sum = lax.psum(
        (grad_first_gain, grad_first_bias, grad_second_gain, grad_second_bias), "seq"
    )
    return (
        sum_one.astype(jnp.bfloat16),
        sum_two.astype(jnp.bfloat16),
        total_low,
        input_grad_two,
        query_part,
        value_part,
        merge_part,
        expand_part,
        shrink_part,
        first_gain_sum,
        first_bias_sum,
        second_gain_sum,
        second_bias_sum,
    )


def flip(index, bit):
    return index + bit - 2 * bit * ((index // bit) % 2)


def flipped(index, bits):
    for bit in (1, 2, 4):
        if bits & bit:
            index = flip(index, bit)
    return index


class Place:
    def __init__(self):
        self.seq, self.head = lax.axis_index("seq"), lax.axis_index("head")
        self.line, self.side = self.seq // 2, self.seq % 2
        self.pair, self.core = self.head // 2, self.head % 2
        self.turn = self.side * 2 + self.core
        self.home = self.line // 2 == self.core
        self.away = self.line // 2 != self.core

    def peer(self, seq_bits, head_bits=0):
        return (flipped(self.seq, seq_bits), flipped(self.head, head_bits))

    def member(self, bits):
        return self.peer(bits // 2, bits % 2)

    def chunk(self, turn, half):
        return (2 * (turn % 2) + half) * 2 + turn // 2

    def greet(self):
        peers = [self.peer(bits) for bits in range(1, 8)]
        peers += [self.peer(0, bits) for bits in range(1, 4)]
        peers += [self.peer(bits, 1) for bits in (1, 2, 4, 6)]
        barrier = pltpu.get_barrier_semaphore()
        for peer in peers:
            pl.semaphore_signal(barrier, inc=1, device_id=peer, device_id_type=MESH)
        return partial(pl.semaphore_wait, barrier, len(peers))


class Copy:
    def __init__(self, copy, starts, lands):
        self.copy, self.starts, self.lands = copy, starts, lands
        self.when(starts, copy.start)

    def when(self, condition, act):
        if condition is None:
            act()
        else:
            pl.when(condition)(act)

    def wait_recv(self):
        self.when(self.lands, self.copy.wait_recv)

    def wait_send(self):
        self.when(self.starts, self.copy.wait_send)


class Wires:
    def __init__(self, send, receive):
        self.send, self.receive, self.copies = send, receive, []

    def push(self, source, target, device, starts=None, lands=None):
        index = len(self.copies)
        copy = pltpu.make_async_remote_copy(
            src_ref=source,
            dst_ref=target,
            send_sem=self.send.at[index],
            recv_sem=self.receive.at[index],
            device_id=device,
            device_id_type=MESH,
        )
        self.copies.append(Copy(copy, starts, lands))
        return self.copies[-1]

    def settle(self, copies):
        for copy in copies:
            copy.wait_send()
        done = [id(copy) for copy in copies]
        self.copies = [None if id(copy) in done else copy for copy in self.copies]

    def drain(self):
        self.settle([copy for copy in self.copies if copy is not None])


class Spread:
    def __init__(self, wires, place):
        self.wires, self.place, self.copies = wires, place, []

    def start(self, source_at, target, half=None):
        p = self.place
        for bits, starts in ((4, p.away), (6, p.away), (2, p.home)):
            seq = flipped(p.seq, bits)
            head = p.head - p.core + p.line // 2
            lands = starts
            if half is not None:
                starts = jnp.logical_and(starts, (seq // 2) % 2 == half)
                lands = jnp.logical_and(lands, p.line % 2 == half)
            copy = self.wires.push(source_at(seq // 2), target, (seq, head), starts, lands)
            self.copies.append(copy)

    def finish(self):
        for copy in self.copies:
            copy.wait_recv()


class TokenGather:
    def __init__(self, wires, place, everyone, rows):
        self.wires, self.place, self.everyone, self.rows = wires, place, everyone, rows
        self.line = {2: [], 4: [], 6: []}
        self.own = []

    def slot(self, seq, part):
        return columns_at(rows_at(self.everyone, seq, self.rows), part, HEAD_DIM)

    def start(self, packed, part):
        p = self.place
        mine = self.slot(p.seq, part)
        for bits, starts in ((4, p.away), (6, p.away), (2, p.home)):
            seq = flipped(p.seq, bits)
            self.line[bits].append(
                self.wires.push(
                    packed.at[(seq // 2) % 2, part],
                    mine,
                    (seq, p.head - p.core + part),
                    starts,
                    p.core == part,
                )
            )
        source = packed.at[p.line % 2, part]
        self.own.append(self.wires.push(source, mine, p.peer(0, 1), p.home, p.away))

        @pl.when(p.home)
        def _():
            mine[...] = source[...]

    def pass_own(self):
        p = self.place
        for copy in self.own:
            copy.wait_recv()
        block = self.slot(p.seq, p.core)
        self.beside = {0: self.wires.push(block, block, p.peer(1))}
        self.shared = {}

    def forward(self, bits):
        p = self.place
        for copy in self.line[bits]:
            copy.wait_recv()
        block = self.slot(flipped(p.seq, bits), p.core)
        self.beside[bits] = self.wires.push(block, block, p.peer(1))
        self.shared[bits] = self.wires.push(block, block, p.peer(0, 1))

    def share(self, bits):
        p = self.place
        self.beside[bits].wait_recv()
        block = self.slot(flipped(p.seq, bits + 1), p.core)
        self.shared[bits + 1] = self.wires.push(block, block, p.peer(0, 1))

    def land(self, bits):
        self.shared[bits].wait_recv()

    def settle(self):
        lines = [copy for copies in self.line.values() for copy in copies]
        self.wires.settle(lines + self.own + [*self.beside.values(), *self.shared.values()])


class SeqGather:
    def __init__(self, wires, place, slot):
        self.wires, self.place, self.slot = wires, place, slot

    def start(self, source, for_far=None):
        p, mine = self.place, self.slot(self.place.seq)
        far = source if for_far is None else for_far
        self.arriving = {4: self.wires.push(far, mine, p.peer(4))}
        self.arriving[2] = self.wires.push(source, mine, p.peer(2))
        self.beside = {0: self.wires.push(source, mine, p.peer(1))}

    def forward(self, bits):
        p = self.place
        self.arriving[bits].wait_recv()
        block = self.slot(flipped(p.seq, bits))
        if bits == 4:
            self.arriving[6] = self.wires.push(block, block, p.peer(2))
        self.beside[bits] = self.wires.push(block, block, p.peer(1))

    def land(self, bits):
        self.beside[bits].wait_recv()

    def settle(self):
        self.wires.settle([*self.arriving.values(), *self.beside.values()])

    def finish(self):
        for bits in self.beside:
            self.land(bits)
        self.settle()


class PairGather:
    def __init__(self, wires, place, slot, both):
        self.wires, self.place, self.slot, self.both = wires, place, slot, both

    def start(self, source):
        p = self.place
        self.first = self.wires.push(source, self.slot(p.seq), p.peer(1))

    def along(self):
        p = self.place
        self.first.wait_recv()
        pair = self.both(p.seq // 2)
        self.far = self.wires.push(pair, pair, p.peer(4))
        self.near = self.wires.push(pair, pair, p.peer(2))

    def forward(self):
        p = self.place
        self.far.wait_recv()
        pair = self.both(flip(p.seq, 4) // 2)
        self.last = self.wires.push(pair, pair, p.peer(2))

    def finish(self):
        self.near.wait_recv()
        self.last.wait_recv()
        self.wires.settle([self.first, self.far, self.near, self.last])


class HeadGather:
    def __init__(self, wires, place, slot):
        self.wires, self.place, self.slot = wires, place, slot

    def start(self, source):
        p = self.place
        mine = self.slot(p.head)
        self.long = self.wires.push(source, mine, p.peer(0, 2))
        self.short = self.wires.push(source, mine, p.peer(0, 1))

    def relay(self):
        p = self.place
        self.long.wait_recv()
        moved = self.slot(flip(p.head, 2))
        self.last = self.wires.push(moved, moved, p.peer(0, 1))

    def finish(self):
        self.short.wait_recv()
        self.last.wait_recv()
        self.wires.settle([self.long, self.short, self.last])


def columns_at(ref, index, width):
    return ref.at[:, pl.ds(pl.multiple_of(index * width, width), width)]


def rows_at(ref, index, width):
    return ref.at[pl.ds(pl.multiple_of(index * width, width), width)]


def span(index, width):
    return pl.ds(pl.multiple_of(index * width, width), width)


def dot(left, right, contract=((1,), (0,))):
    return lax.dot_general(
        left, right, (contract, ((), ())), preferred_element_type=jnp.float32
    )


def diagonal(size):
    return lax.broadcasted_iota(jnp.int32, (size, size), 0) == lax.broadcasted_iota(
        jnp.int32, (size, size), 1
    )


def to_row(column):
    return jnp.sum(jnp.where(diagonal(column.shape[0]), column, 0.0), 0, keepdims=True)


def to_column(row):
    return jnp.sum(jnp.where(diagonal(row.shape[1]), row, 0.0), 1, keepdims=True)


def in_lanes(total):
    bf16, f32 = jnp.bfloat16, jnp.float32
    high = total.astype(bf16).astype(f32)
    middle = (total - high).astype(bf16).astype(f32)
    low = total - high - middle
    lane = lax.broadcasted_iota(jnp.int32, (total.shape[0], 128), 1)
    parts = jnp.where(lane == 0, high, jnp.where(lane == 1, middle, low))
    return jnp.where(lane < 3, parts, 0.0).astype(bf16)


class SeqScatter:
    def __init__(self, wires, place, piece, pair, line):
        self.wires, self.place, self.piece = wires, place, piece
        self.pair, self.line = pair, line

    def start(self):
        p = self.place
        self.beside = {}
        for bits in (6, 2, 4, 0):
            source = self.piece(flipped(p.seq, bits + 1))
            self.beside[bits] = self.wires.push(source, self.pair.at[bits // 2], p.peer(1))

    def add(self, bits, more=None):
        at, f32 = self.pair.at[bits // 2], jnp.float32
        self.beside[bits].wait_recv()
        mine = self.piece(flipped(self.place.seq, bits))[...]
        total = at[...].astype(f32) + mine.astype(f32)
        if more is not None:
            total += more[...].astype(f32)
        at[...] = total.astype(jnp.bfloat16)
        return at

    def along(self):
        device = self.place.peer(2)
        self.shares = self.wires.push(self.add(6), self.line.at[0], device)
        self.near = self.wires.push(self.add(2), self.line.at[1], device)

    def across(self):
        self.shares.wait_recv()
        total = self.add(4, self.line.at[0])
        self.far = self.wires.push(total, self.line.at[2], self.place.peer(4))

    def finish(self, target):
        p, f32 = self.place, jnp.float32
        self.beside[0].wait_recv()
        total = self.piece(p.seq)[...].astype(f32) + self.pair.at[0][...].astype(f32)
        self.near.wait_recv()
        total += self.line.at[1][...].astype(f32)
        self.far.wait_recv()
        target[...] = total + self.line.at[2][...].astype(f32)


class PairScatter:
    def __init__(self, wires, place, piece, both, line, pair):
        self.wires, self.place, self.piece, self.both = wires, place, piece, both
        self.line, self.pair = line, pair

    def start(self):
        p, device = self.place, self.place.peer(2)
        share, near = (self.both(flipped(p.seq, bits) // 2) for bits in (6, 2))
        self.shares = self.wires.push(share, self.line.at[0], device)
        self.near = self.wires.push(near, self.line.at[1], device)

    def across(self):
        p, f32 = self.place, jnp.float32
        self.shares.wait_recv()
        mine = self.both(flip(p.seq, 4) // 2)
        at = self.line.at[0]
        at[...] = (at[...].astype(f32) + mine[...].astype(f32)).astype(jnp.bfloat16)
        self.far = self.wires.push(at, self.line.at[2], p.peer(4))

    def side(self):
        p, f32 = self.place, jnp.float32
        self.near.wait_recv()
        self.far.wait_recv()
        mine = self.both(p.seq // 2)
        total = mine[...].astype(f32) + self.line.at[1][...].astype(f32)
        total += self.line.at[2][...].astype(f32)
        self.wires.settle([self.near])
        mine[...] = total.astype(jnp.bfloat16)
        self.last = self.wires.push(self.piece(flip(p.seq, 1)), self.pair, p.peer(1))

    def finish(self, target):
        self.last.wait_recv()
        f32 = jnp.float32
        target[...] = self.piece(self.place.seq)[...].astype(f32) + self.pair[...].astype(f32)


class Phases:
    def __init__(self, r, turns):
        self.r, self.turns = r, turns
        self.place = Place()
        self.wires = Wires(r.send, r.receive)
        self.rows, self.width = r.two.shape
        self.wide = r.rows_one.shape[1]
        self.count = self.wide // self.width
        self.devices = r.everyone.shape[0] // self.rows
        self.pair = self.devices // turns
        self.units = self.devices


    def spread_columns(self, ref, index):
        column = ref[span(index, self.rows), :].astype(jnp.int32)
        lane = lax.broadcasted_iota(jnp.int32, column.shape, 1)
        parts = [
            jnp.where(column == lane + 128 * i, 1.0, 0.0).astype(jnp.bfloat16)
            for i in range(self.rows // 128)
        ]
        return jnp.concatenate(parts, 1)

    def spread_rows(self, ref, index):
        row = ref[index]
        place = lax.broadcasted_iota(jnp.int32, (self.rows, self.rows), 0)
        return jnp.where(row == place, 1.0, 0.0).astype(jnp.bfloat16)

    def from_units(self, ref, table, index):
        return jnp.concatenate([ref[table[index, unit]] for unit in range(self.units)], 0)

    def to_units(self, index, rows):
        first, step = index * self.units, self.rows // self.units
        for unit in range(self.units):
            self.r.mid[first + unit] = rows[unit * step : (unit + 1) * step].astype(jnp.bfloat16)

    def sort_chunk(self, source, index):
        r = self.r
        here = span(index, self.rows)
        self.to_units(index, dot(self.spread_columns(r.chunk_column, index), source[here, :]))

    def sorted_block(self, index):
        r = self.r
        return dot(
            self.spread_columns(r.block_column, index), self.from_units(r.mid, r.units, index)
        )

    def unsort_block(self, source, index):
        r = self.r
        here = span(index, self.rows)
        self.to_units(index, dot(self.spread_rows(r.block_row, index), source[here, :]))

    def unsorted_chunk(self, index):
        r = self.r
        return dot(
            self.spread_rows(r.chunk_row, index), self.from_units(r.mid, r.units_back, index)
        )

    def column_of(self, row):
        pieces = [to_column(row[:, i : i + 128]) for i in range(0, self.rows, 128)]
        return jnp.concatenate(pieces, 0)

    def row_of(self, column):
        pieces = [to_row(column[i : i + 128]) for i in range(0, self.rows, 128)]
        return jnp.concatenate(pieces, 1)

    def wide_column(self, column):
        return jnp.broadcast_to(column, (self.rows, 128)).astype(jnp.int32).astype(jnp.int16)

    def line_of(self, ref, block):
        return ref[pl.ds(self.place.turn, 1), span(block, self.rows)]

    def unit_tables(self):
        r = self.r
        bf16, f32, i32 = jnp.bfloat16, jnp.float32, jnp.int32
        unit = self.rows // self.units
        row = lax.broadcasted_iota(i32, (128, 128), 0)
        column = lax.broadcasted_iota(i32, (128, 128), 1)
        by_chunk = r.shares[...].astype(bf16)
        by_block = dot(by_chunk, jnp.where(row == column, 1.0, 0.0).astype(bf16)[:8], ((0,), (0,)))
        by_block = by_block[:8].astype(bf16)
        earlier = jnp.where(row < column, 1.0, 0.0).astype(bf16)
        below = jnp.where(row > column, 1.0, 0.0).astype(bf16)[:8, :8]
        start = (column[:8] * unit).astype(f32)

        def find(share, offset, other):
            segment, move = jnp.zeros((8, 128), f32), jnp.zeros((8, 128), f32)
            ends = offset + share.astype(f32)
            for i in range(self.units):
                segment += jnp.where(ends[:, i : i + 1] <= start, 1.0, 0.0)
            for i in range(self.units):
                shift = (other - offset)[:, i : i + 1]
                move += jnp.where(segment == float(i), shift, 0.0)
            place = ((segment * self.rows + start + move) * (1.0 / unit)).astype(i32)
            return jnp.clip(place, 0, self.units * self.units - 1)

        in_chunk, in_block = dot(by_chunk, earlier), dot(below, by_chunk)
        r.unit_rows[1] = find(by_chunk, in_chunk, in_block)
        r.unit_rows[0] = find(by_block, dot(by_block, earlier), dot(below, by_block))
        copies = [
            pltpu.make_async_copy(r.unit_rows.at[i], target, r.local.at[i])
            for i, target in enumerate((r.units, r.units_back))
        ]
        for copy in copies:
            copy.start()
        for copy in copies:
            copy.wait()

    def bucket_tables(self):
        r = self.r
        f32, i32 = jnp.float32, jnp.int32
        rows = self.rows
        most = -(-(self.devices * (rows // GROUP + 1) + 1) // 128) * 128

        value = lax.broadcasted_iota(i32, (most, rows), 0)

        def count(block, until):
            return until + jnp.sum(
                jnp.where(self.line_of(r.bucket, block) <= value, 1.0, 0.0), 1, keepdims=True
            )

        until = lax.fori_loop(0, self.devices, count, jnp.zeros((most, 1), f32))
        r.until[...] = jnp.broadcast_to(until, (most, 128))

    def block_tables(self, start, stop):
        r = self.r
        bf16, f32, i32 = jnp.bfloat16, jnp.float32, jnp.int32
        rows, lines = self.rows, self.rows // 128
        tokens = rows * self.devices

        def first(block, carry):
            order = self.line_of(r.order, block)
            until = r.until[:, 0:1].astype(i32)
            lane = lax.broadcasted_iota(i32, (1, rows), 1)
            bucket = jnp.sum(
                jnp.where(until <= lane + block * rows, 1.0, 0.0), 0, keepdims=True
            )
            key = bucket * tokens + order.astype(f32)
            for i in range(lines):
                r.keys[block * lines + i] = key[:, i * 128 : (i + 1) * 128]
            chunk = order // rows
            each = lax.broadcasted_iota(i32, (8, rows), 0)
            share = jnp.sum(jnp.where(chunk == each, 1.0, 0.0), 1, keepdims=True)
            at = lax.broadcasted_iota(i32, (8, 128), 1)
            r.shares[...] += jnp.where(at == block, share, 0.0)
            place = (chunk * rows + lane).astype(f32)
            slot = jnp.sum(jnp.where(place < self.column_of(place), 1.0, 0.0), 1, keepdims=True)
            r.block_column[span(block, rows), :] = self.wide_column(slot)
            r.block_row[block] = self.row_of(slot).astype(i32)
            local = self.column_of((order - chunk * rows).astype(f32))
            high = jnp.floor(local * 0.0625)
            at = lax.broadcasted_iota(i32, (rows, 2 * HEAD_DIM), 1)
            parts = jnp.where(at == 0, high, jnp.where(at == 1, local - 16.0 * high, 0.0))
            r.round_rows[span(block, rows), :] = parts.astype(bf16)
            self.unsort_block(r.round_rows, block)
            return carry

        lax.fori_loop(start, stop, first, 0)

    def chunk_tables(self):
        r = self.r
        f32, i32 = jnp.float32, jnp.int32
        rows = self.rows

        def second(chunk, carry):
            parts = self.from_units(r.mid, r.units_back, chunk)[:, 0:128].astype(f32)
            token = 16.0 * parts[:, 0:1] + parts[:, 1:2]
            r.chunk_column[span(chunk, rows), :] = self.wide_column(token)
            r.chunk_row[chunk] = self.row_of(token).astype(i32)
            return carry

        lax.fori_loop(0, self.devices, second, 0, unroll=2)

    def codes(self, index):
        r = self.r
        tokens = self.rows * self.devices
        groups = tokens // 128
        low = lax.broadcasted_iota(jnp.int32, (1, 128), 1) < GROUP
        result = []
        for i in range(2):
            here = 2 * index + i
            keys, before = r.keys[here], r.keys[(here + groups - 1) % groups]
            query = to_column(keys)
            least = jnp.floor(query * (1.0 / tokens)) * tokens
            for half, window in enumerate((jnp.where(low, keys, before), keys)):
                at = slice(half * GROUP, (half + 1) * GROUP)
                allowed = (window <= query[at]) & (window >= least[at])
                result.append(
                    jnp.where(window == query[at], 1.0, jnp.where(allowed, 0.0, 2.0))
                )
        return jnp.concatenate(result, 0)

    def window(self, rows, block):
        before = rows[block * GROUP : (block + 1) * GROUP]
        own = rows[(block + 1) * GROUP : (block + 2) * GROUP]
        return jnp.concatenate([own, before] if block % 2 == 0 else [before, own], 0)

    def over_rows(self, ref):
        step = ref.shape[0] // self.devices
        return SeqGather(self.wires, self.place, lambda seq: rows_at(ref, seq, step))

    def over_columns(self, ref):
        step = ref.shape[1] // self.devices
        return SeqGather(self.wires, self.place, lambda seq: columns_at(ref, seq, step))

    def start_seq(self, gather, source):
        gather.start(source)
        gather.slot(self.place.seq)[...] = source[...]

    def start_head(self, gather, source):
        gather.start(source)
        gather.slot(self.place.head)[...] = source[...]

    def over_head(self, ref):
        return HeadGather(self.wires, self.place, lambda head: columns_at(ref, head, self.width))

    def project(self):
        r, place, wires = self.r, self.place, self.wires
        bf16, f32 = jnp.bfloat16, jnp.float32
        arrived = place.greet()
        half = self.devices // 2
        r.shares[...] = jnp.zeros_like(r.shares)
        self.bucket_tables()
        self.block_tables(0, half)
        arrived()
        stream = self.over_head(r.two_full)
        small = self.over_head(r.params_full)
        self.start_head(stream, r.two)
        for row, item in enumerate((r.gain_one, r.bias_one, r.gain_two, r.bias_two)):
            r.params[row : row + 1, :] = item[...]
        r.params[4:8, :] = jnp.zeros((4, self.width), f32)
        self.start_head(small, r.params)
        query, value = self.over_rows(r.query_full), self.over_rows(r.value_full)
        self.start_seq(query, r.query)
        self.start_seq(value, r.value)
        self.bulk()
        self.begin(self.merge)
        self.begin(self.expand[0])
        self.block_tables(half, self.devices)
        for weight in (query, value):
            for bits in (4, 2):
                weight.forward(bits)
        self.begin(self.expand[1])
        small.relay()
        stream.relay()
        query.forward(6)
        value.forward(6)
        small.finish()
        stream.finish()

        def normalise(tile, carry):
            here = span(tile, 128)
            rows = r.two_full[here, :].astype(f32)
            center = jnp.mean(rows, 1, keepdims=True)
            offset = rows - center
            factor = lax.rsqrt(jnp.mean(offset * offset, 1, keepdims=True) + 1e-05)
            r.center_one[here, :] = jnp.broadcast_to(center, (128, 128))
            r.factor_one[here, :] = jnp.broadcast_to(factor, (128, 128))
            r.rows_one[here, :] = (
                offset * factor * r.params_full[0:1, :] + r.params_full[1:2, :]
            ).astype(bf16)
            return carry

        lax.fori_loop(0, self.rows // 128, normalise, 0)
        self.tokens = TokenGather(self.wires, place, r.everyone, self.rows)
        self.project_one(query, r.query_full, 0)
        self.project_one(value, r.value_full, 1)

    def project_one(self, weight, full, part):
        r = self.r
        weight.finish()

        def multiply(tile, carry):
            here = span(tile, 256)
            result = dot(r.rows_one[here, :], full[...]).astype(jnp.bfloat16)
            for which in range(self.pair):
                r.packed[which, part, here, :] = result[
                    :, which * HEAD_DIM : (which + 1) * HEAD_DIM
                ]
            return carry

        lax.fori_loop(0, self.rows // 256, multiply, 0)
        self.tokens.start(r.packed, part)

    def bulk(self):
        r, place = self.r, self.place
        my_rows = rows_at(r.merge_full, place.head, r.merge.shape[0])
        self.merge = SeqGather(
            self.wires, place, lambda seq: columns_at(my_rows, seq, r.merge.shape[1])
        )
        self.merge.source = r.merge
        self.expand, self.shrink = [], []
        for part in range(2):
            step, columns = r.expand.shape[0], r.expand.shape[1] // 2
            cut = pl.ds(part * columns, columns)
            slot = lambda seq, cut=cut: rows_at(r.expand_full, seq, step).at[:, cut]
            if part:
                gather = SeqGather(self.wires, place, slot)
            else:
                both = lambda pair: rows_at(r.expand_full, pair, 2 * step).at[:, 0:columns]
                gather = PairGather(self.wires, place, slot, both)
            gather.source = r.expand.at[:, cut]
            self.expand.append(gather)
            rows, width = r.shrink.shape[0] // 2, r.shrink.shape[1]
            down = pl.ds(part * rows, rows)
            gather = SeqGather(
                self.wires,
                place,
                lambda seq, down=down: columns_at(r.shrink_full.at[down], seq, width),
            )
            gather.source = r.shrink.at[down]
            self.shrink.append(gather)
        self.one, self.grads = self.over_head(r.one_full), self.over_head(r.grad_full)

    def begin(self, gather):
        self.start_seq(gather, gather.source)

    def go_on(self, gather):
        for bits in (4, 2, 6):
            gather.forward(bits)

    def begin_streams(self):
        self.start_head(self.one, self.r.one)
        self.start_head(self.grads, self.r.grad_two)

    def begin_merge_rows(self):
        r, place = self.r, self.place
        self.merge.finish()
        self.heads = HeadGather(
            self.wires, place, lambda head: rows_at(r.merge_full, head, r.merge.shape[0])
        )
        self.heads.start(self.heads.slot(place.head))

    def sort_tokens(self):
        r, place = self.r, self.place
        bf16, f32 = jnp.bfloat16, jnp.float32
        tokens = self.tokens
        self.unit_tables()
        tokens.pass_own()
        for bits in (2, 4, 6):
            tokens.forward(bits)
        self.go_on(self.merge)
        self.go_on(self.expand[1])
        self.expand[0].along()
        self.begin_streams()
        self.begin(self.shrink[0])
        self.chunk_tables()
        self.sort_chunk(r.everyone, place.seq)
        for bits in (2, 4, 6):
            tokens.land(bits)
            self.sort_chunk(r.everyone, flipped(place.seq, bits))
        for bits in (0, 2, 4, 6):
            tokens.share(bits)
        for bits in (0, 2, 4, 6):
            tokens.land(bits + 1)
            self.sort_chunk(r.everyone, flipped(place.seq, bits + 1))
        tokens.settle()

        def second(block, carry):
            rows = self.sorted_block(block)
            here = span(block, self.rows)
            later = pl.ds(pl.multiple_of(block * self.rows + GROUP, GROUP), self.rows)
            query = rows[:, :HEAD_DIM]
            r.sorted_query[here, :] = query.astype(bf16)
            factor = lax.rsqrt(jnp.sum(query * query, 1, keepdims=True) + 1e-06)
            r.unit[later, :] = (query * factor).astype(bf16)
            r.key_value[later, :] = rows[:, HEAD_DIM:].astype(bf16)
            return carry

        lax.fori_loop(0, self.devices, second, 0, unroll=2)
        last = pl.ds(self.devices * self.rows, GROUP)
        r.unit[0:GROUP, :] = r.unit[last, :]
        r.key_value[0:GROUP, :] = r.key_value[last, :]

    def attend(self):
        r = self.r
        bf16, f32 = jnp.bfloat16, jnp.float32
        scale = HEAD_DIM ** (-0.5)
        some = 4 * GROUP

        def group(index, carry):
            here = span(index, some)
            longer = pl.ds(pl.multiple_of(index * some, some), some + GROUP)
            query, unit, value = r.sorted_query[here, :], r.unit[longer, :], r.key_value[longer, :]
            raw = [
                dot(query[i * GROUP : (i + 1) * GROUP], self.window(unit, i), ((1,), (1,)))
                for i in range(4)
            ]
            code = self.codes(index)
            scores = jnp.where(
                code == 0.0,
                jnp.concatenate(raw, 0) * scale,
                jnp.where(code == 1.0, own_score, masked_score),
            )
            peak = jnp.max(scores, 1, keepdims=True)
            power = jnp.exp(scores - peak)
            total = jnp.sum(power, 1, keepdims=True)
            probs = power * (1.0 / total)
            r.probs[here, :] = probs
            probs = probs.astype(bf16)
            result = [
                dot(probs[i * GROUP : (i + 1) * GROUP], self.window(value, i)) for i in range(4)
            ]
            r.round_rows[here, :HEAD_DIM] = jnp.concatenate(result, 0).astype(bf16)
            r.round_rows[here, HEAD_DIM:] = in_lanes(peak + jnp.log(total))
            return carry

        lax.fori_loop(0, self.devices * self.rows // some, group, 0, unroll=2)

    def return_rows(self):
        r, place, wires = self.r, self.place, self.wires
        bf16, f32 = jnp.bfloat16, jnp.float32

        def first(block, carry):
            self.unsort_block(r.round_rows, block)
            return carry

        lax.fori_loop(0, self.devices, first, 0, unroll=2)
        self.shares, self.sides = {}, []
        for half in range(self.pair):
            for bits in (3, 1, 2, 0):
                turn = flipped(place.turn, bits)
                rows = self.unsorted_chunk(place.chunk(turn, half))
                total = jnp.sum(rows[:, HEAD_DIM:], 1, keepdims=True)
                lines = [to_row(total[i : i + 128]) for i in range(0, self.rows, 128)]
                r.out[bits, half] = rows[:, :HEAD_DIM].astype(bf16)
                r.total[bits, half] = jnp.concatenate(lines, 0)
                if bits % 2:
                    self.shares[bits, half] = [
                        wires.push(
                            source.at[bits, half], target.at[bits // 2, half], place.peer(0, 1)
                        )
                        for source, target in ((r.total, r.share_total), (r.out, r.share))
                    ]
            for copy in self.shares[3, half]:
                copy.wait_recv()
            r.merged_total[half] = self.combine(
                (
                    (r.total.at[2, half], r.out.at[2, half]),
                    (r.share_total.at[1, half], r.share.at[1, half]),
                ),
                (r.merged.at[half],),
            )
            self.sides.append(
                [
                    wires.push(source.at[half], target.at[half], place.peer(1))
                    for source, target in ((r.merged_total, r.side_total), (r.merged, r.side))
                ]
            )

    def combine(self, terms, targets):
        f32 = jnp.float32
        totals = [total[...] for total, _ in terms]
        peak = totals[0]
        for total in totals[1:]:
            peak = jnp.maximum(peak, total)
        power = [jnp.exp(total - peak) for total in totals]
        joint = sum(power[1:], power[0])
        whole = peak + jnp.log(joint)
        mixes = [item / joint for item in power]
        for part in range(self.rows // 128):
            here = pl.ds(part * 128, 128)
            rows = jnp.zeros((128, HEAD_DIM), f32)
            for weight, (_, out) in zip(mixes, terms):
                mix = to_column(weight[part : part + 1, :])
                rows += mix * out[here, :].astype(f32)
            for target in targets:
                target[here, :] = rows.astype(target.dtype)
        return whole

    def mix_rounds(self):
        r, place, wires = self.r, self.place, self.wires
        mine = columns_at(r.attended_full, place.pair * 4 + place.line, HEAD_DIM)
        back = Spread(wires, place)
        self.wholes = []
        for half in range(self.pair):
            for copy in self.shares[1, half] + self.sides[half]:
                copy.wait_recv()
            r.whole_total[place.turn, half] = self.combine(
                (
                    (r.total.at[0, half], r.out.at[0, half]),
                    (r.share_total.at[0, half], r.share.at[0, half]),
                    (r.side_total.at[half], r.side.at[half]),
                ),
                (r.attended.at[half], r.attended_wide.at[half]),
            )
            back.start(lambda line: r.attended.at[line % 2], mine, half)
            whole = r.whole_total.at[place.turn, half]
            for bits in (1, 2, 3):
                self.wholes.append(wires.push(whole, whole, place.member(bits)))

        @pl.when(place.home)
        def _():
            mine[...] = r.attended[place.line % 2]

        back.finish()
        gather = self.over_head(r.attended_full)
        gather.start(gather.slot(place.head))
        gather.relay()
        gather.finish()


    def normalise_sum(self):
        r, place = self.r, self.place
        bf16, f32 = jnp.bfloat16, jnp.float32
        tile_rows = self.rows // 2
        for tile in range(2):
            here = pl.ds(tile * tile_rows, tile_rows)
            total = r.one_full[here, :].astype(f32) + dot(r.attended_full[here, :], r.merge_full[...])
            center = jnp.mean(total, 1, keepdims=True)
            offset = total - center
            factor = lax.rsqrt(jnp.mean(offset * offset, 1, keepdims=True) + 1e-05)
            normal = offset * factor
            r.tall[here, :] = total
            mine = columns_at(r.tall.at[here], place.head, self.width)
            r.result_one[here, :] = mine[...].astype(bf16)
            r.tall[here, :] = normal
            r.normal_two[here, :] = mine[...]
            r.factor_two[here, :] = jnp.broadcast_to(factor, (tile_rows, 128))
            r.rows_two[here, :] = (normal * r.params_full[2:3, :] + r.params_full[3:4, :]).astype(
                bf16
            )

    def feed_half(self, half, tile):
        r = self.r
        bf16 = jnp.bfloat16
        tile_rows, step = self.rows // 2, r.active.shape[1] // 2
        here, units = pl.ds(tile * tile_rows, tile_rows), pl.ds(half * step, step)
        hidden = dot(r.rows_two[here, :], r.expand_full[:, units])
        below = 0.5 * (1.0 + lax.erf(hidden * (0.5**0.5)))
        r.active[here, units] = (hidden * below).astype(bf16)
        slope = below + hidden * jnp.exp(-0.5 * hidden * hidden) * ((2.0 * jnp.pi) ** -0.5)
        grad = dot(r.grad_full[here, :], r.shrink_full[units, :], ((1,), (1,)))
        r.grad_hidden[here, units] = (grad * slope).astype(bf16)

    def shrink_grads(self, half):
        r = self.r
        step = r.active.shape[1] // 2
        units = pl.ds(half * step, step)
        self.weights(r.active.at[:, units], r.grad_full, r.grad_shrink.at[units])
        width = r.shrink.shape[1]
        scatter = SeqScatter(
            self.wires, self.place,
            lambda seq: columns_at(r.grad_shrink.at[units], seq, width),
            r.shrink_pair.at[:, units], r.shrink_line.at[:, units],
        )
        scatter.start()
        self.shrink_out.append(scatter)

    def feed_forward(self):
        r, place, wires = self.r, self.place, self.wires
        self.parts_two, self.shrink_out = [], []
        tile_rows = self.rows // 2
        self.normalise_sum()
        self.expand[0].finish()
        self.shrink[0].finish()
        for tile in range(2):
            self.feed_half(0, tile)
        self.shrink_grads(0)
        self.expand[1].finish()
        self.shrink[1].finish()
        for tile in range(2):
            here = pl.ds(tile * tile_rows, tile_rows)
            self.feed_half(1, tile)
            part = dot(r.grad_hidden[here, :], r.expand_full[...], ((1,), (1,)))
            self.send_part(
                tile, part, r.tall[here, :], r.params_full[2:3, :], r.part_two, r.stat_two,
                r.parts_two, self.parts_two,
            )
        for tile in range(2):
            self.relay_part(tile, r.part_two, r.parts_two, self.parts_two)
        self.send_stats(r.stat_two, r.stats_two, self.parts_two)
        self.shrink_grads(1)

    def send_part(self, tile, part, normal, gain, part_ref, stat_ref, target, copies):
        tile_rows = part.shape[0]
        here = pl.ds(tile * tile_rows, tile_rows)
        scaled = part * gain
        first = jnp.sum(scaled, 1, keepdims=True)
        second = jnp.sum(scaled * normal, 1, keepdims=True)
        lines = tile_rows // 128
        for line in range(lines):
            at = slice(line * 128, (line + 1) * 128)
            row = tile * lines + line
            stat_ref[row : row + 1, :] = to_row(first[at])
            row += self.rows // 128
            stat_ref[row : row + 1, :] = to_row(second[at])
        part_ref[here, :] = part.astype(jnp.bfloat16)
        twin = self.place.peer(0, 1)
        for slot, head in ((1, flip(twin[1], 2)), (0, twin[1])):
            source = columns_at(part_ref.at[here], head, self.width)
            copies.append(self.wires.push(source, target.at[slot, here], twin))

    def relay_part(self, tile, part_ref, target, copies):
        tile_rows = self.rows // 2
        here = pl.ds(tile * tile_rows, tile_rows)
        far = self.place.peer(0, 2)
        copies[2 * tile].wait_recv()
        mine = columns_at(part_ref.at[here], far[1], self.width)[...].astype(jnp.float32)
        total = mine + target[1, here, :].astype(jnp.float32)
        target[1, here, :] = total.astype(jnp.bfloat16)
        copies.append(self.wires.push(target.at[1, here], target.at[2, here], far))

    def send_stats(self, stat_ref, target, copies):
        for bits in (2, 3, 1):
            device = self.place.peer(0, bits)
            copies.append(self.wires.push(stat_ref, target.at[bits - 1], device))

    def norm_back(self, part_ref, parts, stat_ref, stats, normal_at, factor_ref, gain, finish):
        f32 = jnp.float32
        lines = self.rows // 128

        def piece(line, carry):
            here = span(line, 128)
            grad = columns_at(part_ref.at[here], self.place.head, self.width)[...].astype(f32)
            first, second = stat_ref[pl.ds(line, 1), :], stat_ref[pl.ds(line + lines, 1), :]
            for other in range(3):
                if other != 1:
                    grad += parts[other, here, :].astype(f32)
                first += stats[other, pl.ds(line, 1), :]
                second += stats[other, pl.ds(line + lines, 1), :]
            normal = normal_at(here)
            first, second = to_column(first) / self.wide, to_column(second) / self.wide
            finish(here, factor_ref[here, 0:1] * (grad * gain - first - normal * second))
            gains, biases = carry
            return (
                gains + jnp.sum(grad * normal, 0, keepdims=True),
                biases + jnp.sum(grad, 0, keepdims=True),
            )

        zero = jnp.zeros((1, self.width), f32)
        return lax.fori_loop(0, lines, piece, (zero, zero))

    def my_params(self, row):
        return columns_at(self.r.params_full, self.place.head, self.width)[row : row + 1, :]

    def feed_back(self):
        r, place, wires = self.r, self.place, self.wires
        bf16, f32 = jnp.bfloat16, jnp.float32
        self.weights(r.rows_two, r.grad_hidden, r.grad_expand)
        rows, half = r.expand.shape[0], r.expand.shape[1] // 2
        first, second = pl.ds(0, half), pl.ds(half, half)
        self.expand_out = [
            PairScatter(
                wires, place,
                lambda seq: rows_at(r.grad_expand, seq, rows).at[:, first],
                lambda pair: rows_at(r.grad_expand, pair, 2 * rows).at[:, first],
                r.expand_lines, r.expand_side,
            ),
            SeqScatter(
                wires, place,
                lambda seq: rows_at(r.grad_expand, seq, rows).at[:, second],
                r.expand_pair, r.expand_line,
            ),
        ]
        self.expand_out[0].start()
        for copy in self.parts_two[1:2] + self.parts_two[3:]:
            copy.wait_recv()
        wires.settle(self.parts_two)

        def finish(here, change):
            total = r.grad_one[here, :].astype(f32) + change
            r.input_grad_one[here, :] = total.astype(bf16)

        gains, biases = self.norm_back(
            r.part_two, r.parts_two, r.stat_two, r.stats_two,
            lambda here: r.normal_two[here, :], r.factor_two, self.my_params(2), finish,
        )
        r.norm_send[2:3, :], r.norm_send[3:4, :] = gains, biases
        gather = self.over_head(r.grad_rows_one)
        self.start_head(gather, r.input_grad_one)
        gather.relay()

        def feed(tile, carry):
            here = span(tile, 256)
            r.feed[here, :] = dot(r.active[here, :], r.shrink_full[...]).astype(bf16)
            return carry

        lax.fori_loop(0, self.rows // 256, feed, 0)
        gather.finish()

    def weights(self, left, right, target):
        step = min(256, left.shape[1])

        def piece(index, carry):
            columns = span(index, step)
            result = dot(left[:, columns], right[...], ((0,), (0,)))
            target[columns, :] = result.astype(jnp.bfloat16)
            return carry

        lax.fori_loop(0, left.shape[1] // step, piece, 0)

    def send_feed(self):
        r = self.r
        self.feeds = []
        for bits in (2, 3, 1):
            device = self.place.peer(0, bits)
            source = columns_at(r.feed, device[1], self.width)
            self.feeds.append(self.wires.push(source, r.feeds.at[bits - 1], device))

    def finish_feed(self):
        r = self.r
        f32 = jnp.float32
        for copy in self.feeds:
            copy.wait_recv()
        total = r.two[...].astype(f32)
        total += columns_at(r.feed, self.place.head, self.width)[...].astype(f32)
        for other in range(3):
            total += r.feeds[other].astype(f32)
        r.result_two[...] = total.astype(jnp.bfloat16)


    def grad_rounds(self):
        r, place, wires = self.r, self.place, self.wires
        bf16, f32 = jnp.bfloat16, jnp.float32
        my_rows = rows_at(r.merge_full, place.head, r.merge.shape[0])

        def attended(tile, carry):
            here = span(tile, 256)
            grad = dot(r.grad_rows_one[here, :], my_rows[...], ((1,), (1,))).astype(bf16)
            for which in range(self.pair):
                r.grad_heads[which, here, :] = grad[:, which * HEAD_DIM : (which + 1) * HEAD_DIM]
            return carry

        lax.fori_loop(0, self.rows // 256, attended, 0)
        mine = r.grad_attended.at[place.line % 2]
        there = Spread(wires, place)
        there.start(lambda line: r.grad_heads.at[line % 2], mine)

        @pl.when(place.home)
        def _():
            mine[...] = r.grad_heads[place.line % 2]

        self.shrink_out[0].along()
        self.weights(columns_at(r.attended_full, place.head, self.width), r.grad_rows_one, r.grad_merge)
        there.finish()
        self.grads_coming = []
        for half in range(self.pair):
            for part in range(self.rows // 128):
                here = pl.ds(part * 128, 128)
                rows = r.attended_wide[half, here, :] * r.grad_attended[half, here, :].astype(f32)
                r.means[place.turn, half, part : part + 1, :] = to_row(
                    jnp.sum(rows, 1, keepdims=True)
                )
            own = [item.at[place.turn, half] for item in (r.means, r.grad_outs)]
            own[1][...] = r.grad_attended[half]
            self.grads_coming.append(
                {
                    2: [wires.push(item, item, place.peer(1)) for item in own],
                    1: [wires.push(item, item, place.peer(0, 1)) for item in own],
                }
            )
        self.shrink_out[1].along()
        self.merge_out = SeqScatter(
            wires, place, lambda seq: columns_at(r.grad_merge, seq, r.merge.shape[1]),
            r.merge_pair, r.merge_line,
        )

    def sort_grads(self):
        r, place = self.r, self.place
        bf16 = jnp.bfloat16
        f32 = jnp.float32
        lines = self.rows // 128
        for copy in self.wholes:
            copy.wait_recv()
        for bits in (0, 1, 2, 3):
            turn = flipped(place.turn, bits)
            for half, coming in enumerate(self.grads_coming):
                for copy in coming.get(bits, ()):
                    copy.wait_recv()
                if bits == 2:
                    items = [item.at[turn, half] for item in (r.means, r.grad_outs)]
                    coming[3] = [self.wires.push(item, item, place.peer(0, 1)) for item in items]
                chunk = place.chunk(turn, half)

                def piece(part, carry, turn=turn, half=half, bits=bits, chunk=chunk):
                    here, line = span(part, 128), pl.ds(part, 1)
                    grad = r.grad_outs[turn, half, here, :].astype(f32)
                    out = r.out[bits, half, here, :].astype(f32)
                    mix = to_column(
                        jnp.exp(r.total[bits, half, line, :] - r.whole_total[turn, half, line, :])
                    )
                    mean = to_column(r.means[turn, half, line, :])
                    dots = jnp.sum(out * grad, 1, keepdims=True)
                    rows = span(chunk * lines + part, 128)
                    r.everyone[rows, :HEAD_DIM] = (mix * grad).astype(bf16)
                    r.everyone[rows, HEAD_DIM:] = in_lanes(mix * (dots - mean))
                    return carry

                lax.fori_loop(0, lines, piece, 0)
                self.sort_chunk(r.everyone, chunk)
        self.expand_out[1].start()
        self.merge_out.start()
        for scatter in self.shrink_out:
            scatter.across()

        def second(block, carry):
            r.round_rows[span(block, self.rows), :] = self.sorted_block(block).astype(bf16)
            return carry

        lax.fori_loop(0, self.devices, second, 0, unroll=2)

    def attend_back(self):
        r = self.r
        bf16, f32 = jnp.bfloat16, jnp.float32
        scale = HEAD_DIM ** (-0.5)
        some = 4 * GROUP
        r.grad_unit[0:GROUP, :] = jnp.zeros((GROUP, HEAD_DIM), f32)
        r.grad_value[0:GROUP, :] = jnp.zeros((GROUP, HEAD_DIM), f32)

        def one(rows, block):
            return rows[block * GROUP : (block + 1) * GROUP]

        def fold(pieces):
            owns = [piece[:GROUP] if i % 2 == 0 else piece[GROUP:] for i, piece in enumerate(pieces)]
            befores = [piece[GROUP:] if i % 2 == 0 else piece[:GROUP] for i, piece in enumerate(pieces)]
            middle = [owns[i] + befores[i + 1] for i in range(3)]
            return befores[0], jnp.concatenate(middle + [owns[3]], 0)

        def group(index, carry):
            here = span(index, some)
            longer = pl.ds(pl.multiple_of(index * some, some), some + GROUP)
            before = pl.ds(pl.multiple_of(index * some, some), GROUP)
            after = pl.ds(pl.multiple_of(index * some + GROUP, GROUP), some)
            query, unit, value = r.sorted_query[here, :], r.unit[longer, :], r.key_value[longer, :]
            grad = r.round_rows[here, :HEAD_DIM]
            total = jnp.sum(r.round_rows[here, HEAD_DIM:].astype(f32), 1, keepdims=True)
            probs = r.probs[here, :]
            low = probs.astype(bf16)
            live = jnp.where(self.codes(index) == 0.0, probs, 0.0)
            grad_probs = jnp.concatenate(
                [dot(one(grad, i), self.window(value, i), ((1,), (1,))) for i in range(4)], 0
            )
            inner = jnp.sum(probs * grad_probs, 1, keepdims=True)
            scores = (live * (grad_probs - inner + total)).astype(bf16)
            r.probs[here, :] = (
                jnp.concatenate([dot(one(scores, i), self.window(unit, i)) for i in range(4)], 0) * scale
            )
            for target, left, right, factor in (
                (r.grad_unit, scores, query, scale),
                (r.grad_value, low, grad, 1.0),
            ):
                first, rest = fold(
                    [dot(one(left, i), one(right, i), ((0,), (0,))) * factor for i in range(4)]
                )
                target[before, :] += first
                target[after, :] = rest
            return carry

        lax.fori_loop(0, self.devices * self.rows // some, group, 0, unroll=2)
        last = pl.ds(self.devices * self.rows, GROUP)
        r.grad_unit[last, :] += r.grad_unit[0:GROUP, :]
        r.grad_value[last, :] += r.grad_value[0:GROUP, :]

        def whole(index, carry):
            here = span(index, some)
            after = pl.ds(pl.multiple_of(index * some + GROUP, GROUP), some)
            query = r.sorted_query[here, :].astype(f32)
            factor = lax.rsqrt(jnp.sum(query * query, 1, keepdims=True) + 1e-06)
            unit = query * factor
            grad = r.grad_unit[after, :]
            along = jnp.sum(unit * grad, 1, keepdims=True)
            grad = r.probs[here, :] + factor * (grad - unit * along)
            r.round_rows[here, :HEAD_DIM] = grad.astype(bf16)
            r.round_rows[here, HEAD_DIM:] = r.grad_value[after, :].astype(bf16)
            return carry

        lax.fori_loop(0, self.devices * self.rows // some, whole, 0, unroll=2)

    def return_grads(self):
        r, place, wires = self.r, self.place, self.wires
        bf16, f32 = jnp.bfloat16, jnp.float32

        def first(block, carry):
            self.unsort_block(r.round_rows, block)
            return carry

        lax.fori_loop(0, self.devices, first, 0, unroll=2)
        self.backs = {}

        def rows_for(bits, half):
            return self.unsorted_chunk(place.chunk(flipped(place.turn, bits), half)).astype(bf16)

        def block(slot, half):
            return pl.ds((slot * 2 + half) * self.rows, self.rows)

        for bits in (3, 1, 2, 0):
            for half in range(self.pair):
                r.everyone[block(bits, half), :] = rows_for(bits, half)
        parts = {part: pl.ds(part * HEAD_DIM, HEAD_DIM) for part in (1, 0)}
        both = self.pair * self.rows
        shares, sides = {}, {}
        for part, columns in parts.items():
            for bits in (3, 1):
                source = r.everyone.at[pl.ds(bits * both, both), columns]
                shares[part, bits] = wires.push(
                    source, r.grad_pairs.at[bits // 2, :, columns], place.peer(0, 1)
                )
        for part, columns in parts.items():
            shares[part, 3].wait_recv()
            total = r.everyone[pl.ds(2 * both, both), columns].astype(f32)
            total += r.grad_pairs[1, :, columns].astype(f32)
            r.grad_pairs[1, :, columns] = total.astype(bf16)
            sides[part] = wires.push(
                r.grad_pairs.at[1, :, columns], r.grad_pairs.at[2, :, columns], place.peer(1)
            )
        for part, columns in parts.items():
            shares[part, 1].wait_recv()
            sides[part].wait_recv()
            for half in range(self.pair):
                rows = pl.ds(half * self.rows, self.rows)
                total = r.everyone[block(0, half), columns].astype(f32)
                total += r.grad_pairs[0, rows, columns].astype(f32)
                total += r.grad_pairs[2, rows, columns].astype(f32)
                r.grad_pair[part, half] = total.astype(bf16)
            target = r.grad_key if part else r.grad_query
            mine = columns_at(target, place.line % 2, HEAD_DIM)
            back = Spread(wires, place)
            back.start(lambda line, part=part: r.grad_pair.at[part, line % 2], mine)
            pl.when(place.home)(partial(self.keep_grad, mine, part))
            self.backs[part] = back
        self.backs[1].finish()
        self.value_weights()
        self.backs[0].finish()

    def keep_grad(self, mine, part):
        mine[...] = self.r.grad_pair[part, self.place.line % 2]

    def value_weights(self):
        r = self.r
        self.weights(r.rows_one, r.grad_key, r.grad_value_full)
        self.value_out = SeqScatter(
            self.wires, self.place,
            lambda seq: rows_at(r.grad_value_full, seq, r.value.shape[0]),
            r.value_pair, r.value_line,
        )
        self.value_out.start()

    def project_back(self):
        r, place, wires = self.r, self.place, self.wires
        bf16, f32 = jnp.bfloat16, jnp.float32
        self.weights(r.rows_one, r.grad_query, r.grad_query_full)
        self.query_out = SeqScatter(
            wires, place, lambda seq: rows_at(r.grad_query_full, seq, r.query.shape[0]),
            r.query_pair, r.query_line,
        )
        self.query_out.start()
        copies = []
        tile_rows = self.rows // 2
        for tile in range(2):
            here = pl.ds(tile * tile_rows, tile_rows)
            part = dot(r.grad_query[here, :], r.query_full[...], ((1,), (1,)))
            part += dot(r.grad_key[here, :], r.value_full[...], ((1,), (1,)))
            normal = (r.two_full[here, :].astype(f32) - r.center_one[here, 0:1]) * r.factor_one[
                here, 0:1
            ]
            self.send_part(
                tile, part, normal, r.params_full[0:1, :], r.part_one, r.stat_one,
                r.parts_one, copies,
            )
        for tile in range(2):
            self.relay_part(tile, r.part_one, r.parts_one, copies)
        self.send_stats(r.stat_one, r.stats_one, copies)
        self.value_out.along()
        self.query_out.along()
        for copy in copies[1:2] + copies[3:]:
            copy.wait_recv()

        def normal_at(here):
            rows = columns_at(r.two_full.at[here], place.head, self.width)[...].astype(f32)
            return (rows - r.center_one[here, 0:1]) * r.factor_one[here, 0:1]

        def finish(here, change):
            total = r.grad_two[here, :].astype(f32) + change
            r.input_grad_two[here, :] = total.astype(bf16)

        gains, biases = self.norm_back(
            r.part_one, r.parts_one, r.stat_one, r.stats_one, normal_at, r.factor_one,
            self.my_params(0), finish,
        )
        r.norm_send[0:1, :], r.norm_send[1:2, :] = gains, biases
        norms = [
            wires.push(r.norm_send, r.norms.at[bits - 1], place.peer(bits)) for bits in range(1, 8)
        ]
        self.value_out.across()
        self.query_out.across()
        half = r.expand.shape[1] // 2
        for part, scatter in enumerate(self.expand_out):
            scatter.finish(r.expand_part.at[:, pl.ds(part * half, half)])
        step = r.shrink.shape[0] // 2
        for half, scatter in enumerate(self.shrink_out):
            scatter.finish(r.shrink_part.at[pl.ds(half * step, step)])
        self.merge_out.finish(r.merge_part)
        self.finish_feed()
        total = r.norm_send[...]
        for bits, copy in enumerate(norms):
            copy.wait_recv()
            total += r.norms[bits]
        r.norm_grads[...] = total
        self.query_out.finish(r.query_part)
        self.value_out.finish(r.value_part)


def on_device(names, turns, *refs):
    r = SimpleNamespace(**dict(zip(names, refs)))
    r.result_one, r.result_two, r.input_grad_one, r.input_grad_two = (
        r.streams.at[i] for i in range(4)
    )
    r.query_part, r.value_part = r.projections.at[0], r.projections.at[1]
    merge_rows, shrink_rows = r.merge.shape[0], r.shrink.shape[0]
    r.merge_part = r.columns.at[pl.ds(0, merge_rows)]
    r.shrink_part = r.columns.at[pl.ds(merge_rows, shrink_rows)]
    r.feed, r.grad_expand = r.one_full, r.expand_full
    r.grad_pair, r.part_one = r.packed, r.part_two
    steps = Phases(r, turns)
    steps.project()
    steps.sort_tokens()
    steps.begin_merge_rows()
    steps.expand[0].forward()
    steps.begin(steps.shrink[1])
    steps.attend()
    steps.return_rows()
    steps.heads.relay()
    steps.go_on(steps.shrink[0])
    steps.mix_rounds()
    steps.go_on(steps.shrink[1])
    steps.one.relay()
    steps.grads.relay()
    steps.one.finish()
    steps.grads.finish()
    steps.heads.finish()
    steps.feed_forward()
    steps.feed_back()
    steps.grad_rounds()
    steps.send_feed()
    steps.expand_out[0].across()
    steps.sort_grads()
    steps.expand_out[0].side()
    steps.attend_back()
    steps.expand_out[1].along()
    steps.merge_out.along()
    steps.return_grads()
    steps.expand_out[1].across()
    steps.merge_out.across()
    steps.project_back()
    steps.wires.drain()
    assert len(steps.wires.copies) <= r.send.shape[0]


def whole(turns, arguments):
    bf16, f32 = jnp.bfloat16, jnp.float32
    heads, devices = lax.axis_size("head"), lax.axis_size("seq")
    pair = devices // turns
    rows, width = arguments["two"].shape
    tokens, wide = devices * rows, heads * width
    hidden = arguments["expand"].shape[1]
    lines = rows // 128
    shape = {name: value.shape for name, value in arguments.items()}
    results = dict(
        streams=((4, rows, width), bf16),
        projections=((2,) + shape["query"], f32),
        expand_part=(shape["expand"], f32),
        columns=((shape["merge"][0] + shape["shrink"][0], shape["merge"][1]), f32),
        norm_grads=((8, width), f32),
    )
    scratch = dict(
        params=((8, width), f32),
        keys=((tokens // 128, 1, 128), f32),
        shares=((8, 128), f32),
        unit_rows=((2, 8, 128), jnp.int32),
        until=((-(-(devices * (rows // GROUP + 1) + 1) // 128) * 128, 128), f32),
        block_row=((devices, 1, rows), jnp.int32),
        block_column=((tokens, 128), jnp.int16),
        chunk_row=((devices, 1, rows), jnp.int32),
        chunk_column=((tokens, 128), jnp.int16),
        sorted_query=((tokens, HEAD_DIM), bf16),
        unit=((tokens + GROUP, HEAD_DIM), bf16),
        key_value=((tokens + GROUP, HEAD_DIM), bf16),
        probs=((tokens, 2 * GROUP), f32),
        rows_one=((rows, wide), bf16),
        center_one=((rows, 128), f32),
        factor_one=((rows, 128), f32),
        query_full=((wide, width), bf16),
        value_full=((wide, width), bf16),
        merge_full=((wide, wide), bf16),
        expand_full=((wide, hidden), bf16),
        shrink_full=((hidden, wide), bf16),
        one_full=((rows, wide), bf16),
        two_full=((rows, wide), bf16),
        grad_full=((rows, wide), bf16),
        attended_full=((rows, wide), bf16),
        everyone=((tokens, 2 * HEAD_DIM), bf16),
        mid=((devices * devices, rows // devices, 2 * HEAD_DIM), bf16),
        params_full=((8, wide), f32),
        packed=((pair, 2, rows, HEAD_DIM), bf16),
        round_rows=((tokens, 2 * HEAD_DIM), bf16),
        attended=((pair, rows, HEAD_DIM), bf16),
        attended_wide=((pair, rows, HEAD_DIM), f32),
        out=((turns, pair, rows, HEAD_DIM), bf16),
        total=((turns, pair, lines, 128), f32),
        share=((2, pair, rows, HEAD_DIM), bf16),
        share_total=((2, pair, lines, 128), f32),
        merged=((pair, rows, HEAD_DIM), bf16),
        merged_total=((pair, lines, 128), f32),
        side=((pair, rows, HEAD_DIM), bf16),
        side_total=((pair, lines, 128), f32),
        whole_total=((turns, pair, lines, 128), f32),
        means=((turns, pair, lines, 128), f32),
        tall=((rows, wide), f32),
        normal_two=((rows, width), f32),
        factor_two=((rows, 128), f32),
        rows_two=((rows, wide), bf16),
        active=((rows, hidden), bf16),
        grad_hidden=((rows, hidden), bf16),
        part_two=((rows, wide), bf16),
        stat_two=((2 * lines, 128), f32),
        parts_two=((heads - 1, rows, width), bf16),
        stats_two=((heads - 1, 2 * lines, 128), f32),
        stat_one=((2 * lines, 128), f32),
        parts_one=((heads - 1, rows, width), bf16),
        stats_one=((heads - 1, 2 * lines, 128), f32),
        feeds=((heads - 1, rows, width), bf16),
        grad_rows_one=((rows, wide), bf16),
        grad_heads=((pair, rows, HEAD_DIM), bf16),
        grad_attended=((pair, rows, HEAD_DIM), bf16),
        grad_outs=((turns, pair, rows, HEAD_DIM), bf16),
        grad_unit=((tokens + GROUP, HEAD_DIM), f32),
        grad_value=((tokens + GROUP, HEAD_DIM), f32),
        grad_pairs=((3, pair * rows, 2 * HEAD_DIM), bf16),
        grad_query=((rows, width), bf16),
        grad_key=((rows, width), bf16),
        expand_lines=((3, 2 * shape["expand"][0], hidden // 2), bf16),
        expand_side=((shape["expand"][0], hidden // 2), bf16),
        norm_send=((8, width), f32),
        norms=((devices - 1, 8, width), f32),
    )
    for name, full in (
        ("query", (wide, width)),
        ("value", (wide, width)),
        ("merge", (width, wide)),
        ("expand", (wide, hidden)),
        ("shrink", (hidden, wide)),
    ):
        own = "grad_" + name + ("_full" if name in ("query", "value") else "")
        if name != "expand":
            scratch[own] = (full, bf16)
        height, across = shape[name]
        if name == "expand":
            across = across // 2
        scratch[name + "_pair"] = ((devices // 2, height, across), bf16)
        scratch[name + "_line"] = ((devices // 2 - 1, height, across), bf16)
    wires = dict(send=224, receive=224, local=2)
    vmem = pl.BlockSpec(memory_space=pltpu.VMEM)
    tables = dict(units=(8, 128), units_back=(8, 128))
    names = [*arguments, *results, *scratch, *tables, *wires]
    out = pl.pallas_call(
        partial(on_device, names, turns),
        out_shape=[jax.ShapeDtypeStruct(*item) for item in results.values()],
        in_specs=[vmem] * len(arguments),
        out_specs=[vmem] * len(results),
        scratch_shapes=[pltpu.VMEM(*item) for item in scratch.values()]
        + [pltpu.SMEM(item, jnp.int32) for item in tables.values()]
        + [pltpu.SemaphoreType.DMA((number,)) for number in wires.values()],
        compiler_params=pltpu.CompilerParams(
            collective_id=0, has_side_effects=True, vmem_limit_bytes=63 << 20
        ),
    )(*arguments.values())
    return SimpleNamespace(**dict(zip(results, out)))


def by_rounds(
    stream_one,
    stream_two,
    grad_one,
    grad_two,
    query_weight,
    value_weight,
    merge_weight,
    expand_weight,
    shrink_weight,
    first_gain,
    first_bias,
    second_gain,
    second_bias,
    bucket_ids,
    sort_order,
):
    arguments = dict(
        one=stream_one,
        two=stream_two,
        grad_one=grad_one,
        grad_two=grad_two,
        query=query_weight,
        value=value_weight,
        merge=merge_weight,
        expand=expand_weight,
        shrink=shrink_weight,
        gain_one=first_gain[None],
        bias_one=first_bias[None],
        gain_two=second_gain[None],
        bias_two=second_bias[None],
        bucket=bucket_ids,
        order=sort_order,
    )
    k = whole(sort_order.shape[0], arguments)
    merge_rows = merge_weight.shape[0]
    return (
        *(k.streams[i] for i in range(4)),
        k.projections[0],
        k.projections[1],
        k.columns[:merge_rows],
        k.expand_part,
        k.columns[merge_rows:],
        *(k.norm_grads[i] for i in range(4)),
    )


def solution(mesh):
    placed = (
        P("seq", "head"),
        P("seq", "head"),
        P("seq", "head"),
        P("seq", "head"),
        P("seq", "head"),
        P("seq", "head"),
        P("head", "seq"),
        P("seq", "head"),
        P("head", "seq"),
        P("head"),
        P("head"),
        P("head"),
        P("head"),
        P(),
        P(),
    )

    def local(*arguments):
        rounds = arguments[-1].shape[0]
        if mesh.shape["seq"] == HEADS == 2 * rounds and mesh.shape["head"] == rounds:
            return by_rounds(*arguments)
        return by_blocks(*arguments)

    return jax.shard_map(
        local,
        mesh=mesh,
        in_specs=placed,
        out_specs=(
            P("seq", "head"),
            P("seq", "head"),
            P("seq", "head"),
            P("seq", "head"),
            P("seq", "head"),
            P("seq", "head"),
            P("head", "seq"),
            P("seq", "head"),
            P("head", "seq"),
            P("head"),
            P("head"),
            P("head"),
            P("head"),
        ),
        check_vma=False,
    )
```
